32 devices in a mesh: dp: 8 (over z, x), heads: 2 (over y), feat: 2 (over core).
Axes of the slice: x: 2, y: 2, z: 4, core: 2. Of those that a mesh axis runs over, the one named last changes fastest.
Arguments:
- tokens: bfloat16 [4096, 1024], P(('dp', 'feat')), may hold values from -6 to 6
- qkv_weight: bfloat16 [1024, 3, 1024], P(('dp', 'feat'), None, 'heads'), may hold values from -0.1875 to 0.1875
- qkv_bias: bfloat16 [3, 16, 64], P(None, 'heads', ('dp', 'feat')), may hold values from -1.5 to 1.5
- out_weight: bfloat16 [1024, 1024], P('heads', ('dp', 'feat')), may hold values from -2 to 2
- norm_gains: bfloat16 [2, 1024], P(None, ('dp', 'feat')), may hold values from 0.099609375 to 1.8984375
- row_biases: bfloat16 [4, 1024], P(None, ('dp', 'feat')), may hold values from -2.5 to 2.5
- up_weight: bfloat16 [1024, 4096], P(('dp', 'feat'), 'heads'), may hold values from -0.1875 to 0.1875
- up_bias: bfloat16 [64, 64], P('heads', ('dp', 'feat')), may hold values from -2.5 to 2.5
- down_weight: bfloat16 [4096, 1024], P('heads', ('dp', 'feat')), may hold values from -0.09375 to 0.09375
- rpe_bias: bfloat16 [16, 1024], P('heads', ('dp', 'feat')), may hold values from -3 to 3
- omega: bfloat16 [16, 64, 64], P('heads', None, 'feat'), may hold values from -2.5 to 2.5
- bucket: int32 [8], P('dp'), may hold values from 0 to 2, as said below
- cotangent: bfloat16 [4096, 1024], P(('dp', 'feat')), may hold values from -6 to 6
Outputs:
- mixed: bfloat16 [4096, 1024], P(('dp', 'feat'))
- grad_tokens: float32 [4096, 1024], P(('dp', 'feat'))
- grad_qkv_weight: float32 [1024, 3, 1024], P(('dp', 'feat'), None, 'heads')
- grad_qkv_bias: float32 [3, 16, 64], P(None, 'heads', ('dp', 'feat'))
- grad_out_weight: float32 [1024, 1024], P('heads', ('dp', 'feat'))
- grad_norm_gains: float32 [2, 1024], P(None, ('dp', 'feat'))
- grad_row_biases: float32 [4, 1024], P(None, ('dp', 'feat'))
- grad_up_weight: float32 [1024, 4096], P(('dp', 'feat'), 'heads')
- grad_up_bias: float32 [64, 64], P('heads', ('dp', 'feat'))
- grad_down_weight: float32 [4096, 1024], P('heads', ('dp', 'feat'))
- grad_rpe_bias: float32 [16, 1024], P('heads', ('dp', 'feat'))
The draws below stay inside these ranges and needn't reach their ends.
Inputs may be any that keep to these rules, and one draw needn't show every extreme that they name: Every one of 0, 1, 2 occurs; group g holds sequences of 128 * 2**bucket[g] tokens each, end to end.
All inputs are finite; a program needn't handle non-finite values.
Results may differ from the reference program's by a relative error of at most 0.03.
Values may be sent and summed in bfloat16 or wider, within the bound.
A program may use at most 128 MiB of HBM per device.

```python
import jax
import jax.numpy as jnp
from jax import lax

D = 1024
H = 16
HEAD = 64
M = 64
FF = 4096
ROWS_GRP = 512
GROUPS = 8
FGRP = 2
TOKENS = 4096


def draw_bucket(key, part):
    key = jax.random.fold_in(key, 7)
    order = jax.random.permutation(jax.random.fold_in(key, 1), GROUPS)
    offset = jax.random.randint(jax.random.fold_in(key, 2), (), 0, 3)
    return ((order + offset) % 3).astype(jnp.int32)


def block_scale(key, shape, cuts, smallest, largest):
    loudness, own = 1.0, jax.random.fold_in(key, 6)
    for axis_at, shards_of in cuts:
        steps = jnp.exp(jax.random.uniform(jax.random.fold_in(own, axis_at), (shards_of,), jnp.float32, smallest / len(cuts), largest / len(cuts)))
        loudness = loudness * jnp.repeat(steps, shape[axis_at] // shards_of).reshape([-1 if axis == axis_at else 1 for axis in range(len(shape))])
    return loudness


def normal_values(stream_key, dims, deviation, most, cuts=(), dtype=jnp.bfloat16):
    values = jax.random.normal(stream_key, dims, jnp.float32) * deviation
    if len(cuts) > 0:
        values = block_scale(stream_key, dims, cuts, -0.22, 0.18) * values
    return jnp.clip(values, min=-most, max=most).astype(dtype)


def setup_inputs(seed: int = 0) -> dict:
    splits = jax.random.split(jax.random.key(seed), 14)
    tokens = normal_values(splits[0], (TOKENS, D), 1.0, 6.0, ((0, 16),))
    qkv_weight = normal_values(splits[1], (D, 3, D), D ** -0.5, 0.1875, ((0, 16), (2, 2)))
    qkv_bias = normal_values(splits[2], (3, H, HEAD), 0.3, 1.5, ((1, 2), (2, 16)))
    out_weight = normal_values(splits[3], (D, D), (max(1, 4 * D // ROWS_GRP)) ** -0.5, 2.0, ((0, 2), (1, 16)))
    norm_gains = jnp.clip(1.0 + 0.18 * jax.random.normal(splits[4], (2, D), jnp.float32), 0.099609375, 1.8984375).astype(jnp.bfloat16)
    row_biases = normal_values(splits[5], (4, D), 0.5, 2.5, ((1, 16),))
    up_weight = normal_values(splits[6], (D, FF), D ** -0.5, 0.1875, ((0, 16), (1, 2)))
    up_bias = normal_values(splits[7], (FF // HEAD, HEAD), 0.5, 2.5, ((0, 2), (1, 16)))
    down_weight = normal_values(splits[8], (FF, D), FF ** -0.5, 0.09375, ((0, 2), (1, 16)))
    rpe_bias = normal_values(splits[9], (H, 2 * ROWS_GRP), 0.7, 3.0, ((0, 2), (1, 16)))
    omega = normal_values(splits[10], (H, HEAD, M), 1.0, 2.5, ((0, 2), (2, 2)))
    bucket = draw_bucket(jax.random.fold_in(splits[13], 71), 0)
    cotangent = normal_values(splits[12], (TOKENS, D), 1.0, 6.0, ((0, 16),))
    return dict(tokens=tokens, qkv_weight=qkv_weight, qkv_bias=qkv_bias, out_weight=out_weight, norm_gains=norm_gains, row_biases=row_biases, up_weight=up_weight, up_bias=up_bias, down_weight=down_weight, rpe_bias=rpe_bias, omega=omega, bucket=bucket, cotangent=cotangent)


@jax.custom_vjp
def low(v):
    return lax.optimization_barrier(v.astype(jnp.bfloat16)).astype(jnp.float32)

@jax.custom_vjp
def low_back(v):
    return v

def low_keep(v):
    return (low(v), None)

def low_pass(kept, grad):
    return (grad,)

def back_keep(v):
    return (v, None)

def back_low(kept, grad):
    return (low(grad),)
low.defvjp(low_keep, low_pass)
low_back.defvjp(back_keep, back_low)

def matmul(left, right):
    return jnp.dot(left, right, precision=lax.Precision.HIGHEST, preferred_element_type=jnp.float32)

def norm_rows(values, gain, shift):
    centred = values - lax.optimization_barrier(jnp.mean(values, axis=-1, keepdims=True))
    inverse = lax.rsqrt(lax.optimization_barrier(jnp.mean(centred * centred, axis=-1, keepdims=True)) + 1e-12)
    return centred * inverse * gain + shift

def features(entries, omega_head):
    factor = HEAD ** (-0.25)
    unit = entries * lax.rsqrt(lax.optimization_barrier(jnp.mean(entries * entries, axis=-1, keepdims=True)) + 1e-06)
    logits = factor * matmul(unit, omega_head) - 0.5 * factor * factor * lax.optimization_barrier(jnp.sum(unit * unit, axis=-1, keepdims=True))
    return low(jnp.exp(low_back(logits)) * M ** (-0.5))

def head_attention(queries, keys_rows, values_rows, omega_head, rpe_head, seq_length):
    positions = jnp.arange(ROWS_GRP)
    coefficient = jnp.exp(jnp.take(rpe_head, positions[:, None] - positions[None, :] + ROWS_GRP))
    same_seq = positions[:, None] // seq_length == positions[None, :] // seq_length
    feat_query = features(queries, omega_head)
    feat_key = features(keys_rows, omega_head)
    group_width = M // FGRP
    numerator = jnp.zeros((ROWS_GRP, HEAD), jnp.float32)
    denominator = jnp.zeros((ROWS_GRP,), jnp.float32)
    for group_index in range(FGRP):
        lower = group_index * group_width
        scores = low_back(matmul(feat_query[:, lower:lower + group_width], feat_key[:, lower:lower + group_width].T))
        weights = low(jnp.where(same_seq, coefficient * scores, 0.0))
        numerator = numerator + matmul(weights, values_rows)
        denominator = denominator + lax.optimization_barrier(jnp.sum(weights, axis=-1))
    return low_back(numerator) / low_back(denominator)[:, None]

def block_forward(tokens, qkv_weight, qkv_bias, out_weight, norm_gains, row_biases, up_weight, up_bias, down_weight, rpe_bias, omega, seq_length):
    projected = matmul(tokens, qkv_weight.reshape(D, 3 * D)).reshape(ROWS_GRP, 3, D) + qkv_bias.reshape(3, D)
    qkv_rounded = low(low_back(projected))
    heads_first = qkv_rounded.reshape(ROWS_GRP, 3, H, HEAD).transpose(1, 2, 0, 3)

    def one_head(group_item):
        return jax.checkpoint(head_attention)(group_item[0], group_item[1], group_item[2], group_item[3], group_item[4], seq_length)
    attention = lax.map(one_head, (heads_first[0], heads_first[1], heads_first[2], omega, rpe_bias))
    attention = low(attention.transpose(1, 0, 2).reshape(ROWS_GRP, D))
    mixed_z = low_back(matmul(attention, out_weight) + row_biases[0])
    first_out = norm_rows(tokens + mixed_z, norm_gains[0], row_biases[1])
    pre_act = low_back(matmul(low(first_out), up_weight) + up_bias.reshape(FF))
    hidden = low(jax.nn.gelu(pre_act, approximate=False))
    ffn_out = low_back(matmul(hidden, down_weight) + row_biases[2])
    return norm_rows(first_out + ffn_out, norm_gains[1], row_biases[3])

def reference(tokens, qkv_weight, qkv_bias, out_weight, norm_gains, row_biases, up_weight, up_bias, down_weight, rpe_bias, omega, bucket, cotangent):
    params = tuple((param.astype(jnp.float32) for param in (qkv_weight, qkv_bias, out_weight, norm_gains, row_biases, up_weight, up_bias, down_weight, rpe_bias)))
    omega_wide = omega.astype(jnp.float32)
    token_groups = tokens.astype(jnp.float32).reshape(GROUPS, ROWS_GRP, D)
    cot_groups = cotangent.astype(jnp.float32).reshape(GROUPS, ROWS_GRP, D)
    seq_lengths = ROWS_GRP // 4 * jnp.where(bucket == 0, 1, jnp.where(bucket == 1, 2, 4))

    def group_step(totals, group_item):
        group_tokens, group_cot, seq_length = group_item

        def forward(inputs_rows, *weights):
            return block_forward(inputs_rows, *weights, omega_wide, seq_length)
        result, pull = jax.vjp(forward, group_tokens, *params)
        gradients = pull(group_cot)
        totals = tuple((total + gradient for total, gradient in zip(totals, gradients[1:])))
        return (totals, (result.astype(jnp.bfloat16), gradients[0]))
    start_totals = tuple((jnp.zeros_like(param) for param in params))
    totals, (mixed_rows, grad_rows) = lax.scan(group_step, start_totals, (token_groups, cot_groups, seq_lengths))
    return (mixed_rows.reshape(TOKENS, D), grad_rows.reshape(TOKENS, D), totals[0], totals[1], totals[2], totals[3], totals[4], totals[5], totals[6], totals[7], totals[8])
```

```python
import functools

import jax
import jax.numpy as jnp
from jax import lax
from jax.experimental import pallas as pl
from jax.experimental.pallas import tpu as pltpu
from jax.sharding import PartitionSpec as P

HEAD = 64
M = 64


EPSILON = 1e-12
UNIT_EPS = 1e-06


def toeplitz_block(window, extent):
    leading = window.shape[0]
    tiled_rows = jnp.broadcast_to(window[:, None, :], (leading, extent, 2 * extent - 1)).reshape(
        leading, -1
    )
    padded = jnp.pad(tiled_rows, ((0, 0), (0, extent)))
    sheared = padded.reshape(leading, extent, 2 * extent)[:, :, :extent]
    return sheared[:, :, ::-1]


def diagonal_sums(values_grid, extent):
    leading = values_grid.shape[0]
    flipped = values_grid[:, :, ::-1]
    padded = jnp.pad(flipped, ((0, 0), (0, 0), (0, extent))).reshape(leading, -1)
    sheared = padded[:, : extent * (2 * extent - 1)].reshape(leading, extent, 2 * extent - 1)
    return jnp.sum(sheared, axis=1)


def norm_forward(values, gain, shift):
    centred = values - jnp.mean(values, axis=-1, keepdims=True)
    inverse = lax.rsqrt(jnp.mean(centred * centred, axis=-1, keepdims=True) + EPSILON)
    normed = centred * inverse
    return (normed * gain + shift, normed, inverse)


def norm_backward(upstream, normed, inverse, gain):
    scaled_grad = upstream * gain
    return inverse * (
        scaled_grad
        - jnp.mean(scaled_grad, axis=-1, keepdims=True)
        - normed * jnp.mean(scaled_grad * normed, axis=-1, keepdims=True)
    )


def feature_logits(entries, omega_local):
    factor = HEAD ** (-0.25)
    wide = entries.astype(jnp.float32)
    inverse = lax.rsqrt(jnp.mean(wide * wide, axis=-1, keepdims=True) + UNIT_EPS)
    unit = wide * inverse
    projected = jnp.einsum(
        "rhe,hem->hmr",
        unit,
        omega_local.astype(jnp.float32),
        precision=lax.Precision.HIGHEST,
        preferred_element_type=jnp.float32,
    )
    squares = jnp.sum(unit * unit, axis=-1)
    return (factor * projected - 0.5 * factor * factor * squares.T[:, None, :], unit, inverse)


def feature_back(grad_phi, logits, unit, inverse, omega_local):
    factor = HEAD ** (-0.25)
    grad_logits = (grad_phi * (jnp.exp(logits) * M ** (-0.5))).astype(jnp.bfloat16)
    projected = jnp.einsum(
        "hmr,hem->rhe", grad_logits, omega_local, preferred_element_type=jnp.float32
    )
    totals = jnp.sum(grad_logits.astype(jnp.float32), axis=1)
    grad_unit = factor * projected - factor * factor * totals.T[:, :, None] * unit
    return inverse * (grad_unit - unit * jnp.mean(grad_unit * unit, axis=-1, keepdims=True))


def window_begin(row_start, col_start, extent, rows_total):
    return row_start - col_start + rows_total - extent + 1


def block_coeff(rpe_exp, window_start, extent):
    window = lax.dynamic_slice_in_dim(rpe_exp, window_start, 2 * extent - 1, 1)
    return toeplitz_block(window, extent)


def local(
    tokens,
    qkv_weight,
    qkv_bias,
    out_weight,
    norm_gains,
    row_biases,
    up_weight,
    up_bias,
    down_weight,
    rpe_bias,
    omega,
    bucket,
    cotangent,
):
    qkv_full, out_full, up_full, down_full, gains_all, biases_all, bias_qkv, bias_up, rpe_all = (
        lax.all_gather(qkv_weight, ("dp", "feat"), axis=0, tiled=True),
        lax.all_gather(out_weight, ("dp", "feat"), axis=1, tiled=True),
        lax.all_gather(up_weight, ("dp", "feat"), axis=0, tiled=True),
        lax.all_gather(down_weight, ("dp", "feat"), axis=1, tiled=True),
        lax.all_gather(norm_gains, ("dp", "feat"), axis=1, tiled=True),
        lax.all_gather(row_biases, ("dp", "feat"), axis=1, tiled=True),
        lax.all_gather(qkv_bias, ("dp", "feat"), axis=2, tiled=True),
        lax.all_gather(up_bias, ("dp", "feat"), axis=1, tiled=True),
        lax.all_gather(rpe_bias, ("dp", "feat"), axis=1, tiled=True),
    )
    model_width = qkv_full.shape[0]
    head_cols = qkv_full.shape[2]
    local_heads = omega.shape[0]
    local_feats = omega.shape[2]
    rows_own = tokens.shape[0]
    rows_total = rows_own * lax.axis_size("feat")
    block_rows = min(512, rows_total // 4)
    blocks = rows_total // block_rows
    seq_length = rows_total // 4 * jnp.where(bucket[0] == 0, 1, jnp.where(bucket[0] == 1, 2, 4))
    block_count = seq_length // block_rows
    gain_rows = gains_all.astype(jnp.float32)
    bias_rows = biases_all.astype(jnp.float32)
    rpe_exp = jnp.exp(rpe_all.astype(jnp.float32))
    projected = jnp.dot(
        tokens, qkv_full.reshape(model_width, 3 * head_cols), preferred_element_type=jnp.float32
    )
    projected = projected + bias_qkv.reshape(-1).astype(jnp.float32)
    qkv_own = projected.astype(jnp.bfloat16)
    qkv_all = lax.all_gather(qkv_own, "feat", axis=0, tiled=True).reshape(
        rows_total, 3, local_heads, HEAD
    )
    queries = qkv_all[:, 0]
    keys_rows = qkv_all[:, 1]
    values_rows = qkv_all[:, 2]
    logits_query, unit_query, inverse_query = feature_logits(queries, omega)
    logits_key, unit_key, inverse_key = feature_logits(keys_rows, omega)
    feat_query = (jnp.exp(logits_query) * M ** (-0.5)).astype(jnp.bfloat16)
    feat_key = (jnp.exp(logits_key) * M ** (-0.5)).astype(jnp.bfloat16)
    numer_parts = []
    denom_parts = []
    for row_block in range(blocks):
        row_start = row_block * block_rows
        first_block = row_start // seq_length * block_count
        phi_rows = feat_query[:, :, row_start : row_start + block_rows]

        def visit(column_block, carried, phi_rows=phi_rows, row_start=row_start):
            numer_acc, denom_acc = carried
            col_start = column_block * block_rows
            phi_cols = lax.dynamic_slice_in_dim(feat_key, col_start, block_rows, 2)
            value_cols = lax.dynamic_slice_in_dim(values_rows, col_start, block_rows, 0)
            coefficient = block_coeff(
                rpe_exp, window_begin(row_start, col_start, block_rows, rows_total), block_rows
            )
            scores = jnp.einsum(
                "hmi,hmj->hij", phi_rows, phi_cols, preferred_element_type=jnp.float32
            )
            weights = (coefficient * scores).astype(jnp.bfloat16)
            numer_acc = numer_acc + jnp.einsum(
                "hij,jhe->ihe", weights, value_cols, preferred_element_type=jnp.float32
            )
            denom_acc = denom_acc + jnp.sum(weights.astype(jnp.float32), axis=-1)
            return (numer_acc, denom_acc)

        start_pair = (
            jnp.zeros((block_rows, local_heads, HEAD), jnp.float32),
            jnp.zeros((local_heads, block_rows), jnp.float32),
        )
        numer_block, denom_block = lax.fori_loop(
            first_block, first_block + block_count, visit, start_pair
        )
        numer_parts.append(numer_block)
        denom_parts.append(denom_block)
    numer_all = jnp.concatenate(numer_parts, axis=0).reshape(rows_total, head_cols)
    denom_all = jnp.concatenate(denom_parts, axis=1)
    numer_own, denom_own = (
        lax.psum_scatter(
            numer_all.astype(jnp.bfloat16), "feat", scatter_dimension=0, tiled=True
        ).astype(jnp.float32),
        lax.psum_scatter(
            denom_all.astype(jnp.bfloat16), "feat", scatter_dimension=1, tiled=True
        ).astype(jnp.float32),
    )
    denom_rows = denom_own.T
    quotient = numer_own.reshape(rows_own, local_heads, HEAD) / denom_rows[:, :, None]
    attn_low = quotient.reshape(rows_own, head_cols).astype(jnp.bfloat16)
    z_part = jnp.dot(attn_low, out_full, preferred_element_type=jnp.float32)
    mixed_z = lax.psum(z_part.astype(jnp.bfloat16), "heads").astype(jnp.float32) + bias_rows[0]
    first_out, normed_one, inverse_one = norm_forward(
        tokens.astype(jnp.float32) + mixed_z, gain_rows[0], bias_rows[1]
    )
    first_low = first_out.astype(jnp.bfloat16)
    pre_act = jnp.dot(first_low, up_full, preferred_element_type=jnp.float32) + bias_up.reshape(
        -1
    ).astype(jnp.float32)
    act_value, act_pull = jax.vjp(lambda inner: jax.nn.gelu(inner, approximate=False), pre_act)
    act_low = act_value.astype(jnp.bfloat16)
    ffn_part = jnp.dot(act_low, down_full, preferred_element_type=jnp.float32)
    ffn_out = lax.psum(ffn_part.astype(jnp.bfloat16), "heads").astype(jnp.float32) + bias_rows[2]
    final_rows, normed_two, inverse_two = norm_forward(
        first_out + ffn_out, gain_rows[1], bias_rows[3]
    )
    mixed = final_rows.astype(jnp.bfloat16)
    qkv_full, out_full, up_full, down_full, gains_all, rpe_all = (
        lax.all_gather(qkv_weight, ("dp", "feat"), axis=0, tiled=True),
        lax.all_gather(out_weight, ("dp", "feat"), axis=1, tiled=True),
        lax.all_gather(up_weight, ("dp", "feat"), axis=0, tiled=True),
        lax.all_gather(down_weight, ("dp", "feat"), axis=1, tiled=True),
        lax.all_gather(norm_gains, ("dp", "feat"), axis=1, tiled=True),
        lax.all_gather(rpe_bias, ("dp", "feat"), axis=1, tiled=True),
    )
    gain_rows = gains_all.astype(jnp.float32)
    rpe_exp = jnp.exp(rpe_all.astype(jnp.float32))
    upstream = cotangent.astype(jnp.float32)
    grad_gain_two = jnp.sum(upstream * normed_two, axis=0)
    grad_shift_two = jnp.sum(upstream, axis=0)
    resid_two = norm_backward(upstream, normed_two, inverse_two, gain_rows[1])
    resid_low = resid_two.astype(jnp.bfloat16)
    grad_bias_down = jnp.sum(resid_low.astype(jnp.float32), axis=0)
    grad_down = jnp.einsum("rf,rd->fd", act_low, resid_low, preferred_element_type=jnp.float32)
    grad_act = jnp.einsum("rd,fd->rf", resid_low, down_full, preferred_element_type=jnp.float32)
    grad_pre = act_pull(grad_act)[0].astype(jnp.bfloat16)
    grad_up = jnp.einsum("rd,rf->df", first_low, grad_pre, preferred_element_type=jnp.float32)
    grad_bias_up = jnp.sum(grad_pre.astype(jnp.float32), axis=0).reshape(bias_up.shape)
    first_back = lax.psum(
        jnp.einsum("rf,df->rd", grad_pre, up_full, preferred_element_type=jnp.float32).astype(
            jnp.bfloat16
        ),
        "heads",
    ).astype(jnp.float32)
    grad_first = resid_two + first_back
    grad_gain_one = jnp.sum(grad_first * normed_one, axis=0)
    grad_shift_one = jnp.sum(grad_first, axis=0)
    resid_one = norm_backward(grad_first, normed_one, inverse_one, gain_rows[0])
    resid_one_low = resid_one.astype(jnp.bfloat16)
    grad_bias_out = jnp.sum(resid_one_low.astype(jnp.float32), axis=0)
    grad_out = jnp.einsum("rc,rd->cd", attn_low, resid_one_low, preferred_element_type=jnp.float32)
    grad_attn = jnp.einsum(
        "rd,cd->rc", resid_one_low, out_full, preferred_element_type=jnp.float32
    ).reshape(rows_own, local_heads, HEAD)
    grad_numer = (grad_attn / denom_rows[:, :, None]).astype(jnp.bfloat16)
    grad_denom = (-jnp.sum(grad_attn * quotient, axis=-1) / denom_rows).astype(jnp.bfloat16)
    numer_grad_all, denom_grad_all = (
        lax.all_gather(grad_numer.reshape(rows_own, head_cols), "feat", axis=0, tiled=True),
        lax.all_gather(grad_denom.T, "feat", axis=1, tiled=True),
    )
    numer_grad_all = numer_grad_all.reshape(rows_total, local_heads, HEAD)
    dphi_key = jnp.zeros((local_heads, local_feats, rows_total), jnp.float32)
    dvalues = jnp.zeros((rows_total, local_heads, HEAD), jnp.float32)
    grad_rpe = jnp.zeros(rpe_exp.shape, jnp.float32)
    dquery_parts = []
    for row_block in range(blocks):
        row_start = row_block * block_rows
        first_block = row_start // seq_length * block_count
        phi_rows = feat_query[:, :, row_start : row_start + block_rows]
        numer_rows = numer_grad_all[row_start : row_start + block_rows]
        denom_cols = denom_grad_all[:, row_start : row_start + block_rows].astype(jnp.float32)

        def visit_back(
            column_block,
            carried,
            phi_rows=phi_rows,
            row_start=row_start,
            numer_rows=numer_rows,
            denom_cols=denom_cols,
        ):
            dquery_acc, dkey_all, dvalue_all, drpe_all = carried
            col_start = column_block * block_rows
            phi_cols = lax.dynamic_slice_in_dim(feat_key, col_start, block_rows, 2)
            value_cols = lax.dynamic_slice_in_dim(values_rows, col_start, block_rows, 0)
            window_start = window_begin(row_start, col_start, block_rows, rows_total)
            coefficient = block_coeff(rpe_exp, window_start, block_rows)
            scores = jnp.einsum(
                "hmi,hmj->hij", phi_rows, phi_cols, preferred_element_type=jnp.float32
            )
            weights = (coefficient * scores).astype(jnp.bfloat16)
            grad_weights = (
                jnp.einsum(
                    "ihe,jhe->hij", numer_rows, value_cols, preferred_element_type=jnp.float32
                )
                + denom_cols[:, :, None]
            )
            dvalue_block = jnp.einsum(
                "hij,ihe->jhe", weights, numer_rows, preferred_element_type=jnp.float32
            )
            dvalue_all = lax.dynamic_update_slice_in_dim(
                dvalue_all,
                lax.dynamic_slice_in_dim(dvalue_all, col_start, block_rows, 0) + dvalue_block,
                col_start,
                0,
            )
            grad_scores = (grad_weights * coefficient).astype(jnp.bfloat16)
            diagonal = diagonal_sums(grad_weights * scores * coefficient, block_rows)
            drpe_all = lax.dynamic_update_slice_in_dim(
                drpe_all,
                lax.dynamic_slice_in_dim(drpe_all, window_start, 2 * block_rows - 1, 1) + diagonal,
                window_start,
                1,
            )
            dquery_acc = dquery_acc + jnp.einsum(
                "hij,hmj->hmi", grad_scores, phi_cols, preferred_element_type=jnp.float32
            )
            dkey_block = jnp.einsum(
                "hij,hmi->hmj", grad_scores, phi_rows, preferred_element_type=jnp.float32
            )
            dkey_all = lax.dynamic_update_slice_in_dim(
                dkey_all,
                lax.dynamic_slice_in_dim(dkey_all, col_start, block_rows, 2) + dkey_block,
                col_start,
                2,
            )
            return (dquery_acc, dkey_all, dvalue_all, drpe_all)

        start_state = (
            jnp.zeros((local_heads, local_feats, block_rows), jnp.float32),
            dphi_key,
            dvalues,
            grad_rpe,
        )
        dquery_block, dphi_key, dvalues, grad_rpe = lax.fori_loop(
            first_block, first_block + block_count, visit_back, start_state
        )
        dquery_parts.append(dquery_block)
    dphi_query = jnp.concatenate(dquery_parts, axis=2)
    grad_query = feature_back(dphi_query, logits_query, unit_query, inverse_query, omega)
    grad_key = feature_back(dphi_key, logits_key, unit_key, inverse_key, omega)
    grad_qkv_all = jnp.stack((grad_query, grad_key, dvalues), axis=1).reshape(
        rows_total, 3 * head_cols
    )
    grad_qkv_own = lax.psum_scatter(
        grad_qkv_all.astype(jnp.bfloat16), "feat", scatter_dimension=0, tiled=True
    )
    grad_bias_qkv = jnp.sum(grad_qkv_own.astype(jnp.float32), axis=0).reshape(bias_qkv.shape)
    grad_qkv_weight = jnp.einsum(
        "rd,rc->dc", tokens, grad_qkv_own, preferred_element_type=jnp.float32
    ).reshape(qkv_full.shape)
    input_terms = jnp.einsum(
        "rc,dc->rd",
        grad_qkv_own,
        qkv_full.reshape(model_width, 3 * head_cols),
        preferred_element_type=jnp.float32,
    )
    grad_tokens = resid_one + lax.psum(input_terms.astype(jnp.bfloat16), "heads").astype(
        jnp.float32
    )
    grad_gains = jnp.stack((grad_gain_one, grad_gain_two), axis=0)
    grad_shifts = jnp.stack((grad_bias_out, grad_shift_one, grad_bias_down, grad_shift_two), axis=0)
    (
        sent_qkv,
        sent_out,
        sent_up,
        sent_down,
        sent_gains,
        sent_shifts,
        sent_bias_qkv,
        sent_bias_up,
        sent_rpe,
    ) = (
        lax.psum_scatter(
            grad_qkv_weight.astype(jnp.bfloat16), ("dp", "feat"), scatter_dimension=0, tiled=True
        ).astype(jnp.float32),
        lax.psum_scatter(
            grad_out.astype(jnp.bfloat16), ("dp", "feat"), scatter_dimension=1, tiled=True
        ).astype(jnp.float32),
        lax.psum_scatter(
            grad_up.astype(jnp.bfloat16), ("dp", "feat"), scatter_dimension=0, tiled=True
        ).astype(jnp.float32),
        lax.psum_scatter(
            grad_down.astype(jnp.bfloat16), ("dp", "feat"), scatter_dimension=1, tiled=True
        ).astype(jnp.float32),
        lax.psum_scatter(
            grad_gains.astype(jnp.bfloat16), ("dp", "feat"), scatter_dimension=1, tiled=True
        ).astype(jnp.float32),
        lax.psum_scatter(
            grad_shifts.astype(jnp.bfloat16), ("dp", "feat"), scatter_dimension=1, tiled=True
        ).astype(jnp.float32),
        lax.psum_scatter(
            grad_bias_qkv.astype(jnp.bfloat16), ("dp", "feat"), scatter_dimension=2, tiled=True
        ).astype(jnp.float32),
        lax.psum_scatter(
            grad_bias_up.astype(jnp.bfloat16), ("dp", "feat"), scatter_dimension=1, tiled=True
        ).astype(jnp.float32),
        lax.psum_scatter(
            grad_rpe.astype(jnp.bfloat16), ("dp", "feat"), scatter_dimension=1, tiled=True
        ).astype(jnp.float32),
    )
    return (
        mixed,
        grad_tokens,
        sent_qkv,
        sent_bias_qkv,
        sent_out,
        sent_gains,
        sent_shifts,
        sent_up,
        sent_bias_up,
        sent_down,
        sent_rpe,
    )


MESH = pl.DeviceIdType.MESH
PLANES = 4
F32 = jnp.float32
BF16 = jnp.bfloat16
SCALE = HEAD ** (-0.25)
NT = (((1,), (1,)), ((), ()))
TN = (((0,), (0,)), ((), ()))
NN = (((1,), (0,)), ((), ()))


def dot(left, right, dims=NN):
    return lax.dot_general(left, right, dims, preferred_element_type=F32)


def split_dot(left, right, dims=NN):
    high = left.astype(BF16)
    rest = (left - high.astype(F32)).astype(BF16)
    return dot(high, right, dims) + dot(rest, right, dims)


def iota(shape, axis):
    return lax.broadcasted_iota(jnp.int32, shape, axis)


class Sems:
    def __init__(self):
        self.used = 0

    def take(self, count=1):
        first = self.used
        self.used += count
        return first


def layer_kernel(
    tok, cot, wq_in, wo_in, wu_in, wd_in, small_in, omega_in,
    mixed_o, gtok_o, gq_o, go_o, gu_o, gd_o, dvec_o, tvec_o,
    wq, wo, wu, wd, small, om2, xg, cotb,
    qkv, phi, ex, unit, inv, r0, pp, num, den, quo, att,
    pb, rb_z, rb_f, rb_d, rb_i, fb, hid, dgel, efb, dub, dzb,
    fst, n1, i1, dr,
    dn, dd, ds_, gg, dph, dvv, dqkv, anti, ones64, rows_v,
    g_q, g_o, g_u, g_d, r1_q, r1_o, r1_u, r1_d, t_q, t_o, t_u, t_d,
    rz_q, rz_o, rz_u, rz_d, cb_q, cb_o, cb_u, cb_d, fs, xs, xr_q, xr_o, xr_u, xr_d,
    sd, sd_r, st, st_r, mix_s, mix_r, gt_s, gt_r,
    ss, rs,
):
    dp, y, c = lax.axis_index("dp"), lax.axis_index("heads"), lax.axis_index("feat")
    z, x = dp // 2, dp % 2
    sems = Sems()
    pending = []

    def dev(zz, xx, yy, cc):
        return {"dp": zz * 2 + xx, "heads": yy, "feat": cc}

    sib, xn, yn, dg = dev(z, x, y, 1 - c), dev(z, 1 - x, y, c), dev(z, x, 1 - y, c), dev(z, 1 - x, 1 - y, c)
    xs_dev, ds_dev = dev(z, 1 - x, y, 1 - c), dev(z, 1 - x, 1 - y, 1 - c)
    plane = (dg, xn, yn)
    own_block = 2 * x + y
    plane_block = (2 * (1 - x) + 1 - y, 2 * (1 - x) + y, 2 * x + 1 - y)

    def rc(src, dst, s, r, device):
        return pltpu.make_async_remote_copy(
            src_ref=src, dst_ref=dst, send_sem=ss.at[s], recv_sem=rs.at[r], device_id=device, device_id_type=MESH
        )

    def send(src, dst, s, r, device, cond=None):
        def go():
            rc(src, dst, s, r, device).start()

        def done():
            rc(src, dst, s, r, device).wait_send()

        if cond is None:
            go()
            pending.append(done)
        else:
            pl.when(cond)(go)
            pending.append(lambda: pl.when(cond)(done))

    def got(dst, r):
        rc(dst, dst, r, r, sib).wait_recv()

    def valid(dz):
        return jnp.logical_and(z + dz >= 0, z + dz < PLANES)

    barrier = pltpu.get_barrier_semaphore()
    for other in (sib, xn, yn, dg, xs_dev, ds_dev):
        pl.semaphore_signal(barrier, inc=1, device_id=other, device_id_type=MESH)
    for zz in range(PLANES):
        @pl.when(z != zz)
        def _(zz=zz):
            pl.semaphore_signal(barrier, inc=1, device_id=dev(zz, x, y, c), device_id_type=MESH)
    pl.semaphore_wait(barrier, 9)

    class Item:
        def __init__(self, ref, kind):
            self.ref, self.kind = ref, kind
            self.zs, self.fw, self.sb = sems.take(PLANES), sems.take(), sems.take(PLANES)

        def block(self, zz, cc):
            if self.kind == "both":
                return self.ref.at[pl.ds(2 * zz, 2), cc]
            return self.ref.at[2 * zz + (x if self.kind == "own" else 1 - x), cc]

        def start(self):
            mine = self.block(z, c)
            for dz in (1, -1, 2, -2):
                send(mine, mine, self.zs + z + dz, self.zs + z, dev(z + dz, x, y, c), valid(dz))
            send(mine, mine, self.sb + z, self.sb + z, sib)

        def pump(self):
            for dz in (1, -1, 2, -2, 3, -3):
                here = self.block(z + dz, c)
                cond = valid(dz)
                pl.when(cond)(lambda here=here, dz=dz: got(here, self.zs + z + dz))
                if dz == 2:
                    send(here, here, self.fw, self.zs + z + dz, dev(z - 1, x, y, c), z == 1)
                if dz == -2:
                    send(here, here, self.fw, self.zs + z + dz, dev(z + 1, x, y, c), z == 2)
                send(here, here, self.sb + z + dz, self.sb + z + dz, sib, cond)

        def need(self):
            for zz in range(PLANES):
                got(self.block(zz, 1 - c), self.sb + zz)

    def weight(ref, rows=None):
        return ref

    half_of = {}

    def give_half(name, src, ref):
        i = sems.take()
        half_of[name] = (ref, i)
        ref[2 * z + x, c] = src[x]
        send(src.at[1 - x], ref.at[2 * z + x, c], i, i, xn)

    def have_half(name):
        ref, i = half_of[name]
        got(ref.at[2 * z + 1 - x, c], i)

    give_half("q", wq_in, wq)
    it_qa, it_s, it_qb = Item(wq, "own"), Item(small, "both"), Item(wq, "other")
    it_o, it_u, it_d = Item(wo, "both"), Item(wu, "both"), Item(wd, "both")
    it_qa.start()
    give_half("s", small_in, small)
    i_om = sems.take()
    send(omega_in, om2, i_om, i_om, sib)
    t1, t2 = sems.take(), sems.take(2)
    mine_rows = xg.at[pl.ds(c * 256, 256)]
    send(tok, mine_rows, t1, t1, sib, c != x)
    send(tok, mine_rows, t2 + c, t2 + c, dev(z, 1 - x, y, x))
    give_half("o", wo_in, wo)
    give_half("u", wu_in, wu)
    give_half("d", wd_in, wd)
    t3 = sems.take()
    cot_part = cot.at[pl.ds(pl.multiple_of(y * 128, 128), 128)]
    send(cot_part, cotb, t3, t3, xs_dev, c != x)

    @pl.when(c == x)
    def _():
        xg[pl.ds(pl.multiple_of(c * 256, 256), 256)] = tok[...]
        cotb[...] = cot[pl.ds(pl.multiple_of(y * 128, 128), 128)]

    same = (iota((256, 256), 0) // HEAD) == (iota((256, 256), 1) // HEAD)
    ones64[...] = jnp.where(same, 1.0, 0.0).astype(BF16)
    anti[...] = jnp.where(iota((512, 512), 0) + iota((512, 512), 1) == 511, 1.0, 0.0).astype(BF16)

    have_half("s")
    it_s.start()
    have_half("q")
    it_qb.start()
    it_qa.pump()
    have_half("o")
    it_o.start()
    it_s.pump()
    it_qb.pump()

    it_s.need()
    for t in range(8):
        tile = small[t, 0].astype(F32) + small[t, 1].astype(F32)
        rows_v[0:8, t * 128 : (t + 1) * 128] = tile[0:8]
        rows_v[8:16, (7 - t) * 128 : (8 - t) * 128] = tile[8:16]
        total = tile[16:32] if t == 0 else total + tile[16:32]
    for r in range(6):
        rows_v[16:17, r * 128 : (r + 1) * 128] = total[r : r + 1]
    for r in range(8):
        rows_v[17:18, r * 128 : (r + 1) * 128] = total[8 + r : 9 + r]
    level = small[2 * z + c, 0][6:7].astype(F32)
    wide1 = jnp.where(level > 0.5, 1.0, 0.0)
    wide2 = jnp.where(level > 1.5, 1.0, 0.0)
    one_row = jnp.ones((1, 128), F32)

    def mask_row(bi):
        parts = [one_row if bj == bi else (wide1 if bj // 2 == bi // 2 else wide2) for bj in range(4)]
        return jnp.concatenate(parts, axis=1)

    masks = [mask_row(bi) for bi in range(4)]

    def coeff_body(h, carry):
        row = jnp.exp(rows_v[pl.ds(8 + h, 1), :])
        r0[h] = pltpu.roll(jnp.broadcast_to(row, (128, 1024)), 1, 1, stride=1, stride_axis=0)
        return carry

    lax.fori_loop(0, 4, coeff_body, 0)

    have_half("u")
    it_u.start()
    pl.when(c == x)(lambda: got(xg.at[pl.ds(pl.multiple_of((1 - c) * 256, 256), 256)], t1))

    @pl.when(c != x)
    def _():
        got(xg.at[pl.ds(0, 256)], t2)
        got(xg.at[pl.ds(256, 256)], t2 + 1)
        got(cotb, t3)

    it_qa.need()
    it_qb.need()

    def qkv_body(p, carry):
        cols = pl.ds(pl.multiple_of(p * 256, 256), 256)
        qkv[p] = (dot(xg[...], wq[:, :, :, cols].reshape(1024, 256)) + rows_v[16:17, cols]).astype(BF16)
        return carry

    lax.fori_loop(0, 3, qkv_body, 0)
    got(om2, i_om)
    om2[...] = om2[...] + omega_in[...]

    def feature_body(t, carry):
        wide = qkv[t].astype(F32)
        sums = split_dot(wide * wide, ones64[...])
        inverse = lax.rsqrt(sums * (1.0 / HEAD) + UNIT_EPS)
        units = wide * inverse
        logits = SCALE * split_dot(units, om2[...]) - 0.5 * SCALE * SCALE * (sums * inverse * inverse)
        value = jnp.exp(logits) * M ** (-0.5)
        ex[t] = value
        unit[t] = units
        inv[t] = inverse
        phi[t] = value.astype(BF16)
        return carry

    lax.fori_loop(0, 2, feature_body, 0)
    have_half("d")
    it_d.start()
    it_o.pump()

    lane_head = iota((1, 128), 1) // HEAD
    num[...] = jnp.zeros_like(num)
    den[...] = jnp.zeros_like(den)

    def head_cols(h):
        return pl.ds(pl.multiple_of((h // 2) * 128, 128), 128), (lane_head == h % 2)

    def head_body(h, carry):
        cols, mine = head_cols(h)
        keep = jnp.where(mine, 1.0, 0.0).astype(BF16)
        scores = dot(phi[0, :, cols] * keep, phi[1, :, cols], NT)
        for b in range(4):
            coefficient = r0[h, :, 512 - 128 * b : 1024 - 128 * b] * masks[b]
            pp[h, b * 128 : (b + 1) * 128] = (scores[b * 128 : (b + 1) * 128] * coefficient).astype(BF16)
        right = jnp.concatenate([qkv[2, :, cols] * keep, jnp.broadcast_to(keep, (512, 128))], axis=1)
        both = dot(pp[h], right)
        num[:, cols] += both[:, :128]
        den[:, cols] += both[:, 128:]
        return carry

    lax.fori_loop(0, 4, head_body, 0)
    quo[...] = num[...] / den[...]
    att[...] = quo[...].astype(BF16)

    class Scatter:
        def __init__(self, ref):
            self.ref, self.base = ref, sems.take(12)

        def part(self, n):
            cols = pl.ds(pl.multiple_of(n * 256, 256), 256)
            for slot in range(3):
                i = self.base + slot * 4 + n
                rc(pb.at[plane_block[slot], :, cols], self.ref.at[slot, :, cols], i, i, plane[slot]).start()

        def total(self):
            for slot in range(3):
                for n in range(4):
                    got(self.ref.at[slot, :, n * 256 : (n + 1) * 256], self.base + slot * 4 + n)
            value = pb[own_block].astype(F32)
            for slot in range(3):
                value = value + self.ref[slot].astype(F32)
            return value

        def sent(self):
            for slot in range(3):
                for n in range(4):
                    i = self.base + slot * 4 + n
                    src = pb.at[plane_block[slot], :, n * 256 : (n + 1) * 256]
                    rc(src, src, i, i, plane[slot]).wait_send()

    class Gather:
        def __init__(self, ref):
            self.ref, self.base = ref, sems.take(3)

        def start(self):
            mine = self.ref.at[own_block]
            for slot in range(3):
                send(mine, mine, self.base + slot, self.base + slot, plane[slot])

        def need(self):
            for slot in range(3):
                got(self.ref.at[plane_block[slot]], self.base + slot)

    def scatter(ref, part):
        s = Scatter(ref)

        def body(n, carry):
            cols = pl.ds(pl.multiple_of(n * 256, 256), 256)
            pb[:, :, cols] = part(n).astype(BF16).reshape(4, 128, 256)
            s.part(n)
            return carry

        lax.fori_loop(0, 4, body, 0)
        return s

    it_o.need()
    sc_z = scatter(rb_z, lambda n: dot(att[...], wo[pl.ds(2 * n, 2)].reshape(256, 256), NT))
    it_u.pump()
    it_u.need()

    def norm(values):
        centred = values - jnp.mean(values, axis=-1, keepdims=True)
        inverse = lax.rsqrt(jnp.mean(centred * centred, axis=-1, keepdims=True) + EPSILON)
        return centred * inverse, inverse

    own_rows = pl.ds(pl.multiple_of(own_block * 128, 128), 128)
    residual = sc_z.total() + xg[own_rows].astype(F32) + rows_v[2:3, :]
    normed, inverse = norm(residual)
    first = normed * rows_v[0:1, :] + rows_v[3:4, :]
    fst[...] = first
    n1[...] = normed
    i1[...] = jnp.broadcast_to(inverse, (128, 128))
    fb[own_block] = first.astype(BF16)
    g_first = Gather(fb)
    g_first.start()
    sc_z.sent()
    g_first.need()

    def hidden_body(n, carry):
        cols = pl.ds(pl.multiple_of(n * 256, 256), 256)
        pre = dot(fb[...].reshape(512, 1024), wu[:, :, :, cols].reshape(1024, 256)) + rows_v[17:18, cols]
        cdf = 0.5 * (1.0 + lax.erf(pre * 0.7071067811865476))
        hid[:, cols] = (pre * cdf).astype(BF16)
        dgel[:, cols] = cdf + pre * (0.3989422804014327 * jnp.exp(-0.5 * pre * pre))
        return carry

    lax.fori_loop(0, 4, hidden_body, 0)
    it_d.pump()
    it_d.need()
    sc_f = scatter(rb_f, lambda n: dot(hid[...], wd[pl.ds(2 * n, 2)].reshape(256, 1024), NT))
    second = fst[...] + sc_f.total() + rows_v[4:5, :]
    normed2, inverse2 = norm(second)
    mix_s[...] = (normed2 * rows_v[1:2, :] + rows_v[5:6, :]).astype(BF16)

    def norm_back(upstream, normed, inverse, gain):
        scaled = upstream * gain
        mean = jnp.mean(scaled, axis=-1, keepdims=True)
        slope = jnp.mean(scaled * normed, axis=-1, keepdims=True)
        return inverse * (scaled - mean - normed * slope)

    def down(values):
        return jnp.sum(values, axis=0, keepdims=True)

    upstream = cotb[...].astype(F32)
    sd[1:2, :] = down(upstream * normed2)
    sd[5:6, :] = down(upstream)
    err = norm_back(upstream, normed2, inverse2, rows_v[1:2, :])
    efb[own_block] = err.astype(BF16)
    sd[4:5, :] = down(efb[own_block].astype(F32))
    g_ef = Gather(efb)
    g_ef.start()
    dr[...] = err
    sc_f.sent()

    i_mix, i_gt = sems.take(2), sems.take(2)

    def to_owner(src, dst, i):
        rows = pl.ds(pl.multiple_of(y * 128, 128), 128)
        home = c == x

        @pl.when(home)
        def _():
            dst[rows] = src[...]

        send(src, dst.at[rows], i + 1, i + 1, yn, home)
        away = jnp.logical_not(home)
        send(src, dst.at[rows], i, i + y, xs_dev, away)
        send(src, dst.at[rows], i + 1, i + y, ds_dev, away)

    def from_owner(dst, i):
        for half in range(2):
            part = dst.at[half * 128 : (half + 1) * 128]

            @pl.when(jnp.logical_and(c == x, y != half))
            def _(part=part):
                got(part, i + 1)

            @pl.when(c != x)
            def _(part=part, half=half):
                got(part, i + half)

    to_owner(mix_s, mixed_o, i_mix)
    g_ef.need()

    class Grad:
        def __init__(self, g, r1, t, rz, cb, xr):
            self.g, self.r1, self.t, self.rz, self.cb, self.xr = g, r1, t, rz, cb, xr
            self.d, self.z, self.k, self.x = sems.take(4), sems.take(PLANES), sems.take(), sems.take()

        def make(self, part):
            def body(m, carry):
                part(m)
                i = self.d + m
                rc(self.g.at[m, :, 1 - c], self.r1.at[m], i, i, sib).start()
                return carry

            lax.fori_loop(0, PLANES, body, 0)

            def done():
                for m in range(PLANES):
                    src = self.g.at[m, :, 1 - c]
                    rc(src, src, self.d + m, self.d + m, sib).wait_send()

            pending.append(done)

        def pair(self):
            def body(m, carry):
                got(self.r1.at[m], self.d + m)
                self.t[m] = (self.g[m, :, c].astype(F32) + self.r1[m].astype(F32)).astype(BF16)
                return carry

            lax.fori_loop(0, PLANES, body, 0)
            send(self.t.at[PLANES - 1], self.cb, self.k, self.k, dev(1, x, y, c), z == 0)
            send(self.t.at[0], self.cb, self.k, self.k, dev(2, x, y, c), z == 3)
            for dz in (1, -1):
                send(self.t.at[z + dz], self.rz.at[z], self.z + z + dz, self.z + z, dev(z + dz, x, y, c), valid(dz))
            for dz, at in ((2, 0), (-2, 3)):
                send(self.t.at[z + dz], self.rz.at[z], self.z + z + dz, self.z + z, dev(z + dz, x, y, c), z == at)

        def relay(self):
            for dz, at in ((2, 1), (-2, 2)):
                @pl.when(z == at)
                def _(dz=dz):
                    got(self.cb, self.k)
                    self.t[z + dz] = (self.t[z + dz].astype(F32) + self.cb[...].astype(F32)).astype(BF16)

                send(self.t.at[z + dz], self.rz.at[z], self.z + z + dz, self.z + z, dev(z + dz, x, y, c), z == at)

        def finish(self):
            width = self.t.shape[-1]
            acc = fs.at[:, :, 0:width]
            acc[...] = self.t[z].astype(F32)
            for dz in (1, -1, 2, -2):
                @pl.when(valid(dz))
                def _(dz=dz):
                    got(self.rz.at[z + dz], self.z + z + dz)
                    acc[...] += self.rz[z + dz].astype(F32)
            keep = xs.at[self.slot, :, 0:width]
            keep[...] = fs[1 - x, :, 0:width].astype(BF16)
            send(keep, self.xr, self.x, self.x, xn)

        def columns(self, out, half, parts, value):
            width = self.t.shape[-1]
            step = width // parts
            for p in range(parts):
                at = pl.multiple_of(p * 2 * step + half * step, 128)
                out[:, pl.ds(at, step)] = value[:, p * step : (p + 1) * step]

        def write_own(self, out, parts=1):
            width = self.t.shape[-1]
            self.columns(out, x, parts, fs[x, :, 0:width])

        def write_other(self, out, parts=1):
            got(self.xr, self.x)
            self.columns(out, 1 - x, parts, self.xr[...].astype(F32))

    gr_d = Grad(g_d, r1_d, t_d, rz_d, cb_d, xr_d)
    gr_u = Grad(g_u, r1_u, t_u, rz_u, cb_u, xr_u)
    gr_o = Grad(g_o, r1_o, t_o, rz_o, cb_o, xr_o)
    gr_q = Grad(g_q, r1_q, t_q, rz_q, cb_q, xr_q)
    for slot, gr in enumerate((gr_d, gr_u, gr_o, gr_q)):
        gr.slot = slot

    def d_cols(ref, m):
        return ref[:, :, pl.ds(pl.multiple_of(m * 256, 256), 256)].reshape(512, 256)

    def make_down(m):
        g_d[m] = dot(d_cols(efb, m), hid[...], TN).astype(BF16).reshape(2, 2, 64, 1024)

    gr_d.make(make_down)

    def du_body(n, carry):
        cols = pl.ds(pl.multiple_of(n * 256, 256), 256)
        dact = dot(efb[...].reshape(512, 1024), wd[:, :, :, cols].reshape(1024, 256))
        du = (dact * dgel[:, cols]).astype(BF16)
        dub[:, cols] = du
        st[0:1, cols] = down(du.astype(F32))
        return carry

    lax.fori_loop(0, 4, du_body, 0)
    sc_d = scatter(rb_d, lambda n: dot(dub[...], wu[pl.ds(2 * n, 2)].reshape(256, 1024), NT))
    gr_d.pair()

    def make_up(m):
        g_u[m] = dot(d_cols(fb, m), dub[...], TN).astype(BF16).reshape(2, 2, 64, 1024)

    gr_u.make(make_up)
    gr_u.pair()
    gr_d.relay()
    dfirst = dr[...] + sc_d.total()
    sd[0:1, :] = down(dfirst * n1[...])
    sd[3:4, :] = down(dfirst)
    back = norm_back(dfirst, n1[...], i1[:, 0:1], rows_v[0:1, :])
    dr[...] = back
    dzb[own_block] = back.astype(BF16)
    sd[2:3, :] = down(dzb[own_block].astype(F32))
    g_dz = Gather(dzb)
    g_dz.start()
    sc_d.sent()

    class Small:
        def __init__(self, ref, recv):
            self.ref, self.recv, self.base = ref, recv, sems.take(7)

        def swap(self, device, i):
            send(self.ref.at[self.at], self.recv.at[i], self.base + i, self.base + i, device)

        def add(self, i):
            got(self.recv.at[i], self.base + i)

    def small_sum(now, recv, base, device, count):
        pass

    i_sd = sems.take(3)
    sd[6:8, :] = jnp.zeros((2, 1024), F32)
    for k, device in enumerate(plane):
        send(sd, sd_r.at[k], i_sd + k, i_sd + k, device)
    g_dz.need()

    dattn = dot(dzb[...].reshape(512, 1024), wo[...].reshape(1024, 256))

    def make_out(m):
        g_o[m] = dot(d_cols(dzb, m), att[...], TN).astype(BF16).reshape(2, 2, 64, 256)

    gr_o.make(make_out)
    recip = 1.0 / den[...]
    dn[...] = (dattn * recip).astype(BF16)
    dsum = split_dot(dattn * quo[...], ones64[...])
    dd[...] = ((-dsum * recip).astype(BF16).astype(F32) * (1.0 / HEAD)).astype(BF16)
    gr_o.pair()
    gr_u.relay()
    dph[...] = jnp.zeros_like(dph)
    dvv[...] = jnp.zeros_like(dvv)

    def head_back(h, carry):
        cols, mine = head_cols(h)
        keep = jnp.where(mine, 1.0, 0.0).astype(BF16)
        dnum = dn[:, cols] * keep
        left = jnp.concatenate([dnum, dd[:, cols] * keep], axis=1)
        right = jnp.concatenate([qkv[2, :, cols], jnp.ones((512, 128), BF16)], axis=1)
        grad_p = dot(left, right, NT)
        for b in range(4):
            rows = slice(b * 128, (b + 1) * 128)
            coefficient = r0[h, :, 512 - 128 * b : 1024 - 128 * b] * masks[b]
            part = grad_p[rows]
            ds_[rows] = (part * coefficient).astype(BF16)
            gg[rows] = (part * pp[h, rows].astype(F32)).astype(BF16)
        dvv[:, cols] += dot(pp[h], dnum, TN)
        dph[0, :, cols] += dot(ds_[...], phi[1, :, cols] * keep)
        dph[1, :, cols] += dot(ds_[...], phi[0, :, cols] * keep, TN)
        flipped = dot(anti[...], gg[...])
        sums = jnp.zeros((1, 1024), F32)
        for b in range(4):
            wide = jnp.concatenate([flipped[b * 128 : (b + 1) * 128], jnp.zeros((128, 128), F32)], axis=1)
            line = down(pltpu.roll(wide, 0, 1, stride=1, stride_axis=0))
            pieces = [line]
            if b > 0:
                pieces = [jnp.zeros((1, 128 * b), F32)] + pieces
            if b < 3:
                pieces = pieces + [jnp.zeros((1, 384 - 128 * b), F32)]
            sums = sums + jnp.concatenate(pieces, axis=1)
        st[pl.ds(2 + h, 1), :] = sums
        return carry

    lax.fori_loop(0, 4, head_back, 0)
    gr_o.relay()

    def feature_back_body(t, carry):
        dlog = (dph[t] * ex[t]).astype(BF16)
        units = unit[t]
        dunit = SCALE * dot(dlog, om2[...], NT) - SCALE * SCALE * dot(dlog, ones64[...]) * units
        mean = split_dot(dunit * units, ones64[...]) * (1.0 / HEAD)
        dqkv[t] = (inv[t] * (dunit - units * mean)).astype(BF16)
        return carry

    lax.fori_loop(0, 2, feature_back_body, 0)
    dqkv[2] = dvv[...].astype(BF16)

    def input_part(n):
        value = jnp.zeros((512, 256), F32)
        for p in range(3):
            value = value + dot(dqkv[p], wq[pl.ds(2 * n, 2), :, :, p * 256 : (p + 1) * 256].reshape(256, 256), NT)
        return value

    sc_i = scatter(rb_i, input_part)

    def make_qkv(m):
        left = xg[:, pl.ds(pl.multiple_of(m * 256, 256), 256)]
        for p in range(3):
            value = dot(left, dqkv[p], TN).astype(BF16).reshape(2, 2, 64, 256)
            g_q[m, :, :, :, p * 256 : (p + 1) * 256] = value

    gr_q.make(make_qkv)
    for p in range(3):
        st[1:2, p * 256 : (p + 1) * 256] = down(dqkv[p].astype(F32))
    st[1:2, 768:1024] = jnp.zeros((1, 256), F32)
    st[6:8, :] = jnp.zeros((2, 1024), F32)
    gr_q.pair()

    i_c, i_zz, i_h = sems.take(), sems.take(PLANES), sems.take()
    for k in range(3):
        got(sd_r.at[k], i_sd + k)
    st[8:16, :] = sd[...] + sd_r[0] + sd_r[1] + sd_r[2]
    send(st, st_r.at[0], i_c, i_c, sib)
    got(st_r.at[0], i_c)
    st_r[1] = st[...] + st_r[0]
    for zz in range(PLANES):
        send(st_r.at[1], st_r.at[2 + z], i_zz + zz, i_zz + z, dev(zz, x, y, c), z != zz)

    gr_d.finish()
    gr_d.write_own(gd_o)
    gr_u.finish()
    gr_u.write_own(gu_o)
    gr_o.finish()
    gr_o.write_own(go_o)
    back = dr[...] + sc_i.total()
    gt_s[...] = back.astype(BF16)
    to_owner(gt_s, gt_r, i_gt)
    sc_i.sent()
    gr_q.relay()
    total = st_r[1]
    for zz in range(PLANES):
        @pl.when(z != zz)
        def _(zz=zz):
            got(st_r.at[2 + zz], i_zz + zz)

        @pl.when(z == zz)
        def _(zz=zz):
            st_r[2 + zz] = jnp.zeros((16, 1024), F32)
        total = total + st_r[2 + zz]
    tvec_o[x] = total[0:8]
    dvec_o[...] = total[8:16]
    send(tvec_o.at[x], tvec_o.at[x], i_h, i_h, xn)
    gr_d.write_other(gd_o)
    gr_u.write_other(gu_o)
    gr_o.write_other(go_o)
    gr_q.finish()
    gr_q.write_own(gq_o, 3)
    from_owner(mixed_o, i_mix)
    from_owner(gt_r, i_gt)
    gtok_o[...] = gt_r[...].astype(F32)
    got(tvec_o.at[1 - x], i_h)
    gr_q.write_other(gq_o, 3)
    for done in pending:
        done()


def fast_local(
    tokens, qkv_weight, qkv_bias, out_weight, norm_gains, row_biases, up_weight, up_bias, down_weight, rpe_bias, omega,
    bucket, cotangent,
):
    dp, feat = lax.axis_index("dp"), lax.axis_index("feat")
    x = dp % 2
    shard = dp * 2 + feat

    def halves(weight):
        return weight.reshape(64, 2, -1).transpose(1, 0, 2)

    wq = qkv_weight.reshape(64, 3, 2, 256).transpose(2, 0, 1, 3).reshape(2, 64, 768)
    wo, wu, wd = halves(out_weight.T), halves(up_weight), halves(down_weight.T)

    def beside(values, at):
        blank = jnp.zeros_like(values)
        return jnp.where(
            at == 0, jnp.concatenate([values, blank], -1), jnp.concatenate([blank, values], -1)
        )

    def two(rows):
        return jnp.broadcast_to(rows, (2,) + rows.shape)

    vectors = beside(jnp.concatenate([norm_gains, row_biases], 0), feat)
    level = jnp.broadcast_to(bucket.astype(BF16)[:, None], (1, 128))
    top = two(jnp.concatenate([vectors, level, jnp.zeros((1, 128), BF16)], 0))
    position = beside(rpe_bias[:, ::-1], 1 - feat).reshape(2, 4, 128)
    spread = lax.dynamic_update_slice(jnp.zeros((3, 8, 64), BF16), qkv_bias, (0, 0, 4 * shard))
    spread = spread.reshape(3, 2, 256).transpose(1, 0, 2).reshape(2, 6, 128)
    spread_up = lax.dynamic_update_slice(jnp.zeros((32, 64), BF16), up_bias, (0, 4 * shard)).reshape(2, 8, 128)
    small = jnp.concatenate(
        [top, position, jnp.zeros((2, 4, 128), BF16), spread, jnp.zeros((2, 2, 128), BF16), spread_up], 1
    )
    mine = lax.dynamic_slice(omega, (4 * x, 0, 0), (4, 64, 32))
    both = beside(mine, feat) if False else jnp.where(
        feat == 0,
        jnp.concatenate([mine, jnp.zeros_like(mine)], -1),
        jnp.concatenate([jnp.zeros_like(mine), mine], -1),
    )
    blocks = jnp.eye(4, dtype=BF16)[:, None, :, None] * both[:, :, None, :]
    omega_blocks = blocks.reshape(256, 256)

    def vm(shape, dtype=BF16):
        return pltpu.VMEM(shape, dtype)

    widths = (768, 256, 1024, 1024)
    scratch = [vm((8, 2, 64, n)) for n in widths]
    scratch += [vm((8, 2, 32, 128)), vm((256, 256)), vm((512, 1024)), vm((128, 1024))]
    scratch += [vm((3, 512, 256)), vm((2, 512, 256))] + [vm((2, 512, 256), F32)] * 3
    scratch += [vm((4, 128, 1024), F32), vm((4, 512, 512))] + [vm((512, 256), F32)] * 3 + [vm((512, 256))]
    scratch += [vm((4, 128, 1024))] + [vm((3, 128, 1024))] * 4
    scratch += [vm((4, 128, 1024)), vm((512, 1024)), vm((512, 1024), F32)]
    scratch += [vm((4, 128, 1024)), vm((512, 1024)), vm((4, 128, 1024))]
    scratch += [vm((128, 1024), F32)] * 2 + [vm((128, 128), F32), vm((128, 1024), F32)]
    scratch += [vm((512, 256))] * 2 + [vm((512, 512))] * 2 + [vm((2, 512, 256), F32), vm((512, 256), F32)]
    scratch += [vm((3, 512, 256)), vm((512, 512)), vm((256, 256)), vm((24, 1024), F32)]
    scratch += [vm((4, 2, 2, 64, n)) for n in widths]
    scratch += [vm((4, 2, 64, n)) for n in widths] * 2
    scratch += [vm((4, 2, 64, n)) for n in widths] + [vm((2, 64, n)) for n in widths]
    scratch += [vm((2, 64, 1024), F32), vm((4, 64, 1024))] + [vm((64, n)) for n in widths]
    scratch += [vm((8, 1024), F32), vm((3, 8, 1024), F32), vm((16, 1024), F32), vm((6, 16, 1024), F32)]
    scratch += [vm((128, 1024)), vm((16, 128)), vm((128, 1024)), vm((256, 1024))]
    scratch += [pltpu.SemaphoreType.DMA((320,)), pltpu.SemaphoreType.DMA((320,))]

    def out(shape, dtype=F32):
        return jax.ShapeDtypeStruct(shape, dtype)

    mixed, gtok, gq, go, gu, gd, dvec, tvec = pl.pallas_call(
        layer_kernel,
        out_shape=(
            out((256, 1024), BF16), out((256, 1024)), out((64, 1536)), out((64, 512)), out((64, 2048)), out((64, 2048)),
            out((8, 1024)), out((2, 8, 1024)),
        ),
        in_specs=[pl.BlockSpec(memory_space=pltpu.VMEM)] * 8,
        out_specs=(pl.BlockSpec(memory_space=pltpu.VMEM),) * 8,
        scratch_shapes=scratch,
        compiler_params=pltpu.CompilerParams(
            collective_id=0, has_side_effects=True, vmem_limit_bytes=63 * 2**20
        ),
        name="layer",
    )(tokens, cotangent, wq, wo, wu, wd, small, omega_blocks)
    own = lax.dynamic_slice(dvec, (0, 64 * shard), (8, 64))
    grad_up_bias = lax.dynamic_slice(tvec[:, 0].reshape(32, 64), (0, 4 * shard), (32, 4))
    qkv_rows = tvec[:, 1, :768].reshape(2, 3, 4, 64).transpose(1, 0, 2, 3).reshape(3, 8, 64)
    grad_qkv_bias = lax.dynamic_slice(qkv_rows, (0, 0, 4 * shard), (3, 8, 4))
    grad_rpe = lax.dynamic_slice(tvec[:, 2:6].reshape(8, 1024), (0, 64 * (15 - shard)), (8, 64))[:, ::-1]
    return (
        mixed, gtok, gq.reshape(64, 3, 512), grad_qkv_bias, go.T, own[0:2], own[2:6], gu, grad_up_bias, gd.T, grad_rpe,
    )


def solution(mesh):
    sizes = (mesh.shape["dp"], mesh.shape["heads"], mesh.shape["feat"])
    return jax.shard_map(
        fast_local if sizes == (2 * PLANES, 2, 2) else local,
        mesh=mesh,
        in_specs=(
            P(("dp", "feat"), None),
            P(("dp", "feat"), None, "heads"),
            P(None, "heads", ("dp", "feat")),
            P("heads", ("dp", "feat")),
            P(None, ("dp", "feat")),
            P(None, ("dp", "feat")),
            P(("dp", "feat"), "heads"),
            P("heads", ("dp", "feat")),
            P("heads", ("dp", "feat")),
            P("heads", ("dp", "feat")),
            P("heads", None, "feat"),
            P("dp"),
            P(("dp", "feat"), None),
        ),
        out_specs=(
            P(("dp", "feat"), None),
            P(("dp", "feat"), None),
            P(("dp", "feat"), None, "heads"),
            P(None, "heads", ("dp", "feat")),
            P("heads", ("dp", "feat")),
            P(None, ("dp", "feat")),
            P(None, ("dp", "feat")),
            P(("dp", "feat"), "heads"),
            P("heads", ("dp", "feat")),
            P("heads", ("dp", "feat")),
            P("heads", ("dp", "feat")),
        ),
        check_vma=False,
    )
```

```python
import functools

import jax
import jax.numpy as jnp
from jax import lax
from jax.experimental import pallas as pl
from jax.experimental.pallas import tpu as pltpu
from jax.sharding import PartitionSpec as P

HEAD = 64
M = 64


EPSILON = 1e-12
UNIT_EPS = 1e-06


def toeplitz_block(window, extent):
    leading = window.shape[0]
    tiled_rows = jnp.broadcast_to(window[:, None, :], (leading, extent, 2 * extent - 1)).reshape(
        leading, -1
    )
    padded = jnp.pad(tiled_rows, ((0, 0), (0, extent)))
    sheared = padded.reshape(leading, extent, 2 * extent)[:, :, :extent]
    return sheared[:, :, ::-1]


def diagonal_sums(values_grid, extent):
    leading = values_grid.shape[0]
    flipped = values_grid[:, :, ::-1]
    padded = jnp.pad(flipped, ((0, 0), (0, 0), (0, extent))).reshape(leading, -1)
    sheared = padded[:, : extent * (2 * extent - 1)].reshape(leading, extent, 2 * extent - 1)
    return jnp.sum(sheared, axis=1)


def norm_forward(values, gain, shift):
    centred = values - jnp.mean(values, axis=-1, keepdims=True)
    inverse = lax.rsqrt(jnp.mean(centred * centred, axis=-1, keepdims=True) + EPSILON)
    normed = centred * inverse
    return (normed * gain + shift, normed, inverse)


def norm_backward(upstream, normed, inverse, gain):
    scaled_grad = upstream * gain
    return inverse * (
        scaled_grad
        - jnp.mean(scaled_grad, axis=-1, keepdims=True)
        - normed * jnp.mean(scaled_grad * normed, axis=-1, keepdims=True)
    )


def feature_logits(entries, omega_local):
    factor = HEAD ** (-0.25)
    wide = entries.astype(jnp.float32)
    inverse = lax.rsqrt(jnp.mean(wide * wide, axis=-1, keepdims=True) + UNIT_EPS)
    unit = wide * inverse
    projected = jnp.einsum(
        "rhe,hem->hmr",
        unit,
        omega_local.astype(jnp.float32),
        precision=lax.Precision.HIGHEST,
        preferred_element_type=jnp.float32,
    )
    squares = jnp.sum(unit * unit, axis=-1)
    return (factor * projected - 0.5 * factor * factor * squares.T[:, None, :], unit, inverse)


def feature_back(grad_phi, logits, unit, inverse, omega_local):
    factor = HEAD ** (-0.25)
    grad_logits = (grad_phi * (jnp.exp(logits) * M ** (-0.5))).astype(jnp.bfloat16)
    projected = jnp.einsum(
        "hmr,hem->rhe", grad_logits, omega_local, preferred_element_type=jnp.float32
    )
    totals = jnp.sum(grad_logits.astype(jnp.float32), axis=1)
    grad_unit = factor * projected - factor * factor * totals.T[:, :, None] * unit
    return inverse * (grad_unit - unit * jnp.mean(grad_unit * unit, axis=-1, keepdims=True))


def window_begin(row_start, col_start, extent, rows_total):
    return row_start - col_start + rows_total - extent + 1


def block_coeff(rpe_exp, window_start, extent):
    window = lax.dynamic_slice_in_dim(rpe_exp, window_start, 2 * extent - 1, 1)
    return toeplitz_block(window, extent)


def local(
    tokens,
    qkv_weight,
    qkv_bias,
    out_weight,
    norm_gains,
    row_biases,
    up_weight,
    up_bias,
    down_weight,
    rpe_bias,
    omega,
    bucket,
    cotangent,
):
    qkv_full, out_full, up_full, down_full, gains_all, biases_all, bias_qkv, bias_up, rpe_all = (
        lax.all_gather(qkv_weight, ("dp", "feat"), axis=0, tiled=True),
        lax.all_gather(out_weight, ("dp", "feat"), axis=1, tiled=True),
        lax.all_gather(up_weight, ("dp", "feat"), axis=0, tiled=True),
        lax.all_gather(down_weight, ("dp", "feat"), axis=1, tiled=True),
        lax.all_gather(norm_gains, ("dp", "feat"), axis=1, tiled=True),
        lax.all_gather(row_biases, ("dp", "feat"), axis=1, tiled=True),
        lax.all_gather(qkv_bias, ("dp", "feat"), axis=2, tiled=True),
        lax.all_gather(up_bias, ("dp", "feat"), axis=1, tiled=True),
        lax.all_gather(rpe_bias, ("dp", "feat"), axis=1, tiled=True),
    )
    model_width = qkv_full.shape[0]
    head_cols = qkv_full.shape[2]
    local_heads = omega.shape[0]
    local_feats = omega.shape[2]
    rows_own = tokens.shape[0]
    rows_total = rows_own * lax.axis_size("feat")
    block_rows = min(512, rows_total // 4)
    blocks = rows_total // block_rows
    seq_length = rows_total // 4 * jnp.where(bucket[0] == 0, 1, jnp.where(bucket[0] == 1, 2, 4))
    block_count = seq_length // block_rows
    gain_rows = gains_all.astype(jnp.float32)
    bias_rows = biases_all.astype(jnp.float32)
    rpe_exp = jnp.exp(rpe_all.astype(jnp.float32))
    projected = jnp.dot(
        tokens, qkv_full.reshape(model_width, 3 * head_cols), preferred_element_type=jnp.float32
    )
    projected = projected + bias_qkv.reshape(-1).astype(jnp.float32)
    qkv_own = projected.astype(jnp.bfloat16)
    qkv_all = lax.all_gather(qkv_own, "feat", axis=0, tiled=True).reshape(
        rows_total, 3, local_heads, HEAD
    )
    queries = qkv_all[:, 0]
    keys_rows = qkv_all[:, 1]
    values_rows = qkv_all[:, 2]
    logits_query, unit_query, inverse_query = feature_logits(queries, omega)
    logits_key, unit_key, inverse_key = feature_logits(keys_rows, omega)
    feat_query = (jnp.exp(logits_query) * M ** (-0.5)).astype(jnp.bfloat16)
    feat_key = (jnp.exp(logits_key) * M ** (-0.5)).astype(jnp.bfloat16)
    numer_parts = []
    denom_parts = []
    for row_block in range(blocks):
        row_start = row_block * block_rows
        first_block = row_start // seq_length * block_count
        phi_rows = feat_query[:, :, row_start : row_start + block_rows]

        def visit(column_block, carried, phi_rows=phi_rows, row_start=row_start):
            numer_acc, denom_acc = carried
            col_start = column_block * block_rows
            phi_cols = lax.dynamic_slice_in_dim(feat_key, col_start, block_rows, 2)
            value_cols = lax.dynamic_slice_in_dim(values_rows, col_start, block_rows, 0)
            coefficient = block_coeff(
                rpe_exp, window_begin(row_start, col_start, block_rows, rows_total), block_rows
            )
            scores = jnp.einsum(
                "hmi,hmj->hij", phi_rows, phi_cols, preferred_element_type=jnp.float32
            )
            weights = (coefficient * scores).astype(jnp.bfloat16)
            numer_acc = numer_acc + jnp.einsum(
                "hij,jhe->ihe", weights, value_cols, preferred_element_type=jnp.float32
            )
            denom_acc = denom_acc + jnp.sum(weights.astype(jnp.float32), axis=-1)
            return (numer_acc, denom_acc)

        start_pair = (
            jnp.zeros((block_rows, local_heads, HEAD), jnp.float32),
            jnp.zeros((local_heads, block_rows), jnp.float32),
        )
        numer_block, denom_block = lax.fori_loop(
            first_block, first_block + block_count, visit, start_pair
        )
        numer_parts.append(numer_block)
        denom_parts.append(denom_block)
    numer_all = jnp.concatenate(numer_parts, axis=0).reshape(rows_total, head_cols)
    denom_all = jnp.concatenate(denom_parts, axis=1)
    numer_own, denom_own = (
        lax.psum_scatter(
            numer_all.astype(jnp.bfloat16), "feat", scatter_dimension=0, tiled=True
        ).astype(jnp.float32),
        lax.psum_scatter(
            denom_all.astype(jnp.bfloat16), "feat", scatter_dimension=1, tiled=True
        ).astype(jnp.float32),
    )
    denom_rows = denom_own.T
    quotient = numer_own.reshape(rows_own, local_heads, HEAD) / denom_rows[:, :, None]
    attn_low = quotient.reshape(rows_own, head_cols).astype(jnp.bfloat16)
    z_part = jnp.dot(attn_low, out_full, preferred_element_type=jnp.float32)
    mixed_z = lax.psum(z_part.astype(jnp.bfloat16), "heads").astype(jnp.float32) + bias_rows[0]
    first_out, normed_one, inverse_one = norm_forward(
        tokens.astype(jnp.float32) + mixed_z, gain_rows[0], bias_rows[1]
    )
    first_low = first_out.astype(jnp.bfloat16)
    pre_act = jnp.dot(first_low, up_full, preferred_element_type=jnp.float32) + bias_up.reshape(
        -1
    ).astype(jnp.float32)
    act_value, act_pull = jax.vjp(lambda inner: jax.nn.gelu(inner, approximate=False), pre_act)
    act_low = act_value.astype(jnp.bfloat16)
    ffn_part = jnp.dot(act_low, down_full, preferred_element_type=jnp.float32)
    ffn_out = lax.psum(ffn_part.astype(jnp.bfloat16), "heads").astype(jnp.float32) + bias_rows[2]
    final_rows, normed_two, inverse_two = norm_forward(
        first_out + ffn_out, gain_rows[1], bias_rows[3]
    )
    mixed = final_rows.astype(jnp.bfloat16)
    qkv_full, out_full, up_full, down_full, gains_all, rpe_all = (
        lax.all_gather(qkv_weight, ("dp", "feat"), axis=0, tiled=True),
        lax.all_gather(out_weight, ("dp", "feat"), axis=1, tiled=True),
        lax.all_gather(up_weight, ("dp", "feat"), axis=0, tiled=True),
        lax.all_gather(down_weight, ("dp", "feat"), axis=1, tiled=True),
        lax.all_gather(norm_gains, ("dp", "feat"), axis=1, tiled=True),
        lax.all_gather(rpe_bias, ("dp", "feat"), axis=1, tiled=True),
    )
    gain_rows = gains_all.astype(jnp.float32)
    rpe_exp = jnp.exp(rpe_all.astype(jnp.float32))
    upstream = cotangent.astype(jnp.float32)
    grad_gain_two = jnp.sum(upstream * normed_two, axis=0)
    grad_shift_two = jnp.sum(upstream, axis=0)
    resid_two = norm_backward(upstream, normed_two, inverse_two, gain_rows[1])
    resid_low = resid_two.astype(jnp.bfloat16)
    grad_bias_down = jnp.sum(resid_low.astype(jnp.float32), axis=0)
    grad_down = jnp.einsum("rf,rd->fd", act_low, resid_low, preferred_element_type=jnp.float32)
    grad_act = jnp.einsum("rd,fd->rf", resid_low, down_full, preferred_element_type=jnp.float32)
    grad_pre = act_pull(grad_act)[0].astype(jnp.bfloat16)
    grad_up = jnp.einsum("rd,rf->df", first_low, grad_pre, preferred_element_type=jnp.float32)
    grad_bias_up = jnp.sum(grad_pre.astype(jnp.float32), axis=0).reshape(bias_up.shape)
    first_back = lax.psum(
        jnp.einsum("rf,df->rd", grad_pre, up_full, preferred_element_type=jnp.float32).astype(
            jnp.bfloat16
        ),
        "heads",
    ).astype(jnp.float32)
    grad_first = resid_two + first_back
    grad_gain_one = jnp.sum(grad_first * normed_one, axis=0)
    grad_shift_one = jnp.sum(grad_first, axis=0)
    resid_one = norm_backward(grad_first, normed_one, inverse_one, gain_rows[0])
    resid_one_low = resid_one.astype(jnp.bfloat16)
    grad_bias_out = jnp.sum(resid_one_low.astype(jnp.float32), axis=0)
    grad_out = jnp.einsum("rc,rd->cd", attn_low, resid_one_low, preferred_element_type=jnp.float32)
    grad_attn = jnp.einsum(
        "rd,cd->rc", resid_one_low, out_full, preferred_element_type=jnp.float32
    ).reshape(rows_own, local_heads, HEAD)
    grad_numer = (grad_attn / denom_rows[:, :, None]).astype(jnp.bfloat16)
    grad_denom = (-jnp.sum(grad_attn * quotient, axis=-1) / denom_rows).astype(jnp.bfloat16)
    numer_grad_all, denom_grad_all = (
        lax.all_gather(grad_numer.reshape(rows_own, head_cols), "feat", axis=0, tiled=True),
        lax.all_gather(grad_denom.T, "feat", axis=1, tiled=True),
    )
    numer_grad_all = numer_grad_all.reshape(rows_total, local_heads, HEAD)
    dphi_key = jnp.zeros((local_heads, local_feats, rows_total), jnp.float32)
    dvalues = jnp.zeros((rows_total, local_heads, HEAD), jnp.float32)
    grad_rpe = jnp.zeros(rpe_exp.shape, jnp.float32)
    dquery_parts = []
    for row_block in range(blocks):
        row_start = row_block * block_rows
        first_block = row_start // seq_length * block_count
        phi_rows = feat_query[:, :, row_start : row_start + block_rows]
        numer_rows = numer_grad_all[row_start : row_start + block_rows]
        denom_cols = denom_grad_all[:, row_start : row_start + block_rows].astype(jnp.float32)

        def visit_back(
            column_block,
            carried,
            phi_rows=phi_rows,
            row_start=row_start,
            numer_rows=numer_rows,
            denom_cols=denom_cols,
        ):
            dquery_acc, dkey_all, dvalue_all, drpe_all = carried
            col_start = column_block * block_rows
            phi_cols = lax.dynamic_slice_in_dim(feat_key, col_start, block_rows, 2)
            value_cols = lax.dynamic_slice_in_dim(values_rows, col_start, block_rows, 0)
            window_start = window_begin(row_start, col_start, block_rows, rows_total)
            coefficient = block_coeff(rpe_exp, window_start, block_rows)
            scores = jnp.einsum(
                "hmi,hmj->hij", phi_rows, phi_cols, preferred_element_type=jnp.float32
            )
            weights = (coefficient * scores).astype(jnp.bfloat16)
            grad_weights = (
                jnp.einsum(
                    "ihe,jhe->hij", numer_rows, value_cols, preferred_element_type=jnp.float32
                )
                + denom_cols[:, :, None]
            )
            dvalue_block = jnp.einsum(
                "hij,ihe->jhe", weights, numer_rows, preferred_element_type=jnp.float32
            )
            dvalue_all = lax.dynamic_update_slice_in_dim(
                dvalue_all,
                lax.dynamic_slice_in_dim(dvalue_all, col_start, block_rows, 0) + dvalue_block,
                col_start,
                0,
            )
            grad_scores = (grad_weights * coefficient).astype(jnp.bfloat16)
            diagonal = diagonal_sums(grad_weights * scores * coefficient, block_rows)
            drpe_all = lax.dynamic_update_slice_in_dim(
                drpe_all,
                lax.dynamic_slice_in_dim(drpe_all, window_start, 2 * block_rows - 1, 1) + diagonal,
                window_start,
                1,
            )
            dquery_acc = dquery_acc + jnp.einsum(
                "hij,hmj->hmi", grad_scores, phi_cols, preferred_element_type=jnp.float32
            )
            dkey_block = jnp.einsum(
                "hij,hmi->hmj", grad_scores, phi_rows, preferred_element_type=jnp.float32
            )
            dkey_all = lax.dynamic_update_slice_in_dim(
                dkey_all,
                lax.dynamic_slice_in_dim(dkey_all, col_start, block_rows, 2) + dkey_block,
                col_start,
                2,
            )
            return (dquery_acc, dkey_all, dvalue_all, drpe_all)

        start_state = (
            jnp.zeros((local_heads, local_feats, block_rows), jnp.float32),
            dphi_key,
            dvalues,
            grad_rpe,
        )
        dquery_block, dphi_key, dvalues, grad_rpe = lax.fori_loop(
            first_block, first_block + block_count, visit_back, start_state
        )
        dquery_parts.append(dquery_block)
    dphi_query = jnp.concatenate(dquery_parts, axis=2)
    grad_query = feature_back(dphi_query, logits_query, unit_query, inverse_query, omega)
    grad_key = feature_back(dphi_key, logits_key, unit_key, inverse_key, omega)
    grad_qkv_all = jnp.stack((grad_query, grad_key, dvalues), axis=1).reshape(
        rows_total, 3 * head_cols
    )
    grad_qkv_own = lax.psum_scatter(
        grad_qkv_all.astype(jnp.bfloat16), "feat", scatter_dimension=0, tiled=True
    )
    grad_bias_qkv = jnp.sum(grad_qkv_own.astype(jnp.float32), axis=0).reshape(bias_qkv.shape)
    grad_qkv_weight = jnp.einsum(
        "rd,rc->dc", tokens, grad_qkv_own, preferred_element_type=jnp.float32
    ).reshape(qkv_full.shape)
    input_terms = jnp.einsum(
        "rc,dc->rd",
        grad_qkv_own,
        qkv_full.reshape(model_width, 3 * head_cols),
        preferred_element_type=jnp.float32,
    )
    grad_tokens = resid_one + lax.psum(input_terms.astype(jnp.bfloat16), "heads").astype(
        jnp.float32
    )
    grad_gains = jnp.stack((grad_gain_one, grad_gain_two), axis=0)
    grad_shifts = jnp.stack((grad_bias_out, grad_shift_one, grad_bias_down, grad_shift_two), axis=0)
    (
        sent_qkv,
        sent_out,
        sent_up,
        sent_down,
        sent_gains,
        sent_shifts,
        sent_bias_qkv,
        sent_bias_up,
        sent_rpe,
    ) = (
        lax.psum_scatter(
            grad_qkv_weight.astype(jnp.bfloat16), ("dp", "feat"), scatter_dimension=0, tiled=True
        ).astype(jnp.float32),
        lax.psum_scatter(
            grad_out.astype(jnp.bfloat16), ("dp", "feat"), scatter_dimension=1, tiled=True
        ).astype(jnp.float32),
        lax.psum_scatter(
            grad_up.astype(jnp.bfloat16), ("dp", "feat"), scatter_dimension=0, tiled=True
        ).astype(jnp.float32),
        lax.psum_scatter(
            grad_down.astype(jnp.bfloat16), ("dp", "feat"), scatter_dimension=1, tiled=True
        ).astype(jnp.float32),
        lax.psum_scatter(
            grad_gains.astype(jnp.bfloat16), ("dp", "feat"), scatter_dimension=1, tiled=True
        ).astype(jnp.float32),
        lax.psum_scatter(
            grad_shifts.astype(jnp.bfloat16), ("dp", "feat"), scatter_dimension=1, tiled=True
        ).astype(jnp.float32),
        lax.psum_scatter(
            grad_bias_qkv.astype(jnp.bfloat16), ("dp", "feat"), scatter_dimension=2, tiled=True
        ).astype(jnp.float32),
        lax.psum_scatter(
            grad_bias_up.astype(jnp.bfloat16), ("dp", "feat"), scatter_dimension=1, tiled=True
        ).astype(jnp.float32),
        lax.psum_scatter(
            grad_rpe.astype(jnp.bfloat16), ("dp", "feat"), scatter_dimension=1, tiled=True
        ).astype(jnp.float32),
    )
    return (
        mixed,
        grad_tokens,
        sent_qkv,
        sent_bias_qkv,
        sent_out,
        sent_gains,
        sent_shifts,
        sent_up,
        sent_bias_up,
        sent_down,
        sent_rpe,
    )


MESH = pl.DeviceIdType.MESH
PLANES = 4
F32 = jnp.float32
BF16 = jnp.bfloat16
SCALE = HEAD ** (-0.25)
NT = (((1,), (1,)), ((), ()))
TN = (((0,), (0,)), ((), ()))
NN = (((1,), (0,)), ((), ()))


def dot(left, right, dims=NN):
    return lax.dot_general(left, right, dims, preferred_element_type=F32)


def split_dot(left, right, dims=NN):
    high = left.astype(BF16)
    rest = (left - high.astype(F32)).astype(BF16)
    return dot(high, right, dims) + dot(rest, right, dims)


def iota(shape, axis):
    return lax.broadcasted_iota(jnp.int32, shape, axis)


class Sems:
    def __init__(self):
        self.used = 0

    def take(self, count=1):
        first = self.used
        self.used += count
        return first


def layer_kernel(
    tok, wq_h, qb_h, wo_h, gain_h, bias_h, wu_h, ub_h, wd_h, rpe_h, om_h, bk_h, cot,
    mixed_h, gtok_h, gq_h, gqb_h, go_h, ggain_h, gbias_h, gu_h, gub_h, gd_h, grpe_h,
    qb_v, gain_v, bias_v, ub_v, rpe_v, om_v, bk_v, small_s, om_s,
    mixed_o, gtok_o, gq_o, gqb_o, go_o, ggain_o, gbias_o, gu_o, gub_o, gd_o, grpe_o, tvec_o,
    wq, wo, wu, wd, small, om2, xg, cotb,
    qkv, phi, ex, unit, inv, r0, pp, num, den, quo, att,
    pb, rb_z, rb_f, rb_d, rb_i, fb, hid, dgel, efb, dub, dzb,
    fst, n1, i1, dr,
    dn, dd, ds_, gg, dph, dvv, dqkv, anti, ones64, rows_v,
    g_q, g_o, g_u, g_d, r1_q, r1_o, r1_u, r1_d, t_q, t_o, t_u, t_d,
    rz_q, rz_o, rz_u, rz_d, cb_q, cb_o, cb_u, cb_d, fs, xs, xr_q, xr_o, xr_u, xr_d,
    sd, sd_r, st, st_r, mix_s, gt_s, gt_r,
    ss, rs, ls,
):
    dp, y, c = lax.axis_index("dp"), lax.axis_index("heads"), lax.axis_index("feat")
    z, x = dp // 2, dp % 2
    shard = 2 * dp + c
    sems, locals_ = Sems(), Sems()
    pending = []

    def bring(src, dst, cond=None):
        copy = pltpu.make_async_copy(src, dst, ls.at[locals_.take()])
        if cond is None:
            copy.start()
            return copy.wait
        pl.when(cond)(copy.start)
        return lambda: pl.when(cond)(copy.wait)

    home = c == x

    def half_cols(half, width):
        return pl.ds(pl.multiple_of(half * width, width), width)

    in_q = bring(wq_h.at[:, :, half_cols(x, 256)], wq.at[:, 2 * z + x, c])
    in_small = [
        bring(src, dst)
        for src, dst in (
            (gain_h, gain_v), (bias_h, bias_v), (rpe_h, rpe_v), (qb_h, qb_v), (ub_h, ub_v), (om_h, om_v), (bk_h, bk_v),
        )
    ]
    in_o = bring(wo_h.at[:, half_cols(x, 256)], wo.at[2 * z + x, c])
    in_tok = bring(tok, xg.at[pl.ds(pl.multiple_of(c * 256, 256), 256)], home)
    in_cot = bring(cot.at[pl.ds(pl.multiple_of(y * 128, 128), 128)], cotb, home)
    in_u = bring(wu_h.at[:, half_cols(x, 1024)], wu.at[2 * z + x, c])
    in_d = bring(wd_h.at[:, half_cols(x, 1024)], wd.at[2 * z + x, c])

    def dev(zz, xx, yy, cc):
        return {"dp": zz * 2 + xx, "heads": yy, "feat": cc}

    sib, xn, yn, dg = dev(z, x, y, 1 - c), dev(z, 1 - x, y, c), dev(z, x, 1 - y, c), dev(z, 1 - x, 1 - y, c)
    xs_dev, ds_dev = dev(z, 1 - x, y, 1 - c), dev(z, 1 - x, 1 - y, 1 - c)
    plane = (dg, xn, yn)
    own_block = 2 * x + y
    plane_block = (2 * (1 - x) + 1 - y, 2 * (1 - x) + y, 2 * x + 1 - y)

    def rc(src, dst, s, r, device):
        return pltpu.make_async_remote_copy(
            src_ref=src, dst_ref=dst, send_sem=ss.at[s], recv_sem=rs.at[r], device_id=device, device_id_type=MESH
        )

    def send(src, dst, s, r, device, cond=None):
        def go():
            rc(src, dst, s, r, device).start()

        def done():
            rc(src, dst, s, r, device).wait_send()

        if cond is None:
            go()
            pending.append(done)
        else:
            pl.when(cond)(go)
            pending.append(lambda: pl.when(cond)(done))

    def got(dst, r):
        rc(dst, dst, r, r, sib).wait_recv()

    def valid(dz):
        return jnp.logical_and(z + dz >= 0, z + dz < PLANES)

    barrier = pltpu.get_barrier_semaphore()
    for other in (sib, xn, yn, dg, xs_dev, ds_dev):
        pl.semaphore_signal(barrier, inc=1, device_id=other, device_id_type=MESH)
    for zz in range(PLANES):
        @pl.when(z != zz)
        def _(zz=zz):
            pl.semaphore_signal(barrier, inc=1, device_id=dev(zz, x, y, c), device_id_type=MESH)
    pl.semaphore_wait(barrier, 9)

    class Item:
        def __init__(self, ref, kind):
            self.ref, self.kind = ref, kind
            self.zs, self.fw, self.sb = sems.take(PLANES), sems.take(), sems.take(PLANES)

        def block(self, zz, cc):
            if self.kind == "both":
                return self.ref.at[pl.ds(2 * zz, 2), cc]
            return self.ref.at[:, 2 * zz + (x if self.kind == "own" else 1 - x), cc]

        def start(self):
            mine = self.block(z, c)
            for dz in (1, -1, 2, -2):
                send(mine, mine, self.zs + z + dz, self.zs + z, dev(z + dz, x, y, c), valid(dz))
            send(mine, mine, self.sb + z, self.sb + z, sib)

        def pump(self):
            for dz in (1, -1, 2, -2, 3, -3):
                here = self.block(z + dz, c)
                cond = valid(dz)
                pl.when(cond)(lambda here=here, dz=dz: got(here, self.zs + z + dz))
                if dz == 2:
                    send(here, here, self.fw, self.zs + z + dz, dev(z - 1, x, y, c), z == 1)
                if dz == -2:
                    send(here, here, self.fw, self.zs + z + dz, dev(z + 1, x, y, c), z == 2)
                send(here, here, self.sb + z + dz, self.sb + z + dz, sib, cond)

        def need(self):
            for zz in range(PLANES):
                got(self.block(zz, 1 - c), self.sb + zz)

    half_of = {}

    def place(ref, xx):
        return ref.at[:, 2 * z + xx, c] if len(ref.shape) == 5 else ref.at[2 * z + xx, c]

    def give_half(name, src, ref):
        i = sems.take()
        half_of[name] = (ref, i)
        send(src, place(ref, x), i, i, xn)

    def have_half(name):
        ref, i = half_of[name]
        got(place(ref, 1 - x), i)

    give_half("q", wq_h.at[:, :, half_cols(1 - x, 256)], wq)
    in_q()
    it_qa, it_s, it_qb = Item(wq, "own"), Item(small, "both"), Item(wq, "other")
    it_o, it_u, it_d = Item(wo, "both"), Item(wu, "both"), Item(wd, "both")
    it_qa.start()

    for done in in_small:
        done()

    def pick(shape, hit):
        return jnp.where(hit(iota(shape, 0), iota(shape, 1)), 1.0, 0.0)

    vec_sel = pick((64, 128), lambda k, l: l == c * 64 + k).astype(BF16)
    rpe_sel = pick((64, 128), lambda k, l: l == (1 - c) * 64 + 63 - k).astype(BF16)
    bias_sel = [pick((4, 128), lambda k, l, par=par: l == par * 64 + 4 * shard + k).astype(BF16) for par in range(2)]
    small_s[...] = jnp.zeros_like(small_s)
    rpe_rows = dot(rpe_v[...], rpe_sel)
    level = jnp.full((1, 128), bk_v[0].astype(F32))
    top = jnp.concatenate(
        [dot(gain_v[...], vec_sel), dot(bias_v[...], vec_sel), level, jnp.zeros((1, 128), F32)], axis=0
    )

    def spread(values):
        rows = values.shape[1]
        even = (iota((rows, 1), 0) % 2) == 0
        wide = jnp.where(even, dot(values, bias_sel[0], TN), dot(values, bias_sel[1], TN))
        return dot(pick((rows // 2, rows), lambda k, l: l // 2 == k).astype(BF16), wide.astype(BF16))

    up_rows = spread(ub_v[...])
    qkv_rows = [spread(qb_v[p]) for p in range(3)]
    for half in range(2):
        mine = [rows[2 * half : 2 * half + 2] for rows in qkv_rows] + [jnp.zeros((2, 128), F32)]
        position = jnp.concatenate([rpe_rows[4 * half : 4 * half + 4], jnp.zeros((4, 128), F32)], axis=0)
        small_s[half] = jnp.concatenate(
            [top, position] + mine + [up_rows[8 * half : 8 * half + 8]], axis=0
        ).astype(BF16)
    small[2 * z + x, c] = small_s[x]
    give_half("s", small_s.at[1 - x], small)
    for h in range(4):
        sel = pick((32, 256), lambda k, l: l == h * 64 + c * 32 + k).astype(BF16)
        om_s[h * 64 : (h + 1) * 64] = dot(om_v[4 * x + h], sel, TN).astype(BF16)
    i_om = sems.take()
    send(om_s, om2, i_om, i_om, sib)
    t1, t2 = sems.take(), sems.take(2)
    mine_rows = xg.at[pl.ds(pl.multiple_of(c * 256, 256), 256)]
    send(tok, mine_rows, t1, t1, sib, c != x)
    send(tok, mine_rows, t2 + c, t2 + c, dev(z, 1 - x, y, x))
    give_half("o", wo_h.at[:, half_cols(1 - x, 256)], wo)
    give_half("u", wu_h.at[:, half_cols(1 - x, 1024)], wu)
    give_half("d", wd_h.at[:, half_cols(1 - x, 1024)], wd)
    t3 = sems.take()
    send(cot.at[pl.ds(pl.multiple_of(y * 128, 128), 128)], cotb, t3, t3, xs_dev, c != x)

    same = (iota((256, 256), 0) // HEAD) == (iota((256, 256), 1) // HEAD)
    ones64[...] = jnp.where(same, 1.0, 0.0).astype(BF16)
    anti[...] = jnp.where(iota((512, 512), 0) + iota((512, 512), 1) == 511, 1.0, 0.0).astype(BF16)

    have_half("s")
    it_s.start()
    have_half("q")
    it_qb.start()
    it_qa.pump()
    have_half("o")
    in_o()
    it_o.start()
    it_s.pump()
    it_qb.pump()

    it_s.need()
    for t in range(8):
        tile = small[t, 0].astype(F32) + small[t, 1].astype(F32)
        rows_v[0:8, t * 128 : (t + 1) * 128] = tile[0:8]
        rows_v[8:16, (7 - t) * 128 : (8 - t) * 128] = tile[8:16]
        total = tile[16:32] if t == 0 else total + tile[16:32]
    for r in range(6):
        rows_v[16:17, r * 128 : (r + 1) * 128] = total[r : r + 1]
    for r in range(8):
        rows_v[17:18, r * 128 : (r + 1) * 128] = total[8 + r : 9 + r]
    level = small[2 * z + c, 0][6:7].astype(F32)
    wide1 = jnp.where(level > 0.5, 1.0, 0.0)
    wide2 = jnp.where(level > 1.5, 1.0, 0.0)
    one_row = jnp.ones((1, 128), F32)

    def mask_row(bi):
        parts = [one_row if bj == bi else (wide1 if bj // 2 == bi // 2 else wide2) for bj in range(4)]
        return jnp.concatenate(parts, axis=1)

    masks = [mask_row(bi) for bi in range(4)]

    def coeff_body(h, carry):
        row = jnp.exp(rows_v[pl.ds(8 + h, 1), :])
        r0[h] = pltpu.roll(jnp.broadcast_to(row, (128, 1024)), 1, 1, stride=1, stride_axis=0)
        return carry

    lax.fori_loop(0, 4, coeff_body, 0)

    have_half("u")
    in_u()
    it_u.start()
    in_tok()
    in_cot()
    pl.when(c == x)(lambda: got(xg.at[pl.ds(pl.multiple_of((1 - c) * 256, 256), 256)], t1))

    @pl.when(c != x)
    def _():
        got(xg.at[pl.ds(0, 256)], t2)
        got(xg.at[pl.ds(256, 256)], t2 + 1)
        got(cotb, t3)

    it_qa.need()
    it_qb.need()

    def qkv_body(p, carry):
        cols = pl.ds(pl.multiple_of(p * 256, 256), 256)
        qkv[p] = (dot(xg[...], wq[p].reshape(1024, 256)) + rows_v[16:17, cols]).astype(BF16)
        return carry

    lax.fori_loop(0, 3, qkv_body, 0)
    got(om2, i_om)
    om2[...] = om2[...] + om_s[...]

    def feature_body(t, carry):
        wide = qkv[t].astype(F32)
        sums = split_dot(wide * wide, ones64[...])
        inverse = lax.rsqrt(sums * (1.0 / HEAD) + UNIT_EPS)
        units = wide * inverse
        logits = SCALE * split_dot(units, om2[...]) - 0.5 * SCALE * SCALE * (sums * inverse * inverse)
        value = jnp.exp(logits) * M ** (-0.5)
        ex[t] = value
        unit[t] = units
        inv[t] = inverse
        phi[t] = value.astype(BF16)
        return carry

    lax.fori_loop(0, 2, feature_body, 0)
    have_half("d")
    in_d()
    it_d.start()
    it_o.pump()

    lane_head = iota((1, 128), 1) // HEAD
    num[...] = jnp.zeros_like(num)
    den[...] = jnp.zeros_like(den)

    def head_cols(h):
        return pl.ds(pl.multiple_of((h // 2) * 128, 128), 128), (lane_head == h % 2)

    def head_body(h, carry):
        cols, mine = head_cols(h)
        keep = jnp.where(mine, 1.0, 0.0).astype(BF16)
        scores = dot(phi[0, :, cols] * keep, phi[1, :, cols], NT)
        for b in range(4):
            coefficient = r0[h, :, 512 - 128 * b : 1024 - 128 * b] * masks[b]
            pp[h, b * 128 : (b + 1) * 128] = (scores[b * 128 : (b + 1) * 128] * coefficient).astype(BF16)
        right = jnp.concatenate([qkv[2, :, cols] * keep, jnp.broadcast_to(keep, (512, 128))], axis=1)
        both = dot(pp[h], right)
        num[:, cols] += both[:, :128]
        den[:, cols] += both[:, 128:]
        return carry

    lax.fori_loop(0, 4, head_body, 0)
    quo[...] = num[...] / den[...]
    att[...] = quo[...].astype(BF16)

    class Scatter:
        def __init__(self, ref):
            self.ref, self.base = ref, sems.take(12)

        def part(self, n):
            cols = pl.ds(pl.multiple_of(n * 256, 256), 256)
            for slot in range(3):
                i = self.base + slot * 4 + n
                rc(pb.at[plane_block[slot], :, cols], self.ref.at[slot, :, cols], i, i, plane[slot]).start()

        def total(self):
            for slot in range(3):
                for n in range(4):
                    got(self.ref.at[slot, :, n * 256 : (n + 1) * 256], self.base + slot * 4 + n)
            value = pb[own_block].astype(F32)
            for slot in range(3):
                value = value + self.ref[slot].astype(F32)
            return value

        def sent(self):
            for slot in range(3):
                for n in range(4):
                    i = self.base + slot * 4 + n
                    src = pb.at[plane_block[slot], :, n * 256 : (n + 1) * 256]
                    rc(src, src, i, i, plane[slot]).wait_send()

    class Gather:
        def __init__(self, ref):
            self.ref, self.base = ref, sems.take(3)

        def start(self):
            mine = self.ref.at[own_block]
            for slot in range(3):
                send(mine, mine, self.base + slot, self.base + slot, plane[slot])

        def need(self):
            for slot in range(3):
                got(self.ref.at[plane_block[slot]], self.base + slot)

    def scatter(ref, part):
        s = Scatter(ref)

        def body(n, carry):
            cols = pl.ds(pl.multiple_of(n * 256, 256), 256)
            pb[:, :, cols] = part(n).astype(BF16).reshape(4, 128, 256)
            s.part(n)
            return carry

        lax.fori_loop(0, 4, body, 0)
        return s

    it_o.need()
    sc_z = scatter(rb_z, lambda n: dot(att[...], wo[pl.ds(2 * n, 2)].reshape(256, 256), NT))
    it_u.pump()
    it_u.need()

    def norm(values):
        centred = values - jnp.mean(values, axis=-1, keepdims=True)
        inverse = lax.rsqrt(jnp.mean(centred * centred, axis=-1, keepdims=True) + EPSILON)
        return centred * inverse, inverse

    own_rows = pl.ds(pl.multiple_of(own_block * 128, 128), 128)
    residual = sc_z.total() + xg[own_rows].astype(F32) + rows_v[2:3, :]
    normed, inverse = norm(residual)
    first = normed * rows_v[0:1, :] + rows_v[3:4, :]
    fst[...] = first
    n1[...] = normed
    i1[...] = jnp.broadcast_to(inverse, (128, 128))
    fb[own_block] = first.astype(BF16)
    g_first = Gather(fb)
    g_first.start()
    sc_z.sent()
    g_first.need()

    def hidden_body(n, carry):
        cols = pl.ds(pl.multiple_of(n * 256, 256), 256)
        pre = dot(fb[...].reshape(512, 1024), wu[:, :, :, cols].reshape(1024, 256)) + rows_v[17:18, cols]
        cdf = 0.5 * (1.0 + lax.erf(pre * 0.7071067811865476))
        hid[:, cols] = (pre * cdf).astype(BF16)
        dgel[:, cols] = cdf + pre * (0.3989422804014327 * jnp.exp(-0.5 * pre * pre))
        return carry

    lax.fori_loop(0, 4, hidden_body, 0)
    it_d.pump()
    it_d.need()
    sc_f = scatter(rb_f, lambda n: dot(hid[...], wd[pl.ds(2 * n, 2)].reshape(256, 1024), NT))
    second = fst[...] + sc_f.total() + rows_v[4:5, :]
    normed2, inverse2 = norm(second)
    mix_s[...] = (normed2 * rows_v[1:2, :] + rows_v[5:6, :]).astype(BF16)

    def norm_back(upstream, normed, inverse, gain):
        scaled = upstream * gain
        mean = jnp.mean(scaled, axis=-1, keepdims=True)
        slope = jnp.mean(scaled * normed, axis=-1, keepdims=True)
        return inverse * (scaled - mean - normed * slope)

    def down(values):
        return jnp.sum(values, axis=0, keepdims=True)

    upstream = cotb[...].astype(F32)
    sd[1:2, :] = down(upstream * normed2)
    sd[5:6, :] = down(upstream)
    err = norm_back(upstream, normed2, inverse2, rows_v[1:2, :])
    efb[own_block] = err.astype(BF16)
    sd[4:5, :] = down(efb[own_block].astype(F32))
    g_ef = Gather(efb)
    g_ef.start()
    dr[...] = err
    sc_f.sent()

    i_mix, i_gt = sems.take(2), sems.take(2)

    def to_owner(src, dst, i):
        rows = pl.ds(pl.multiple_of(y * 128, 128), 128)
        home = c == x

        @pl.when(home)
        def _():
            dst[rows] = src[...]

        send(src, dst.at[rows], i + 1, i + 1, yn, home)
        away = jnp.logical_not(home)
        send(src, dst.at[rows], i, i + y, xs_dev, away)
        send(src, dst.at[rows], i + 1, i + y, ds_dev, away)

    def from_owner(dst, i):
        for half in range(2):
            part = dst.at[half * 128 : (half + 1) * 128]

            @pl.when(jnp.logical_and(c == x, y != half))
            def _(part=part):
                got(part, i + 1)

            @pl.when(c != x)
            def _(part=part, half=half):
                got(part, i + half)

    to_owner(mix_s, mixed_o, i_mix)
    g_ef.need()

    class Grad:
        def __init__(self, g, r1, t, rz, cb, xr):
            self.g, self.r1, self.t, self.rz, self.cb, self.xr = g, r1, t, rz, cb, xr
            self.d, self.z, self.k, self.x = sems.take(4), sems.take(PLANES), sems.take(), sems.take()

        def make(self, part):
            def body(m, carry):
                part(m)
                i = self.d + m
                rc(self.g.at[m, :, 1 - c], self.r1.at[m], i, i, sib).start()
                return carry

            lax.fori_loop(0, PLANES, body, 0)

            def done():
                for m in range(PLANES):
                    src = self.g.at[m, :, 1 - c]
                    rc(src, src, self.d + m, self.d + m, sib).wait_send()

            pending.append(done)

        def pair(self):
            def body(m, carry):
                got(self.r1.at[m], self.d + m)
                self.t[m] = (self.g[m, :, c].astype(F32) + self.r1[m].astype(F32)).astype(BF16)
                return carry

            lax.fori_loop(0, PLANES, body, 0)
            send(self.t.at[PLANES - 1], self.cb, self.k, self.k, dev(1, x, y, c), z == 0)
            send(self.t.at[0], self.cb, self.k, self.k, dev(2, x, y, c), z == 3)
            for dz in (1, -1):
                send(self.t.at[z + dz], self.rz.at[z], self.z + z + dz, self.z + z, dev(z + dz, x, y, c), valid(dz))
            for dz, at in ((2, 0), (-2, 3)):
                send(self.t.at[z + dz], self.rz.at[z], self.z + z + dz, self.z + z, dev(z + dz, x, y, c), z == at)

        def relay(self):
            for dz, at in ((2, 1), (-2, 2)):
                @pl.when(z == at)
                def _(dz=dz):
                    got(self.cb, self.k)
                    self.t[z + dz] = (self.t[z + dz].astype(F32) + self.cb[...].astype(F32)).astype(BF16)

                send(self.t.at[z + dz], self.rz.at[z], self.z + z + dz, self.z + z, dev(z + dz, x, y, c), z == at)

        def finish(self):
            width = self.t.shape[-1]
            acc = fs.at[:, :, 0:width]
            acc[...] = self.t[z].astype(F32)
            for dz in (1, -1, 2, -2):
                @pl.when(valid(dz))
                def _(dz=dz):
                    got(self.rz.at[z + dz], self.z + z + dz)
                    acc[...] += self.rz[z + dz].astype(F32)
            keep = xs.at[self.slot, :, 0:width]
            keep[...] = fs[1 - x, :, 0:width].astype(BF16)
            send(keep, self.xr, self.x, self.x, xn)

        def columns(self, out, half, value):
            if len(out.shape) == 3:
                for p in range(3):
                    out[p, :, half_cols(half, 256)] = value[:, p * 256 : (p + 1) * 256]
            else:
                out[:, half_cols(half, self.t.shape[-1])] = value

        def write_own(self, out):
            width = self.t.shape[-1]
            self.columns(out, x, fs[x, :, 0:width])

        def write_other(self, out):
            got(self.xr, self.x)
            self.columns(out, 1 - x, self.xr[...].astype(F32))

    gr_d = Grad(g_d, r1_d, t_d, rz_d, cb_d, xr_d)
    gr_u = Grad(g_u, r1_u, t_u, rz_u, cb_u, xr_u)
    gr_o = Grad(g_o, r1_o, t_o, rz_o, cb_o, xr_o)
    gr_q = Grad(g_q, r1_q, t_q, rz_q, cb_q, xr_q)
    for slot, gr in enumerate((gr_d, gr_u, gr_o, gr_q)):
        gr.slot = slot

    def d_cols(ref, m):
        return ref[:, :, pl.ds(pl.multiple_of(m * 256, 256), 256)].reshape(512, 256)

    def make_down(m):
        g_d[m] = dot(d_cols(efb, m), hid[...], TN).astype(BF16).reshape(2, 2, 64, 1024)

    gr_d.make(make_down)

    def du_body(n, carry):
        cols = pl.ds(pl.multiple_of(n * 256, 256), 256)
        dact = dot(efb[...].reshape(512, 1024), wd[:, :, :, cols].reshape(1024, 256))
        du = (dact * dgel[:, cols]).astype(BF16)
        dub[:, cols] = du
        st[0:1, cols] = down(du.astype(F32))
        return carry

    lax.fori_loop(0, 4, du_body, 0)
    sc_d = scatter(rb_d, lambda n: dot(dub[...], wu[pl.ds(2 * n, 2)].reshape(256, 1024), NT))
    gr_d.pair()

    def make_up(m):
        g_u[m] = dot(d_cols(fb, m), dub[...], TN).astype(BF16).reshape(2, 2, 64, 1024)

    gr_u.make(make_up)
    gr_u.pair()
    gr_d.relay()
    dfirst = dr[...] + sc_d.total()
    sd[0:1, :] = down(dfirst * n1[...])
    sd[3:4, :] = down(dfirst)
    back = norm_back(dfirst, n1[...], i1[:, 0:1], rows_v[0:1, :])
    dr[...] = back
    dzb[own_block] = back.astype(BF16)
    sd[2:3, :] = down(dzb[own_block].astype(F32))
    g_dz = Gather(dzb)
    g_dz.start()
    sc_d.sent()

    i_sd = sems.take(3)
    sd[6:8, :] = jnp.zeros((2, 1024), F32)
    for k, device in enumerate(plane):
        send(sd, sd_r.at[k], i_sd + k, i_sd + k, device)
    g_dz.need()

    dattn = dot(dzb[...].reshape(512, 1024), wo[...].reshape(1024, 256))

    def make_out(m):
        g_o[m] = dot(d_cols(dzb, m), att[...], TN).astype(BF16).reshape(2, 2, 64, 256)

    gr_o.make(make_out)
    recip = 1.0 / den[...]
    dn[...] = (dattn * recip).astype(BF16)
    dsum = split_dot(dattn * quo[...], ones64[...])
    dd[...] = ((-dsum * recip).astype(BF16).astype(F32) * (1.0 / HEAD)).astype(BF16)
    gr_o.pair()
    gr_u.relay()
    dph[...] = jnp.zeros_like(dph)
    dvv[...] = jnp.zeros_like(dvv)

    def head_back(h, carry):
        cols, mine = head_cols(h)
        keep = jnp.where(mine, 1.0, 0.0).astype(BF16)
        dnum = dn[:, cols] * keep
        left = jnp.concatenate([dnum, dd[:, cols] * keep], axis=1)
        right = jnp.concatenate([qkv[2, :, cols], jnp.ones((512, 128), BF16)], axis=1)
        grad_p = dot(left, right, NT)
        for b in range(4):
            rows = slice(b * 128, (b + 1) * 128)
            coefficient = r0[h, :, 512 - 128 * b : 1024 - 128 * b] * masks[b]
            part = grad_p[rows]
            ds_[rows] = (part * coefficient).astype(BF16)
            gg[rows] = (part * pp[h, rows].astype(F32)).astype(BF16)
        dvv[:, cols] += dot(pp[h], dnum, TN)
        dph[0, :, cols] += dot(ds_[...], phi[1, :, cols] * keep)
        dph[1, :, cols] += dot(ds_[...], phi[0, :, cols] * keep, TN)
        flipped = dot(anti[...], gg[...])
        sums = jnp.zeros((1, 1024), F32)
        for b in range(4):
            wide = jnp.concatenate([flipped[b * 128 : (b + 1) * 128], jnp.zeros((128, 128), F32)], axis=1)
            line = down(pltpu.roll(wide, 0, 1, stride=1, stride_axis=0))
            pieces = [line]
            if b > 0:
                pieces = [jnp.zeros((1, 128 * b), F32)] + pieces
            if b < 3:
                pieces = pieces + [jnp.zeros((1, 384 - 128 * b), F32)]
            sums = sums + jnp.concatenate(pieces, axis=1)
        st[pl.ds(2 + h, 1), :] = sums
        return carry

    lax.fori_loop(0, 4, head_back, 0)
    gr_o.relay()

    def feature_back_body(t, carry):
        dlog = (dph[t] * ex[t]).astype(BF16)
        units = unit[t]
        dunit = SCALE * dot(dlog, om2[...], NT) - SCALE * SCALE * dot(dlog, ones64[...]) * units
        mean = split_dot(dunit * units, ones64[...]) * (1.0 / HEAD)
        dqkv[t] = (inv[t] * (dunit - units * mean)).astype(BF16)
        return carry

    lax.fori_loop(0, 2, feature_back_body, 0)
    dqkv[2] = dvv[...].astype(BF16)

    def input_part(n):
        value = jnp.zeros((512, 256), F32)
        for p in range(3):
            value = value + dot(dqkv[p], wq[p, pl.ds(2 * n, 2)].reshape(256, 256), NT)
        return value

    sc_i = scatter(rb_i, input_part)

    def make_qkv(m):
        left = xg[:, pl.ds(pl.multiple_of(m * 256, 256), 256)]
        for p in range(3):
            value = dot(left, dqkv[p], TN).astype(BF16).reshape(2, 2, 64, 256)
            g_q[m, :, :, :, p * 256 : (p + 1) * 256] = value

    gr_q.make(make_qkv)
    for p in range(3):
        st[1:2, p * 256 : (p + 1) * 256] = down(dqkv[p].astype(F32))
    st[1:2, 768:1024] = jnp.zeros((1, 256), F32)
    st[6:8, :] = jnp.zeros((2, 1024), F32)
    gr_q.pair()

    i_c, i_zz, i_h = sems.take(), sems.take(PLANES), sems.take()
    for k in range(3):
        got(sd_r.at[k], i_sd + k)
    st[8:16, :] = sd[...] + sd_r[0] + sd_r[1] + sd_r[2]
    send(st, st_r.at[0], i_c, i_c, sib)
    got(st_r.at[0], i_c)
    st_r[1] = st[...] + st_r[0]
    for zz in range(PLANES):
        send(st_r.at[1], st_r.at[2 + z], i_zz + zz, i_zz + z, dev(zz, x, y, c), z != zz)

    gr_d.finish()
    gr_d.write_own(gd_o)
    gr_u.finish()
    gr_u.write_own(gu_o)
    gr_o.finish()
    gr_o.write_own(go_o)
    outs = []
    from_owner(mixed_o, i_mix)
    outs.append(bring(mixed_o, mixed_h))
    gr_d.write_other(gd_o)
    outs.append(bring(gd_o, gd_h))
    back = dr[...] + sc_i.total()
    gt_s[...] = back.astype(BF16)
    to_owner(gt_s, gt_r, i_gt)
    sc_i.sent()
    gr_q.relay()
    total = st_r[1]
    for zz in range(PLANES):
        @pl.when(z != zz)
        def _(zz=zz):
            got(st_r.at[2 + zz], i_zz + zz)

        @pl.when(z == zz)
        def _(zz=zz):
            st_r[2 + zz] = jnp.zeros((16, 1024), F32)
        total = total + st_r[2 + zz]
    st_r[0] = total
    tvec_o[x] = total[0:8]
    send(tvec_o.at[x], tvec_o.at[x], i_h, i_h, xn)
    gr_u.write_other(gu_o)
    outs.append(bring(gu_o, gu_h))
    gr_o.write_other(go_o)
    outs.append(bring(go_o, go_h))

    def exact(left, right):
        return lax.dot_general(left, right, NN, precision=lax.Precision.HIGHEST, preferred_element_type=F32)

    own = exact(
        st_r[0, 8:16, pl.ds(pl.multiple_of(dp * 128, 128), 128)], pick((128, 64), lambda k, l: k == c * 64 + l)
    )
    ggain_o[...] = own[0:2]
    gbias_o[...] = own[2:6]
    outs.append(bring(ggain_o, ggain_h))
    outs.append(bring(gbias_o, gbias_h))
    got(tvec_o.at[1 - x], i_h)
    tile = pl.ds(pl.multiple_of((7 - dp) * 128, 128), 128)
    lines = jnp.concatenate([tvec_o[0, 2:6, tile], tvec_o[1, 2:6, tile]], axis=0)
    grpe_o[...] = exact(lines, pick((128, 64), lambda k, l: k == (1 - c) * 64 + 63 - l))
    outs.append(bring(grpe_o, grpe_h))
    lines = [
        tvec_o[half, 1:2, p * 256 + t * 128 : p * 256 + (t + 1) * 128]
        for p in range(3) for half in range(2) for t in range(2)
    ] + [tvec_o[half, 0:1, t * 128 : (t + 1) * 128] for half in range(2) for t in range(8)]
    lines = jnp.concatenate(lines + [jnp.zeros((4, 128), F32)], axis=0)
    found = jnp.zeros((4, 56), F32)
    for par in range(2):
        hit = pick((4, 128), lambda k, l: l == par * 64 + 4 * shard + k)
        values = lax.dot_general(hit, lines, NT, precision=lax.Precision.HIGHEST, preferred_element_type=F32)
        found = found + exact(values, pick((32, 56), lambda k, l: (l // 2 == k) & (l % 2 == par)))
    for p in range(3):
        gqb_o[p] = found[:, 8 * p : 8 * p + 8]
    gub_o[...] = found[:, 24:56]
    outs.append(bring(gqb_o, gqb_h))
    outs.append(bring(gub_o, gub_h))
    from_owner(gt_r, i_gt)
    gtok_o[...] = gt_r[...].astype(F32)
    outs.append(bring(gtok_o, gtok_h))
    gr_q.finish()
    gr_q.write_own(gq_o)
    gr_q.write_other(gq_o)
    outs.append(bring(gq_o, gq_h))
    for done in pending + outs:
        done()


def copy_kernel(*refs):
    count = len(refs) // 3
    sem = refs[-1]
    ins = [pltpu.make_async_copy(refs[i], refs[2 * count + i], sem.at[0, i]) for i in range(count)]
    outs = [pltpu.make_async_copy(refs[2 * count + i], refs[count + i], sem.at[1, i]) for i in range(count)]
    for copy in ins:
        copy.start()
    for one, two in zip(ins, outs):
        one.wait()
        two.start()
    for copy in outs:
        copy.wait()


def fast_local(
    tokens, qkv_weight, qkv_bias, out_weight, norm_gains, row_biases, up_weight, up_bias, down_weight, rpe_bias, omega,
    bucket, cotangent,
):
    def vm(shape, dtype=BF16):
        return pltpu.VMEM(shape, dtype)

    widths = (768, 256, 1024, 1024)
    scratch = [vm((3, 4, 8)), vm((2, 64)), vm((4, 64)), vm((4, 32)), vm((8, 64)), vm((8, 32, 64))]
    scratch += [pltpu.SMEM((1,), jnp.int32)]
    scratch += [vm((2, 32, 128)), vm((256, 256))]
    results = (
        ((256, 1024), BF16), ((256, 1024), F32), ((3, 64, 512), F32), ((3, 4, 8), F32), ((64, 512), F32), ((2, 64), F32),
        ((4, 64), F32), ((64, 2048), F32), ((4, 32), F32), ((64, 2048), F32), ((8, 64), F32),
    )
    scratch += [vm(*result) for result in results]
    scratch += [vm((2, 8, 1024), F32), vm((3, 8, 2, 64, 256))] + [vm((8, 2, 64, n)) for n in widths[1:]]
    scratch += [vm((8, 2, 32, 128)), vm((256, 256)), vm((512, 1024)), vm((128, 1024))]
    scratch += [vm((3, 512, 256)), vm((2, 512, 256))] + [vm((2, 512, 256), F32)] * 3
    scratch += [vm((4, 128, 1024), F32), vm((4, 512, 512))] + [vm((512, 256), F32)] * 3 + [vm((512, 256))]
    scratch += [vm((4, 128, 1024))] + [vm((3, 128, 1024))] * 4
    scratch += [vm((4, 128, 1024)), vm((512, 1024)), vm((512, 1024), F32)]
    scratch += [vm((4, 128, 1024)), vm((512, 1024)), vm((4, 128, 1024))]
    scratch += [vm((128, 1024), F32)] * 2 + [vm((128, 128), F32), vm((128, 1024), F32)]
    scratch += [vm((512, 256))] * 2 + [vm((512, 512))] * 2 + [vm((2, 512, 256), F32), vm((512, 256), F32)]
    scratch += [vm((3, 512, 256)), vm((512, 512)), vm((256, 256)), vm((24, 1024), F32)]
    scratch += [vm((4, 2, 2, 64, n)) for n in widths]
    scratch += [vm((4, 2, 64, n)) for n in widths] * 2
    scratch += [vm((4, 2, 64, n)) for n in widths] + [vm((2, 64, n)) for n in widths]
    scratch += [vm((2, 64, 1024), F32), vm((4, 64, 1024))] + [vm((64, n)) for n in widths]
    scratch += [vm((8, 1024), F32), vm((3, 8, 1024), F32), vm((16, 1024), F32), vm((6, 16, 1024), F32)]
    scratch += [vm((128, 1024)), vm((128, 1024)), vm((256, 1024))]
    scratch += [pltpu.SemaphoreType.DMA((320,)), pltpu.SemaphoreType.DMA((320,)), pltpu.SemaphoreType.DMA((40,))]

    shapes = tuple(jax.ShapeDtypeStruct(*result) for result in results)
    anywhere = pl.BlockSpec(memory_space=pl.ANY)
    made = pl.pallas_call(
        layer_kernel,
        out_shape=shapes,
        in_specs=[anywhere] * 13,
        out_specs=(anywhere,) * len(shapes),
        scratch_shapes=scratch,
        compiler_params=pltpu.CompilerParams(
            collective_id=0, has_side_effects=True, vmem_limit_bytes=63 * 2**20
        ),
        name="layer",
    )(
        tokens, qkv_weight.transpose(1, 0, 2), qkv_bias.transpose(0, 2, 1), out_weight.T, norm_gains, row_biases, up_weight,
        up_bias.T, down_weight.T, rpe_bias, omega.transpose(0, 2, 1), bucket, cotangent,
    )
    mixed, gtok, gq, gqb, go, ggain, gbias, gu, gub, gd, grpe = pl.pallas_call(
        copy_kernel,
        out_shape=shapes,
        in_specs=[anywhere] * len(shapes),
        out_specs=(anywhere,) * len(shapes),
        scratch_shapes=[vm(*result) for result in results] + [pltpu.SemaphoreType.DMA((2, len(shapes)))],
        compiler_params=pltpu.CompilerParams(vmem_limit_bytes=63 * 2**20),
        name="results",
    )(*made)
    return (
        mixed, gtok, gq.transpose(1, 0, 2), gqb.transpose(0, 2, 1), go.T, ggain, gbias, gu, gub.T, gd.T, grpe,
    )


def solution(mesh):
    sizes = (mesh.shape["dp"], mesh.shape["heads"], mesh.shape["feat"])
    return jax.shard_map(
        fast_local if sizes == (2 * PLANES, 2, 2) else local,
        mesh=mesh,
        in_specs=(
            P(("dp", "feat"), None),
            P(("dp", "feat"), None, "heads"),
            P(None, "heads", ("dp", "feat")),
            P("heads", ("dp", "feat")),
            P(None, ("dp", "feat")),
            P(None, ("dp", "feat")),
            P(("dp", "feat"), "heads"),
            P("heads", ("dp", "feat")),
            P("heads", ("dp", "feat")),
            P("heads", ("dp", "feat")),
            P("heads", None, "feat"),
            P("dp"),
            P(("dp", "feat"), None),
        ),
        out_specs=(
            P(("dp", "feat"), None),
            P(("dp", "feat"), None),
            P(("dp", "feat"), None, "heads"),
            P(None, "heads", ("dp", "feat")),
            P("heads", ("dp", "feat")),
            P(None, ("dp", "feat")),
            P(None, ("dp", "feat")),
            P(("dp", "feat"), "heads"),
            P("heads", ("dp", "feat")),
            P("heads", ("dp", "feat")),
            P("heads", ("dp", "feat")),
        ),
        check_vma=False,
    )
```

```python
import functools

import jax
import jax.numpy as jnp
from jax import lax
from jax.experimental import pallas as pl
from jax.experimental.pallas import tpu as pltpu
from jax.sharding import PartitionSpec as P

HEAD = 64
M = 64


EPSILON = 1e-12
UNIT_EPS = 1e-06


def toeplitz_block(window, extent):
    leading = window.shape[0]
    tiled_rows = jnp.broadcast_to(window[:, None, :], (leading, extent, 2 * extent - 1)).reshape(
        leading, -1
    )
    padded = jnp.pad(tiled_rows, ((0, 0), (0, extent)))
    sheared = padded.reshape(leading, extent, 2 * extent)[:, :, :extent]
    return sheared[:, :, ::-1]


def diagonal_sums(values_grid, extent):
    leading = values_grid.shape[0]
    flipped = values_grid[:, :, ::-1]
    padded = jnp.pad(flipped, ((0, 0), (0, 0), (0, extent))).reshape(leading, -1)
    sheared = padded[:, : extent * (2 * extent - 1)].reshape(leading, extent, 2 * extent - 1)
    return jnp.sum(sheared, axis=1)


def norm_forward(values, gain, shift):
    centred = values - jnp.mean(values, axis=-1, keepdims=True)
    inverse = lax.rsqrt(jnp.mean(centred * centred, axis=-1, keepdims=True) + EPSILON)
    normed = centred * inverse
    return (normed * gain + shift, normed, inverse)


def norm_backward(upstream, normed, inverse, gain):
    scaled_grad = upstream * gain
    return inverse * (
        scaled_grad
        - jnp.mean(scaled_grad, axis=-1, keepdims=True)
        - normed * jnp.mean(scaled_grad * normed, axis=-1, keepdims=True)
    )


def feature_logits(entries, omega_local):
    factor = HEAD ** (-0.25)
    wide = entries.astype(jnp.float32)
    inverse = lax.rsqrt(jnp.mean(wide * wide, axis=-1, keepdims=True) + UNIT_EPS)
    unit = wide * inverse
    projected = jnp.einsum(
        "rhe,hem->hmr",
        unit,
        omega_local.astype(jnp.float32),
        precision=lax.Precision.HIGHEST,
        preferred_element_type=jnp.float32,
    )
    squares = jnp.sum(unit * unit, axis=-1)
    return (factor * projected - 0.5 * factor * factor * squares.T[:, None, :], unit, inverse)


def feature_back(grad_phi, logits, unit, inverse, omega_local):
    factor = HEAD ** (-0.25)
    grad_logits = (grad_phi * (jnp.exp(logits) * M ** (-0.5))).astype(jnp.bfloat16)
    projected = jnp.einsum(
        "hmr,hem->rhe", grad_logits, omega_local, preferred_element_type=jnp.float32
    )
    totals = jnp.sum(grad_logits.astype(jnp.float32), axis=1)
    grad_unit = factor * projected - factor * factor * totals.T[:, :, None] * unit
    return inverse * (grad_unit - unit * jnp.mean(grad_unit * unit, axis=-1, keepdims=True))


def window_begin(row_start, col_start, extent, rows_total):
    return row_start - col_start + rows_total - extent + 1


def block_coeff(rpe_exp, window_start, extent):
    window = lax.dynamic_slice_in_dim(rpe_exp, window_start, 2 * extent - 1, 1)
    return toeplitz_block(window, extent)


def local(
    tokens,
    qkv_weight,
    qkv_bias,
    out_weight,
    norm_gains,
    row_biases,
    up_weight,
    up_bias,
    down_weight,
    rpe_bias,
    omega,
    bucket,
    cotangent,
):
    qkv_full, out_full, up_full, down_full, gains_all, biases_all, bias_qkv, bias_up, rpe_all = (
        lax.all_gather(qkv_weight, ("dp", "feat"), axis=0, tiled=True),
        lax.all_gather(out_weight, ("dp", "feat"), axis=1, tiled=True),
        lax.all_gather(up_weight, ("dp", "feat"), axis=0, tiled=True),
        lax.all_gather(down_weight, ("dp", "feat"), axis=1, tiled=True),
        lax.all_gather(norm_gains, ("dp", "feat"), axis=1, tiled=True),
        lax.all_gather(row_biases, ("dp", "feat"), axis=1, tiled=True),
        lax.all_gather(qkv_bias, ("dp", "feat"), axis=2, tiled=True),
        lax.all_gather(up_bias, ("dp", "feat"), axis=1, tiled=True),
        lax.all_gather(rpe_bias, ("dp", "feat"), axis=1, tiled=True),
    )
    model_width = qkv_full.shape[0]
    head_cols = qkv_full.shape[2]
    local_heads = omega.shape[0]
    local_feats = omega.shape[2]
    rows_own = tokens.shape[0]
    rows_total = rows_own * lax.axis_size("feat")
    block_rows = min(512, rows_total // 4)
    blocks = rows_total // block_rows
    seq_length = rows_total // 4 * jnp.where(bucket[0] == 0, 1, jnp.where(bucket[0] == 1, 2, 4))
    block_count = seq_length // block_rows
    gain_rows = gains_all.astype(jnp.float32)
    bias_rows = biases_all.astype(jnp.float32)
    rpe_exp = jnp.exp(rpe_all.astype(jnp.float32))
    projected = jnp.dot(
        tokens, qkv_full.reshape(model_width, 3 * head_cols), preferred_element_type=jnp.float32
    )
    projected = projected + bias_qkv.reshape(-1).astype(jnp.float32)
    qkv_own = projected.astype(jnp.bfloat16)
    qkv_all = lax.all_gather(qkv_own, "feat", axis=0, tiled=True).reshape(
        rows_total, 3, local_heads, HEAD
    )
    queries = qkv_all[:, 0]
    keys_rows = qkv_all[:, 1]
    values_rows = qkv_all[:, 2]
    logits_query, unit_query, inverse_query = feature_logits(queries, omega)
    logits_key, unit_key, inverse_key = feature_logits(keys_rows, omega)
    feat_query = (jnp.exp(logits_query) * M ** (-0.5)).astype(jnp.bfloat16)
    feat_key = (jnp.exp(logits_key) * M ** (-0.5)).astype(jnp.bfloat16)
    numer_parts = []
    denom_parts = []
    for row_block in range(blocks):
        row_start = row_block * block_rows
        first_block = row_start // seq_length * block_count
        phi_rows = feat_query[:, :, row_start : row_start + block_rows]

        def visit(column_block, carried, phi_rows=phi_rows, row_start=row_start):
            numer_acc, denom_acc = carried
            col_start = column_block * block_rows
            phi_cols = lax.dynamic_slice_in_dim(feat_key, col_start, block_rows, 2)
            value_cols = lax.dynamic_slice_in_dim(values_rows, col_start, block_rows, 0)
            coefficient = block_coeff(
                rpe_exp, window_begin(row_start, col_start, block_rows, rows_total), block_rows
            )
            scores = jnp.einsum(
                "hmi,hmj->hij", phi_rows, phi_cols, preferred_element_type=jnp.float32
            )
            weights = (coefficient * scores).astype(jnp.bfloat16)
            numer_acc = numer_acc + jnp.einsum(
                "hij,jhe->ihe", weights, value_cols, preferred_element_type=jnp.float32
            )
            denom_acc = denom_acc + jnp.sum(weights.astype(jnp.float32), axis=-1)
            return (numer_acc, denom_acc)

        start_pair = (
            jnp.zeros((block_rows, local_heads, HEAD), jnp.float32),
            jnp.zeros((local_heads, block_rows), jnp.float32),
        )
        numer_block, denom_block = lax.fori_loop(
            first_block, first_block + block_count, visit, start_pair
        )
        numer_parts.append(numer_block)
        denom_parts.append(denom_block)
    numer_all = jnp.concatenate(numer_parts, axis=0).reshape(rows_total, head_cols)
    denom_all = jnp.concatenate(denom_parts, axis=1)
    numer_own, denom_own = (
        lax.psum_scatter(
            numer_all.astype(jnp.bfloat16), "feat", scatter_dimension=0, tiled=True
        ).astype(jnp.float32),
        lax.psum_scatter(
            denom_all.astype(jnp.bfloat16), "feat", scatter_dimension=1, tiled=True
        ).astype(jnp.float32),
    )
    denom_rows = denom_own.T
    quotient = numer_own.reshape(rows_own, local_heads, HEAD) / denom_rows[:, :, None]
    attn_low = quotient.reshape(rows_own, head_cols).astype(jnp.bfloat16)
    z_part = jnp.dot(attn_low, out_full, preferred_element_type=jnp.float32)
    mixed_z = lax.psum(z_part.astype(jnp.bfloat16), "heads").astype(jnp.float32) + bias_rows[0]
    first_out, normed_one, inverse_one = norm_forward(
        tokens.astype(jnp.float32) + mixed_z, gain_rows[0], bias_rows[1]
    )
    first_low = first_out.astype(jnp.bfloat16)
    pre_act = jnp.dot(first_low, up_full, preferred_element_type=jnp.float32) + bias_up.reshape(
        -1
    ).astype(jnp.float32)
    act_value, act_pull = jax.vjp(lambda inner: jax.nn.gelu(inner, approximate=False), pre_act)
    act_low = act_value.astype(jnp.bfloat16)
    ffn_part = jnp.dot(act_low, down_full, preferred_element_type=jnp.float32)
    ffn_out = lax.psum(ffn_part.astype(jnp.bfloat16), "heads").astype(jnp.float32) + bias_rows[2]
    final_rows, normed_two, inverse_two = norm_forward(
        first_out + ffn_out, gain_rows[1], bias_rows[3]
    )
    mixed = final_rows.astype(jnp.bfloat16)
    qkv_full, out_full, up_full, down_full, gains_all, rpe_all = (
        lax.all_gather(qkv_weight, ("dp", "feat"), axis=0, tiled=True),
        lax.all_gather(out_weight, ("dp", "feat"), axis=1, tiled=True),
        lax.all_gather(up_weight, ("dp", "feat"), axis=0, tiled=True),
        lax.all_gather(down_weight, ("dp", "feat"), axis=1, tiled=True),
        lax.all_gather(norm_gains, ("dp", "feat"), axis=1, tiled=True),
        lax.all_gather(rpe_bias, ("dp", "feat"), axis=1, tiled=True),
    )
    gain_rows = gains_all.astype(jnp.float32)
    rpe_exp = jnp.exp(rpe_all.astype(jnp.float32))
    upstream = cotangent.astype(jnp.float32)
    grad_gain_two = jnp.sum(upstream * normed_two, axis=0)
    grad_shift_two = jnp.sum(upstream, axis=0)
    resid_two = norm_backward(upstream, normed_two, inverse_two, gain_rows[1])
    resid_low = resid_two.astype(jnp.bfloat16)
    grad_bias_down = jnp.sum(resid_low.astype(jnp.float32), axis=0)
    grad_down = jnp.einsum("rf,rd->fd", act_low, resid_low, preferred_element_type=jnp.float32)
    grad_act = jnp.einsum("rd,fd->rf", resid_low, down_full, preferred_element_type=jnp.float32)
    grad_pre = act_pull(grad_act)[0].astype(jnp.bfloat16)
    grad_up = jnp.einsum("rd,rf->df", first_low, grad_pre, preferred_element_type=jnp.float32)
    grad_bias_up = jnp.sum(grad_pre.astype(jnp.float32), axis=0).reshape(bias_up.shape)
    first_back = lax.psum(
        jnp.einsum("rf,df->rd", grad_pre, up_full, preferred_element_type=jnp.float32).astype(
            jnp.bfloat16
        ),
        "heads",
    ).astype(jnp.float32)
    grad_first = resid_two + first_back
    grad_gain_one = jnp.sum(grad_first * normed_one, axis=0)
    grad_shift_one = jnp.sum(grad_first, axis=0)
    resid_one = norm_backward(grad_first, normed_one, inverse_one, gain_rows[0])
    resid_one_low = resid_one.astype(jnp.bfloat16)
    grad_bias_out = jnp.sum(resid_one_low.astype(jnp.float32), axis=0)
    grad_out = jnp.einsum("rc,rd->cd", attn_low, resid_one_low, preferred_element_type=jnp.float32)
    grad_attn = jnp.einsum(
        "rd,cd->rc", resid_one_low, out_full, preferred_element_type=jnp.float32
    ).reshape(rows_own, local_heads, HEAD)
    grad_numer = (grad_attn / denom_rows[:, :, None]).astype(jnp.bfloat16)
    grad_denom = (-jnp.sum(grad_attn * quotient, axis=-1) / denom_rows).astype(jnp.bfloat16)
    numer_grad_all, denom_grad_all = (
        lax.all_gather(grad_numer.reshape(rows_own, head_cols), "feat", axis=0, tiled=True),
        lax.all_gather(grad_denom.T, "feat", axis=1, tiled=True),
    )
    numer_grad_all = numer_grad_all.reshape(rows_total, local_heads, HEAD)
    dphi_key = jnp.zeros((local_heads, local_feats, rows_total), jnp.float32)
    dvalues = jnp.zeros((rows_total, local_heads, HEAD), jnp.float32)
    grad_rpe = jnp.zeros(rpe_exp.shape, jnp.float32)
    dquery_parts = []
    for row_block in range(blocks):
        row_start = row_block * block_rows
        first_block = row_start // seq_length * block_count
        phi_rows = feat_query[:, :, row_start : row_start + block_rows]
        numer_rows = numer_grad_all[row_start : row_start + block_rows]
        denom_cols = denom_grad_all[:, row_start : row_start + block_rows].astype(jnp.float32)

        def visit_back(
            column_block,
            carried,
            phi_rows=phi_rows,
            row_start=row_start,
            numer_rows=numer_rows,
            denom_cols=denom_cols,
        ):
            dquery_acc, dkey_all, dvalue_all, drpe_all = carried
            col_start = column_block * block_rows
            phi_cols = lax.dynamic_slice_in_dim(feat_key, col_start, block_rows, 2)
            value_cols = lax.dynamic_slice_in_dim(values_rows, col_start, block_rows, 0)
            window_start = window_begin(row_start, col_start, block_rows, rows_total)
            coefficient = block_coeff(rpe_exp, window_start, block_rows)
            scores = jnp.einsum(
                "hmi,hmj->hij", phi_rows, phi_cols, preferred_element_type=jnp.float32
            )
            weights = (coefficient * scores).astype(jnp.bfloat16)
            grad_weights = (
                jnp.einsum(
                    "ihe,jhe->hij", numer_rows, value_cols, preferred_element_type=jnp.float32
                )
                + denom_cols[:, :, None]
            )
            dvalue_block = jnp.einsum(
                "hij,ihe->jhe", weights, numer_rows, preferred_element_type=jnp.float32
            )
            dvalue_all = lax.dynamic_update_slice_in_dim(
                dvalue_all,
                lax.dynamic_slice_in_dim(dvalue_all, col_start, block_rows, 0) + dvalue_block,
                col_start,
                0,
            )
            grad_scores = (grad_weights * coefficient).astype(jnp.bfloat16)
            diagonal = diagonal_sums(grad_weights * scores * coefficient, block_rows)
            drpe_all = lax.dynamic_update_slice_in_dim(
                drpe_all,
                lax.dynamic_slice_in_dim(drpe_all, window_start, 2 * block_rows - 1, 1) + diagonal,
                window_start,
                1,
            )
            dquery_acc = dquery_acc + jnp.einsum(
                "hij,hmj->hmi", grad_scores, phi_cols, preferred_element_type=jnp.float32
            )
            dkey_block = jnp.einsum(
                "hij,hmi->hmj", grad_scores, phi_rows, preferred_element_type=jnp.float32
            )
            dkey_all = lax.dynamic_update_slice_in_dim(
                dkey_all,
                lax.dynamic_slice_in_dim(dkey_all, col_start, block_rows, 2) + dkey_block,
                col_start,
                2,
            )
            return (dquery_acc, dkey_all, dvalue_all, drpe_all)

        start_state = (
            jnp.zeros((local_heads, local_feats, block_rows), jnp.float32),
            dphi_key,
            dvalues,
            grad_rpe,
        )
        dquery_block, dphi_key, dvalues, grad_rpe = lax.fori_loop(
            first_block, first_block + block_count, visit_back, start_state
        )
        dquery_parts.append(dquery_block)
    dphi_query = jnp.concatenate(dquery_parts, axis=2)
    grad_query = feature_back(dphi_query, logits_query, unit_query, inverse_query, omega)
    grad_key = feature_back(dphi_key, logits_key, unit_key, inverse_key, omega)
    grad_qkv_all = jnp.stack((grad_query, grad_key, dvalues), axis=1).reshape(
        rows_total, 3 * head_cols
    )
    grad_qkv_own = lax.psum_scatter(
        grad_qkv_all.astype(jnp.bfloat16), "feat", scatter_dimension=0, tiled=True
    )
    grad_bias_qkv = jnp.sum(grad_qkv_own.astype(jnp.float32), axis=0).reshape(bias_qkv.shape)
    grad_qkv_weight = jnp.einsum(
        "rd,rc->dc", tokens, grad_qkv_own, preferred_element_type=jnp.float32
    ).reshape(qkv_full.shape)
    input_terms = jnp.einsum(
        "rc,dc->rd",
        grad_qkv_own,
        qkv_full.reshape(model_width, 3 * head_cols),
        preferred_element_type=jnp.float32,
    )
    grad_tokens = resid_one + lax.psum(input_terms.astype(jnp.bfloat16), "heads").astype(
        jnp.float32
    )
    grad_gains = jnp.stack((grad_gain_one, grad_gain_two), axis=0)
    grad_shifts = jnp.stack((grad_bias_out, grad_shift_one, grad_bias_down, grad_shift_two), axis=0)
    (
        sent_qkv,
        sent_out,
        sent_up,
        sent_down,
        sent_gains,
        sent_shifts,
        sent_bias_qkv,
        sent_bias_up,
        sent_rpe,
    ) = (
        lax.psum_scatter(
            grad_qkv_weight.astype(jnp.bfloat16), ("dp", "feat"), scatter_dimension=0, tiled=True
        ).astype(jnp.float32),
        lax.psum_scatter(
            grad_out.astype(jnp.bfloat16), ("dp", "feat"), scatter_dimension=1, tiled=True
        ).astype(jnp.float32),
        lax.psum_scatter(
            grad_up.astype(jnp.bfloat16), ("dp", "feat"), scatter_dimension=0, tiled=True
        ).astype(jnp.float32),
        lax.psum_scatter(
            grad_down.astype(jnp.bfloat16), ("dp", "feat"), scatter_dimension=1, tiled=True
        ).astype(jnp.float32),
        lax.psum_scatter(
            grad_gains.astype(jnp.bfloat16), ("dp", "feat"), scatter_dimension=1, tiled=True
        ).astype(jnp.float32),
        lax.psum_scatter(
            grad_shifts.astype(jnp.bfloat16), ("dp", "feat"), scatter_dimension=1, tiled=True
        ).astype(jnp.float32),
        lax.psum_scatter(
            grad_bias_qkv.astype(jnp.bfloat16), ("dp", "feat"), scatter_dimension=2, tiled=True
        ).astype(jnp.float32),
        lax.psum_scatter(
            grad_bias_up.astype(jnp.bfloat16), ("dp", "feat"), scatter_dimension=1, tiled=True
        ).astype(jnp.float32),
        lax.psum_scatter(
            grad_rpe.astype(jnp.bfloat16), ("dp", "feat"), scatter_dimension=1, tiled=True
        ).astype(jnp.float32),
    )
    return (
        mixed,
        grad_tokens,
        sent_qkv,
        sent_bias_qkv,
        sent_out,
        sent_gains,
        sent_shifts,
        sent_up,
        sent_bias_up,
        sent_down,
        sent_rpe,
    )


MESH = pl.DeviceIdType.MESH
PLANES = 4
F32 = jnp.float32
BF16 = jnp.bfloat16
SCALE = HEAD ** (-0.25)
NT = (((1,), (1,)), ((), ()))
TN = (((0,), (0,)), ((), ()))
NN = (((1,), (0,)), ((), ()))


def dot(left, right, dims=NN):
    return lax.dot_general(left, right, dims, preferred_element_type=F32)


def split_dot(left, right, dims=NN):
    high = left.astype(BF16)
    rest = (left - high.astype(F32)).astype(BF16)
    return dot(high, right, dims) + dot(rest, right, dims)


def iota(shape, axis):
    return lax.broadcasted_iota(jnp.int32, shape, axis)


class Sems:
    def __init__(self):
        self.used = 0

    def take(self, count=1):
        first = self.used
        self.used += count
        return first


def layer_kernel(
    tok, wq_h, qb_h, wo_h, gain_h, bias_h, wu_h, ub_h, wd_h, rpe_h, om_h, bk_h, cot,
    mixed_h, gtok_h, gq_h, gqb_h, go_h, ggain_h, gbias_h, gu_h, gub_h, gd_h, grpe_h,
    qb_v, gain_v, bias_v, ub_v, rpe_v, om_v, bk_v, small_s, om_s,
    mixed_o, gtok_o, gq_o, gqb_o, go_o, ggain_o, gbias_o, gu_o, gub_o, gd_o, grpe_o, tvec_o,
    wq, wo, wu, wd, small, om2, xg, cotb,
    qkv, phi, ex, unit, inv, r0, pp, num, den, quo, att, attf,
    pb, rb_f, rb_d, rb_i, fb, hid, dgel, efb, dub, dzb, acc,
    fst, n1, i1, dr, dat_s, dat, out_s, anti, ones64, rows_v,
    dn, dd, ds_, gg, dph, dvv, dqkv,
    g_k, g_v, g_o, g_u, g_d, r_k, r_v, r_o, r_u, r_d, rz_k, rz_v, rz_o, rz_u, rz_d, cb_k, cb_v, cb_o, cb_u, cb_d,
    fs, xs_k, xs_v, xs_o, xs_u, xs_d, xr_k, xr_v, xr_o, xr_u, xr_d,
    sd, sd_r, st, st_r, mix_s, gt_s, gt_r,
    ss, rs, ls,
):
    dp, y, c = lax.axis_index("dp"), lax.axis_index("heads"), lax.axis_index("feat")
    z, x = dp // 2, dp % 2
    shard = 2 * dp + c
    sems, locals_ = Sems(), Sems()
    pending = []

    def bring(src, dst, cond=None):
        copy = pltpu.make_async_copy(src, dst, ls.at[locals_.take()])
        if cond is None:
            copy.start()
            return copy.wait
        pl.when(cond)(copy.start)
        return lambda: pl.when(cond)(copy.wait)

    home = c == x
    away = c != x
    own_block = 2 * x + y

    def half_cols(half, width):
        return pl.ds(pl.multiple_of(half * width, width), width)

    def rows_of(index, count):
        return pl.ds(pl.multiple_of(index * count, count), count)

    in_o = bring(wo_h.at[:, half_cols(x, 256)], wo.at[own_block, 2 * z + x, c])
    in_q = bring(wq_h.at[:, :, half_cols(x, 256)], wq.at[:, 2 * z + x, c])
    in_small = [
        bring(src, dst)
        for src, dst in (
            (gain_h, gain_v), (bias_h, bias_v), (rpe_h, rpe_v), (qb_h, qb_v), (ub_h, ub_v), (om_h, om_v), (bk_h, bk_v),
        )
    ]
    in_tok = bring(tok, xg.at[rows_of(c, 256)], home)
    in_u = bring(wu_h.at[:, half_cols(x, 1024)], wu.at[2 * z + x, c])
    in_d = bring(wd_h.at[:, half_cols(x, 1024)], wd.at[2 * z + x, c])
    in_cot = bring(cot.at[rows_of(y, 128)], cotb, home)

    def dev(zz, xx, yy, cc):
        return {"dp": zz * 2 + xx, "heads": yy, "feat": cc}

    sib, xn, yn, dg = dev(z, x, y, 1 - c), dev(z, 1 - x, y, c), dev(z, x, 1 - y, c), dev(z, 1 - x, 1 - y, c)
    xs_dev, ds_dev = dev(z, 1 - x, y, 1 - c), dev(z, 1 - x, 1 - y, 1 - c)
    plane = (dg, xn, yn)
    plane_block = (2 * (1 - x) + 1 - y, 2 * (1 - x) + y, 2 * x + 1 - y)

    def rc(src, dst, s, r, device):
        return pltpu.make_async_remote_copy(
            src_ref=src, dst_ref=dst, send_sem=ss.at[s], recv_sem=rs.at[r], device_id=device, device_id_type=MESH
        )

    def send(src, dst, s, r, device, cond=None):
        def go():
            rc(src, dst, s, r, device).start()

        def done():
            rc(src, dst, s, r, device).wait_send()

        if cond is None:
            go()
            pending.append(done)
        else:
            pl.when(cond)(go)
            pending.append(lambda: pl.when(cond)(done))

    def got(dst, r):
        rc(dst, dst, r, r, sib).wait_recv()

    def valid(dz):
        return jnp.logical_and(z + dz >= 0, z + dz < PLANES)

    def by_plane(table):
        found = []
        for k in range(PLANES):
            block = jnp.int32(table[0][k])
            for zz in range(1, PLANES):
                block = jnp.where(z == zz, table[zz][k], block)
            found.append(block)
        return found

    arrive = by_plane(((0, 1, 2, 3), (1, 0, 2, 3), (2, 1, 3, 0), (3, 2, 1, 0)))
    leave = by_plane(((3, 2, 1, 0), (3, 2, 0, 1), (0, 1, 3, 2), (0, 1, 2, 3)))

    def at_step(blocks, k):
        block = blocks[0]
        for i in range(1, PLANES):
            block = jnp.where(k == i, blocks[i], block)
        return block

    def cols256(n):
        return pl.ds(pl.multiple_of(n * 256, 256), 256)

    barrier = pltpu.get_barrier_semaphore()
    for other in (sib, xn, yn, dg, xs_dev, ds_dev):
        pl.semaphore_signal(barrier, inc=1, device_id=other, device_id_type=MESH)
    for zz in range(PLANES):
        @pl.when(z != zz)
        def _(zz=zz):
            pl.semaphore_signal(barrier, inc=1, device_id=dev(zz, x, y, c), device_id_type=MESH)
    pl.semaphore_wait(barrier, 9)

    class Item:
        def __init__(self, ref, kind):
            self.ref, self.kind = ref, kind
            self.zs, self.fw, self.sb = sems.take(PLANES), sems.take(), sems.take(PLANES)

        def block(self, zz, cc):
            if self.kind == "both":
                return self.ref.at[pl.ds(2 * zz, 2), cc]
            return self.ref.at[:, 2 * zz + (x if self.kind == "own" else 1 - x), cc]

        def start(self):
            mine = self.block(z, c)
            for dz in (1, -1, 2, -2):
                send(mine, mine, self.zs + z + dz, self.zs + z, dev(z + dz, x, y, c), valid(dz))
            send(mine, mine, self.sb + z, self.sb + z, sib)

        def pump_step(self, n):
            here = self.block(n, c)

            def relay(device):
                rc(here, here, self.fw, self.zs + n, device).start()

            @pl.when(n != z)
            def _():
                got(here, self.zs + n)
                pl.when(jnp.logical_and(z == 1, n == 3))(lambda: relay(dev(z - 1, x, y, c)))
                pl.when(jnp.logical_and(z == 2, n == 0))(lambda: relay(dev(z + 1, x, y, c)))
                rc(here, here, self.sb + n, self.sb + n, sib).start()

        def pump_done(self):
            mine = self.block(z, c)
            pending.append(
                lambda: pl.when((z == 1) | (z == 2))(lambda: rc(mine, mine, self.fw, self.fw, sib).wait_send())
            )
            for dz in (1, -1, 2, -2, 3, -3):
                i = self.sb + z + dz
                pending.append(lambda i=i, dz=dz: pl.when(valid(dz))(lambda: rc(mine, mine, i, i, sib).wait_send()))

        def pump(self):
            for k in range(1, PLANES):
                self.pump_step(arrive[k])
            self.pump_done()

        def need_step(self, n):
            got(self.block(n, 1 - c), self.sb + n)

        def need(self):
            for zz in range(PLANES):
                self.need_step(zz)

    half_of = {}

    def place(ref, xx):
        return ref.at[:, 2 * z + xx, c] if len(ref.shape) == 5 else ref.at[2 * z + xx, c]

    def give_half(name, src, ref):
        i = sems.take()
        half_of[name] = (ref, i)
        send(src, place(ref, x), i, i, xn)

    def have_half(name):
        ref, i = half_of[name]
        got(place(ref, 1 - x), i)

    wo_own = wo.at[own_block]
    i_oh = sems.take()
    send(
        wo_h.at[:, half_cols(1 - x, 256)], wo.at[2 * (1 - x) + y, 2 * z + x, c], i_oh, i_oh, xn
    )
    give_half("q", wq_h.at[:, :, half_cols(1 - x, 256)], wq)
    it_qa, it_s, it_qb = Item(wq, "own"), Item(small, "both"), Item(wq, "other")
    it_o, it_u, it_d = Item(wo_own, "both"), Item(wu, "both"), Item(wd, "both")
    in_q()
    it_qa.start()

    for done in in_small:
        done()

    def pick(shape, hit):
        return jnp.where(hit(iota(shape, 0), iota(shape, 1)), 1.0, 0.0)

    vec_sel = pick((64, 128), lambda k, l: l == c * 64 + k).astype(BF16)
    rpe_sel = pick((64, 128), lambda k, l: l == (1 - c) * 64 + 63 - k).astype(BF16)
    bias_sel = [pick((4, 128), lambda k, l, par=par: l == par * 64 + 4 * shard + k).astype(BF16) for par in range(2)]
    rpe_rows = dot(rpe_v[...], rpe_sel)
    level = jnp.full((1, 128), bk_v[0].astype(F32))
    top = jnp.concatenate(
        [dot(gain_v[...], vec_sel), dot(bias_v[...], vec_sel), level, jnp.zeros((1, 128), F32)], axis=0
    )

    def spread(values):
        rows = values.shape[1]
        even = (iota((rows, 1), 0) % 2) == 0
        wide = jnp.where(even, dot(values, bias_sel[0], TN), dot(values, bias_sel[1], TN))
        return dot(pick((rows // 2, rows), lambda k, l: l // 2 == k).astype(BF16), wide.astype(BF16))

    up_rows = spread(ub_v[...])
    qkv_rows = [spread(qb_v[p]) for p in range(3)]
    for half in range(2):
        mine = [rows[2 * half : 2 * half + 2] for rows in qkv_rows] + [jnp.zeros((2, 128), F32)]
        position = jnp.concatenate([rpe_rows[4 * half : 4 * half + 4], jnp.zeros((4, 128), F32)], axis=0)
        small_s[half] = jnp.concatenate(
            [top, position] + mine + [up_rows[8 * half : 8 * half + 8]], axis=0
        ).astype(BF16)
    small[2 * z + x, c] = small_s[x]
    give_half("s", small_s.at[1 - x], small)
    for h in range(4):
        sel = pick((32, 256), lambda k, l: l == h * 64 + c * 32 + k).astype(BF16)
        om_s[h * 64 : (h + 1) * 64] = dot(om_v[4 * x + h], sel, TN).astype(BF16)
    i_om = sems.take()
    send(om_s, om2, i_om, i_om, sib)
    t1, t2 = sems.take(), sems.take(2)
    send(tok, xg.at[rows_of(c, 256)], t1, t1, sib, away)
    send(tok, xg.at[rows_of(c, 256)], t2 + c, t2 + c, dev(z, 1 - x, y, x))
    give_half("u", wu_h.at[:, half_cols(1 - x, 1024)], wu)

    same = (iota((256, 256), 0) // HEAD) == (iota((256, 256), 1) // HEAD)
    ones64[...] = jnp.where(same, 1.0, 0.0).astype(BF16)
    anti[...] = jnp.where(iota((512, 512), 0) + iota((512, 512), 1) == 511, 1.0, 0.0).astype(BF16)

    have_half("q")
    it_qb.start()
    got(wo.at[own_block, 2 * z + 1 - x, c], i_oh)
    in_o()
    it_o.start()
    have_half("s")
    it_s.start()
    it_qa.pump()
    it_qb.pump()
    it_o.pump()
    i_oq, i_os = sems.take(3), sems.take(3)
    quarter = wo.at[own_block, :, c]
    for slot in range(3):
        send(quarter, quarter, i_oq + slot, i_oq + slot, plane[slot])
    give_half("d", wd_h.at[:, half_cols(1 - x, 1024)], wd)
    t3 = sems.take()
    send(cot.at[rows_of(y, 128)], cotb, t3, t3, xs_dev, away)
    have_half("u")
    in_u()
    it_u.start()
    it_s.pump()

    it_s.need()
    for t in range(8):
        tile = small[t, 0].astype(F32) + small[t, 1].astype(F32)
        rows_v[0:8, t * 128 : (t + 1) * 128] = tile[0:8]
        rows_v[8:16, (7 - t) * 128 : (8 - t) * 128] = tile[8:16]
        total = tile[16:32] if t == 0 else total + tile[16:32]
    for r in range(6):
        rows_v[16:17, r * 128 : (r + 1) * 128] = total[r : r + 1]
    for r in range(8):
        rows_v[17:18, r * 128 : (r + 1) * 128] = total[8 + r : 9 + r]
    level = small[2 * z + c, 0][6:7].astype(F32)
    wide1 = jnp.where(level > 0.5, 1.0, 0.0)
    wide2 = jnp.where(level > 1.5, 1.0, 0.0)
    one_row = jnp.ones((1, 128), F32)

    def mask_row(bi):
        parts = [one_row if bj == bi else (wide1 if bj // 2 == bi // 2 else wide2) for bj in range(4)]
        return jnp.concatenate(parts, axis=1)

    masks = [mask_row(bi) for bi in range(4)]

    def coeff_body(h, carry):
        row = jnp.exp(rows_v[pl.ds(8 + h, 1), :])
        r0[h] = pltpu.roll(jnp.broadcast_to(row, (128, 1024)), 1, 1, stride=1, stride_axis=0)
        return carry

    lax.fori_loop(0, 4, coeff_body, 0)
    num[...] = jnp.zeros_like(num)
    den[...] = jnp.zeros_like(den)

    in_tok()
    pl.when(home)(lambda: got(xg.at[rows_of(1 - c, 256)], t1))

    @pl.when(away)
    def _():
        got(xg.at[pl.ds(0, 256)], t2)
        got(xg.at[pl.ds(256, 256)], t2 + 1)

    it_qa.need()
    it_qb.need()

    def qkv_body(p, carry):
        qkv[p] = (dot(xg[...], wq[p].reshape(1024, 256)) + rows_v[16:17, cols256(p)]).astype(BF16)
        return carry

    lax.fori_loop(0, 3, qkv_body, 0)
    got(om2, i_om)
    om2[...] = om2[...] + om_s[...]

    def feature_body(t, carry):
        wide = qkv[t].astype(F32)
        sums = split_dot(wide * wide, ones64[...])
        inverse = lax.rsqrt(sums * (1.0 / HEAD) + UNIT_EPS)
        units = wide * inverse
        logits = SCALE * split_dot(units, om2[...]) - 0.5 * SCALE * SCALE * (sums * inverse * inverse)
        value = jnp.exp(logits) * M ** (-0.5)
        ex[t] = value
        unit[t] = units
        inv[t] = inverse
        phi[t] = value.astype(BF16)
        return carry

    lax.fori_loop(0, 2, feature_body, 0)
    lane_head = iota((1, 128), 1) // HEAD

    def head_cols(h):
        return pl.ds(pl.multiple_of((h // 2) * 128, 128), 128), (lane_head == h % 2)

    def head_body(h, carry):
        cols, mine = head_cols(h)
        keep = jnp.where(mine, 1.0, 0.0).astype(BF16)
        scores = dot(phi[0, :, cols] * keep, phi[1, :, cols], NT)
        for b in range(4):
            coefficient = r0[h, :, 512 - 128 * b : 1024 - 128 * b] * masks[b]
            pp[h, b * 128 : (b + 1) * 128] = (scores[b * 128 : (b + 1) * 128] * coefficient).astype(BF16)
        right = jnp.concatenate([qkv[2, :, cols] * keep, jnp.broadcast_to(keep, (512, 128))], axis=1)
        both = dot(pp[h], right)
        num[:, cols] += both[:, :128]
        den[:, cols] += both[:, 128:]
        return carry

    lax.fori_loop(0, 4, head_body, 0)
    quo[...] = num[...] / den[...]
    att[...] = quo[...].astype(BF16).reshape(4, 128, 256)

    i_at = sems.take(3)
    for slot in range(3):
        send(att.at[plane_block[slot]], attf.at[own_block], i_at + slot, i_at + slot, plane[slot])
    attf[own_block] = att[own_block]
    for slot in range(3):
        part = wo.at[plane_block[slot], :, c]
        got(part, i_oq + slot)
        send(part, part, i_os + slot, i_os + slot, sib)
    have_half("d")
    in_d()
    it_d.start()
    it_o.need()
    for slot in range(3):
        got(attf.at[plane_block[slot]], i_at + slot)
    for slot in range(3):
        got(wo.at[plane_block[slot], :, 1 - c], i_os + slot)

    def out_body(q, carry):
        return carry + dot(attf[q], wo[q].reshape(1024, 256), NT)

    mixed_z = lax.fori_loop(0, 4, out_body, jnp.zeros((128, 1024), F32))

    def norm(values):
        centred = values - jnp.mean(values, axis=-1, keepdims=True)
        inverse = lax.rsqrt(jnp.mean(centred * centred, axis=-1, keepdims=True) + EPSILON)
        return centred * inverse, inverse

    residual = mixed_z + xg[rows_of(own_block, 128)].astype(F32) + rows_v[2:3, :]
    normed, inverse = norm(residual)
    first = normed * rows_v[0:1, :] + rows_v[3:4, :]
    fb[own_block] = first.astype(BF16)

    class Scatter:
        def __init__(self, ref):
            self.ref, self.base = ref, sems.take(12)

        def part(self, n, value):
            cols = cols256(n)
            pb[:, :, cols] = value.astype(BF16).reshape(4, 128, 256)
            for slot in range(3):
                i = self.base + slot * 4 + n
                rc(pb.at[plane_block[slot], :, cols], self.ref.at[slot, :, cols], i, i, plane[slot]).start()

        def total(self):
            for n in range(4):
                for slot in range(3):
                    got(self.ref.at[slot, :, n * 256 : (n + 1) * 256], self.base + slot * 4 + n)
            value = pb[own_block].astype(F32)
            for slot in range(3):
                value = value + self.ref[slot].astype(F32)
            return value

        def sent(self):
            for slot in range(3):
                for n in range(4):
                    i = self.base + slot * 4 + n
                    src = pb.at[plane_block[slot], :, n * 256 : (n + 1) * 256]
                    rc(src, src, i, i, plane[slot]).wait_send()

    class Gather:
        def __init__(self, ref, order):
            self.ref, self.base, self.order = ref, sems.take(12), order

        def start(self):
            for n in self.order:
                for slot in range(3):
                    mine = self.ref.at[own_block, :, cols256(n)]
                    i = self.base + slot * 4 + n
                    send(mine, mine, i, i, plane[slot])

        def need(self, n):
            for slot in range(3):
                got(self.ref.at[plane_block[slot], :, cols256(n)], self.base + slot * 4 + n)

    g_first = Gather(fb, range(4))
    g_first.start()
    fst[...] = first
    n1[...] = normed
    i1[...] = jnp.broadcast_to(inverse, (128, 128))

    def d_cols(ref, m):
        return ref[:, :, cols256(m)].reshape(512, 256)

    acc[...] = jnp.zeros_like(acc)
    it_u.pump()
    it_u.need()

    def hidden_part(n, carry):
        g_first.need(n)
        left = d_cols(fb, n)
        for j in range(4):
            cols = slice(j * 256, (j + 1) * 256)
            acc[:, cols] += dot(left, wu[pl.ds(2 * n, 2), :, :, cols].reshape(256, 256))
        return carry

    lax.fori_loop(0, 4, hidden_part, 0)

    def hidden_body(n, carry):
        cols = cols256(n)
        pre = acc[:, cols] + rows_v[17:18, cols]
        cdf = 0.5 * (1.0 + lax.erf(pre * 0.7071067811865476))
        hid[:, cols] = (pre * cdf).astype(BF16)
        dgel[:, cols] = cdf + pre * (0.3989422804014327 * jnp.exp(-0.5 * pre * pre))
        return carry

    lax.fori_loop(0, 4, hidden_body, 0)
    sc_f = Scatter(rb_f)

    def down_part(k, carry):
        n = at_step(arrive, k)
        it_d.pump_step(n)
        it_d.need_step(n)
        sc_f.part(n, dot(hid[...], wd[pl.ds(2 * n, 2)].reshape(256, 1024), NT))
        return carry

    lax.fori_loop(0, 4, down_part, 0)
    it_d.pump_done()
    pl.when(away)(lambda: got(cotb, t3))
    in_cot()
    upstream = cotb[...].astype(F32)

    def down(values):
        return jnp.sum(values, axis=0, keepdims=True)

    sd[5:6, :] = down(upstream)
    acc[...] = jnp.zeros_like(acc)
    second = fst[...] + sc_f.total() + rows_v[4:5, :]
    normed2, inverse2 = norm(second)

    def norm_back(upstream, normed, inverse, gain):
        scaled = upstream * gain
        mean = jnp.mean(scaled, axis=-1, keepdims=True)
        slope = jnp.mean(scaled * normed, axis=-1, keepdims=True)
        return inverse * (scaled - mean - normed * slope)

    err = norm_back(upstream, normed2, inverse2, rows_v[1:2, :])
    efb[own_block] = err.astype(BF16)
    g_ef = Gather(efb, leave)
    g_ef.start()
    dr[...] = err
    mix_s[...] = (normed2 * rows_v[1:2, :] + rows_v[5:6, :]).astype(BF16)
    sd[1:2, :] = down(upstream * normed2)
    sd[4:5, :] = down(err.astype(BF16).astype(F32))
    sc_f.sent()

    i_mix, i_gt = sems.take(2), sems.take(2)

    def to_owner(src, dst, i):
        rows = rows_of(y, 128)

        @pl.when(home)
        def _():
            dst[rows] = src[...]

        send(src, dst.at[rows], i + 1, i + 1, yn, home)
        send(src, dst.at[rows], i, i + y, xs_dev, away)
        send(src, dst.at[rows], i + 1, i + y, ds_dev, away)

    def from_owner(dst, i):
        for half in range(2):
            part = dst.at[half * 128 : (half + 1) * 128]

            @pl.when(jnp.logical_and(home, y != half))
            def _(part=part):
                got(part, i + 1)

            @pl.when(away)
            def _(part=part, half=half):
                got(part, i + half)

    class Grad:
        def __init__(self, g, r, rz, cb, xs, xr):
            self.g, self.r, self.rz, self.cb, self.xs, self.xr = g, r, rz, cb, xs, xr
            self.d, self.z, self.k, self.x = sems.take(4), sems.take(PLANES), sems.take(), sems.take()
            self.width = r.shape[-1]

        def give(self, m):
            i = self.d + m
            rc(self.g.at[m, :, 1 - c], self.r.at[m], i, i, sib).start()

        def pair_step(self, m):
            got(self.r.at[m], self.d + m)
            self.r[m] = (self.g[m, :, c].astype(F32) + self.r[m].astype(F32)).astype(BF16)
            far = jnp.abs(m - z)
            part = self.r.at[m]

            def out(device):
                rc(part, self.rz.at[z], self.z + m, self.z + z, device).start()

            pl.when(far == 1)(lambda: out(dev(m, x, y, c)))
            pl.when(jnp.logical_and(far == 2, (z == 0) | (z == 3)))(lambda: out(dev(m, x, y, c)))
            pl.when(far == 3)(
                lambda: rc(part, self.cb, self.k, self.k, dev(jnp.where(z == 0, 1, 2), x, y, c)).start()
            )

        def relay(self):
            for at, m in ((1, 3), (2, 0)):
                @pl.when(z == at)
                def _(at=at, m=m):
                    got(self.cb, self.k)
                    self.r[m] = (self.r[m].astype(F32) + self.cb[...].astype(F32)).astype(BF16)
                    rc(self.r.at[m], self.rz.at[at], self.z + m, self.z + at, dev(m, x, y, c)).start()

        def run(self, make):
            def body(k, carry):
                m = at_step(leave, k)
                make(m)
                self.give(m)
                pl.when(k > 0)(lambda: self.pair_step(at_step(leave, k - 1)))
                return carry

            lax.fori_loop(0, PLANES, body, 0)
            self.pair_step(leave[3])

        def finish(self):
            total = fs.at[:, :, 0 : self.width]
            total[...] = self.r[z].astype(F32)
            for dz in (1, -1, 2, -2):
                @pl.when(valid(dz))
                def _(dz=dz):
                    got(self.rz.at[z + dz], self.z + z + dz)
                    total[...] += self.rz[z + dz].astype(F32)
            self.xs[...] = fs[1 - x, :, 0 : self.width].astype(BF16)
            send(self.xs, self.xr, self.x, self.x, xn)

        def sent(self):
            for m in range(PLANES):
                i = self.d + m
                rc(self.g.at[m, :, c], self.g.at[m, :, c], i, i, sib).wait_send()
            part = self.r.at[0]
            for dz in (1, -1, 2, -2):
                i = self.z + z + dz
                pl.when(valid(dz))(lambda i=i: rc(part, part, i, i, sib).wait_send())
            pl.when((z == 0) | (z == 3))(lambda: rc(part, part, self.k, self.k, sib).wait_send())

        def columns(self, out, half, value, at=0):
            if len(out.shape) == 3:
                for p in range(self.width // 256):
                    out[at + p, :, half_cols(half, 256)] = value[:, p * 256 : (p + 1) * 256]
            else:
                out[:, half_cols(half, self.width)] = value

        def write_own(self, out, at=0):
            self.columns(out, x, fs[x, :, 0 : self.width], at)

        def write_other(self, out, at=0):
            got(self.xr, self.x)
            self.columns(out, 1 - x, self.xr[...].astype(F32), at)

    gr_d = Grad(g_d, r_d, rz_d, cb_d, xs_d, xr_d)
    gr_u = Grad(g_u, r_u, rz_u, cb_u, xs_u, xr_u)
    gr_o = Grad(g_o, r_o, rz_o, cb_o, xs_o, xr_o)
    gr_v = Grad(g_v, r_v, rz_v, cb_v, xs_v, xr_v)
    gr_k = Grad(g_k, r_k, rz_k, cb_k, xs_k, xr_k)

    def make_down(m):
        g_ef.need(m)
        left = d_cols(efb, m)
        g_d[m] = dot(left, hid[...], TN).astype(BF16).reshape(2, 2, 64, 1024)
        gr_d.give(m)
        for j in range(4):
            cols = slice(j * 256, (j + 1) * 256)
            acc[:, cols] += dot(left, wd[pl.ds(2 * m, 2), :, :, cols].reshape(256, 256))

    def down_grads(k, carry):
        m = at_step(leave, k)
        make_down(m)
        pl.when(k > 0)(lambda: gr_d.pair_step(at_step(leave, k - 1)))
        return carry

    lax.fori_loop(0, PLANES, down_grads, 0)
    def du_body(n, carry):
        cols = cols256(n)
        du = (acc[:, cols] * dgel[:, cols]).astype(BF16)
        dub[:, cols] = du
        st[0:1, cols] = down(du.astype(F32))
        return carry

    lax.fori_loop(0, 4, du_body, 0)
    sc_d = Scatter(rb_d)

    def back_part(n, carry):
        sc_d.part(n, dot(dub[...], wu[pl.ds(2 * n, 2)].reshape(256, 1024), NT))
        return carry

    lax.fori_loop(0, 4, back_part, 0)
    gr_d.pair_step(leave[3])

    def make_up(m):
        g_u[m] = dot(d_cols(fb, m), dub[...], TN).astype(BF16).reshape(2, 2, 64, 1024)

    gr_u.run(make_up)
    gr_d.relay()
    to_owner(mix_s, mixed_o, i_mix)
    dfirst = dr[...] + sc_d.total()
    back = norm_back(dfirst, n1[...], i1[:, 0:1], rows_v[0:1, :])
    dz = back.astype(BF16)
    dzb[own_block] = dz

    def dattn_body(q, carry):
        dat_s[q] = dot(dz, wo[q].reshape(1024, 256)).astype(BF16)
        return carry

    lax.fori_loop(0, 4, dattn_body, 0)
    i_da = sems.take(3)
    for slot in range(3):
        send(dat_s.at[plane_block[slot]], dat.at[own_block], i_da + slot, i_da + slot, plane[slot])
    dat[own_block] = dat_s[own_block]
    g_dz = Gather(dzb, leave)
    g_dz.start()
    sd[0:1, :] = down(dfirst * n1[...])
    sd[3:4, :] = down(dfirst)
    sd[2:3, :] = down(dz.astype(F32))
    sd[6:8, :] = jnp.zeros((2, 1024), F32)
    i_sd = sems.take(3)
    for k, device in enumerate(plane):
        send(sd, sd_r.at[k], i_sd + k, i_sd + k, device)
    dr[...] = back
    sc_d.sent()
    dph[...] = jnp.zeros_like(dph)
    dvv[...] = jnp.zeros_like(dvv)
    for slot in range(3):
        got(dat.at[plane_block[slot]], i_da + slot)

    dattn = dat[...].reshape(512, 256).astype(F32)
    recip = 1.0 / den[...]
    dn[...] = (dattn * recip).astype(BF16)
    dsum = split_dot(dattn * quo[...], ones64[...])
    dd[...] = ((-dsum * recip).astype(BF16).astype(F32) * (1.0 / HEAD)).astype(BF16)

    def value_back(h, carry):
        cols, mine = head_cols(h)
        keep = jnp.where(mine, 1.0, 0.0).astype(BF16)
        dvv[:, cols] += dot(pp[h], dn[:, cols] * keep, TN)
        return carry

    lax.fori_loop(0, 4, value_back, 0)
    dqkv[2] = dvv[...].astype(BF16)

    def x_cols(m):
        return xg[:, cols256(m)]

    def make_v(m):
        g_v[m] = dot(x_cols(m), dqkv[2], TN).astype(BF16).reshape(2, 2, 64, 256)

    gr_v.run(make_v)
    gr_u.relay()

    def head_back(h, carry):
        cols, mine = head_cols(h)
        keep = jnp.where(mine, 1.0, 0.0).astype(BF16)
        left = jnp.concatenate([dn[:, cols] * keep, dd[:, cols] * keep], axis=1)
        right = jnp.concatenate([qkv[2, :, cols], jnp.ones((512, 128), BF16)], axis=1)
        grad_p = dot(left, right, NT)
        for b in range(4):
            rows = slice(b * 128, (b + 1) * 128)
            coefficient = r0[h, :, 512 - 128 * b : 1024 - 128 * b] * masks[b]
            part = grad_p[rows]
            ds_[rows] = (part * coefficient).astype(BF16)
            gg[h, rows] = (part * pp[h, rows].astype(F32)).astype(BF16)
        dph[0, :, cols] += dot(ds_[...], phi[1, :, cols] * keep)
        dph[1, :, cols] += dot(ds_[...], phi[0, :, cols] * keep, TN)
        return carry

    lax.fori_loop(0, 4, head_back, 0)

    def feature_back_body(t, carry):
        dlog = (dph[t] * ex[t]).astype(BF16)
        units = unit[t]
        dunit = SCALE * dot(dlog, om2[...], NT) - SCALE * SCALE * dot(dlog, ones64[...]) * units
        mean = split_dot(dunit * units, ones64[...]) * (1.0 / HEAD)
        dqkv[t] = (inv[t] * (dunit - units * mean)).astype(BF16)
        return carry

    lax.fori_loop(0, 2, feature_back_body, 0)
    sc_i = Scatter(rb_i)

    def input_part(n, carry):
        value = jnp.zeros((512, 256), F32)
        for p in range(3):
            value = value + dot(dqkv[p], wq[p, pl.ds(2 * n, 2)].reshape(256, 256), NT)
        sc_i.part(n, value)
        return carry

    lax.fori_loop(0, 4, input_part, 0)

    def make_k(m):
        for p in range(2):
            g_k[m, :, :, :, p * 256 : (p + 1) * 256] = (
                dot(x_cols(m), dqkv[p], TN).astype(BF16).reshape(2, 2, 64, 256)
            )

    gr_k.run(make_k)

    def make_out(m):
        g_dz.need(m)
        g_o[m] = dot(d_cols(dzb, m), att[...].reshape(512, 256), TN).astype(BF16).reshape(2, 2, 64, 256)

    gr_o.run(make_out)
    gr_v.relay()

    def diagonal_body(h, carry):
        flipped = dot(anti[...], gg[h])
        sums = jnp.zeros((1, 1024), F32)
        for b in range(4):
            wide = jnp.concatenate([flipped[b * 128 : (b + 1) * 128], jnp.zeros((128, 128), F32)], axis=1)
            line = down(pltpu.roll(wide, 0, 1, stride=1, stride_axis=0))
            pieces = [line]
            if b > 0:
                pieces = [jnp.zeros((1, 128 * b), F32)] + pieces
            if b < 3:
                pieces = pieces + [jnp.zeros((1, 384 - 128 * b), F32)]
            sums = sums + jnp.concatenate(pieces, axis=1)
        st[pl.ds(2 + h, 1), :] = sums
        return carry

    lax.fori_loop(0, 4, diagonal_body, 0)
    for p in range(3):
        st[1:2, p * 256 : (p + 1) * 256] = down(dqkv[p].astype(F32))
    st[1:2, 768:1024] = jnp.zeros((1, 256), F32)
    st[6:8, :] = jnp.zeros((2, 1024), F32)
    i_c, i_zz, i_h = sems.take(), sems.take(PLANES), sems.take()
    for k in range(3):
        got(sd_r.at[k], i_sd + k)
    st[8:16, :] = sd[...] + sd_r[0] + sd_r[1] + sd_r[2]
    send(st, st_r.at[0], i_c, i_c, sib)
    gr_d.finish()
    gr_d.write_own(gd_o)
    got(st_r.at[0], i_c)
    st_r[1] = st[...] + st_r[0]
    for zz in range(PLANES):
        send(st_r.at[1], st_r.at[2 + z], i_zz + zz, i_zz + z, dev(zz, x, y, c), z != zz)
    outs = []
    from_owner(mixed_o, i_mix)
    outs.append(bring(mixed_o, mixed_h))
    gr_k.relay()
    gr_o.relay()
    gr_u.finish()
    gr_u.write_own(gu_o)
    back = dr[...] + sc_i.total()
    gt_s[...] = back.astype(BF16)
    to_owner(gt_s, gt_r, i_gt)
    gr_d.write_other(gd_o)
    outs.append(bring(gd_o, gd_h))
    gr_v.finish()
    gr_v.write_own(gq_o, 2)
    total = st_r[1]
    for zz in range(PLANES):
        @pl.when(z != zz)
        def _(zz=zz):
            got(st_r.at[2 + zz], i_zz + zz)

        @pl.when(z == zz)
        def _(zz=zz):
            st_r[2 + zz] = jnp.zeros((16, 1024), F32)
        total = total + st_r[2 + zz]
    st_r[0] = total
    tvec_o[x] = total[0:8]
    send(tvec_o.at[x], tvec_o.at[x], i_h, i_h, xn)
    gr_u.write_other(gu_o)
    outs.append(bring(gu_o, gu_h))

    def exact(left, right):
        return lax.dot_general(left, right, NN, precision=lax.Precision.HIGHEST, preferred_element_type=F32)

    own = exact(
        st_r[0, 8:16, pl.ds(pl.multiple_of(dp * 128, 128), 128)], pick((128, 64), lambda k, l: k == c * 64 + l)
    )
    ggain_o[...] = own[0:2]
    gbias_o[...] = own[2:6]
    outs.append(bring(ggain_o, ggain_h))
    outs.append(bring(gbias_o, gbias_h))
    gr_k.finish()
    gr_k.write_own(gq_o)
    gr_o.finish()
    gr_o.write_own(go_o)
    got(tvec_o.at[1 - x], i_h)
    tile = pl.ds(pl.multiple_of((7 - dp) * 128, 128), 128)
    lines = jnp.concatenate([tvec_o[0, 2:6, tile], tvec_o[1, 2:6, tile]], axis=0)
    grpe_o[...] = exact(lines, pick((128, 64), lambda k, l: k == (1 - c) * 64 + 63 - l))
    outs.append(bring(grpe_o, grpe_h))
    lines = [
        tvec_o[half, 1:2, p * 256 + t * 128 : p * 256 + (t + 1) * 128]
        for p in range(3) for half in range(2) for t in range(2)
    ] + [tvec_o[half, 0:1, t * 128 : (t + 1) * 128] for half in range(2) for t in range(8)]
    lines = jnp.concatenate(lines + [jnp.zeros((4, 128), F32)], axis=0)
    found = jnp.zeros((4, 56), F32)
    for par in range(2):
        hit = pick((4, 128), lambda k, l: l == par * 64 + 4 * shard + k)
        values = lax.dot_general(hit, lines, NT, precision=lax.Precision.HIGHEST, preferred_element_type=F32)
        found = found + exact(values, pick((32, 56), lambda k, l: (l // 2 == k) & (l % 2 == par)))
    for p in range(3):
        gqb_o[p] = found[:, 8 * p : 8 * p + 8]
    gub_o[...] = found[:, 24:56]
    outs.append(bring(gqb_o, gqb_h))
    outs.append(bring(gub_o, gub_h))
    from_owner(gt_r, i_gt)
    gtok_o[...] = gt_r[...].astype(F32)
    outs.append(bring(gtok_o, gtok_h))
    gr_v.write_other(gq_o, 2)
    gr_k.write_other(gq_o)
    outs.append(bring(gq_o, gq_h))
    gr_o.write_other(go_o)
    outs.append(bring(go_o, go_h))
    sc_i.sent()
    for gr in (gr_d, gr_u, gr_o, gr_v, gr_k):
        gr.sent()
    for done in pending + outs:
        done()


def copy_kernel(*refs):
    count = len(refs) // 3
    sem = refs[-1]
    ins = [pltpu.make_async_copy(refs[i], refs[2 * count + i], sem.at[0, i]) for i in range(count)]
    outs = [pltpu.make_async_copy(refs[2 * count + i], refs[count + i], sem.at[1, i]) for i in range(count)]
    for copy in ins:
        copy.start()
    for one, two in zip(ins, outs):
        one.wait()
        two.start()
    for copy in outs:
        copy.wait()


def fast_local(
    tokens, qkv_weight, qkv_bias, out_weight, norm_gains, row_biases, up_weight, up_bias, down_weight, rpe_bias, omega,
    bucket, cotangent,
):
    def vm(shape, dtype=BF16):
        return pltpu.VMEM(shape, dtype)

    widths = (512, 256, 256, 1024, 1024)
    scratch = [vm((3, 4, 8)), vm((2, 64)), vm((4, 64)), vm((4, 32)), vm((8, 64)), vm((8, 32, 64))]
    scratch += [pltpu.SMEM((1,), jnp.int32), vm((2, 32, 128)), vm((256, 256))]
    results = (
        ((256, 1024), BF16), ((256, 1024), F32), ((3, 64, 512), F32), ((3, 4, 8), F32), ((64, 512), F32), ((2, 64), F32),
        ((4, 64), F32), ((64, 2048), F32), ((4, 32), F32), ((64, 2048), F32), ((8, 64), F32),
    )
    scratch += [vm(*result) for result in results] + [vm((2, 8, 1024), F32)]
    scratch += [vm((3, 8, 2, 64, 256)), vm((4, 8, 2, 64, 256)), vm((8, 2, 64, 1024)), vm((8, 2, 64, 1024))]
    scratch += [vm((8, 2, 32, 128)), vm((256, 256)), vm((512, 1024)), vm((128, 1024))]
    scratch += [vm((3, 512, 256)), vm((2, 512, 256))] + [vm((2, 512, 256), F32)] * 3
    scratch += [vm((4, 128, 1024), F32), vm((4, 512, 512))] + [vm((512, 256), F32)] * 3 + [vm((4, 128, 256))] * 2
    scratch += [vm((4, 128, 1024))] + [vm((3, 128, 1024))] * 3
    scratch += [vm((4, 128, 1024)), vm((512, 1024)), vm((512, 1024), F32)]
    scratch += [vm((4, 128, 1024)), vm((512, 1024)), vm((4, 128, 1024)), vm((512, 1024), F32)]
    scratch += [vm((128, 1024), F32)] * 2 + [vm((128, 128), F32), vm((128, 1024), F32)]
    scratch += [vm((4, 128, 256))] * 2 + [vm((16, 128)), vm((512, 512)), vm((256, 256)), vm((24, 1024), F32)]
    scratch += [vm((512, 256))] * 2 + [vm((512, 512)), vm((4, 512, 512)), vm((2, 512, 256), F32), vm((512, 256), F32)]
    scratch += [vm((3, 512, 256))]
    scratch += [vm((4, 2, 2, 64, n)) for n in widths]
    scratch += [vm((4, 2, 64, n)) for n in widths] * 2 + [vm((2, 64, n)) for n in widths]
    scratch += [vm((2, 64, 1024), F32)] + [vm((64, n)) for n in widths] * 2
    scratch += [vm((8, 1024), F32), vm((3, 8, 1024), F32), vm((16, 1024), F32), vm((6, 16, 1024), F32)]
    scratch += [vm((128, 1024)), vm((128, 1024)), vm((256, 1024))]
    scratch += [pltpu.SemaphoreType.DMA((400,)), pltpu.SemaphoreType.DMA((400,)), pltpu.SemaphoreType.DMA((40,))]

    shapes = tuple(jax.ShapeDtypeStruct(*result) for result in results)
    anywhere = pl.BlockSpec(memory_space=pl.ANY)
    made = pl.pallas_call(
        layer_kernel,
        out_shape=shapes,
        in_specs=[anywhere] * 13,
        out_specs=(anywhere,) * len(shapes),
        scratch_shapes=scratch,
        compiler_params=pltpu.CompilerParams(
            collective_id=0, has_side_effects=True, vmem_limit_bytes=63 * 2**20
        ),
        name="layer",
    )(
        tokens, qkv_weight.transpose(1, 0, 2), qkv_bias.transpose(0, 2, 1), out_weight.T, norm_gains, row_biases, up_weight,
        up_bias.T, down_weight.T, rpe_bias, omega.transpose(0, 2, 1), bucket, cotangent,
    )
    mixed, gtok, gq, gqb, go, ggain, gbias, gu, gub, gd, grpe = pl.pallas_call(
        copy_kernel,
        out_shape=shapes,
        in_specs=[anywhere] * len(shapes),
        out_specs=(anywhere,) * len(shapes),
        scratch_shapes=[vm(*result) for result in results] + [pltpu.SemaphoreType.DMA((2, len(shapes)))],
        compiler_params=pltpu.CompilerParams(vmem_limit_bytes=63 * 2**20),
        name="results",
    )(*made)
    return (
        mixed, gtok, gq.transpose(1, 0, 2), gqb.transpose(0, 2, 1), go.T, ggain, gbias, gu, gub.T, gd.T, grpe,
    )


def solution(mesh):
    sizes = (mesh.shape["dp"], mesh.shape["heads"], mesh.shape["feat"])
    return jax.shard_map(
        fast_local if sizes == (2 * PLANES, 2, 2) else local,
        mesh=mesh,
        in_specs=(
            P(("dp", "feat"), None),
            P(("dp", "feat"), None, "heads"),
            P(None, "heads", ("dp", "feat")),
            P("heads", ("dp", "feat")),
            P(None, ("dp", "feat")),
            P(None, ("dp", "feat")),
            P(("dp", "feat"), "heads"),
            P("heads", ("dp", "feat")),
            P("heads", ("dp", "feat")),
            P("heads", ("dp", "feat")),
            P("heads", None, "feat"),
            P("dp"),
            P(("dp", "feat"), None),
        ),
        out_specs=(
            P(("dp", "feat"), None),
            P(("dp", "feat"), None),
            P(("dp", "feat"), None, "heads"),
            P(None, "heads", ("dp", "feat")),
            P("heads", ("dp", "feat")),
            P(None, ("dp", "feat")),
            P(None, ("dp", "feat")),
            P(("dp", "feat"), "heads"),
            P("heads", ("dp", "feat")),
            P("heads", ("dp", "feat")),
            P("heads", ("dp", "feat")),
        ),
        check_vma=False,
    )
```

```python
import functools

import jax
import jax.numpy as jnp
from jax import lax
from jax.experimental import pallas as pl
from jax.experimental.pallas import tpu as pltpu
from jax.sharding import PartitionSpec as P

HEAD = 64
M = 64


EPSILON = 1e-12
UNIT_EPS = 1e-06


def toeplitz_block(window, extent):
    leading = window.shape[0]
    tiled_rows = jnp.broadcast_to(window[:, None, :], (leading, extent, 2 * extent - 1)).reshape(
        leading, -1
    )
    padded = jnp.pad(tiled_rows, ((0, 0), (0, extent)))
    sheared = padded.reshape(leading, extent, 2 * extent)[:, :, :extent]
    return sheared[:, :, ::-1]


def diagonal_sums(values_grid, extent):
    leading = values_grid.shape[0]
    flipped = values_grid[:, :, ::-1]
    padded = jnp.pad(flipped, ((0, 0), (0, 0), (0, extent))).reshape(leading, -1)
    sheared = padded[:, : extent * (2 * extent - 1)].reshape(leading, extent, 2 * extent - 1)
    return jnp.sum(sheared, axis=1)


def norm_forward(values, gain, shift):
    centred = values - jnp.mean(values, axis=-1, keepdims=True)
    inverse = lax.rsqrt(jnp.mean(centred * centred, axis=-1, keepdims=True) + EPSILON)
    normed = centred * inverse
    return (normed * gain + shift, normed, inverse)


def norm_backward(upstream, normed, inverse, gain):
    scaled_grad = upstream * gain
    return inverse * (
        scaled_grad
        - jnp.mean(scaled_grad, axis=-1, keepdims=True)
        - normed * jnp.mean(scaled_grad * normed, axis=-1, keepdims=True)
    )


def feature_logits(entries, omega_local):
    factor = HEAD ** (-0.25)
    wide = entries.astype(jnp.float32)
    inverse = lax.rsqrt(jnp.mean(wide * wide, axis=-1, keepdims=True) + UNIT_EPS)
    unit = wide * inverse
    projected = jnp.einsum(
        "rhe,hem->hmr",
        unit,
        omega_local.astype(jnp.float32),
        precision=lax.Precision.HIGHEST,
        preferred_element_type=jnp.float32,
    )
    squares = jnp.sum(unit * unit, axis=-1)
    return (factor * projected - 0.5 * factor * factor * squares.T[:, None, :], unit, inverse)


def feature_back(grad_phi, logits, unit, inverse, omega_local):
    factor = HEAD ** (-0.25)
    grad_logits = (grad_phi * (jnp.exp(logits) * M ** (-0.5))).astype(jnp.bfloat16)
    projected = jnp.einsum(
        "hmr,hem->rhe", grad_logits, omega_local, preferred_element_type=jnp.float32
    )
    totals = jnp.sum(grad_logits.astype(jnp.float32), axis=1)
    grad_unit = factor * projected - factor * factor * totals.T[:, :, None] * unit
    return inverse * (grad_unit - unit * jnp.mean(grad_unit * unit, axis=-1, keepdims=True))


def window_begin(row_start, col_start, extent, rows_total):
    return row_start - col_start + rows_total - extent + 1


def block_coeff(rpe_exp, window_start, extent):
    window = lax.dynamic_slice_in_dim(rpe_exp, window_start, 2 * extent - 1, 1)
    return toeplitz_block(window, extent)


def local(
    tokens,
    qkv_weight,
    qkv_bias,
    out_weight,
    norm_gains,
    row_biases,
    up_weight,
    up_bias,
    down_weight,
    rpe_bias,
    omega,
    bucket,
    cotangent,
):
    qkv_full, out_full, up_full, down_full, gains_all, biases_all, bias_qkv, bias_up, rpe_all = (
        lax.all_gather(qkv_weight, ("dp", "feat"), axis=0, tiled=True),
        lax.all_gather(out_weight, ("dp", "feat"), axis=1, tiled=True),
        lax.all_gather(up_weight, ("dp", "feat"), axis=0, tiled=True),
        lax.all_gather(down_weight, ("dp", "feat"), axis=1, tiled=True),
        lax.all_gather(norm_gains, ("dp", "feat"), axis=1, tiled=True),
        lax.all_gather(row_biases, ("dp", "feat"), axis=1, tiled=True),
        lax.all_gather(qkv_bias, ("dp", "feat"), axis=2, tiled=True),
        lax.all_gather(up_bias, ("dp", "feat"), axis=1, tiled=True),
        lax.all_gather(rpe_bias, ("dp", "feat"), axis=1, tiled=True),
    )
    model_width = qkv_full.shape[0]
    head_cols = qkv_full.shape[2]
    local_heads = omega.shape[0]
    local_feats = omega.shape[2]
    rows_own = tokens.shape[0]
    rows_total = rows_own * lax.axis_size("feat")
    block_rows = min(512, rows_total // 4)
    blocks = rows_total // block_rows
    seq_length = rows_total // 4 * jnp.where(bucket[0] == 0, 1, jnp.where(bucket[0] == 1, 2, 4))
    block_count = seq_length // block_rows
    gain_rows = gains_all.astype(jnp.float32)
    bias_rows = biases_all.astype(jnp.float32)
    rpe_exp = jnp.exp(rpe_all.astype(jnp.float32))
    projected = jnp.dot(
        tokens, qkv_full.reshape(model_width, 3 * head_cols), preferred_element_type=jnp.float32
    )
    projected = projected + bias_qkv.reshape(-1).astype(jnp.float32)
    qkv_own = projected.astype(jnp.bfloat16)
    qkv_all = lax.all_gather(qkv_own, "feat", axis=0, tiled=True).reshape(
        rows_total, 3, local_heads, HEAD
    )
    queries = qkv_all[:, 0]
    keys_rows = qkv_all[:, 1]
    values_rows = qkv_all[:, 2]
    logits_query, unit_query, inverse_query = feature_logits(queries, omega)
    logits_key, unit_key, inverse_key = feature_logits(keys_rows, omega)
    feat_query = (jnp.exp(logits_query) * M ** (-0.5)).astype(jnp.bfloat16)
    feat_key = (jnp.exp(logits_key) * M ** (-0.5)).astype(jnp.bfloat16)
    numer_parts = []
    denom_parts = []
    for row_block in range(blocks):
        row_start = row_block * block_rows
        first_block = row_start // seq_length * block_count
        phi_rows = feat_query[:, :, row_start : row_start + block_rows]

        def visit(column_block, carried, phi_rows=phi_rows, row_start=row_start):
            numer_acc, denom_acc = carried
            col_start = column_block * block_rows
            phi_cols = lax.dynamic_slice_in_dim(feat_key, col_start, block_rows, 2)
            value_cols = lax.dynamic_slice_in_dim(values_rows, col_start, block_rows, 0)
            coefficient = block_coeff(
                rpe_exp, window_begin(row_start, col_start, block_rows, rows_total), block_rows
            )
            scores = jnp.einsum(
                "hmi,hmj->hij", phi_rows, phi_cols, preferred_element_type=jnp.float32
            )
            weights = (coefficient * scores).astype(jnp.bfloat16)
            numer_acc = numer_acc + jnp.einsum(
                "hij,jhe->ihe", weights, value_cols, preferred_element_type=jnp.float32
            )
            denom_acc = denom_acc + jnp.sum(weights.astype(jnp.float32), axis=-1)
            return (numer_acc, denom_acc)

        start_pair = (
            jnp.zeros((block_rows, local_heads, HEAD), jnp.float32),
            jnp.zeros((local_heads, block_rows), jnp.float32),
        )
        numer_block, denom_block = lax.fori_loop(
            first_block, first_block + block_count, visit, start_pair
        )
        numer_parts.append(numer_block)
        denom_parts.append(denom_block)
    numer_all = jnp.concatenate(numer_parts, axis=0).reshape(rows_total, head_cols)
    denom_all = jnp.concatenate(denom_parts, axis=1)
    numer_own, denom_own = (
        lax.psum_scatter(
            numer_all.astype(jnp.bfloat16), "feat", scatter_dimension=0, tiled=True
        ).astype(jnp.float32),
        lax.psum_scatter(
            denom_all.astype(jnp.bfloat16), "feat", scatter_dimension=1, tiled=True
        ).astype(jnp.float32),
    )
    denom_rows = denom_own.T
    quotient = numer_own.reshape(rows_own, local_heads, HEAD) / denom_rows[:, :, None]
    attn_low = quotient.reshape(rows_own, head_cols).astype(jnp.bfloat16)
    z_part = jnp.dot(attn_low, out_full, preferred_element_type=jnp.float32)
    mixed_z = lax.psum(z_part.astype(jnp.bfloat16), "heads").astype(jnp.float32) + bias_rows[0]
    first_out, normed_one, inverse_one = norm_forward(
        tokens.astype(jnp.float32) + mixed_z, gain_rows[0], bias_rows[1]
    )
    first_low = first_out.astype(jnp.bfloat16)
    pre_act = jnp.dot(first_low, up_full, preferred_element_type=jnp.float32) + bias_up.reshape(
        -1
    ).astype(jnp.float32)
    act_value, act_pull = jax.vjp(lambda inner: jax.nn.gelu(inner, approximate=False), pre_act)
    act_low = act_value.astype(jnp.bfloat16)
    ffn_part = jnp.dot(act_low, down_full, preferred_element_type=jnp.float32)
    ffn_out = lax.psum(ffn_part.astype(jnp.bfloat16), "heads").astype(jnp.float32) + bias_rows[2]
    final_rows, normed_two, inverse_two = norm_forward(
        first_out + ffn_out, gain_rows[1], bias_rows[3]
    )
    mixed = final_rows.astype(jnp.bfloat16)
    qkv_full, out_full, up_full, down_full, gains_all, rpe_all = (
        lax.all_gather(qkv_weight, ("dp", "feat"), axis=0, tiled=True),
        lax.all_gather(out_weight, ("dp", "feat"), axis=1, tiled=True),
        lax.all_gather(up_weight, ("dp", "feat"), axis=0, tiled=True),
        lax.all_gather(down_weight, ("dp", "feat"), axis=1, tiled=True),
        lax.all_gather(norm_gains, ("dp", "feat"), axis=1, tiled=True),
        lax.all_gather(rpe_bias, ("dp", "feat"), axis=1, tiled=True),
    )
    gain_rows = gains_all.astype(jnp.float32)
    rpe_exp = jnp.exp(rpe_all.astype(jnp.float32))
    upstream = cotangent.astype(jnp.float32)
    grad_gain_two = jnp.sum(upstream * normed_two, axis=0)
    grad_shift_two = jnp.sum(upstream, axis=0)
    resid_two = norm_backward(upstream, normed_two, inverse_two, gain_rows[1])
    resid_low = resid_two.astype(jnp.bfloat16)
    grad_bias_down = jnp.sum(resid_low.astype(jnp.float32), axis=0)
    grad_down = jnp.einsum("rf,rd->fd", act_low, resid_low, preferred_element_type=jnp.float32)
    grad_act = jnp.einsum("rd,fd->rf", resid_low, down_full, preferred_element_type=jnp.float32)
    grad_pre = act_pull(grad_act)[0].astype(jnp.bfloat16)
    grad_up = jnp.einsum("rd,rf->df", first_low, grad_pre, preferred_element_type=jnp.float32)
    grad_bias_up = jnp.sum(grad_pre.astype(jnp.float32), axis=0).reshape(bias_up.shape)
    first_back = lax.psum(
        jnp.einsum("rf,df->rd", grad_pre, up_full, preferred_element_type=jnp.float32).astype(
            jnp.bfloat16
        ),
        "heads",
    ).astype(jnp.float32)
    grad_first = resid_two + first_back
    grad_gain_one = jnp.sum(grad_first * normed_one, axis=0)
    grad_shift_one = jnp.sum(grad_first, axis=0)
    resid_one = norm_backward(grad_first, normed_one, inverse_one, gain_rows[0])
    resid_one_low = resid_one.astype(jnp.bfloat16)
    grad_bias_out = jnp.sum(resid_one_low.astype(jnp.float32), axis=0)
    grad_out = jnp.einsum("rc,rd->cd", attn_low, resid_one_low, preferred_element_type=jnp.float32)
    grad_attn = jnp.einsum(
        "rd,cd->rc", resid_one_low, out_full, preferred_element_type=jnp.float32
    ).reshape(rows_own, local_heads, HEAD)
    grad_numer = (grad_attn / denom_rows[:, :, None]).astype(jnp.bfloat16)
    grad_denom = (-jnp.sum(grad_attn * quotient, axis=-1) / denom_rows).astype(jnp.bfloat16)
    numer_grad_all, denom_grad_all = (
        lax.all_gather(grad_numer.reshape(rows_own, head_cols), "feat", axis=0, tiled=True),
        lax.all_gather(grad_denom.T, "feat", axis=1, tiled=True),
    )
    numer_grad_all = numer_grad_all.reshape(rows_total, local_heads, HEAD)
    dphi_key = jnp.zeros((local_heads, local_feats, rows_total), jnp.float32)
    dvalues = jnp.zeros((rows_total, local_heads, HEAD), jnp.float32)
    grad_rpe = jnp.zeros(rpe_exp.shape, jnp.float32)
    dquery_parts = []
    for row_block in range(blocks):
        row_start = row_block * block_rows
        first_block = row_start // seq_length * block_count
        phi_rows = feat_query[:, :, row_start : row_start + block_rows]
        numer_rows = numer_grad_all[row_start : row_start + block_rows]
        denom_cols = denom_grad_all[:, row_start : row_start + block_rows].astype(jnp.float32)

        def visit_back(
            column_block,
            carried,
            phi_rows=phi_rows,
            row_start=row_start,
            numer_rows=numer_rows,
            denom_cols=denom_cols,
        ):
            dquery_acc, dkey_all, dvalue_all, drpe_all = carried
            col_start = column_block * block_rows
            phi_cols = lax.dynamic_slice_in_dim(feat_key, col_start, block_rows, 2)
            value_cols = lax.dynamic_slice_in_dim(values_rows, col_start, block_rows, 0)
            window_start = window_begin(row_start, col_start, block_rows, rows_total)
            coefficient = block_coeff(rpe_exp, window_start, block_rows)
            scores = jnp.einsum(
                "hmi,hmj->hij", phi_rows, phi_cols, preferred_element_type=jnp.float32
            )
            weights = (coefficient * scores).astype(jnp.bfloat16)
            grad_weights = (
                jnp.einsum(
                    "ihe,jhe->hij", numer_rows, value_cols, preferred_element_type=jnp.float32
                )
                + denom_cols[:, :, None]
            )
            dvalue_block = jnp.einsum(
                "hij,ihe->jhe", weights, numer_rows, preferred_element_type=jnp.float32
            )
            dvalue_all = lax.dynamic_update_slice_in_dim(
                dvalue_all,
                lax.dynamic_slice_in_dim(dvalue_all, col_start, block_rows, 0) + dvalue_block,
                col_start,
                0,
            )
            grad_scores = (grad_weights * coefficient).astype(jnp.bfloat16)
            diagonal = diagonal_sums(grad_weights * scores * coefficient, block_rows)
            drpe_all = lax.dynamic_update_slice_in_dim(
                drpe_all,
                lax.dynamic_slice_in_dim(drpe_all, window_start, 2 * block_rows - 1, 1) + diagonal,
                window_start,
                1,
            )
            dquery_acc = dquery_acc + jnp.einsum(
                "hij,hmj->hmi", grad_scores, phi_cols, preferred_element_type=jnp.float32
            )
            dkey_block = jnp.einsum(
                "hij,hmi->hmj", grad_scores, phi_rows, preferred_element_type=jnp.float32
            )
            dkey_all = lax.dynamic_update_slice_in_dim(
                dkey_all,
                lax.dynamic_slice_in_dim(dkey_all, col_start, block_rows, 2) + dkey_block,
                col_start,
                2,
            )
            return (dquery_acc, dkey_all, dvalue_all, drpe_all)

        start_state = (
            jnp.zeros((local_heads, local_feats, block_rows), jnp.float32),
            dphi_key,
            dvalues,
            grad_rpe,
        )
        dquery_block, dphi_key, dvalues, grad_rpe = lax.fori_loop(
            first_block, first_block + block_count, visit_back, start_state
        )
        dquery_parts.append(dquery_block)
    dphi_query = jnp.concatenate(dquery_parts, axis=2)
    grad_query = feature_back(dphi_query, logits_query, unit_query, inverse_query, omega)
    grad_key = feature_back(dphi_key, logits_key, unit_key, inverse_key, omega)
    grad_qkv_all = jnp.stack((grad_query, grad_key, dvalues), axis=1).reshape(
        rows_total, 3 * head_cols
    )
    grad_qkv_own = lax.psum_scatter(
        grad_qkv_all.astype(jnp.bfloat16), "feat", scatter_dimension=0, tiled=True
    )
    grad_bias_qkv = jnp.sum(grad_qkv_own.astype(jnp.float32), axis=0).reshape(bias_qkv.shape)
    grad_qkv_weight = jnp.einsum(
        "rd,rc->dc", tokens, grad_qkv_own, preferred_element_type=jnp.float32
    ).reshape(qkv_full.shape)
    input_terms = jnp.einsum(
        "rc,dc->rd",
        grad_qkv_own,
        qkv_full.reshape(model_width, 3 * head_cols),
        preferred_element_type=jnp.float32,
    )
    grad_tokens = resid_one + lax.psum(input_terms.astype(jnp.bfloat16), "heads").astype(
        jnp.float32
    )
    grad_gains = jnp.stack((grad_gain_one, grad_gain_two), axis=0)
    grad_shifts = jnp.stack((grad_bias_out, grad_shift_one, grad_bias_down, grad_shift_two), axis=0)
    (
        sent_qkv,
        sent_out,
        sent_up,
        sent_down,
        sent_gains,
        sent_shifts,
        sent_bias_qkv,
        sent_bias_up,
        sent_rpe,
    ) = (
        lax.psum_scatter(
            grad_qkv_weight.astype(jnp.bfloat16), ("dp", "feat"), scatter_dimension=0, tiled=True
        ).astype(jnp.float32),
        lax.psum_scatter(
            grad_out.astype(jnp.bfloat16), ("dp", "feat"), scatter_dimension=1, tiled=True
        ).astype(jnp.float32),
        lax.psum_scatter(
            grad_up.astype(jnp.bfloat16), ("dp", "feat"), scatter_dimension=0, tiled=True
        ).astype(jnp.float32),
        lax.psum_scatter(
            grad_down.astype(jnp.bfloat16), ("dp", "feat"), scatter_dimension=1, tiled=True
        ).astype(jnp.float32),
        lax.psum_scatter(
            grad_gains.astype(jnp.bfloat16), ("dp", "feat"), scatter_dimension=1, tiled=True
        ).astype(jnp.float32),
        lax.psum_scatter(
            grad_shifts.astype(jnp.bfloat16), ("dp", "feat"), scatter_dimension=1, tiled=True
        ).astype(jnp.float32),
        lax.psum_scatter(
            grad_bias_qkv.astype(jnp.bfloat16), ("dp", "feat"), scatter_dimension=2, tiled=True
        ).astype(jnp.float32),
        lax.psum_scatter(
            grad_bias_up.astype(jnp.bfloat16), ("dp", "feat"), scatter_dimension=1, tiled=True
        ).astype(jnp.float32),
        lax.psum_scatter(
            grad_rpe.astype(jnp.bfloat16), ("dp", "feat"), scatter_dimension=1, tiled=True
        ).astype(jnp.float32),
    )
    return (
        mixed,
        grad_tokens,
        sent_qkv,
        sent_bias_qkv,
        sent_out,
        sent_gains,
        sent_shifts,
        sent_up,
        sent_bias_up,
        sent_down,
        sent_rpe,
    )


MESH = pl.DeviceIdType.MESH
PLANES = 4
SENDS, RECEIVES = 84, 204
F32 = jnp.float32
BF16 = jnp.bfloat16
SCALE = HEAD ** (-0.25)
NT = (((1,), (1,)), ((), ()))
TN = (((0,), (0,)), ((), ()))
NN = (((1,), (0,)), ((), ()))


def dot(left, right, dims=NN):
    return lax.dot_general(left, right, dims, preferred_element_type=F32)


def split_dot(left, right, dims=NN):
    high = left.astype(BF16)
    rest = (left - high.astype(F32)).astype(BF16)
    return dot(high, right, dims) + dot(rest, right, dims)


def iota(shape, axis):
    return lax.broadcasted_iota(jnp.int32, shape, axis)


class Sems:
    def __init__(self):
        self.used = 0

    def take(self, count=1):
        first = self.used
        self.used += count
        return first


def layer_kernel(
    tok, wq_h, qb_h, wo_h, gain_h, bias_h, wu_h, ub_h, wd_h, rpe_h, om_h, bk_h, cot,
    mixed_h, gtok_h, gq_h, gqb_h, go_h, ggain_h, gbias_h, gu_h, gub_h, gd_h, grpe_h,
    qb_v, gain_v, bias_v, ub_v, rpe_v, om_v, bk_v, small_s, om_s,
    mixed_o, gtok_o, gq_o, gqb_o, go_o, ggain_o, gbias_o, gu_o, gub_o, gd_o, grpe_o,
    wq, wo, wu, wd, small, om2, xg, cotb,
    qkv, phi, ex, unit, inv, r0, pp, num, den, quo, att, attf,
    pb, rb_f, rb_d, rb_i, fb, hid, dgel, efb, dub, dzb, acc,
    fst, n1, i1, dr, dat_s, dat, out_s, anti, ones64, rows_v,
    dn, dd, ds_, gg, dph, dvv, dqkv,
    g_k, g_v, g_o, g_u, g_d, r_k, r_v, r_o, r_u, r_d, rz_k, rz_v, rz_o, rz_u, rz_d, cb_k, cb_v, cb_o, cb_u, cb_d,
    fs, xs_k, xs_v, xs_o, xs_u, xs_d, xr_k, xr_v, xr_o, xr_u, xr_d,
    sd, sd_r, st_a, st_b, work_a, work_b, mix_s, gt_r,
    ss, rs, ls,
):
    dp, y, c = lax.axis_index("dp"), lax.axis_index("heads"), lax.axis_index("feat")
    z, x = dp // 2, dp % 2
    shard = 2 * dp + c
    s_sems, r_sems, locals_ = Sems(), Sems(), Sems()
    pending = []

    def bring(src, dst, cond=None):
        copy = pltpu.make_async_copy(src, dst, ls.at[locals_.take()])
        if cond is None:
            copy.start()
            return copy.wait
        pl.when(cond)(copy.start)
        return lambda: pl.when(cond)(copy.wait)

    home = c == x
    away = c != x
    own_block = 2 * x + y

    def half_cols(half, width):
        return pl.ds(pl.multiple_of(half * width, width), width)

    def rows_of(index, count):
        return pl.ds(pl.multiple_of(index * count, count), count)

    in_o = bring(wo_h.at[:, half_cols(x, 256)], wo.at[own_block, 2 * z + x, c])
    in_q = bring(wq_h.at[:, :, half_cols(x, 256)], wq.at[:, 2 * z + x, c])
    in_small = [
        bring(src, dst)
        for src, dst in (
            (gain_h, gain_v), (bias_h, bias_v), (rpe_h, rpe_v), (qb_h, qb_v), (ub_h, ub_v), (om_h, om_v), (bk_h, bk_v),
        )
    ]
    in_tok = bring(tok, xg.at[rows_of(c, 256)], home)
    in_u = bring(wu_h.at[:, half_cols(x, 1024)], wu.at[2 * z + x, c])
    in_d = bring(wd_h.at[:, half_cols(x, 1024)], wd.at[2 * z + x, c])
    in_cot = bring(cot.at[rows_of(y, 128)], cotb, home)

    def dev(zz, xx, yy, cc):
        return {"dp": zz * 2 + xx, "heads": yy, "feat": cc}

    sib, xn, yn, dg = dev(z, x, y, 1 - c), dev(z, 1 - x, y, c), dev(z, x, 1 - y, c), dev(z, 1 - x, 1 - y, c)
    xs_dev, ds_dev = dev(z, 1 - x, y, 1 - c), dev(z, 1 - x, 1 - y, 1 - c)
    plane = (dg, xn, yn)
    plane_block = (2 * (1 - x) + 1 - y, 2 * (1 - x) + y, 2 * x + 1 - y)

    def rc(src, dst, s, r, device):
        return pltpu.make_async_remote_copy(
            src_ref=src, dst_ref=dst, send_sem=ss.at[s], recv_sem=rs.at[r], device_id=device, device_id_type=MESH
        )

    def send(src, dst, s, r, device, cond=None):
        def go():
            rc(src, dst, s, r, device).start()

        def done():
            rc(src, dst, s, r, device).wait_send()

        if cond is None:
            go()
            pending.append(done)
        else:
            pl.when(cond)(go)
            pending.append(lambda: pl.when(cond)(done))

    def got(dst, r):
        rc(dst, dst, r, r, sib).wait_recv()

    def take(count=1):
        return s_sems.take(count), r_sems.take(count)

    def give(src, dst, pair, device, cond=None, s=0, r=0):
        send(src, dst, pair[0] + s, pair[1] + r, device, cond)

    def valid(dz):
        return jnp.logical_and(z + dz >= 0, z + dz < PLANES)

    def by_plane(table):
        found = []
        for k in range(PLANES):
            block = jnp.int32(table[0][k])
            for zz in range(1, PLANES):
                block = jnp.where(z == zz, table[zz][k], block)
            found.append(block)
        return found

    arrive = by_plane(((0, 1, 2, 3), (1, 2, 3, 0), (2, 1, 0, 3), (3, 2, 1, 0)))
    leave = by_plane(((3, 2, 1, 0), (0, 3, 2, 1), (3, 0, 1, 2), (0, 1, 2, 3)))

    def at_step(blocks, k):
        block = blocks[0]
        for i in range(1, PLANES):
            block = jnp.where(k == i, blocks[i], block)
        return block

    def cols256(n):
        return pl.ds(pl.multiple_of(n * 256, 256), 256)

    barrier = pltpu.get_barrier_semaphore()
    for other in (sib, xn, yn, dg, xs_dev, ds_dev, dev(z, x, 1 - y, 1 - c)):
        pl.semaphore_signal(barrier, inc=1, device_id=other, device_id_type=MESH)
    for zz in range(PLANES):
        @pl.when(z != zz)
        def _(zz=zz):
            pl.semaphore_signal(barrier, inc=1, device_id=dev(zz, x, y, c), device_id_type=MESH)
    pl.semaphore_wait(barrier, 10)

    class Item:
        def __init__(self, ref, kind):
            self.ref, self.kind = ref, kind
            self.z_out, self.c_out = s_sems.take(), s_sems.take()
            self.zs, self.sb = r_sems.take(PLANES), r_sems.take(PLANES)

        def block(self, zz, cc):
            if self.kind == "both":
                return self.ref.at[pl.ds(2 * zz, 2), cc]
            at = 2 * zz + (x if self.kind == "own" else 1 - x)
            return self.ref.at[:, at, cc] if len(self.ref.shape) == 5 else self.ref.at[at, cc]

        def some(self, count):
            if self.kind == "both":
                return self.ref.at[pl.ds(0, count)]
            return self.ref.at[:, pl.ds(0, count), 0] if len(self.ref.shape) == 5 else self.ref.at[pl.ds(0, count), 0]

        def onward(self, n, step):
            here = self.block(n, c)
            rc(here, here, self.z_out, self.zs + n, dev(z + step, x, y, c)).start()

        def start(self):
            pl.when(z == 0)(lambda: self.onward(z, 2))
            pl.when(z == 3)(lambda: self.onward(z, -2))
            pl.when(z > 0)(lambda: self.onward(z, -1))
            pl.when(z < PLANES - 1)(lambda: self.onward(z, 1))
            mine = self.block(z, c)
            rc(mine, mine, self.c_out, self.sb + z, sib).start()

        def pump_step(self, n):
            here = self.block(n, c)

            @pl.when(n != z)
            def _():
                got(here, self.zs + n)
                pl.when(jnp.logical_and(z == 1, n > z))(lambda: self.onward(n, -1))
                pl.when(jnp.logical_and(z == 2, n < z))(lambda: self.onward(n, 1))
                rc(here, here, self.c_out, self.sb + n, sib).start()

        def pump_done(self):
            def sent(sem, count):
                rc(self.some(count), self.some(count), sem, 0, sib).wait_send()

            pending.append(lambda: sent(self.c_out, 4))
            pending.append(lambda: pl.when((z == 0) | (z == 3))(lambda: sent(self.z_out, 2)))
            pending.append(lambda: pl.when((z == 1) | (z == 2))(lambda: sent(self.z_out, 4)))

        def pump(self):
            for k in range(1, PLANES):
                self.pump_step(arrive[k])
            self.pump_done()

        def need_step(self, n):
            got(self.block(n, 1 - c), self.sb + n)

        def need(self):
            for zz in range(PLANES):
                self.need_step(zz)

    half_of = {}

    def place(ref, xx):
        return ref.at[:, 2 * z + xx, c] if len(ref.shape) == 5 else ref.at[2 * z + xx, c]

    def give_half(name, src, ref):
        i = take()
        half_of[name] = (ref, i[1])
        give(src, place(ref, x), i, xn)

    def have_half(name):
        ref, i = half_of[name]
        got(place(ref, 1 - x), i)

    wo_own = wo.at[own_block]
    i_oh = take()
    give(wo_h.at[:, half_cols(1 - x, 256)], wo.at[2 * (1 - x) + y, 2 * z + x, c], i_oh, xn)
    give_half("q", wq_h.at[:, :, half_cols(1 - x, 256)], wq)
    i_tok, i_tx, i_ty = take(), take(2), take(2)
    give(tok, xg.at[rows_of(c, 256)], i_tok, sib, away)
    give(tok.at[rows_of(y, 128)], xg.at[rows_of(2 * c + y, 128)], i_tx, dev(z, 1 - x, y, x), None, 0, c)
    it_oa, it_ob = Item(wo_own, "own"), Item(wo_own, "other")
    it_qa, it_s, it_qb = Item(wq, "own"), Item(small, "both"), Item(wq, "other")
    it_ua, it_ub, it_da, it_db = Item(wu, "own"), Item(wu, "other"), Item(wd, "own"), Item(wd, "other")
    in_o()
    it_oa.start()
    in_q()
    it_qa.start()

    for done in in_small:
        done()

    def pick(shape, hit):
        return jnp.where(hit(iota(shape, 0), iota(shape, 1)), 1.0, 0.0)

    vec_sel = pick((64, 128), lambda k, l: l == c * 64 + k).astype(BF16)
    rpe_sel = pick((64, 128), lambda k, l: l == (1 - c) * 64 + 63 - k).astype(BF16)
    bias_sel = [pick((4, 128), lambda k, l, par=par: l == par * 64 + 4 * shard + k).astype(BF16) for par in range(2)]
    rpe_rows = dot(rpe_v[...], rpe_sel)
    level = jnp.full((1, 128), bk_v[0].astype(F32))
    top = jnp.concatenate(
        [dot(gain_v[...], vec_sel), dot(bias_v[...], vec_sel), level, jnp.zeros((1, 128), F32)], axis=0
    )

    def spread(values):
        rows = values.shape[1]
        even = (iota((rows, 1), 0) % 2) == 0
        wide = jnp.where(even, dot(values, bias_sel[0], TN), dot(values, bias_sel[1], TN))
        return dot(pick((rows // 2, rows), lambda k, l: l // 2 == k).astype(BF16), wide.astype(BF16))

    up_rows = spread(ub_v[...])
    qkv_rows = [spread(qb_v[p]) for p in range(3)]
    for half in range(2):
        mine = [rows[2 * half : 2 * half + 2] for rows in qkv_rows] + [jnp.zeros((2, 128), F32)]
        position = jnp.concatenate([rpe_rows[4 * half : 4 * half + 4], jnp.zeros((4, 128), F32)], axis=0)
        small_s[half] = jnp.concatenate(
            [top, position] + mine + [up_rows[8 * half : 8 * half + 8]], axis=0
        ).astype(BF16)
    small[2 * z + x, c] = small_s[x]
    give_half("s", small_s.at[1 - x], small)
    for h in range(4):
        sel = pick((32, 256), lambda k, l: l == h * 64 + c * 32 + k).astype(BF16)
        om_s[h * 64 : (h + 1) * 64] = dot(om_v[4 * x + h], sel, TN).astype(BF16)
    i_om = take()
    give(om_s, om2, i_om, sib)
    give_half("u", wu_h.at[:, half_cols(1 - x, 1024)], wu)

    same = (iota((256, 256), 0) // HEAD) == (iota((256, 256), 1) // HEAD)
    ones64[...] = jnp.where(same, 1.0, 0.0).astype(BF16)
    anti[...] = jnp.where(iota((512, 512), 0) + iota((512, 512), 1) == 511, 1.0, 0.0).astype(BF16)

    got(wo.at[own_block, 2 * z + 1 - x, c], i_oh[1])
    it_ob.start()
    have_half("q")
    it_qb.start()
    it_oa.pump()
    it_qa.pump()
    it_ob.pump()
    i_oq, i_os = take(3), take(3)
    quarter = wo.at[own_block, :, c]
    give(quarter, quarter, i_oq, yn, None, 2, 2)
    give(quarter, quarter, i_oq, xn, None, 1, 1)
    have_half("s")
    it_s.start()
    in_u()
    it_ua.start()

    @pl.when(away)
    def _():
        for f in range(2):
            got(xg.at[rows_of(2 * f + y, 128)], i_tx[1] + f)

    for f in range(2):
        part = xg.at[rows_of(2 * f + y, 128)]
        give(part, part, i_ty, yn, away, f, f)
    it_qb.pump()
    have_half("u")
    it_ub.start()

    def other_quarter(slot):
        part = wo.at[plane_block[slot], :, c]
        got(part, i_oq[1] + slot)
        give(part, part, i_os, sib, None, slot, slot)
        return part

    it_s.pump()

    it_s.need()
    for t in range(8):
        tile = small[t, 0].astype(F32) + small[t, 1].astype(F32)
        rows_v[0:8, t * 128 : (t + 1) * 128] = tile[0:8]
        rows_v[8:16, (7 - t) * 128 : (8 - t) * 128] = tile[8:16]
        total = tile[16:32] if t == 0 else total + tile[16:32]
    for r in range(6):
        rows_v[16:17, r * 128 : (r + 1) * 128] = total[r : r + 1]
    for r in range(8):
        rows_v[17:18, r * 128 : (r + 1) * 128] = total[8 + r : 9 + r]
    level = small[2 * z + c, 0][6:7].astype(F32)
    wide1 = jnp.where(level > 0.5, 1.0, 0.0)
    wide2 = jnp.where(level > 1.5, 1.0, 0.0)
    one_row = jnp.ones((1, 128), F32)

    def mask_row(bi):
        parts = [one_row if bj == bi else (wide1 if bj // 2 == bi // 2 else wide2) for bj in range(4)]
        return jnp.concatenate(parts, axis=1)

    masks = [mask_row(bi) for bi in range(4)]

    def coeff_body(h, carry):
        row = jnp.exp(rows_v[pl.ds(8 + h, 1), :])
        r0[h] = pltpu.roll(jnp.broadcast_to(row, (128, 1024)), 1, 1, stride=1, stride_axis=0)
        return carry

    lax.fori_loop(0, 4, coeff_body, 0)
    num[...] = jnp.zeros_like(num)
    den[...] = jnp.zeros_like(den)

    in_tok()
    pl.when(home)(lambda: got(xg.at[rows_of(1 - c, 256)], i_tok[1]))

    @pl.when(away)
    def _():
        for f in range(2):
            got(xg.at[rows_of(2 * f + 1 - y, 128)], i_ty[1] + f)

    other_quarter(2)
    part = other_quarter(1)
    give(part, part, i_oq, yn, None, 0, 0)
    it_qa.need()
    it_qb.need()

    def qkv_body(p, carry):
        qkv[p] = (dot(xg[...], wq[p].reshape(1024, 256)) + rows_v[16:17, cols256(p)]).astype(BF16)
        return carry

    lax.fori_loop(0, 3, qkv_body, 0)
    got(om2, i_om[1])
    om2[...] = om2[...] + om_s[...]

    def feature_body(t, carry):
        wide = qkv[t].astype(F32)
        sums = split_dot(wide * wide, ones64[...])
        inverse = lax.rsqrt(sums * (1.0 / HEAD) + UNIT_EPS)
        units = wide * inverse
        logits = SCALE * split_dot(units, om2[...]) - 0.5 * SCALE * SCALE * (sums * inverse * inverse)
        value = jnp.exp(logits) * M ** (-0.5)
        ex[t] = value
        unit[t] = units
        inv[t] = inverse
        phi[t] = value.astype(BF16)
        return carry

    lax.fori_loop(0, 2, feature_body, 0)
    it_ua.pump()
    lane_head = iota((1, 128), 1) // HEAD

    def head_cols(h):
        return pl.ds(pl.multiple_of((h // 2) * 128, 128), 128), (lane_head == h % 2)

    def head_body(h, carry):
        cols, mine = head_cols(h)
        keep = jnp.where(mine, 1.0, 0.0).astype(BF16)
        scores = dot(phi[0, :, cols] * keep, phi[1, :, cols], NT)
        for b in range(4):
            coefficient = r0[h, :, 512 - 128 * b : 1024 - 128 * b] * masks[b]
            pp[h, b * 128 : (b + 1) * 128] = (scores[b * 128 : (b + 1) * 128] * coefficient).astype(BF16)
        right = jnp.concatenate([qkv[2, :, cols] * keep, jnp.broadcast_to(keep, (512, 128))], axis=1)
        both = dot(pp[h], right)
        num[:, cols] += both[:, :128]
        den[:, cols] += both[:, 128:]
        return carry

    lax.fori_loop(0, 4, head_body, 0)
    quo[...] = num[...] / den[...]
    att[...] = quo[...].astype(BF16).reshape(4, 128, 256)

    i_at = take(3)
    for slot in range(3):
        give(att.at[plane_block[slot]], attf.at[own_block], i_at, plane[slot], None, slot, slot)
    attf[own_block] = att[own_block]
    in_d()
    it_da.start()
    other_quarter(0)
    give_half("d", wd_h.at[:, half_cols(1 - x, 1024)], wd)
    i_cot = take()
    give(cot.at[rows_of(y, 128)], cotb, i_cot, xs_dev, away)
    it_oa.need()
    it_ob.need()
    for slot in range(3):
        got(wo.at[plane_block[slot], :, 1 - c], i_os[1] + slot)
    for slot in range(3):
        got(attf.at[plane_block[slot]], i_at[1] + slot)

    def out_body(q, carry):
        return carry + dot(attf[q], wo[q].reshape(1024, 256), NT)

    mixed_z = lax.fori_loop(0, 4, out_body, jnp.zeros((128, 1024), F32))

    def norm(values):
        centred = values - jnp.mean(values, axis=-1, keepdims=True)
        inverse = lax.rsqrt(jnp.mean(centred * centred, axis=-1, keepdims=True) + EPSILON)
        return centred * inverse, inverse

    residual = mixed_z + xg[rows_of(own_block, 128)].astype(F32) + rows_v[2:3, :]
    normed, inverse = norm(residual)
    first = normed * rows_v[0:1, :] + rows_v[3:4, :]
    fb[own_block] = first.astype(BF16)

    class Scatter:
        def __init__(self, ref):
            self.ref, self.out, self.base = ref, s_sems.take(), r_sems.take(4)

        def part(self, n, value):
            cols = cols256(n)
            pb[:, :, cols] = value.astype(BF16).reshape(4, 128, 256)
            for slot in range(3):
                rc(
                    pb.at[plane_block[slot], :, cols], self.ref.at[slot, :, cols], self.out, self.base + n, plane[slot]
                ).start()

        def column(self, n):
            cols = slice(n * 256, (n + 1) * 256)
            got(self.ref.at[:, :, cols], self.base + n)
            value = pb[own_block, :, cols].astype(F32)
            for slot in range(3):
                value = value + self.ref[slot, :, cols].astype(F32)
            return value

        def total(self):
            return jnp.concatenate([self.column(n) for n in range(4)], axis=1)

        def sent(self):
            rc(self.ref, self.ref, self.out, 0, sib).wait_send()

    class Gather:
        def __init__(self, ref, order):
            self.ref, self.out, self.base, self.order = ref, s_sems.take(), r_sems.take(4), order
            pending.append(lambda: rc(ref.at[pl.ds(0, 3)], ref.at[pl.ds(0, 3)], self.out, 0, sib).wait_send())

        def start(self):
            for n in self.order:
                for slot in range(3):
                    mine = self.ref.at[own_block, :, cols256(n)]
                    rc(mine, mine, self.out, self.base + n, plane[slot]).start()

        def need(self, n):
            got(self.ref.at[pl.ds(0, 3), :, cols256(n)], self.base + n)

    class RelayGather:
        def __init__(self, ref, order):
            self.ref, self.out, self.base, self.order = ref, s_sems.take(), r_sems.take(12), order
            pending.append(lambda: rc(ref.at[pl.ds(0, 3)], ref.at[pl.ds(0, 3)], self.out, 0, sib).wait_send())

        def piece(self, slot, n):
            return self.ref.at[plane_block[slot], :, cols256(n)]

        def start(self):
            for n in self.order:
                mine = self.ref.at[own_block, :, cols256(n)]
                for slot in (1, 2):
                    rc(mine, mine, self.out, self.base + slot * 4 + n, plane[slot]).start()

        def pass_on(self, k):
            n, slot = self.order[k], 1 + k % 2
            part = self.piece(slot, n)
            got(part, self.base + slot * 4 + n)
            rc(part, part, self.out, self.base + n, plane[3 - slot]).start()

        def need(self, k):
            n, slot = self.order[k], 2 - k % 2
            got(self.piece(slot, n), self.base + slot * 4 + n)
            got(self.piece(0, n), self.base + n)

    g_first = Gather(fb, range(4))
    g_first.start()
    it_ub.pump()
    have_half("d")
    it_db.start()
    fst[...] = first
    n1[...] = normed
    i1[...] = jnp.broadcast_to(inverse, (128, 128))

    def d_cols(ref, m):
        return ref[:, :, cols256(m)].reshape(512, 256)

    acc[...] = jnp.zeros_like(acc)
    it_ua.need()
    it_ub.need()

    def hidden_part(n, carry):
        g_first.need(n)
        left = d_cols(fb, n)
        for j in range(4):
            cols = slice(j * 256, (j + 1) * 256)
            acc[:, cols] += dot(left, wu[pl.ds(2 * n, 2), :, :, cols].reshape(256, 256))
        return carry

    lax.fori_loop(0, 2, hidden_part, 0)
    it_da.pump()
    lax.fori_loop(2, 4, hidden_part, 0)

    def hidden_body(n, carry):
        cols = cols256(n)
        pre = acc[:, cols] + rows_v[17:18, cols]
        cdf = 0.5 * (1.0 + lax.erf(pre * 0.7071067811865476))
        hid[:, cols] = (pre * cdf).astype(BF16)
        dgel[:, cols] = cdf + pre * (0.3989422804014327 * jnp.exp(-0.5 * pre * pre))
        return carry

    lax.fori_loop(0, 4, hidden_body, 0)
    sc_f = Scatter(rb_f)

    def down_part(k, carry):
        n = at_step(arrive, k)
        it_db.pump_step(n)
        it_da.need_step(n)
        it_db.need_step(n)
        sc_f.part(n, dot(hid[...], wd[pl.ds(2 * n, 2)].reshape(256, 1024), NT))
        return carry

    lax.fori_loop(0, 4, down_part, 0)
    it_db.pump_done()
    pl.when(away)(lambda: got(cotb, i_cot[1]))
    in_cot()
    upstream = cotb[...].astype(F32)

    def down(values):
        return jnp.sum(values, axis=0, keepdims=True)

    sd[5:6, :] = down(upstream)
    acc[...] = jnp.zeros_like(acc)
    second = fst[...] + sc_f.total() + rows_v[4:5, :]
    normed2, inverse2 = norm(second)

    def norm_back(upstream, normed, inverse, gain):
        scaled = upstream * gain
        mean = jnp.mean(scaled, axis=-1, keepdims=True)
        slope = jnp.mean(scaled * normed, axis=-1, keepdims=True)
        return inverse * (scaled - mean - normed * slope)

    err = norm_back(upstream, normed2, inverse2, rows_v[1:2, :])
    efb[own_block] = err.astype(BF16)
    g_ef = Gather(efb, leave)
    g_ef.start()
    mix_s[...] = (normed2 * rows_v[1:2, :] + rows_v[5:6, :]).astype(BF16)
    dr[...] = err
    sd[1:2, :] = down(upstream * normed2)
    sd[4:5, :] = down(err.astype(BF16).astype(F32))
    sc_f.sent()

    class Owner:
        def __init__(self, dst, pieces):
            self.dst, self.width = dst, 1024 // pieces
            self.ids = [take(2) for _ in range(pieces)]

        def part(self, half, n):
            return self.dst.at[rows_of(half, 128), n * self.width : (n + 1) * self.width]

        def start(self, src, n):
            cols = slice(n * self.width, (n + 1) * self.width)

            @pl.when(home)
            def _():
                self.dst[rows_of(y, 128), cols] = src[:, cols]

            give(src.at[:, cols], self.part(y, n), self.ids[n], yn, home, 1, 1)
            give(src.at[:, cols], self.part(y, n), self.ids[n], xs_dev, away, 0, 0)

        def pass_on(self, n):
            part = self.part(y, n)
            pl.when(away)(lambda: got(part, self.ids[n][1]))
            give(part, part, self.ids[n], yn, away, 1, 1)

        def need(self, n):
            got(self.part(1 - y, n), self.ids[n][1] + 1)

    own_mix = Owner(mixed_o, 1)
    own_mix.start(mix_s, 0)

    class Grad:
        def __init__(self, g, r, rz, cb, xs, xr):
            self.g, self.r, self.rz, self.cb, self.xs, self.xr = g, r, rz, cb, xs, xr
            self.d, self.z, self.k, self.x = r_sems.take(4), r_sems.take(PLANES), r_sems.take(2), take()
            self.d_out, self.z_out = s_sems.take(), s_sems.take()
            self.width = r.shape[-1]

        def give(self, m):
            rc(self.g.at[m, :, 1 - c], self.r.at[m], self.d_out, self.d + m, sib).start()

        def pair_step(self, m):
            got(self.r.at[m], self.d + m)
            self.r[m] = (self.g[m, :, c].astype(F32) + self.r[m].astype(F32)).astype(BF16)
            far = jnp.abs(m - z)
            part = self.r.at[m]
            outer = (z == 0) | (z == 3)
            beside = dev(jnp.where(z == 0, 1, jnp.where(z == 1, 0, jnp.where(z == 2, 3, 2))), x, y, c)

            @pl.when(jnp.logical_or(outer, m == jnp.where(z == 1, 0, 3)) & (far == 1))
            def _():
                rc(part, self.rz.at[z], self.z_out, self.z + z, beside).start()

            for slot in range(2):
                @pl.when(outer & (far == 3 - slot))
                def _(slot=slot):
                    rc(part, self.cb.at[slot], self.z_out, self.k + slot, beside).start()

        def relay(self):
            for at, blocks in ((1, (3, 2)), (2, (0, 1))):
                @pl.when(z == at)
                def _(at=at, blocks=blocks):
                    for slot, m in enumerate(blocks):
                        got(self.cb.at[slot], self.k + slot)
                        self.r[m] = (self.r[m].astype(F32) + self.cb[slot].astype(F32)).astype(BF16)
                        rc(self.r.at[m], self.rz.at[at], self.z_out, self.z + at, dev(m, x, y, c)).start()

        def run(self, make):
            def body(k, carry):
                m = at_step(leave, k)
                make(m)
                self.give(m)
                pl.when(k > 0)(lambda: self.pair_step(at_step(leave, k - 1)))
                return carry

            lax.fori_loop(0, PLANES, body, 0)
            self.pair_step(leave[3])

        def finish(self):
            total = fs.at[:, :, 0 : self.width]
            total[...] = self.r[z].astype(F32)
            for dz in (1, -1, 2, -2):
                @pl.when(valid(dz) if abs(dz) == 1 else z == (0 if dz > 0 else 3))
                def _(dz=dz):
                    got(self.rz.at[z + dz], self.z + z + dz)
                    total[...] += self.rz[z + dz].astype(F32)
            self.xs[...] = fs[1 - x, :, 0 : self.width].astype(BF16)
            give(self.xs, self.xr, self.x, xn)

        def sent(self):
            rc(self.r, self.r, self.d_out, 0, sib).wait_send()
            part = self.r.at[pl.ds(0, 3)]
            rc(part, part, self.z_out, 0, sib).wait_send()

        def columns(self, out, half, value, at=0):
            if len(out.shape) == 3:
                for p in range(self.width // 256):
                    out[at + p, :, half_cols(half, 256)] = value[:, p * 256 : (p + 1) * 256]
            else:
                out[:, half_cols(half, self.width)] = value

        def write_own(self, out, at=0):
            self.columns(out, x, fs[x, :, 0 : self.width], at)

        def write_other(self, out, at=0):
            got(self.xr, self.x[1])
            self.columns(out, 1 - x, self.xr[...].astype(F32), at)

    gr_d = Grad(g_d, r_d, rz_d, cb_d, xs_d, xr_d)
    gr_u = Grad(g_u, r_u, rz_u, cb_u, xs_u, xr_u)
    gr_o = Grad(g_o, r_o, rz_o, cb_o, xs_o, xr_o)
    gr_v = Grad(g_v, r_v, rz_v, cb_v, xs_v, xr_v)
    gr_k = Grad(g_k, r_k, rz_k, cb_k, xs_k, xr_k)

    def make_down(m):
        g_ef.need(m)
        left = d_cols(efb, m)
        g_d[m] = dot(left, hid[...], TN).astype(BF16).reshape(2, 2, 64, 1024)
        gr_d.give(m)
        for j in range(4):
            cols = slice(j * 256, (j + 1) * 256)
            acc[:, cols] += dot(left, wd[pl.ds(2 * m, 2), :, :, cols].reshape(256, 256))
        gr_d.pair_step(m)

    def down_grads(k, carry):
        make_down(at_step(leave, k))
        return carry

    lax.fori_loop(0, PLANES, down_grads, 0)
    def du_body(n, carry):
        cols = cols256(n)
        du = (acc[:, cols] * dgel[:, cols]).astype(BF16)
        dub[:, cols] = du
        st_a[6:7, cols] = down(du.astype(F32))
        return carry

    lax.fori_loop(0, 4, du_body, 0)
    sc_d = Scatter(rb_d)

    def back_part(n, carry):
        sc_d.part(n, dot(dub[...], wu[pl.ds(2 * n, 2)].reshape(256, 1024), NT))
        return carry

    lax.fori_loop(0, 4, back_part, 0)
    own_mix.pass_on(0)

    def make_up(m):
        g_u[m] = dot(d_cols(fb, m), dub[...], TN).astype(BF16).reshape(2, 2, 64, 1024)

    gr_d.relay()
    gr_u.run(make_up)
    dfirst = dr[...] + sc_d.total()
    back = norm_back(dfirst, n1[...], i1[:, 0:1], rows_v[0:1, :])
    dz = back.astype(BF16)
    dzb[own_block] = dz

    def dattn_body(q, carry):
        dat_s[q] = dot(dz, wo[q].reshape(1024, 256)).astype(BF16)
        return carry

    lax.fori_loop(0, 4, dattn_body, 0)
    i_da = take(3)
    for slot in range(3):
        give(dat_s.at[plane_block[slot]], dat.at[own_block], i_da, plane[slot], None, slot, slot)
    dat[own_block] = dat_s[own_block]
    g_dz = RelayGather(dzb, leave)
    g_dz.start()
    sd[0:1, :] = down(dfirst * n1[...])
    sd[3:4, :] = down(dfirst)
    sd[2:3, :] = down(dz.astype(F32))
    sd[6:8, :] = jnp.zeros((2, 1024), F32)
    class Total:
        def __init__(self, ref, work):
            self.ref, self.work = ref, work
            self.c, self.z, self.h = take(), take(PLANES), take()

        def pair(self):
            give(self.ref, self.work.at[0], self.c, sib)

        def over_planes(self):
            got(self.work.at[0], self.c[1])
            self.work[1] = self.ref[...] + self.work[0]
            for zz in range(PLANES):
                give(self.work.at[1], self.work.at[2 + z], self.z, dev(zz, x, y, c), z != zz, zz, z)

        def finish(self):
            total = self.work[1]
            for zz in range(PLANES):
                @pl.when(z != zz)
                def _(zz=zz):
                    got(self.work.at[2 + zz], self.z[1] + zz)

                @pl.when(z == zz)
                def _(zz=zz):
                    self.work[2 + zz] = jnp.zeros((8, 1024), F32)
                total = total + self.work[2 + zz]
            self.work[6] = total
            give(self.work.at[6], self.work.at[7], self.h, xn)

        def need(self):
            got(self.work.at[7], self.h[1])

        def of_half(self, half):
            return jnp.where(x == half, self.work[6], self.work[7])

    early, late = Total(st_a, work_a), Total(st_b, work_b)
    i_sd = take(3)
    for k, device in enumerate(plane):
        give(sd, sd_r.at[k], i_sd, device, None, k, k)
    dr[...] = back
    sc_d.sent()
    dph[...] = jnp.zeros_like(dph)
    dvv[...] = jnp.zeros_like(dvv)
    for slot in range(3):
        got(dat.at[plane_block[slot]], i_da[1] + slot)

    dattn = dat[...].reshape(512, 256).astype(F32)
    recip = 1.0 / den[...]
    dn[...] = (dattn * recip).astype(BF16)
    dsum = split_dot(dattn * quo[...], ones64[...])
    dd[...] = ((-dsum * recip).astype(BF16).astype(F32) * (1.0 / HEAD)).astype(BF16)

    def value_back(h, carry):
        cols, mine = head_cols(h)
        keep = jnp.where(mine, 1.0, 0.0).astype(BF16)
        dvv[:, cols] += dot(pp[h], dn[:, cols] * keep, TN)
        return carry

    lax.fori_loop(0, 4, value_back, 0)
    dqkv[2] = dvv[...].astype(BF16)

    def x_cols(m):
        return xg[:, cols256(m)]

    def make_v(m):
        g_v[m] = dot(x_cols(m), dqkv[2], TN).astype(BF16).reshape(2, 2, 64, 256)

    def head_back(h, carry):
        cols, mine = head_cols(h)
        keep = jnp.where(mine, 1.0, 0.0).astype(BF16)
        left = jnp.concatenate([dn[:, cols] * keep, dd[:, cols] * keep], axis=1)
        right = jnp.concatenate([qkv[2, :, cols], jnp.ones((512, 128), BF16)], axis=1)
        grad_p = dot(left, right, NT)
        for b in range(4):
            rows = slice(b * 128, (b + 1) * 128)
            coefficient = r0[h, :, 512 - 128 * b : 1024 - 128 * b] * masks[b]
            part = grad_p[rows]
            ds_[rows] = (part * coefficient).astype(BF16)
            gg[h, rows] = (part * pp[h, rows].astype(F32)).astype(BF16)
        dph[0, :, cols] += dot(ds_[...], phi[1, :, cols] * keep)
        dph[1, :, cols] += dot(ds_[...], phi[0, :, cols] * keep, TN)
        return carry

    g_dz.pass_on(0)
    lax.fori_loop(0, 4, head_back, 0)
    g_dz.pass_on(1)
    g_dz.pass_on(2)
    gr_v.run(make_v)
    g_dz.pass_on(3)
    gr_u.relay()

    def feature_back_body(t, carry):
        dlog = (dph[t] * ex[t]).astype(BF16)
        units = unit[t]
        dunit = SCALE * dot(dlog, om2[...], NT) - SCALE * SCALE * dot(dlog, ones64[...]) * units
        mean = split_dot(dunit * units, ones64[...]) * (1.0 / HEAD)
        dqkv[t] = (inv[t] * (dunit - units * mean)).astype(BF16)
        return carry

    lax.fori_loop(0, 2, feature_back_body, 0)
    class Return:
        def __init__(self, ref):
            self.ref, self.out, self.base, self.last = ref, s_sems.take(), r_sems.take(4), take(4)
            pending.append(lambda: pl.when(home)(lambda: rc(ref.at[0:3], ref.at[0:3], self.out, 0, sib).wait_send()))
            pending.append(lambda: pl.when(away)(lambda: rc(ref, ref, self.out, 0, sib).wait_send()))

        def part(self, n, value):
            cols = cols256(n)
            for b in range(4):
                rows = value[b * 128 : (b + 1) * 128]
                pb[b, :, cols] = jnp.where(own_block == b, rows + dr[:, cols], rows).astype(BF16)
                here = home & (c == b // 2) & (y == b % 2)

                @pl.when(here)
                def _(b=b):
                    self.ref[own_block, :, cols] = pb[b, :, cols]

                @pl.when(jnp.logical_not(here))
                def _(b=b):
                    there = self.ref.at[own_block, :, cols]
                    rc(pb.at[b, :, cols], there, self.out, self.base + n, dev(z, c, b % 2, b // 2)).start()

        def column(self, n):
            cols = slice(n * 256, (n + 1) * 256)
            pl.when(home)(lambda: got(self.ref.at[0:3, :, cols], self.base + n))
            pl.when(away)(lambda: got(self.ref.at[0:4, :, cols], self.base + n))
            value = self.ref[0, :, cols].astype(F32)
            for slot in range(1, 4):
                value = value + self.ref[slot, :, cols].astype(F32)
            mine = gt_r.at[rows_of(y, 128), cols]
            mine[...] = value.astype(BF16)
            give(mine, mine, self.last, yn, None, n, n)
            gtok_o[rows_of(y, 128), cols] = value

        def need(self, n):
            cols = slice(n * 256, (n + 1) * 256)
            rows = rows_of(1 - y, 128)
            got(gt_r.at[rows, cols], self.last[1] + n)
            gtok_o[rows, cols] = gt_r[rows, cols].astype(F32)

    sc_i = Return(rb_i)

    def input_part(n, carry):
        value = jnp.zeros((512, 256), F32)
        for p in range(3):
            value = value + dot(dqkv[p], wq[p, pl.ds(2 * n, 2)].reshape(256, 256), NT)
        sc_i.part(n, value)
        return carry

    lax.fori_loop(0, 4, input_part, 0)
    for k in range(3):
        got(sd_r.at[k], i_sd[1] + k)
    st_a[0:6, :] = (sd[...] + sd_r[0] + sd_r[1] + sd_r[2])[0:6]
    st_a[7:8, :] = jnp.zeros((1, 1024), F32)
    early.pair()
    gr_d.finish()
    gr_d.write_own(gd_o)

    def diagonal_body(h, carry):
        flipped = dot(anti[...], gg[h])
        sums = jnp.zeros((1, 1024), F32)
        for b in range(4):
            wide = jnp.concatenate([flipped[b * 128 : (b + 1) * 128], jnp.zeros((128, 128), F32)], axis=1)
            line = down(pltpu.roll(wide, 0, 1, stride=1, stride_axis=0))
            pieces = [line]
            if b > 0:
                pieces = [jnp.zeros((1, 128 * b), F32)] + pieces
            if b < 3:
                pieces = pieces + [jnp.zeros((1, 384 - 128 * b), F32)]
            sums = sums + jnp.concatenate(pieces, axis=1)
        st_b[pl.ds(1 + h, 1), :] = sums
        return carry

    lax.fori_loop(0, 4, diagonal_body, 0)
    for p in range(3):
        st_b[0:1, p * 256 : (p + 1) * 256] = down(dqkv[p].astype(F32))
    st_b[0:1, 768:1024] = jnp.zeros((1, 256), F32)
    st_b[5:8, :] = jnp.zeros((3, 1024), F32)
    late.pair()
    early.over_planes()

    def make_k(m):
        for p in range(2):
            g_k[m, :, :, :, p * 256 : (p + 1) * 256] = (
                dot(x_cols(m), dqkv[p], TN).astype(BF16).reshape(2, 2, 64, 256)
            )

    gr_k.run(make_k)

    def make_out(m):
        g_o[m] = dot(d_cols(dzb, m), att[...].reshape(512, 256), TN).astype(BF16).reshape(2, 2, 64, 256)

    for k in range(4):
        g_dz.need(k)
    gr_o.run(make_out)

    late.over_planes()
    outs = []
    own_mix.need(0)
    outs.append(bring(mixed_o, mixed_h))
    gr_v.relay()
    gr_u.finish()
    gr_u.write_own(gu_o)
    early.finish()
    sc_i.column(0)
    sc_i.column(1)
    gr_k.relay()
    sc_i.column(2)
    sc_i.column(3)
    gr_d.write_other(gd_o)
    outs.append(bring(gd_o, gd_h))
    gr_o.relay()
    gr_v.finish()
    gr_v.write_own(gq_o, 2)
    gr_u.write_other(gu_o)
    outs.append(bring(gu_o, gu_h))

    def exact(left, right):
        return lax.dot_general(left, right, NN, precision=lax.Precision.HIGHEST, preferred_element_type=F32)

    early.need()
    mine = early.work[6, :, pl.ds(pl.multiple_of(dp * 128, 128), 128)]
    own = exact(mine, pick((128, 64), lambda k, l: k == c * 64 + l))
    ggain_o[...] = own[0:2]
    gbias_o[...] = own[2:6]
    outs.append(bring(ggain_o, ggain_h))
    outs.append(bring(gbias_o, gbias_h))
    late.finish()
    gr_k.finish()
    gr_k.write_own(gq_o)
    gr_o.finish()
    gr_o.write_own(go_o)
    for n in range(4):
        sc_i.need(n)
    outs.append(bring(gtok_o, gtok_h))
    late.need()
    ups = [early.of_half(half) for half in range(2)]
    rest = [late.of_half(half) for half in range(2)]
    tile = pl.ds(pl.multiple_of((7 - dp) * 128, 128), 128)
    sd_r[0] = rest[0]
    sd_r[1] = rest[1]
    lines = jnp.concatenate([sd_r[0, 1:5, tile], sd_r[1, 1:5, tile]], axis=0)
    grpe_o[...] = exact(lines, pick((128, 64), lambda k, l: k == (1 - c) * 64 + 63 - l))
    outs.append(bring(grpe_o, grpe_h))
    lines = [
        rest[half][0:1, p * 256 + t * 128 : p * 256 + (t + 1) * 128]
        for p in range(3) for half in range(2) for t in range(2)
    ] + [ups[half][6:7, t * 128 : (t + 1) * 128] for half in range(2) for t in range(8)]
    lines = jnp.concatenate(lines + [jnp.zeros((4, 128), F32)], axis=0)
    found = jnp.zeros((4, 56), F32)
    for par in range(2):
        hit = pick((4, 128), lambda k, l: l == par * 64 + 4 * shard + k)
        values = lax.dot_general(hit, lines, NT, precision=lax.Precision.HIGHEST, preferred_element_type=F32)
        found = found + exact(values, pick((32, 56), lambda k, l: (l // 2 == k) & (l % 2 == par)))
    for p in range(3):
        gqb_o[p] = found[:, 8 * p : 8 * p + 8]
    gub_o[...] = found[:, 24:56]
    outs.append(bring(gqb_o, gqb_h))
    outs.append(bring(gub_o, gub_h))
    gr_v.write_other(gq_o, 2)
    gr_k.write_other(gq_o)
    outs.append(bring(gq_o, gq_h))
    gr_o.write_other(go_o)
    outs.append(bring(go_o, go_h))
    for gr in (gr_d, gr_u, gr_o, gr_v, gr_k):
        gr.sent()
    assert (s_sems.used, r_sems.used, locals_.used) == (SENDS, RECEIVES, 24), (s_sems.used, r_sems.used, locals_.used)
    for done in pending + outs:
        done()


def copy_kernel(*refs):
    count = len(refs) // 3
    sem = refs[-1]
    ins = [pltpu.make_async_copy(refs[i], refs[2 * count + i], sem.at[0, i]) for i in range(count)]
    outs = [pltpu.make_async_copy(refs[2 * count + i], refs[count + i], sem.at[1, i]) for i in range(count)]
    for copy in ins:
        copy.start()
    for one, two in zip(ins, outs):
        one.wait()
        two.start()
    for copy in outs:
        copy.wait()


def fast_local(
    tokens, qkv_weight, qkv_bias, out_weight, norm_gains, row_biases, up_weight, up_bias, down_weight, rpe_bias, omega,
    bucket, cotangent,
):
    def vm(shape, dtype=BF16):
        return pltpu.VMEM(shape, dtype)

    widths = (512, 256, 256, 1024, 1024)
    scratch = [vm((3, 4, 8)), vm((2, 64)), vm((4, 64)), vm((4, 32)), vm((8, 64)), vm((8, 32, 64))]
    scratch += [pltpu.SMEM((1,), jnp.int32), vm((2, 32, 128)), vm((256, 256))]
    results = (
        ((256, 1024), BF16), ((256, 1024), F32), ((3, 64, 512), F32), ((3, 4, 8), F32), ((64, 512), F32), ((2, 64), F32),
        ((4, 64), F32), ((64, 2048), F32), ((4, 32), F32), ((64, 2048), F32), ((8, 64), F32),
    )
    scratch += [vm(*result) for result in results]
    scratch += [vm((3, 8, 2, 64, 256)), vm((4, 8, 2, 64, 256)), vm((8, 2, 64, 1024)), vm((8, 2, 64, 1024))]
    scratch += [vm((8, 2, 32, 128)), vm((256, 256)), vm((512, 1024)), vm((128, 1024))]
    scratch += [vm((3, 512, 256)), vm((2, 512, 256))] + [vm((2, 512, 256), F32)] * 3
    scratch += [vm((4, 128, 1024), F32), vm((4, 512, 512))] + [vm((512, 256), F32)] * 3 + [vm((4, 128, 256))] * 2
    scratch += [vm((4, 128, 1024))] + [vm((3, 128, 1024))] * 2 + [vm((4, 128, 1024))]
    scratch += [vm((4, 128, 1024)), vm((512, 1024)), vm((512, 1024), F32)]
    scratch += [vm((4, 128, 1024)), vm((512, 1024)), vm((4, 128, 1024)), vm((512, 1024), F32)]
    scratch += [vm((128, 1024), F32)] * 2 + [vm((128, 128), F32), vm((128, 1024), F32)]
    scratch += [vm((4, 128, 256))] * 2 + [vm((16, 128)), vm((512, 512)), vm((256, 256)), vm((24, 1024), F32)]
    scratch += [vm((512, 256))] * 2 + [vm((512, 512)), vm((4, 512, 512)), vm((2, 512, 256), F32), vm((512, 256), F32)]
    scratch += [vm((3, 512, 256))]
    scratch += [vm((4, 2, 2, 64, n)) for n in widths]
    scratch += [vm((4, 2, 64, n)) for n in widths] * 2 + [vm((2, 2, 64, n)) for n in widths]
    scratch += [vm((2, 64, 1024), F32)] + [vm((64, n)) for n in widths] * 2
    scratch += [vm((8, 1024), F32), vm((3, 8, 1024), F32)] + [vm((8, 1024), F32)] * 2 + [vm((8, 8, 1024), F32)] * 2
    scratch += [vm((128, 1024)), vm((256, 1024))]
    scratch += [pltpu.SemaphoreType.DMA((SENDS,)), pltpu.SemaphoreType.DMA((RECEIVES,)), pltpu.SemaphoreType.DMA((24,))]

    shapes = tuple(jax.ShapeDtypeStruct(*result) for result in results)
    anywhere = pl.BlockSpec(memory_space=pl.ANY)
    made = pl.pallas_call(
        layer_kernel,
        out_shape=shapes,
        in_specs=[anywhere] * 13,
        out_specs=(anywhere,) * len(shapes),
        scratch_shapes=scratch,
        compiler_params=pltpu.CompilerParams(
            collective_id=0, has_side_effects=True, vmem_limit_bytes=63 * 2**20
        ),
        name="layer",
    )(
        tokens, qkv_weight.transpose(1, 0, 2), qkv_bias.transpose(0, 2, 1), out_weight.T, norm_gains, row_biases, up_weight,
        up_bias.T, down_weight.T, rpe_bias, omega.transpose(0, 2, 1), bucket, cotangent,
    )
    mixed, gtok, gq, gqb, go, ggain, gbias, gu, gub, gd, grpe = pl.pallas_call(
        copy_kernel,
        out_shape=shapes,
        in_specs=[anywhere] * len(shapes),
        out_specs=(anywhere,) * len(shapes),
        scratch_shapes=[vm(*result) for result in results] + [pltpu.SemaphoreType.DMA((2, len(shapes)))],
        compiler_params=pltpu.CompilerParams(vmem_limit_bytes=63 * 2**20),
        name="results",
    )(*made)
    return (
        mixed, gtok, gq.transpose(1, 0, 2), gqb.transpose(0, 2, 1), go.T, ggain, gbias, gu, gub.T, gd.T, grpe,
    )


def solution(mesh):
    sizes = (mesh.shape["dp"], mesh.shape["heads"], mesh.shape["feat"])
    return jax.shard_map(
        fast_local if sizes == (2 * PLANES, 2, 2) else local,
        mesh=mesh,
        in_specs=(
            P(("dp", "feat"), None),
            P(("dp", "feat"), None, "heads"),
            P(None, "heads", ("dp", "feat")),
            P("heads", ("dp", "feat")),
            P(None, ("dp", "feat")),
            P(None, ("dp", "feat")),
            P(("dp", "feat"), "heads"),
            P("heads", ("dp", "feat")),
            P("heads", ("dp", "feat")),
            P("heads", ("dp", "feat")),
            P("heads", None, "feat"),
            P("dp"),
            P(("dp", "feat"), None),
        ),
        out_specs=(
            P(("dp", "feat"), None),
            P(("dp", "feat"), None),
            P(("dp", "feat"), None, "heads"),
            P(None, "heads", ("dp", "feat")),
            P("heads", ("dp", "feat")),
            P(None, ("dp", "feat")),
            P(None, ("dp", "feat")),
            P(("dp", "feat"), "heads"),
            P("heads", ("dp", "feat")),
            P("heads", ("dp", "feat")),
            P("heads", ("dp", "feat")),
        ),
        check_vma=False,
    )
```

```python
import functools

import jax
import jax.numpy as jnp
from jax import lax
from jax.experimental import pallas as pl
from jax.experimental.pallas import tpu as pltpu
from jax.sharding import PartitionSpec as P

HEAD = 64
M = 64


EPSILON = 1e-12
UNIT_EPS = 1e-06


def toeplitz_block(window, extent):
    leading = window.shape[0]
    tiled_rows = jnp.broadcast_to(window[:, None, :], (leading, extent, 2 * extent - 1)).reshape(
        leading, -1
    )
    padded = jnp.pad(tiled_rows, ((0, 0), (0, extent)))
    sheared = padded.reshape(leading, extent, 2 * extent)[:, :, :extent]
    return sheared[:, :, ::-1]


def diagonal_sums(values_grid, extent):
    leading = values_grid.shape[0]
    flipped = values_grid[:, :, ::-1]
    padded = jnp.pad(flipped, ((0, 0), (0, 0), (0, extent))).reshape(leading, -1)
    sheared = padded[:, : extent * (2 * extent - 1)].reshape(leading, extent, 2 * extent - 1)
    return jnp.sum(sheared, axis=1)


def norm_forward(values, gain, shift):
    centred = values - jnp.mean(values, axis=-1, keepdims=True)
    inverse = lax.rsqrt(jnp.mean(centred * centred, axis=-1, keepdims=True) + EPSILON)
    normed = centred * inverse
    return (normed * gain + shift, normed, inverse)


def norm_backward(upstream, normed, inverse, gain):
    scaled_grad = upstream * gain
    return inverse * (
        scaled_grad
        - jnp.mean(scaled_grad, axis=-1, keepdims=True)
        - normed * jnp.mean(scaled_grad * normed, axis=-1, keepdims=True)
    )


def feature_logits(entries, omega_local):
    factor = HEAD ** (-0.25)
    wide = entries.astype(jnp.float32)
    inverse = lax.rsqrt(jnp.mean(wide * wide, axis=-1, keepdims=True) + UNIT_EPS)
    unit = wide * inverse
    projected = jnp.einsum(
        "rhe,hem->hmr",
        unit,
        omega_local.astype(jnp.float32),
        precision=lax.Precision.HIGHEST,
        preferred_element_type=jnp.float32,
    )
    squares = jnp.sum(unit * unit, axis=-1)
    return (factor * projected - 0.5 * factor * factor * squares.T[:, None, :], unit, inverse)


def feature_back(grad_phi, logits, unit, inverse, omega_local):
    factor = HEAD ** (-0.25)
    grad_logits = (grad_phi * (jnp.exp(logits) * M ** (-0.5))).astype(jnp.bfloat16)
    projected = jnp.einsum(
        "hmr,hem->rhe", grad_logits, omega_local, preferred_element_type=jnp.float32
    )
    totals = jnp.sum(grad_logits.astype(jnp.float32), axis=1)
    grad_unit = factor * projected - factor * factor * totals.T[:, :, None] * unit
    return inverse * (grad_unit - unit * jnp.mean(grad_unit * unit, axis=-1, keepdims=True))


def window_begin(row_start, col_start, extent, rows_total):
    return row_start - col_start + rows_total - extent + 1


def block_coeff(rpe_exp, window_start, extent):
    window = lax.dynamic_slice_in_dim(rpe_exp, window_start, 2 * extent - 1, 1)
    return toeplitz_block(window, extent)


def local(
    tokens,
    qkv_weight,
    qkv_bias,
    out_weight,
    norm_gains,
    row_biases,
    up_weight,
    up_bias,
    down_weight,
    rpe_bias,
    omega,
    bucket,
    cotangent,
):
    qkv_full, out_full, up_full, down_full, gains_all, biases_all, bias_qkv, bias_up, rpe_all = (
        lax.all_gather(qkv_weight, ("dp", "feat"), axis=0, tiled=True),
        lax.all_gather(out_weight, ("dp", "feat"), axis=1, tiled=True),
        lax.all_gather(up_weight, ("dp", "feat"), axis=0, tiled=True),
        lax.all_gather(down_weight, ("dp", "feat"), axis=1, tiled=True),
        lax.all_gather(norm_gains, ("dp", "feat"), axis=1, tiled=True),
        lax.all_gather(row_biases, ("dp", "feat"), axis=1, tiled=True),
        lax.all_gather(qkv_bias, ("dp", "feat"), axis=2, tiled=True),
        lax.all_gather(up_bias, ("dp", "feat"), axis=1, tiled=True),
        lax.all_gather(rpe_bias, ("dp", "feat"), axis=1, tiled=True),
    )
    model_width = qkv_full.shape[0]
    head_cols = qkv_full.shape[2]
    local_heads = omega.shape[0]
    local_feats = omega.shape[2]
    rows_own = tokens.shape[0]
    rows_total = rows_own * lax.axis_size("feat")
    block_rows = min(512, rows_total // 4)
    blocks = rows_total // block_rows
    seq_length = rows_total // 4 * jnp.where(bucket[0] == 0, 1, jnp.where(bucket[0] == 1, 2, 4))
    block_count = seq_length // block_rows
    gain_rows = gains_all.astype(jnp.float32)
    bias_rows = biases_all.astype(jnp.float32)
    rpe_exp = jnp.exp(rpe_all.astype(jnp.float32))
    projected = jnp.dot(
        tokens, qkv_full.reshape(model_width, 3 * head_cols), preferred_element_type=jnp.float32
    )
    projected = projected + bias_qkv.reshape(-1).astype(jnp.float32)
    qkv_own = projected.astype(jnp.bfloat16)
    qkv_all = lax.all_gather(qkv_own, "feat", axis=0, tiled=True).reshape(
        rows_total, 3, local_heads, HEAD
    )
    queries = qkv_all[:, 0]
    keys_rows = qkv_all[:, 1]
    values_rows = qkv_all[:, 2]
    logits_query, unit_query, inverse_query = feature_logits(queries, omega)
    logits_key, unit_key, inverse_key = feature_logits(keys_rows, omega)
    feat_query = (jnp.exp(logits_query) * M ** (-0.5)).astype(jnp.bfloat16)
    feat_key = (jnp.exp(logits_key) * M ** (-0.5)).astype(jnp.bfloat16)
    numer_parts = []
    denom_parts = []
    for row_block in range(blocks):
        row_start = row_block * block_rows
        first_block = row_start // seq_length * block_count
        phi_rows = feat_query[:, :, row_start : row_start + block_rows]

        def visit(column_block, carried, phi_rows=phi_rows, row_start=row_start):
            numer_acc, denom_acc = carried
            col_start = column_block * block_rows
            phi_cols = lax.dynamic_slice_in_dim(feat_key, col_start, block_rows, 2)
            value_cols = lax.dynamic_slice_in_dim(values_rows, col_start, block_rows, 0)
            coefficient = block_coeff(
                rpe_exp, window_begin(row_start, col_start, block_rows, rows_total), block_rows
            )
            scores = jnp.einsum(
                "hmi,hmj->hij", phi_rows, phi_cols, preferred_element_type=jnp.float32
            )
            weights = (coefficient * scores).astype(jnp.bfloat16)
            numer_acc = numer_acc + jnp.einsum(
                "hij,jhe->ihe", weights, value_cols, preferred_element_type=jnp.float32
            )
            denom_acc = denom_acc + jnp.sum(weights.astype(jnp.float32), axis=-1)
            return (numer_acc, denom_acc)

        start_pair = (
            jnp.zeros((block_rows, local_heads, HEAD), jnp.float32),
            jnp.zeros((local_heads, block_rows), jnp.float32),
        )
        numer_block, denom_block = lax.fori_loop(
            first_block, first_block + block_count, visit, start_pair
        )
        numer_parts.append(numer_block)
        denom_parts.append(denom_block)
    numer_all = jnp.concatenate(numer_parts, axis=0).reshape(rows_total, head_cols)
    denom_all = jnp.concatenate(denom_parts, axis=1)
    numer_own, denom_own = (
        lax.psum_scatter(
            numer_all.astype(jnp.bfloat16), "feat", scatter_dimension=0, tiled=True
        ).astype(jnp.float32),
        lax.psum_scatter(
            denom_all.astype(jnp.bfloat16), "feat", scatter_dimension=1, tiled=True
        ).astype(jnp.float32),
    )
    denom_rows = denom_own.T
    quotient = numer_own.reshape(rows_own, local_heads, HEAD) / denom_rows[:, :, None]
    attn_low = quotient.reshape(rows_own, head_cols).astype(jnp.bfloat16)
    z_part = jnp.dot(attn_low, out_full, preferred_element_type=jnp.float32)
    mixed_z = lax.psum(z_part.astype(jnp.bfloat16), "heads").astype(jnp.float32) + bias_rows[0]
    first_out, normed_one, inverse_one = norm_forward(
        tokens.astype(jnp.float32) + mixed_z, gain_rows[0], bias_rows[1]
    )
    first_low = first_out.astype(jnp.bfloat16)
    pre_act = jnp.dot(first_low, up_full, preferred_element_type=jnp.float32) + bias_up.reshape(
        -1
    ).astype(jnp.float32)
    act_value, act_pull = jax.vjp(lambda inner: jax.nn.gelu(inner, approximate=False), pre_act)
    act_low = act_value.astype(jnp.bfloat16)
    ffn_part = jnp.dot(act_low, down_full, preferred_element_type=jnp.float32)
    ffn_out = lax.psum(ffn_part.astype(jnp.bfloat16), "heads").astype(jnp.float32) + bias_rows[2]
    final_rows, normed_two, inverse_two = norm_forward(
        first_out + ffn_out, gain_rows[1], bias_rows[3]
    )
    mixed = final_rows.astype(jnp.bfloat16)
    qkv_full, out_full, up_full, down_full, gains_all, rpe_all = (
        lax.all_gather(qkv_weight, ("dp", "feat"), axis=0, tiled=True),
        lax.all_gather(out_weight, ("dp", "feat"), axis=1, tiled=True),
        lax.all_gather(up_weight, ("dp", "feat"), axis=0, tiled=True),
        lax.all_gather(down_weight, ("dp", "feat"), axis=1, tiled=True),
        lax.all_gather(norm_gains, ("dp", "feat"), axis=1, tiled=True),
        lax.all_gather(rpe_bias, ("dp", "feat"), axis=1, tiled=True),
    )
    gain_rows = gains_all.astype(jnp.float32)
    rpe_exp = jnp.exp(rpe_all.astype(jnp.float32))
    upstream = cotangent.astype(jnp.float32)
    grad_gain_two = jnp.sum(upstream * normed_two, axis=0)
    grad_shift_two = jnp.sum(upstream, axis=0)
    resid_two = norm_backward(upstream, normed_two, inverse_two, gain_rows[1])
    resid_low = resid_two.astype(jnp.bfloat16)
    grad_bias_down = jnp.sum(resid_low.astype(jnp.float32), axis=0)
    grad_down = jnp.einsum("rf,rd->fd", act_low, resid_low, preferred_element_type=jnp.float32)
    grad_act = jnp.einsum("rd,fd->rf", resid_low, down_full, preferred_element_type=jnp.float32)
    grad_pre = act_pull(grad_act)[0].astype(jnp.bfloat16)
    grad_up = jnp.einsum("rd,rf->df", first_low, grad_pre, preferred_element_type=jnp.float32)
    grad_bias_up = jnp.sum(grad_pre.astype(jnp.float32), axis=0).reshape(bias_up.shape)
    first_back = lax.psum(
        jnp.einsum("rf,df->rd", grad_pre, up_full, preferred_element_type=jnp.float32).astype(
            jnp.bfloat16
        ),
        "heads",
    ).astype(jnp.float32)
    grad_first = resid_two + first_back
    grad_gain_one = jnp.sum(grad_first * normed_one, axis=0)
    grad_shift_one = jnp.sum(grad_first, axis=0)
    resid_one = norm_backward(grad_first, normed_one, inverse_one, gain_rows[0])
    resid_one_low = resid_one.astype(jnp.bfloat16)
    grad_bias_out = jnp.sum(resid_one_low.astype(jnp.float32), axis=0)
    grad_out = jnp.einsum("rc,rd->cd", attn_low, resid_one_low, preferred_element_type=jnp.float32)
    grad_attn = jnp.einsum(
        "rd,cd->rc", resid_one_low, out_full, preferred_element_type=jnp.float32
    ).reshape(rows_own, local_heads, HEAD)
    grad_numer = (grad_attn / denom_rows[:, :, None]).astype(jnp.bfloat16)
    grad_denom = (-jnp.sum(grad_attn * quotient, axis=-1) / denom_rows).astype(jnp.bfloat16)
    numer_grad_all, denom_grad_all = (
        lax.all_gather(grad_numer.reshape(rows_own, head_cols), "feat", axis=0, tiled=True),
        lax.all_gather(grad_denom.T, "feat", axis=1, tiled=True),
    )
    numer_grad_all = numer_grad_all.reshape(rows_total, local_heads, HEAD)
    dphi_key = jnp.zeros((local_heads, local_feats, rows_total), jnp.float32)
    dvalues = jnp.zeros((rows_total, local_heads, HEAD), jnp.float32)
    grad_rpe = jnp.zeros(rpe_exp.shape, jnp.float32)
    dquery_parts = []
    for row_block in range(blocks):
        row_start = row_block * block_rows
        first_block = row_start // seq_length * block_count
        phi_rows = feat_query[:, :, row_start : row_start + block_rows]
        numer_rows = numer_grad_all[row_start : row_start + block_rows]
        denom_cols = denom_grad_all[:, row_start : row_start + block_rows].astype(jnp.float32)

        def visit_back(
            column_block,
            carried,
            phi_rows=phi_rows,
            row_start=row_start,
            numer_rows=numer_rows,
            denom_cols=denom_cols,
        ):
            dquery_acc, dkey_all, dvalue_all, drpe_all = carried
            col_start = column_block * block_rows
            phi_cols = lax.dynamic_slice_in_dim(feat_key, col_start, block_rows, 2)
            value_cols = lax.dynamic_slice_in_dim(values_rows, col_start, block_rows, 0)
            window_start = window_begin(row_start, col_start, block_rows, rows_total)
            coefficient = block_coeff(rpe_exp, window_start, block_rows)
            scores = jnp.einsum(
                "hmi,hmj->hij", phi_rows, phi_cols, preferred_element_type=jnp.float32
            )
            weights = (coefficient * scores).astype(jnp.bfloat16)
            grad_weights = (
                jnp.einsum(
                    "ihe,jhe->hij", numer_rows, value_cols, preferred_element_type=jnp.float32
                )
                + denom_cols[:, :, None]
            )
            dvalue_block = jnp.einsum(
                "hij,ihe->jhe", weights, numer_rows, preferred_element_type=jnp.float32
            )
            dvalue_all = lax.dynamic_update_slice_in_dim(
                dvalue_all,
                lax.dynamic_slice_in_dim(dvalue_all, col_start, block_rows, 0) + dvalue_block,
                col_start,
                0,
            )
            grad_scores = (grad_weights * coefficient).astype(jnp.bfloat16)
            diagonal = diagonal_sums(grad_weights * scores * coefficient, block_rows)
            drpe_all = lax.dynamic_update_slice_in_dim(
                drpe_all,
                lax.dynamic_slice_in_dim(drpe_all, window_start, 2 * block_rows - 1, 1) + diagonal,
                window_start,
                1,
            )
            dquery_acc = dquery_acc + jnp.einsum(
                "hij,hmj->hmi", grad_scores, phi_cols, preferred_element_type=jnp.float32
            )
            dkey_block = jnp.einsum(
                "hij,hmi->hmj", grad_scores, phi_rows, preferred_element_type=jnp.float32
            )
            dkey_all = lax.dynamic_update_slice_in_dim(
                dkey_all,
                lax.dynamic_slice_in_dim(dkey_all, col_start, block_rows, 2) + dkey_block,
                col_start,
                2,
            )
            return (dquery_acc, dkey_all, dvalue_all, drpe_all)

        start_state = (
            jnp.zeros((local_heads, local_feats, block_rows), jnp.float32),
            dphi_key,
            dvalues,
            grad_rpe,
        )
        dquery_block, dphi_key, dvalues, grad_rpe = lax.fori_loop(
            first_block, first_block + block_count, visit_back, start_state
        )
        dquery_parts.append(dquery_block)
    dphi_query = jnp.concatenate(dquery_parts, axis=2)
    grad_query = feature_back(dphi_query, logits_query, unit_query, inverse_query, omega)
    grad_key = feature_back(dphi_key, logits_key, unit_key, inverse_key, omega)
    grad_qkv_all = jnp.stack((grad_query, grad_key, dvalues), axis=1).reshape(
        rows_total, 3 * head_cols
    )
    grad_qkv_own = lax.psum_scatter(
        grad_qkv_all.astype(jnp.bfloat16), "feat", scatter_dimension=0, tiled=True
    )
    grad_bias_qkv = jnp.sum(grad_qkv_own.astype(jnp.float32), axis=0).reshape(bias_qkv.shape)
    grad_qkv_weight = jnp.einsum(
        "rd,rc->dc", tokens, grad_qkv_own, preferred_element_type=jnp.float32
    ).reshape(qkv_full.shape)
    input_terms = jnp.einsum(
        "rc,dc->rd",
        grad_qkv_own,
        qkv_full.reshape(model_width, 3 * head_cols),
        preferred_element_type=jnp.float32,
    )
    grad_tokens = resid_one + lax.psum(input_terms.astype(jnp.bfloat16), "heads").astype(
        jnp.float32
    )
    grad_gains = jnp.stack((grad_gain_one, grad_gain_two), axis=0)
    grad_shifts = jnp.stack((grad_bias_out, grad_shift_one, grad_bias_down, grad_shift_two), axis=0)
    (
        sent_qkv,
        sent_out,
        sent_up,
        sent_down,
        sent_gains,
        sent_shifts,
        sent_bias_qkv,
        sent_bias_up,
        sent_rpe,
    ) = (
        lax.psum_scatter(
            grad_qkv_weight.astype(jnp.bfloat16), ("dp", "feat"), scatter_dimension=0, tiled=True
        ).astype(jnp.float32),
        lax.psum_scatter(
            grad_out.astype(jnp.bfloat16), ("dp", "feat"), scatter_dimension=1, tiled=True
        ).astype(jnp.float32),
        lax.psum_scatter(
            grad_up.astype(jnp.bfloat16), ("dp", "feat"), scatter_dimension=0, tiled=True
        ).astype(jnp.float32),
        lax.psum_scatter(
            grad_down.astype(jnp.bfloat16), ("dp", "feat"), scatter_dimension=1, tiled=True
        ).astype(jnp.float32),
        lax.psum_scatter(
            grad_gains.astype(jnp.bfloat16), ("dp", "feat"), scatter_dimension=1, tiled=True
        ).astype(jnp.float32),
        lax.psum_scatter(
            grad_shifts.astype(jnp.bfloat16), ("dp", "feat"), scatter_dimension=1, tiled=True
        ).astype(jnp.float32),
        lax.psum_scatter(
            grad_bias_qkv.astype(jnp.bfloat16), ("dp", "feat"), scatter_dimension=2, tiled=True
        ).astype(jnp.float32),
        lax.psum_scatter(
            grad_bias_up.astype(jnp.bfloat16), ("dp", "feat"), scatter_dimension=1, tiled=True
        ).astype(jnp.float32),
        lax.psum_scatter(
            grad_rpe.astype(jnp.bfloat16), ("dp", "feat"), scatter_dimension=1, tiled=True
        ).astype(jnp.float32),
    )
    return (
        mixed,
        grad_tokens,
        sent_qkv,
        sent_bias_qkv,
        sent_out,
        sent_gains,
        sent_shifts,
        sent_up,
        sent_bias_up,
        sent_down,
        sent_rpe,
    )


MESH = pl.DeviceIdType.MESH
PLANES = 4
SENDS, RECEIVES = 86, 214
F32 = jnp.float32
BF16 = jnp.bfloat16
SCALE = HEAD ** (-0.25)
NT = (((1,), (1,)), ((), ()))
TN = (((0,), (0,)), ((), ()))
NN = (((1,), (0,)), ((), ()))


def dot(left, right, dims=NN):
    return lax.dot_general(left, right, dims, preferred_element_type=F32)


def split_dot(left, right, dims=NN):
    high = left.astype(BF16)
    rest = (left - high.astype(F32)).astype(BF16)
    return dot(high, right, dims) + dot(rest, right, dims)


def iota(shape, axis):
    return lax.broadcasted_iota(jnp.int32, shape, axis)


class Sems:
    def __init__(self):
        self.used = 0

    def take(self, count=1):
        first = self.used
        self.used += count
        return first


def layer_kernel(
    tok, wq_h, qb_h, wo_h, gain_h, bias_h, wu_h, ub_h, wd_h, rpe_h, om_h, bk_h, cot,
    mixed_h, gtok_h, gq_h, gqb_h, go_h, ggain_h, gbias_h, gu_h, gub_h, gd_h, grpe_h,
    qb_v, gain_v, bias_v, ub_v, rpe_v, om_v, bk_v, small_s, om_s,
    mixed_o, gtok_o, gq_o, gqb_o, go_o, ggain_o, gbias_o, gu_o, gub_o, gd_o, grpe_o,
    wq, wo, wu, wd, small, om2, xg, cotb,
    qkv, phi, ex, unit, inv, r0, pp, num, den, quo, att, attf,
    pb, rb_f, rb_d, rb_i, fb, hid, dgel, efb, dub, dzb, acc,
    fst, n1, i1, dr, dat_s, dat, out_s, anti, ones64, rows_v,
    dn, dd, ds_, gg, dph, dvv, dqkv, xt,
    g_k, g_v, g_o, g_u, g_d, r_k, r_v, r_o, r_u, r_d, rz_k, rz_v, rz_o, rz_u, rz_d, cb_k, cb_v, cb_o, cb_u, cb_d,
    fs, xs_k, xs_v, xs_o, xs_u, xs_d, xr_k, xr_v, xr_o, xr_u, xr_d,
    sd, sd_r, st_a, st_b, work_a, work_b, recv_a, recv_b, swap, mix_s, gt_r,
    ss, rs, ls,
):
    dp, y, c = lax.axis_index("dp"), lax.axis_index("heads"), lax.axis_index("feat")
    z, x = dp // 2, dp % 2
    shard = 2 * dp + c

    def dev(zz, xx, yy, cc):
        return {"dp": zz * 2 + xx, "heads": yy, "feat": cc}

    sib, xn, yn, dg = dev(z, x, y, 1 - c), dev(z, 1 - x, y, c), dev(z, x, 1 - y, c), dev(z, 1 - x, 1 - y, c)
    xs_dev, ds_dev = dev(z, 1 - x, y, 1 - c), dev(z, 1 - x, 1 - y, 1 - c)

    barrier = pltpu.get_barrier_semaphore()
    for other in (sib, xn, yn, dg, xs_dev, ds_dev, dev(z, x, 1 - y, 1 - c)):
        pl.semaphore_signal(barrier, inc=1, device_id=other, device_id_type=MESH)
    for zz in range(PLANES):
        @pl.when(z != zz)
        def _(zz=zz):
            pl.semaphore_signal(barrier, inc=1, device_id=dev(zz, x, y, c), device_id_type=MESH)

    s_sems, r_sems, locals_ = Sems(), Sems(), Sems()
    pending = []

    def bring(src, dst, cond=None):
        copy = pltpu.make_async_copy(src, dst, ls.at[locals_.take()])
        if cond is None:
            copy.start()
            return copy.wait
        pl.when(cond)(copy.start)
        return lambda: pl.when(cond)(copy.wait)

    home = c == x
    away = c != x
    own_block = 2 * x + y

    def half_cols(half, width):
        return pl.ds(pl.multiple_of(half * width, width), width)

    def rows_of(index, count):
        return pl.ds(pl.multiple_of(index * count, count), count)

    in_o = bring(wo_h.at[:, half_cols(x, 256)], wo.at[own_block, 2 * z + x, c])
    in_q = bring(wq_h.at[:, :, half_cols(x, 256)], wq.at[:, 2 * z + x, c])
    in_small = [
        bring(src, dst)
        for src, dst in (
            (gain_h, gain_v), (bias_h, bias_v), (rpe_h, rpe_v), (qb_h, qb_v), (ub_h, ub_v), (om_h, om_v), (bk_h, bk_v),
        )
    ]
    in_tok = bring(tok, xg.at[rows_of(c, 256)], home)
    in_u = bring(wu_h.at[:, half_cols(x, 1024)], wu.at[2 * z + x, c])
    in_d = bring(wd_h.at[:, half_cols(x, 1024)], wd.at[2 * z + x, c])
    in_cot = bring(cot.at[rows_of(y, 128)], cotb, home)

    plane = (dg, xn, yn)
    plane_block = (2 * (1 - x) + 1 - y, 2 * (1 - x) + y, 2 * x + 1 - y)

    def rc(src, dst, s, r, device):
        return pltpu.make_async_remote_copy(
            src_ref=src, dst_ref=dst, send_sem=ss.at[s], recv_sem=rs.at[r], device_id=device, device_id_type=MESH
        )

    def send(src, dst, s, r, device, cond=None):
        def go():
            rc(src, dst, s, r, device).start()

        def done():
            rc(src, dst, s, r, device).wait_send()

        if cond is None:
            go()
            pending.append(done)
        else:
            pl.when(cond)(go)
            pending.append(lambda: pl.when(cond)(done))

    def got(dst, r):
        rc(dst, dst, r, r, sib).wait_recv()

    def take(count=1):
        return s_sems.take(count), r_sems.take(count)

    def give(src, dst, pair, device, cond=None, s=0, r=0):
        send(src, dst, pair[0] + s, pair[1] + r, device, cond)

    def valid(dz):
        return jnp.logical_and(z + dz >= 0, z + dz < PLANES)

    def by_plane(table):
        found = []
        for k in range(PLANES):
            block = jnp.int32(table[0][k])
            for zz in range(1, PLANES):
                block = jnp.where(z == zz, table[zz][k], block)
            found.append(block)
        return found

    arrive = by_plane(((0, 1, 2, 3), (1, 2, 3, 0), (2, 1, 0, 3), (3, 2, 1, 0)))
    leave = by_plane(((3, 2, 1, 0), (0, 3, 2, 1), (3, 0, 1, 2), (0, 1, 2, 3)))

    def at_step(blocks, k):
        block = blocks[0]
        for i in range(1, PLANES):
            block = jnp.where(k == i, blocks[i], block)
        return block

    def cols256(n):
        return pl.ds(pl.multiple_of(n * 256, 256), 256)

    pl.semaphore_wait(barrier, 10)

    inner, outer = (z == 1) | (z == 2), (z == 0) | (z == 3)

    class Item:
        def __init__(self, ref, kind):
            self.ref, self.kind = ref, kind
            self.z_out, self.c_out = s_sems.take(), s_sems.take()
            self.zs, self.sb = r_sems.take(PLANES), r_sems.take(PLANES)

        def block(self, zz, cc):
            if self.kind == "both":
                return self.ref.at[pl.ds(2 * zz, 2), cc]
            at = 2 * zz + (x if self.kind == "own" else 1 - x)
            return self.ref.at[:, at, cc] if len(self.ref.shape) == 5 else self.ref.at[at, cc]

        def some(self, count):
            if self.kind == "both":
                return self.ref.at[pl.ds(0, count)]
            return self.ref.at[:, pl.ds(0, count), 0] if len(self.ref.shape) == 5 else self.ref.at[pl.ds(0, count), 0]

        def onward(self, n, step):
            here = self.block(n, c)
            rc(here, here, self.z_out, self.zs + n, dev(z + step, x, y, c)).start()

        def start(self):
            pl.when(z == 0)(lambda: self.onward(z, 2))
            pl.when(z == 3)(lambda: self.onward(z, -2))
            pl.when(z > 0)(lambda: self.onward(z, -1))
            pl.when(z < PLANES - 1)(lambda: self.onward(z, 1))
            mine = self.block(z, c)
            rc(mine, mine, self.c_out, self.sb + z, sib).start()

        def pump_step(self, n):
            here = self.block(n, c)

            @pl.when(n != z)
            def _():
                got(here, self.zs + n)
                pl.when(jnp.logical_and(z == 1, n > z))(lambda: self.onward(n, -1))
                pl.when(jnp.logical_and(z == 2, n < z))(lambda: self.onward(n, 1))
                rc(here, here, self.c_out, self.sb + n, sib).start()

        def pump_done(self):
            def sent(sem, count):
                rc(self.some(count), self.some(count), sem, 0, sib).wait_send()

            pending.append(lambda: sent(self.c_out, 4))
            pending.append(lambda: pl.when(outer)(lambda: sent(self.z_out, 2)))
            pending.append(lambda: pl.when(inner)(lambda: sent(self.z_out, 4)))

        def pump(self, where):
            @pl.when(where)
            def _():
                for k in range(1, PLANES):
                    self.pump_step(arrive[k])

            if where is outer:
                self.pump_done()

        def need_step(self, n):
            got(self.block(n, 1 - c), self.sb + n)

        def need(self):
            for zz in range(PLANES):
                self.need_step(zz)

    half_of = {}

    def place(ref, xx):
        return ref.at[:, 2 * z + xx, c] if len(ref.shape) == 5 else ref.at[2 * z + xx, c]

    def give_half(name, src, ref):
        i = take()
        half_of[name] = (ref, i[1])
        give(src, place(ref, x), i, xn)

    def have_half(name):
        ref, i = half_of[name]
        got(place(ref, 1 - x), i)

    wo_own = wo.at[own_block]
    i_oh = take()
    give(wo_h.at[:, half_cols(1 - x, 256)], wo.at[2 * (1 - x) + y, 2 * z + x, c], i_oh, xn)
    give_half("q", wq_h.at[:, :, half_cols(1 - x, 256)], wq)
    i_tok, i_tx, i_ty = take(), take(2), take(2)
    give(tok, xg.at[rows_of(c, 256)], i_tok, sib, away)
    give(tok.at[rows_of(y, 128)], xg.at[rows_of(2 * c + y, 128)], i_tx, dev(z, 1 - x, y, x), None, 0, c)
    it_oa, it_ob = Item(wo_own, "own"), Item(wo_own, "other")
    it_qa, it_s, it_qb = Item(wq, "own"), Item(small, "both"), Item(wq, "other")
    it_ua, it_ub, it_da, it_db = Item(wu, "own"), Item(wu, "other"), Item(wd, "own"), Item(wd, "other")
    in_o()
    it_oa.start()
    in_q()
    it_qa.start()

    for done in in_small:
        done()

    def pick(shape, hit):
        return jnp.where(hit(iota(shape, 0), iota(shape, 1)), 1.0, 0.0)

    vec_sel = pick((64, 128), lambda k, l: l == c * 64 + k).astype(BF16)
    rpe_sel = pick((64, 128), lambda k, l: l == (1 - c) * 64 + 63 - k).astype(BF16)
    bias_sel = [pick((4, 128), lambda k, l, par=par: l == par * 64 + 4 * shard + k).astype(BF16) for par in range(2)]
    rpe_rows = dot(rpe_v[...], rpe_sel)
    level = jnp.full((1, 128), bk_v[0].astype(F32))
    top = jnp.concatenate(
        [dot(gain_v[...], vec_sel), dot(bias_v[...], vec_sel), level, jnp.zeros((1, 128), F32)], axis=0
    )

    def spread(values):
        rows = values.shape[1]
        even = (iota((rows, 1), 0) % 2) == 0
        wide = jnp.where(even, dot(values, bias_sel[0], TN), dot(values, bias_sel[1], TN))
        return dot(pick((rows // 2, rows), lambda k, l: l // 2 == k).astype(BF16), wide.astype(BF16))

    up_rows = spread(ub_v[...])
    qkv_rows = [spread(qb_v[p]) for p in range(3)]
    for half in range(2):
        mine = [rows[2 * half : 2 * half + 2] for rows in qkv_rows] + [jnp.zeros((2, 128), F32)]
        position = jnp.concatenate([rpe_rows[4 * half : 4 * half + 4], jnp.zeros((4, 128), F32)], axis=0)
        small_s[half] = jnp.concatenate(
            [top, position] + mine + [up_rows[8 * half : 8 * half + 8]], axis=0
        ).astype(BF16)
    small[2 * z + x, c] = small_s[x]
    give_half("s", small_s.at[1 - x], small)
    for h in range(4):
        sel = pick((32, 256), lambda k, l: l == h * 64 + c * 32 + k).astype(BF16)
        om_s[h * 64 : (h + 1) * 64] = dot(om_v[4 * x + h], sel, TN).astype(BF16)
    i_om = take()
    give(om_s, om2, i_om, sib)
    give_half("u", wu_h.at[:, half_cols(1 - x, 1024)], wu)

    same = (iota((256, 256), 0) // HEAD) == (iota((256, 256), 1) // HEAD)
    ones64[...] = jnp.where(same, 1.0, 0.0).astype(BF16)
    anti[...] = jnp.where(iota((128, 128), 0) + iota((128, 128), 1) == 127, 1.0, 0.0).astype(BF16)

    it_oa.pump(inner)
    got(wo.at[own_block, 2 * z + 1 - x, c], i_oh[1])
    it_ob.start()
    have_half("q")
    it_qb.start()
    it_qa.pump(inner)
    it_ob.pump(inner)
    it_qb.pump(inner)

    @pl.when(away)
    def _():
        for f in range(2):
            got(xg.at[rows_of(2 * f + y, 128)], i_tx[1] + f)

    for f in range(2):
        part = xg.at[rows_of(2 * f + y, 128)]
        give(part, part, i_ty, yn, away, f, f)
    it_oa.pump(outer)
    it_ob.pump(outer)
    i_oq, i_os = take(3), take(3)
    quarter = wo.at[own_block, :, c]
    give(quarter, quarter, i_oq, yn, None, 2, 2)
    give(quarter, quarter, i_oq, xn, None, 1, 1)
    give_half("d", wd_h.at[:, half_cols(1 - x, 1024)], wd)
    have_half("s")
    it_s.start()
    in_u()
    it_ua.start()
    it_s.pump(inner)
    it_qa.pump(outer)
    have_half("u")
    it_ub.start()
    in_d()
    it_da.start()
    it_qb.pump(outer)

    def other_quarter(slot):
        part = wo.at[plane_block[slot], :, c]
        got(part, i_oq[1] + slot)
        give(part, part, i_os, sib, None, slot, slot)
        return part

    it_s.pump(outer)

    it_s.need()
    for t in range(8):
        tile = small[t, 0].astype(F32) + small[t, 1].astype(F32)
        rows_v[0:8, t * 128 : (t + 1) * 128] = tile[0:8]
        rows_v[8:16, (7 - t) * 128 : (8 - t) * 128] = tile[8:16]
        total = tile[16:32] if t == 0 else total + tile[16:32]
    for r in range(6):
        rows_v[16:17, r * 128 : (r + 1) * 128] = total[r : r + 1]
    for r in range(8):
        rows_v[17:18, r * 128 : (r + 1) * 128] = total[8 + r : 9 + r]
    level = small[2 * z + c, 0][6:7].astype(F32)
    wide1 = jnp.where(level > 0.5, 1.0, 0.0)
    wide2 = jnp.where(level > 1.5, 1.0, 0.0)
    one_row = jnp.ones((1, 128), F32)

    def mask_row(bi):
        parts = [one_row if bj == bi else (wide1 if bj // 2 == bi // 2 else wide2) for bj in range(4)]
        return jnp.concatenate(parts, axis=1)

    masks = [mask_row(bi) for bi in range(4)]

    def coeff_body(h, carry):
        row = jnp.exp(rows_v[pl.ds(8 + h, 1), :])
        r0[h] = pltpu.roll(jnp.broadcast_to(row, (128, 1024)), 1, 1, stride=1, stride_axis=0)
        return carry

    lax.fori_loop(0, 4, coeff_body, 0)
    num[...] = jnp.zeros_like(num)
    den[...] = jnp.zeros_like(den)

    in_tok()
    pl.when(home)(lambda: got(xg.at[rows_of(1 - c, 256)], i_tok[1]))

    @pl.when(away)
    def _():
        for f in range(2):
            got(xg.at[rows_of(2 * f + 1 - y, 128)], i_ty[1] + f)

    other_quarter(2)
    part = other_quarter(1)
    give(part, part, i_oq, yn, None, 0, 0)
    it_ua.pump(inner)
    it_qa.need()
    it_qb.need()

    def qkv_body(p, carry):
        qkv[p] = (dot(xg[...], wq[p].reshape(1024, 256)) + rows_v[16:17, cols256(p)]).astype(BF16)
        return carry

    lax.fori_loop(0, 3, qkv_body, 0)
    got(om2, i_om[1])
    om2[...] = om2[...] + om_s[...]

    def feature_body(t, carry):
        wide = qkv[t].astype(F32)
        sums = split_dot(wide * wide, ones64[...])
        inverse = lax.rsqrt(sums * (1.0 / HEAD) + UNIT_EPS)
        units = wide * inverse
        logits = SCALE * split_dot(units, om2[...]) - 0.5 * SCALE * SCALE * (sums * inverse * inverse)
        value = jnp.exp(logits) * M ** (-0.5)
        ex[t] = value
        unit[t] = units
        inv[t] = inverse
        phi[t] = value.astype(BF16)
        return carry

    lax.fori_loop(0, 2, feature_body, 0)
    lane_head = iota((1, 128), 1) // HEAD

    def head_cols(h):
        return pl.ds(pl.multiple_of((h // 2) * 128, 128), 128), (lane_head == h % 2)

    def head_body(h, carry):
        cols, mine = head_cols(h)
        keep = jnp.where(mine, 1.0, 0.0).astype(BF16)
        scores = dot(phi[0, :, cols] * keep, phi[1, :, cols], NT)
        for b in range(4):
            coefficient = r0[h, :, 512 - 128 * b : 1024 - 128 * b] * masks[b]
            pp[h, b * 128 : (b + 1) * 128] = (scores[b * 128 : (b + 1) * 128] * coefficient).astype(BF16)
        right = jnp.concatenate([qkv[2, :, cols] * keep, jnp.broadcast_to(keep, (512, 128))], axis=1)
        both = dot(pp[h], right)
        num[:, cols] += both[:, :128]
        den[:, cols] += both[:, 128:]
        return carry

    i_at = [take(3), take(3)]

    def tile_of(ref, block, t):
        return ref.at[block, :, t * 128 : (t + 1) * 128]

    for t in range(2):
        lax.fori_loop(2 * t, 2 * t + 2, head_body, 0)
        cols = slice(t * 128, (t + 1) * 128)
        quo[:, cols] = num[:, cols] / den[:, cols]
        att[:, :, cols] = quo[:, cols].astype(BF16).reshape(4, 128, 128)
        for slot in range(3):
            give(tile_of(att, plane_block[slot], t), tile_of(attf, own_block, t), i_at[t], plane[slot], None, slot, slot)
    have_half("d")
    it_db.start()
    i_cot = take()
    give(cot.at[rows_of(y, 128)], cotb, i_cot, xs_dev, away)
    it_ub.pump(inner)
    other_quarter(0)
    it_oa.need()
    it_ob.need()

    def out_part(rows, block):
        return dot(rows, wo[block].reshape(1024, 256), NT)

    mixed_z = out_part(att[own_block], own_block)
    for slot in (2, 1, 0):
        got(wo.at[plane_block[slot], :, 1 - c], i_os[1] + slot)
        for t in range(2):
            got(tile_of(attf, plane_block[slot], t), i_at[t][1] + slot)
        mixed_z = mixed_z + out_part(attf[plane_block[slot]], plane_block[slot])

    def norm(values):
        centred = values - jnp.mean(values, axis=-1, keepdims=True)
        inverse = lax.rsqrt(jnp.mean(centred * centred, axis=-1, keepdims=True) + EPSILON)
        return centred * inverse, inverse

    residual = mixed_z + xg[rows_of(own_block, 128)].astype(F32) + rows_v[2:3, :]
    normed, inverse = norm(residual)
    first = normed * rows_v[0:1, :] + rows_v[3:4, :]
    fb[own_block] = first.astype(BF16)

    class Scatter:
        def __init__(self, ref):
            self.ref, self.out, self.base = ref, s_sems.take(), r_sems.take(4)

        def part(self, n, value):
            cols = cols256(n)
            pb[:, :, cols] = value.astype(BF16).reshape(4, 128, 256)
            for slot in range(3):
                rc(
                    pb.at[plane_block[slot], :, cols], self.ref.at[slot, :, cols], self.out, self.base + n, plane[slot]
                ).start()

        def column(self, n):
            cols = slice(n * 256, (n + 1) * 256)
            got(self.ref.at[:, :, cols], self.base + n)
            value = pb[own_block, :, cols].astype(F32)
            for slot in range(3):
                value = value + self.ref[slot, :, cols].astype(F32)
            return value

        def total(self):
            return jnp.concatenate([self.column(n) for n in range(4)], axis=1)

        def sent(self):
            rc(self.ref, self.ref, self.out, 0, sib).wait_send()

    class Gather:
        def __init__(self, ref, order):
            self.ref, self.out, self.base, self.order = ref, s_sems.take(), r_sems.take(4), order
            pending.append(lambda: rc(ref.at[pl.ds(0, 3)], ref.at[pl.ds(0, 3)], self.out, 0, sib).wait_send())

        def start(self):
            for n in self.order:
                for slot in range(3):
                    mine = self.ref.at[own_block, :, cols256(n)]
                    rc(mine, mine, self.out, self.base + n, plane[slot]).start()

        def need(self, n):
            got(self.ref.at[pl.ds(0, 3), :, cols256(n)], self.base + n)

    class RelayGather:
        def __init__(self, ref, order):
            self.ref, self.out, self.base, self.order = ref, s_sems.take(), r_sems.take(12), order
            pending.append(lambda: rc(ref.at[pl.ds(0, 3)], ref.at[pl.ds(0, 3)], self.out, 0, sib).wait_send())

        def piece(self, slot, n):
            return self.ref.at[plane_block[slot], :, cols256(n)]

        def start(self):
            for n in self.order:
                mine = self.ref.at[own_block, :, cols256(n)]
                for slot in (1, 2):
                    rc(mine, mine, self.out, self.base + slot * 4 + n, plane[slot]).start()

        def pass_on(self, k):
            n, slot = self.order[k], 1 + k % 2
            part = self.piece(slot, n)
            got(part, self.base + slot * 4 + n)
            rc(part, part, self.out, self.base + n, plane[3 - slot]).start()

        def need(self, k):
            n, slot = self.order[k], 2 - k % 2
            got(self.piece(slot, n), self.base + slot * 4 + n)
            got(self.piece(0, n), self.base + n)

    g_first = RelayGather(fb, range(4))
    g_first.start()
    it_da.pump(inner)
    g_first.pass_on(0)
    it_db.pump(inner)
    for k in range(1, 4):
        g_first.pass_on(k)
    it_ua.pump(outer)
    it_ub.pump(outer)
    fst[...] = first
    n1[...] = normed
    i1[...] = jnp.broadcast_to(inverse, (128, 128))

    def d_cols(ref, m):
        return ref[:, :, cols256(m)].reshape(512, 256)

    acc[...] = jnp.zeros_like(acc)
    it_ua.need()
    it_ub.need()

    for k in range(4):
        g_first.need(k)
        left = d_cols(fb, k)
        if k == 2:
            it_da.pump(outer)

        def hidden_part(j, carry, k=k, left=left):
            cols = cols256(j)
            acc[:, cols] += dot(left, wu[2 * k : 2 * k + 2, :, :, cols].reshape(256, 256))
            return carry

        lax.fori_loop(0, 4, hidden_part, 0)

    def hidden_body(n, carry):
        cols = cols256(n)
        pre = acc[:, cols] + rows_v[17:18, cols]
        cdf = 0.5 * (1.0 + lax.erf(pre * 0.7071067811865476))
        hid[:, cols] = (pre * cdf).astype(BF16)
        dgel[:, cols] = cdf + pre * (0.3989422804014327 * jnp.exp(-0.5 * pre * pre))
        return carry

    lax.fori_loop(0, 4, hidden_body, 0)
    sc_f = Scatter(rb_f)

    def down_part(k, carry):
        n = at_step(arrive, k)
        pl.when(outer)(lambda: it_db.pump_step(n))
        it_da.need_step(n)
        it_db.need_step(n)
        sc_f.part(n, dot(hid[...], wd[pl.ds(2 * n, 2)].reshape(256, 1024), NT))
        return carry

    lax.fori_loop(0, 4, down_part, 0)
    it_db.pump_done()
    pl.when(away)(lambda: got(cotb, i_cot[1]))
    in_cot()
    upstream = cotb[...].astype(F32)

    def down(values):
        return jnp.sum(values, axis=0, keepdims=True)

    sd[5:6, :] = down(upstream)
    acc[...] = jnp.zeros_like(acc)
    second = fst[...] + sc_f.total() + rows_v[4:5, :]
    normed2, inverse2 = norm(second)

    def norm_back(upstream, normed, inverse, gain):
        scaled = upstream * gain
        mean = jnp.mean(scaled, axis=-1, keepdims=True)
        slope = jnp.mean(scaled * normed, axis=-1, keepdims=True)
        return inverse * (scaled - mean - normed * slope)

    err = norm_back(upstream, normed2, inverse2, rows_v[1:2, :])
    efb[own_block] = err.astype(BF16)
    g_ef = Gather(efb, leave)
    g_ef.start()
    mix_s[...] = (normed2 * rows_v[1:2, :] + rows_v[5:6, :]).astype(BF16)
    dr[...] = err
    sd[1:2, :] = down(upstream * normed2)
    sd[4:5, :] = down(err.astype(BF16).astype(F32))
    sc_f.sent()

    class Owner:
        def __init__(self, dst, pieces):
            self.dst, self.width = dst, 1024 // pieces
            self.ids = [take(2) for _ in range(pieces)]

        def part(self, half, n):
            return self.dst.at[rows_of(half, 128), n * self.width : (n + 1) * self.width]

        def start(self, src, n):
            cols = slice(n * self.width, (n + 1) * self.width)

            @pl.when(home)
            def _():
                self.dst[rows_of(y, 128), cols] = src[:, cols]

            give(src.at[:, cols], self.part(y, n), self.ids[n], yn, home, 1, 1)
            give(src.at[:, cols], self.part(y, n), self.ids[n], xs_dev, away, 0, 0)

        def pass_on(self, n):
            part = self.part(y, n)
            pl.when(away)(lambda: got(part, self.ids[n][1]))
            give(part, part, self.ids[n], yn, away, 1, 1)

        def need(self, n):
            got(self.part(1 - y, n), self.ids[n][1] + 1)

    own_mix = Owner(mixed_o, 1)
    own_mix.start(mix_s, 0)

    class Grad:
        def __init__(self, g, r, rz, cb, xs, xr, first):
            self.first = first
            self.g, self.r, self.rz, self.cb, self.xs, self.xr = g, r, rz, cb, xs, xr
            self.d, self.z, self.k, self.x = r_sems.take(4), r_sems.take(PLANES), r_sems.take(2), take()
            self.d_out, self.z_out = s_sems.take(), s_sems.take()
            self.width = r.shape[-1]

        def give(self, m):
            rc(self.g.at[m, :, 1 - c], self.r.at[m], self.d_out, self.d + m, sib).start()

        def pair_step(self, m):
            got(self.r.at[m], self.d + m)
            self.r[m] = (self.g[m, :, c].astype(F32) + self.r[m].astype(F32)).astype(BF16)
            far = jnp.abs(m - z)
            part = self.r.at[m]
            beside = dev(jnp.where(z == 0, 1, jnp.where(z == 1, 0, jnp.where(z == 2, 3, 2))), x, y, c)

            @pl.when(jnp.logical_or(outer if self.first else False, m == jnp.where(z == 1, 0, 3)) & (far == 1))
            def _():
                rc(part, self.rz.at[z], self.z_out, self.z + z, beside).start()

            for slot in range(2):
                @pl.when(outer & (far == 3 - slot))
                def _(slot=slot):
                    rc(part, self.cb.at[slot], self.z_out, self.k + slot, beside).start()

        def near(self):
            for at, m in ((0, 1), (3, 2)):
                @pl.when(z == at)
                def _(at=at, m=m):
                    rc(self.r.at[m], self.rz.at[at], self.z_out, self.z + at, dev(m, x, y, c)).start()

        def relay(self):
            for at, blocks in ((1, (3, 2)), (2, (0, 1))):
                @pl.when(z == at)
                def _(at=at, blocks=blocks):
                    for slot, m in enumerate(blocks):
                        got(self.cb.at[slot], self.k + slot)
                        self.r[m] = (self.r[m].astype(F32) + self.cb[slot].astype(F32)).astype(BF16)
                        rc(self.r.at[m], self.rz.at[at], self.z_out, self.z + at, dev(m, x, y, c)).start()

        def run(self, make):
            def body(k, carry):
                m = at_step(leave, k)
                make(m)
                self.give(m)
                pl.when(k > 0)(lambda: self.pair_step(at_step(leave, k - 1)))
                return carry

            lax.fori_loop(0, PLANES, body, 0)
            self.pair_step(leave[3])

        def finish(self):
            total = fs.at[:, :, 0 : self.width]
            total[...] = self.r[z].astype(F32)
            for dz in (1, -1, 2, -2):
                @pl.when(valid(dz) if abs(dz) == 1 else z == (0 if dz > 0 else 3))
                def _(dz=dz):
                    got(self.rz.at[z + dz], self.z + z + dz)
                    total[...] += self.rz[z + dz].astype(F32)
            self.xs[...] = fs[1 - x, :, 0 : self.width].astype(BF16)
            give(self.xs, self.xr, self.x, xn)

        def sent(self):
            rc(self.r, self.r, self.d_out, 0, sib).wait_send()
            part = self.r.at[pl.ds(0, 3)]
            rc(part, part, self.z_out, 0, sib).wait_send()

        def columns(self, out, half, value, at=0):
            if len(out.shape) == 3:
                for p in range(self.width // 256):
                    out[at + p, :, half_cols(half, 256)] = value[:, p * 256 : (p + 1) * 256]
            else:
                out[:, half_cols(half, self.width)] = value

        def write_own(self, out, at=0):
            self.columns(out, x, fs[x, :, 0 : self.width], at)

        def write_other(self, out, at=0):
            got(self.xr, self.x[1])
            self.columns(out, 1 - x, self.xr[...].astype(F32), at)

    gr_d = Grad(g_d, r_d, rz_d, cb_d, xs_d, xr_d, True)
    gr_u = Grad(g_u, r_u, rz_u, cb_u, xs_u, xr_u, True)
    gr_o = Grad(g_o, r_o, rz_o, cb_o, xs_o, xr_o, False)
    gr_v = Grad(g_v, r_v, rz_v, cb_v, xs_v, xr_v, False)
    gr_k = Grad(g_k, r_k, rz_k, cb_k, xs_k, xr_k, False)

    def make_down(m):
        g_ef.need(m)
        left = d_cols(efb, m)
        g_d[m] = dot(left, hid[...], TN).astype(BF16).reshape(2, 2, 64, 1024)
        gr_d.give(m)
        for j in range(4):
            cols = slice(j * 256, (j + 1) * 256)
            acc[:, cols] += dot(left, wd[pl.ds(2 * m, 2), :, :, cols].reshape(256, 256))
        gr_d.pair_step(m)

    def down_grads(k, carry):
        make_down(at_step(leave, k))
        return carry

    lax.fori_loop(0, PLANES, down_grads, 0)
    def du_body(n, carry):
        cols = cols256(n)
        du = (acc[:, cols] * dgel[:, cols]).astype(BF16)
        dub[:, cols] = du
        for zz in range(PLANES):
            st_b[zz, pl.ds(8 + n, 1), :] = down(du.astype(F32))
        return carry

    lax.fori_loop(0, 4, du_body, 0)
    sc_d = Scatter(rb_d)

    def back_part(n, carry):
        sc_d.part(n, dot(dub[...], wu[pl.ds(2 * n, 2)].reshape(256, 1024), NT))
        return carry

    lax.fori_loop(0, 4, back_part, 0)
    own_mix.pass_on(0)
    for m in range(4):
        xt[m * 256 : (m + 1) * 256] = xg[:, m * 256 : (m + 1) * 256].T

    def make_up(m):
        g_u[m] = dot(d_cols(fb, m), dub[...], TN).astype(BF16).reshape(2, 2, 64, 1024)

    gr_d.relay()
    gr_u.run(make_up)
    dfirst = dr[...] + sc_d.total()
    back = norm_back(dfirst, n1[...], i1[:, 0:1], rows_v[0:1, :])
    dz = back.astype(BF16)
    dzb[own_block] = dz

    i_da = take(3)

    def attention_grad(block):
        dat_s[block] = dot(dz, wo[block].reshape(1024, 256)).astype(BF16)

    for slot in range(3):
        attention_grad(plane_block[slot])
        give(dat_s.at[plane_block[slot]], dat.at[own_block], i_da, plane[slot], None, slot, slot)
    attention_grad(own_block)
    dat[own_block] = dat_s[own_block]
    g_dz = RelayGather(dzb, leave)
    g_dz.start()
    sd[0:1, :] = down(dfirst * n1[...])
    sd[3:4, :] = down(dfirst)
    sd[2:3, :] = down(dz.astype(F32))
    sd[6:8, :] = jnp.zeros((2, 1024), F32)
    class Total:
        def __init__(self, ref, work, recv):
            self.ref, self.work, self.recv = ref, work, recv
            self.c, self.z = take(), take(PLANES)

        def pair(self):
            give(self.ref, self.work, self.c, sib)

        def over_planes(self):
            got(self.work, self.c[1])
            self.work[...] = self.ref[...] + self.work[...]
            for zz in range(PLANES):
                give(self.work.at[zz], self.recv.at[z], self.z, dev(zz, x, y, c), z != zz, zz, z)

        def finish(self):
            for zz in range(PLANES):
                @pl.when(z != zz)
                def _(zz=zz):
                    got(self.recv.at[zz], self.z[1] + zz)

                @pl.when(z == zz)
                def _(zz=zz):
                    self.recv[zz] = self.work[zz]
            return self.recv[0] + self.recv[1] + self.recv[2] + self.recv[3]

    early, late = Total(st_a, work_a, recv_a), Total(st_b, work_b, recv_b)
    i_swap = take()
    i_sd = take(3)
    for k, device in enumerate(plane):
        give(sd, sd_r.at[k], i_sd, device, None, k, k)
    dr[...] = back
    sc_d.sent()
    dph[...] = jnp.zeros_like(dph)
    dvv[...] = jnp.zeros_like(dvv)
    for slot in range(3):
        got(dat.at[plane_block[slot]], i_da[1] + slot)

    dattn = dat[...].reshape(512, 256).astype(F32)
    recip = 1.0 / den[...]
    dn[...] = (dattn * recip).astype(BF16)
    dsum = split_dot(dattn * quo[...], ones64[...])
    dd[...] = ((-dsum * recip).astype(BF16).astype(F32) * (1.0 / HEAD)).astype(BF16)

    def value_back(h, carry):
        cols, mine = head_cols(h)
        keep = jnp.where(mine, 1.0, 0.0).astype(BF16)
        dvv[:, cols] += dot(pp[h], dn[:, cols] * keep, TN)
        return carry

    lax.fori_loop(0, 4, value_back, 0)
    dqkv[2] = dvv[...].astype(BF16)

    def x_rows(m):
        return xt[rows_of(m, 256)]

    def make_v(m):
        g_v[m] = dot(x_rows(m), dqkv[2]).astype(BF16).reshape(2, 2, 64, 256)

    def head_back(h, carry):
        cols, mine = head_cols(h)
        keep = jnp.where(mine, 1.0, 0.0).astype(BF16)
        left = jnp.concatenate([dn[:, cols] * keep, dd[:, cols] * keep], axis=1)
        right = jnp.concatenate([qkv[2, :, cols], jnp.ones((512, 128), BF16)], axis=1)
        grad_p = dot(left, right, NT)
        for b in range(4):
            rows = slice(b * 128, (b + 1) * 128)
            coefficient = r0[h, :, 512 - 128 * b : 1024 - 128 * b] * masks[b]
            part = grad_p[rows]
            ds_[rows] = (part * coefficient).astype(BF16)
            gg[h, rows] = (part * pp[h, rows].astype(F32)).astype(BF16)
        dph[0, :, cols] += dot(ds_[...], phi[1, :, cols] * keep)
        dph[1, :, cols] += dot(ds_[...], phi[0, :, cols] * keep, TN)
        return carry

    g_dz.pass_on(0)
    lax.fori_loop(0, 4, head_back, 0)
    g_dz.pass_on(1)
    g_dz.pass_on(2)
    gr_v.run(make_v)
    g_dz.pass_on(3)
    gr_u.relay()

    def feature_back_body(t, carry):
        dlog = (dph[t] * ex[t]).astype(BF16)
        units = unit[t]
        dunit = SCALE * dot(dlog, om2[...], NT) - SCALE * SCALE * dot(dlog, ones64[...]) * units
        mean = split_dot(dunit * units, ones64[...]) * (1.0 / HEAD)
        dqkv[t] = (inv[t] * (dunit - units * mean)).astype(BF16)
        return carry

    lax.fori_loop(0, 2, feature_back_body, 0)
    class Return:
        def __init__(self, ref):
            self.ref, self.out, self.base, self.last = ref, s_sems.take(), r_sems.take(4), take(4)
            pending.append(lambda: pl.when(home)(lambda: rc(ref.at[0:3], ref.at[0:3], self.out, 0, sib).wait_send()))
            pending.append(lambda: pl.when(away)(lambda: rc(ref, ref, self.out, 0, sib).wait_send()))

        def part(self, n, value):
            cols = cols256(n)
            for b in range(4):
                rows = value[b * 128 : (b + 1) * 128]
                pb[b, :, cols] = jnp.where(own_block == b, rows + dr[:, cols], rows).astype(BF16)
                here = home & (c == b // 2) & (y == b % 2)

                @pl.when(here)
                def _(b=b):
                    self.ref[own_block, :, cols] = pb[b, :, cols]

                @pl.when(jnp.logical_not(here))
                def _(b=b):
                    there = self.ref.at[own_block, :, cols]
                    rc(pb.at[b, :, cols], there, self.out, self.base + n, dev(z, c, b % 2, b // 2)).start()

        def column(self, n):
            cols = slice(n * 256, (n + 1) * 256)
            pl.when(home)(lambda: got(self.ref.at[0:3, :, cols], self.base + n))
            pl.when(away)(lambda: got(self.ref.at[0:4, :, cols], self.base + n))
            value = self.ref[0, :, cols].astype(F32)
            for slot in range(1, 4):
                value = value + self.ref[slot, :, cols].astype(F32)
            mine = gt_r.at[rows_of(y, 128), cols]
            mine[...] = value.astype(BF16)
            give(mine, mine, self.last, yn, None, n, n)
            gtok_o[rows_of(y, 128), cols] = value

        def need(self, n):
            cols = slice(n * 256, (n + 1) * 256)
            rows = rows_of(1 - y, 128)
            got(gt_r.at[rows, cols], self.last[1] + n)
            gtok_o[rows, cols] = gt_r[rows, cols].astype(F32)

    sc_i = Return(rb_i)

    def input_part(n, carry):
        value = jnp.zeros((512, 256), F32)
        for p in range(3):
            value = value + dot(dqkv[p], wq[p, pl.ds(2 * n, 2)].reshape(256, 256), NT)
        sc_i.part(n, value)
        return carry

    lax.fori_loop(0, 4, input_part, 0)
    for k in range(3):
        got(sd_r.at[k], i_sd[1] + k)
    sums = sd[...] + sd_r[0] + sd_r[1] + sd_r[2]
    for zz in range(PLANES):
        st_a[zz] = sums[:, zz * 256 : (zz + 1) * 256]
    early.pair()
    gr_d.finish()
    gr_d.write_own(gd_o)

    def make_k(m):
        for p in range(2):
            g_k[m, :, :, :, p * 256 : (p + 1) * 256] = (
                dot(x_rows(m), dqkv[p]).astype(BF16).reshape(2, 2, 64, 256)
            )

    early.over_planes()
    gr_k.run(make_k)

    def diagonal_body(h, carry):
        sums = jnp.zeros((1, 1024), F32)
        for b in range(4):
            flipped = dot(anti[...], gg[h, (3 - b) * 128 : (4 - b) * 128])
            wide = jnp.concatenate([flipped, jnp.zeros((128, 128), F32)], axis=1)
            line = down(pltpu.roll(wide, 0, 1, stride=1, stride_axis=0))
            pieces = [line]
            if b > 0:
                pieces = [jnp.zeros((1, 128 * b), F32)] + pieces
            if b < 3:
                pieces = pieces + [jnp.zeros((1, 384 - 128 * b), F32)]
            sums = sums + jnp.concatenate(pieces, axis=1)
        for zz in range(PLANES):
            st_b[zz, pl.ds(h, 1), :] = sums[:, (3 - zz) * 256 : (4 - zz) * 256]
        return carry

    lax.fori_loop(0, 4, diagonal_body, 0)
    for p in range(3):
        line = down(dqkv[p].astype(F32))
        for zz in range(PLANES):
            st_b[zz, 12 + p : 13 + p, :] = line
    for zz in range(PLANES):
        st_b[zz, 4:8, :] = jnp.zeros((4, 256), F32)
        st_b[zz, 15:16, :] = jnp.zeros((1, 256), F32)
    late.pair()


    def make_out(m):
        g_o[m] = dot(d_cols(dzb, m), att[...].reshape(512, 256), TN).astype(BF16).reshape(2, 2, 64, 256)

    for k in range(4):
        g_dz.need(k)
    late.over_planes()
    gr_o.run(make_out)
    for gr in (gr_v, gr_k, gr_o):
        gr.near()
    outs = []
    own_mix.need(0)
    outs.append(bring(mixed_o, mixed_h))
    gr_v.relay()
    gr_u.finish()
    gr_u.write_own(gu_o)
    sc_i.column(0)
    sc_i.column(1)
    gr_k.relay()
    sc_i.column(2)
    sc_i.column(3)
    gr_d.write_other(gd_o)
    outs.append(bring(gd_o, gd_h))
    gr_o.relay()
    gr_v.finish()
    gr_v.write_own(gq_o, 2)
    gr_u.write_other(gu_o)
    outs.append(bring(gu_o, gu_h))

    def exact(left, right):
        return lax.dot_general(left, right, NN, precision=lax.Precision.HIGHEST, preferred_element_type=F32)

    sd_r[0, :, 0:256] = early.finish()
    mine = sd_r[0, :, pl.ds(pl.multiple_of(x * 128, 128), 128)]
    own = exact(mine, pick((128, 64), lambda k, l: k == c * 64 + l))
    ggain_o[...] = own[0:2]
    gbias_o[...] = own[2:6]
    outs.append(bring(ggain_o, ggain_h))
    outs.append(bring(gbias_o, gbias_h))
    swap[0] = late.finish()
    give(swap.at[0], swap.at[1], i_swap, xn)
    gr_k.finish()
    gr_k.write_own(gq_o)
    gr_o.finish()
    gr_o.write_own(go_o)
    for n in range(4):
        sc_i.need(n)
    outs.append(bring(gtok_o, gtok_h))
    got(swap.at[1], i_swap[1])
    tile = pl.ds(pl.multiple_of((1 - x) * 128, 128), 128)
    ours, theirs = swap[0, 0:4, tile], swap[1, 0:4, tile]
    lines = jnp.concatenate([jnp.where(x == 0, ours, theirs), jnp.where(x == 0, theirs, ours)], axis=0)
    grpe_o[...] = exact(lines, pick((128, 64), lambda k, l: k == (1 - c) * 64 + 63 - l))
    outs.append(bring(grpe_o, grpe_h))
    ours, theirs = swap[0, 8:16], swap[1, 8:16]
    rest = [jnp.where(x == half, ours, theirs) for half in range(2)]
    lines = [rest[half][4 + p : 5 + p, t * 128 : (t + 1) * 128] for p in range(3) for half in range(2) for t in range(2)]
    lines += [
        rest[half][t // 2 : t // 2 + 1, (t % 2) * 128 : (t % 2 + 1) * 128] for half in range(2) for t in range(8)
    ]
    lines = jnp.concatenate(lines + [jnp.zeros((4, 128), F32)], axis=0)
    found = jnp.zeros((4, 56), F32)
    for par in range(2):
        hit = pick((4, 128), lambda k, l: l == par * 64 + 4 * shard + k)
        values = lax.dot_general(hit, lines, NT, precision=lax.Precision.HIGHEST, preferred_element_type=F32)
        found = found + exact(values, pick((32, 56), lambda k, l: (l // 2 == k) & (l % 2 == par)))
    for p in range(3):
        gqb_o[p] = found[:, 8 * p : 8 * p + 8]
    gub_o[...] = found[:, 24:56]
    outs.append(bring(gqb_o, gqb_h))
    outs.append(bring(gub_o, gub_h))
    gr_v.write_other(gq_o, 2)
    gr_k.write_other(gq_o)
    outs.append(bring(gq_o, gq_h))
    gr_o.write_other(go_o)
    outs.append(bring(go_o, go_h))
    for gr in (gr_d, gr_u, gr_o, gr_v, gr_k):
        gr.sent()
    assert (s_sems.used, r_sems.used, locals_.used) == (SENDS, RECEIVES, 24), (s_sems.used, r_sems.used, locals_.used)
    for done in pending + outs:
        done()


def copy_kernel(*refs):
    count = len(refs) // 3
    sem = refs[-1]
    ins = [pltpu.make_async_copy(refs[i], refs[2 * count + i], sem.at[0, i]) for i in range(count)]
    outs = [pltpu.make_async_copy(refs[2 * count + i], refs[count + i], sem.at[1, i]) for i in range(count)]
    for copy in ins:
        copy.start()
    for one, two in zip(ins, outs):
        one.wait()
        two.start()
    for copy in outs:
        copy.wait()


def fast_local(
    tokens, qkv_weight, qkv_bias, out_weight, norm_gains, row_biases, up_weight, up_bias, down_weight, rpe_bias, omega,
    bucket, cotangent,
):
    def vm(shape, dtype=BF16):
        return pltpu.VMEM(shape, dtype)

    widths = (512, 256, 256, 1024, 1024)
    scratch = [vm((3, 4, 8)), vm((2, 64)), vm((4, 64)), vm((4, 32)), vm((8, 64)), vm((8, 32, 64))]
    scratch += [pltpu.SMEM((1,), jnp.int32), vm((2, 32, 128)), vm((256, 256))]
    results = (
        ((256, 1024), BF16), ((256, 1024), F32), ((3, 64, 512), F32), ((3, 4, 8), F32), ((64, 512), F32), ((2, 64), F32),
        ((4, 64), F32), ((64, 2048), F32), ((4, 32), F32), ((64, 2048), F32), ((8, 64), F32),
    )
    scratch += [vm(*result) for result in results]
    scratch += [vm((3, 8, 2, 64, 256)), vm((4, 8, 2, 64, 256)), vm((8, 2, 64, 1024)), vm((8, 2, 64, 1024))]
    scratch += [vm((8, 2, 32, 128)), vm((256, 256)), vm((512, 1024)), vm((128, 1024))]
    scratch += [vm((3, 512, 256)), vm((2, 512, 256))] + [vm((2, 512, 256), F32)] * 3
    scratch += [vm((4, 128, 1024), F32), vm((4, 512, 512))] + [vm((512, 256), F32)] * 3 + [vm((4, 128, 256))] * 2
    scratch += [vm((4, 128, 1024))] + [vm((3, 128, 1024))] * 2 + [vm((4, 128, 1024))]
    scratch += [vm((4, 128, 1024)), vm((512, 1024)), vm((512, 1024), F32)]
    scratch += [vm((4, 128, 1024)), vm((512, 1024)), vm((4, 128, 1024)), vm((512, 1024), F32)]
    scratch += [vm((128, 1024), F32)] * 2 + [vm((128, 128), F32), vm((128, 1024), F32)]
    scratch += [vm((4, 128, 256))] * 2 + [vm((16, 128)), vm((128, 128)), vm((256, 256)), vm((24, 1024), F32)]
    scratch += [vm((512, 256))] * 2 + [vm((512, 512)), vm((4, 512, 512)), vm((2, 512, 256), F32), vm((512, 256), F32)]
    scratch += [vm((3, 512, 256)), vm((1024, 512))]
    scratch += [vm((4, 2, 2, 64, n)) for n in widths]
    scratch += [vm((4, 2, 64, n)) for n in widths] * 2 + [vm((2, 2, 64, n)) for n in widths]
    scratch += [vm((2, 64, 1024), F32)] + [vm((64, n)) for n in widths] * 2
    scratch += [vm((8, 1024), F32), vm((3, 8, 1024), F32)] + [vm((4, 8, 256), F32), vm((4, 16, 256), F32)] * 3
    scratch += [vm((2, 16, 256), F32)]
    scratch += [vm((128, 1024)), vm((256, 1024))]
    scratch += [pltpu.SemaphoreType.DMA((SENDS,)), pltpu.SemaphoreType.DMA((RECEIVES,)), pltpu.SemaphoreType.DMA((24,))]

    shapes = tuple(jax.ShapeDtypeStruct(*result) for result in results)
    anywhere = pl.BlockSpec(memory_space=pl.ANY)
    made = pl.pallas_call(
        layer_kernel,
        out_shape=shapes,
        in_specs=[anywhere] * 13,
        out_specs=(anywhere,) * len(shapes),
        scratch_shapes=scratch,
        compiler_params=pltpu.CompilerParams(
            collective_id=0, has_side_effects=True, vmem_limit_bytes=63 * 2**20
        ),
        name="layer",
    )(
        tokens, qkv_weight.transpose(1, 0, 2), qkv_bias.transpose(0, 2, 1), out_weight.T, norm_gains, row_biases, up_weight,
        up_bias.T, down_weight.T, rpe_bias, omega.transpose(0, 2, 1), bucket, cotangent,
    )
    mixed, gtok, gq, gqb, go, ggain, gbias, gu, gub, gd, grpe = pl.pallas_call(
        copy_kernel,
        out_shape=shapes,
        in_specs=[anywhere] * len(shapes),
        out_specs=(anywhere,) * len(shapes),
        scratch_shapes=[vm(*result) for result in results] + [pltpu.SemaphoreType.DMA((2, len(shapes)))],
        compiler_params=pltpu.CompilerParams(vmem_limit_bytes=63 * 2**20),
        name="results",
    )(*made)
    return (
        mixed, gtok, gq.transpose(1, 0, 2), gqb.transpose(0, 2, 1), go.T, ggain, gbias, gu, gub.T, gd.T, grpe,
    )


def solution(mesh):
    sizes = (mesh.shape["dp"], mesh.shape["heads"], mesh.shape["feat"])
    return jax.shard_map(
        fast_local if sizes == (2 * PLANES, 2, 2) else local,
        mesh=mesh,
        in_specs=(
            P(("dp", "feat"), None),
            P(("dp", "feat"), None, "heads"),
            P(None, "heads", ("dp", "feat")),
            P("heads", ("dp", "feat")),
            P(None, ("dp", "feat")),
            P(None, ("dp", "feat")),
            P(("dp", "feat"), "heads"),
            P("heads", ("dp", "feat")),
            P("heads", ("dp", "feat")),
            P("heads", ("dp", "feat")),
            P("heads", None, "feat"),
            P("dp"),
            P(("dp", "feat"), None),
        ),
        out_specs=(
            P(("dp", "feat"), None),
            P(("dp", "feat"), None),
            P(("dp", "feat"), None, "heads"),
            P(None, "heads", ("dp", "feat")),
            P("heads", ("dp", "feat")),
            P(None, ("dp", "feat")),
            P(None, ("dp", "feat")),
            P(("dp", "feat"), "heads"),
            P("heads", ("dp", "feat")),
            P("heads", ("dp", "feat")),
            P("heads", ("dp", "feat")),
        ),
        check_vma=False,
    )
```

```python
import functools

import jax
import jax.numpy as jnp
from jax import lax
from jax.experimental import pallas as pl
from jax.experimental.pallas import tpu as pltpu
from jax.sharding import PartitionSpec as P

HEAD = 64
M = 64


EPSILON = 1e-12
UNIT_EPS = 1e-06


def toeplitz_block(window, extent):
    leading = window.shape[0]
    tiled_rows = jnp.broadcast_to(window[:, None, :], (leading, extent, 2 * extent - 1)).reshape(
        leading, -1
    )
    padded = jnp.pad(tiled_rows, ((0, 0), (0, extent)))
    sheared = padded.reshape(leading, extent, 2 * extent)[:, :, :extent]
    return sheared[:, :, ::-1]


def diagonal_sums(values_grid, extent):
    leading = values_grid.shape[0]
    flipped = values_grid[:, :, ::-1]
    padded = jnp.pad(flipped, ((0, 0), (0, 0), (0, extent))).reshape(leading, -1)
    sheared = padded[:, : extent * (2 * extent - 1)].reshape(leading, extent, 2 * extent - 1)
    return jnp.sum(sheared, axis=1)


def norm_forward(values, gain, shift):
    centred = values - jnp.mean(values, axis=-1, keepdims=True)
    inverse = lax.rsqrt(jnp.mean(centred * centred, axis=-1, keepdims=True) + EPSILON)
    normed = centred * inverse
    return (normed * gain + shift, normed, inverse)


def norm_backward(upstream, normed, inverse, gain):
    scaled_grad = upstream * gain
    return inverse * (
        scaled_grad
        - jnp.mean(scaled_grad, axis=-1, keepdims=True)
        - normed * jnp.mean(scaled_grad * normed, axis=-1, keepdims=True)
    )


def feature_logits(entries, omega_local):
    factor = HEAD ** (-0.25)
    wide = entries.astype(jnp.float32)
    inverse = lax.rsqrt(jnp.mean(wide * wide, axis=-1, keepdims=True) + UNIT_EPS)
    unit = wide * inverse
    projected = jnp.einsum(
        "rhe,hem->hmr",
        unit,
        omega_local.astype(jnp.float32),
        precision=lax.Precision.HIGHEST,
        preferred_element_type=jnp.float32,
    )
    squares = jnp.sum(unit * unit, axis=-1)
    return (factor * projected - 0.5 * factor * factor * squares.T[:, None, :], unit, inverse)


def feature_back(grad_phi, logits, unit, inverse, omega_local):
    factor = HEAD ** (-0.25)
    grad_logits = (grad_phi * (jnp.exp(logits) * M ** (-0.5))).astype(jnp.bfloat16)
    projected = jnp.einsum(
        "hmr,hem->rhe", grad_logits, omega_local, preferred_element_type=jnp.float32
    )
    totals = jnp.sum(grad_logits.astype(jnp.float32), axis=1)
    grad_unit = factor * projected - factor * factor * totals.T[:, :, None] * unit
    return inverse * (grad_unit - unit * jnp.mean(grad_unit * unit, axis=-1, keepdims=True))


def window_begin(row_start, col_start, extent, rows_total):
    return row_start - col_start + rows_total - extent + 1


def block_coeff(rpe_exp, window_start, extent):
    window = lax.dynamic_slice_in_dim(rpe_exp, window_start, 2 * extent - 1, 1)
    return toeplitz_block(window, extent)


def local(
    tokens,
    qkv_weight,
    qkv_bias,
    out_weight,
    norm_gains,
    row_biases,
    up_weight,
    up_bias,
    down_weight,
    rpe_bias,
    omega,
    bucket,
    cotangent,
):
    qkv_full, out_full, up_full, down_full, gains_all, biases_all, bias_qkv, bias_up, rpe_all = (
        lax.all_gather(qkv_weight, ("dp", "feat"), axis=0, tiled=True),
        lax.all_gather(out_weight, ("dp", "feat"), axis=1, tiled=True),
        lax.all_gather(up_weight, ("dp", "feat"), axis=0, tiled=True),
        lax.all_gather(down_weight, ("dp", "feat"), axis=1, tiled=True),
        lax.all_gather(norm_gains, ("dp", "feat"), axis=1, tiled=True),
        lax.all_gather(row_biases, ("dp", "feat"), axis=1, tiled=True),
        lax.all_gather(qkv_bias, ("dp", "feat"), axis=2, tiled=True),
        lax.all_gather(up_bias, ("dp", "feat"), axis=1, tiled=True),
        lax.all_gather(rpe_bias, ("dp", "feat"), axis=1, tiled=True),
    )
    model_width = qkv_full.shape[0]
    head_cols = qkv_full.shape[2]
    local_heads = omega.shape[0]
    local_feats = omega.shape[2]
    rows_own = tokens.shape[0]
    rows_total = rows_own * lax.axis_size("feat")
    block_rows = min(512, rows_total // 4)
    blocks = rows_total // block_rows
    seq_length = rows_total // 4 * jnp.where(bucket[0] == 0, 1, jnp.where(bucket[0] == 1, 2, 4))
    block_count = seq_length // block_rows
    gain_rows = gains_all.astype(jnp.float32)
    bias_rows = biases_all.astype(jnp.float32)
    rpe_exp = jnp.exp(rpe_all.astype(jnp.float32))
    projected = jnp.dot(
        tokens, qkv_full.reshape(model_width, 3 * head_cols), preferred_element_type=jnp.float32
    )
    projected = projected + bias_qkv.reshape(-1).astype(jnp.float32)
    qkv_own = projected.astype(jnp.bfloat16)
    qkv_all = lax.all_gather(qkv_own, "feat", axis=0, tiled=True).reshape(
        rows_total, 3, local_heads, HEAD
    )
    queries = qkv_all[:, 0]
    keys_rows = qkv_all[:, 1]
    values_rows = qkv_all[:, 2]
    logits_query, unit_query, inverse_query = feature_logits(queries, omega)
    logits_key, unit_key, inverse_key = feature_logits(keys_rows, omega)
    feat_query = (jnp.exp(logits_query) * M ** (-0.5)).astype(jnp.bfloat16)
    feat_key = (jnp.exp(logits_key) * M ** (-0.5)).astype(jnp.bfloat16)
    numer_parts = []
    denom_parts = []
    for row_block in range(blocks):
        row_start = row_block * block_rows
        first_block = row_start // seq_length * block_count
        phi_rows = feat_query[:, :, row_start : row_start + block_rows]

        def visit(column_block, carried, phi_rows=phi_rows, row_start=row_start):
            numer_acc, denom_acc = carried
            col_start = column_block * block_rows
            phi_cols = lax.dynamic_slice_in_dim(feat_key, col_start, block_rows, 2)
            value_cols = lax.dynamic_slice_in_dim(values_rows, col_start, block_rows, 0)
            coefficient = block_coeff(
                rpe_exp, window_begin(row_start, col_start, block_rows, rows_total), block_rows
            )
            scores = jnp.einsum(
                "hmi,hmj->hij", phi_rows, phi_cols, preferred_element_type=jnp.float32
            )
            weights = (coefficient * scores).astype(jnp.bfloat16)
            numer_acc = numer_acc + jnp.einsum(
                "hij,jhe->ihe", weights, value_cols, preferred_element_type=jnp.float32
            )
            denom_acc = denom_acc + jnp.sum(weights.astype(jnp.float32), axis=-1)
            return (numer_acc, denom_acc)

        start_pair = (
            jnp.zeros((block_rows, local_heads, HEAD), jnp.float32),
            jnp.zeros((local_heads, block_rows), jnp.float32),
        )
        numer_block, denom_block = lax.fori_loop(
            first_block, first_block + block_count, visit, start_pair
        )
        numer_parts.append(numer_block)
        denom_parts.append(denom_block)
    numer_all = jnp.concatenate(numer_parts, axis=0).reshape(rows_total, head_cols)
    denom_all = jnp.concatenate(denom_parts, axis=1)
    numer_own, denom_own = (
        lax.psum_scatter(
            numer_all.astype(jnp.bfloat16), "feat", scatter_dimension=0, tiled=True
        ).astype(jnp.float32),
        lax.psum_scatter(
            denom_all.astype(jnp.bfloat16), "feat", scatter_dimension=1, tiled=True
        ).astype(jnp.float32),
    )
    denom_rows = denom_own.T
    quotient = numer_own.reshape(rows_own, local_heads, HEAD) / denom_rows[:, :, None]
    attn_low = quotient.reshape(rows_own, head_cols).astype(jnp.bfloat16)
    z_part = jnp.dot(attn_low, out_full, preferred_element_type=jnp.float32)
    mixed_z = lax.psum(z_part.astype(jnp.bfloat16), "heads").astype(jnp.float32) + bias_rows[0]
    first_out, normed_one, inverse_one = norm_forward(
        tokens.astype(jnp.float32) + mixed_z, gain_rows[0], bias_rows[1]
    )
    first_low = first_out.astype(jnp.bfloat16)
    pre_act = jnp.dot(first_low, up_full, preferred_element_type=jnp.float32) + bias_up.reshape(
        -1
    ).astype(jnp.float32)
    act_value, act_pull = jax.vjp(lambda inner: jax.nn.gelu(inner, approximate=False), pre_act)
    act_low = act_value.astype(jnp.bfloat16)
    ffn_part = jnp.dot(act_low, down_full, preferred_element_type=jnp.float32)
    ffn_out = lax.psum(ffn_part.astype(jnp.bfloat16), "heads").astype(jnp.float32) + bias_rows[2]
    final_rows, normed_two, inverse_two = norm_forward(
        first_out + ffn_out, gain_rows[1], bias_rows[3]
    )
    mixed = final_rows.astype(jnp.bfloat16)
    qkv_full, out_full, up_full, down_full, gains_all, rpe_all = (
        lax.all_gather(qkv_weight, ("dp", "feat"), axis=0, tiled=True),
        lax.all_gather(out_weight, ("dp", "feat"), axis=1, tiled=True),
        lax.all_gather(up_weight, ("dp", "feat"), axis=0, tiled=True),
        lax.all_gather(down_weight, ("dp", "feat"), axis=1, tiled=True),
        lax.all_gather(norm_gains, ("dp", "feat"), axis=1, tiled=True),
        lax.all_gather(rpe_bias, ("dp", "feat"), axis=1, tiled=True),
    )
    gain_rows = gains_all.astype(jnp.float32)
    rpe_exp = jnp.exp(rpe_all.astype(jnp.float32))
    upstream = cotangent.astype(jnp.float32)
    grad_gain_two = jnp.sum(upstream * normed_two, axis=0)
    grad_shift_two = jnp.sum(upstream, axis=0)
    resid_two = norm_backward(upstream, normed_two, inverse_two, gain_rows[1])
    resid_low = resid_two.astype(jnp.bfloat16)
    grad_bias_down = jnp.sum(resid_low.astype(jnp.float32), axis=0)
    grad_down = jnp.einsum("rf,rd->fd", act_low, resid_low, preferred_element_type=jnp.float32)
    grad_act = jnp.einsum("rd,fd->rf", resid_low, down_full, preferred_element_type=jnp.float32)
    grad_pre = act_pull(grad_act)[0].astype(jnp.bfloat16)
    grad_up = jnp.einsum("rd,rf->df", first_low, grad_pre, preferred_element_type=jnp.float32)
    grad_bias_up = jnp.sum(grad_pre.astype(jnp.float32), axis=0).reshape(bias_up.shape)
    first_back = lax.psum(
        jnp.einsum("rf,df->rd", grad_pre, up_full, preferred_element_type=jnp.float32).astype(
            jnp.bfloat16
        ),
        "heads",
    ).astype(jnp.float32)
    grad_first = resid_two + first_back
    grad_gain_one = jnp.sum(grad_first * normed_one, axis=0)
    grad_shift_one = jnp.sum(grad_first, axis=0)
    resid_one = norm_backward(grad_first, normed_one, inverse_one, gain_rows[0])
    resid_one_low = resid_one.astype(jnp.bfloat16)
    grad_bias_out = jnp.sum(resid_one_low.astype(jnp.float32), axis=0)
    grad_out = jnp.einsum("rc,rd->cd", attn_low, resid_one_low, preferred_element_type=jnp.float32)
    grad_attn = jnp.einsum(
        "rd,cd->rc", resid_one_low, out_full, preferred_element_type=jnp.float32
    ).reshape(rows_own, local_heads, HEAD)
    grad_numer = (grad_attn / denom_rows[:, :, None]).astype(jnp.bfloat16)
    grad_denom = (-jnp.sum(grad_attn * quotient, axis=-1) / denom_rows).astype(jnp.bfloat16)
    numer_grad_all, denom_grad_all = (
        lax.all_gather(grad_numer.reshape(rows_own, head_cols), "feat", axis=0, tiled=True),
        lax.all_gather(grad_denom.T, "feat", axis=1, tiled=True),
    )
    numer_grad_all = numer_grad_all.reshape(rows_total, local_heads, HEAD)
    dphi_key = jnp.zeros((local_heads, local_feats, rows_total), jnp.float32)
    dvalues = jnp.zeros((rows_total, local_heads, HEAD), jnp.float32)
    grad_rpe = jnp.zeros(rpe_exp.shape, jnp.float32)
    dquery_parts = []
    for row_block in range(blocks):
        row_start = row_block * block_rows
        first_block = row_start // seq_length * block_count
        phi_rows = feat_query[:, :, row_start : row_start + block_rows]
        numer_rows = numer_grad_all[row_start : row_start + block_rows]
        denom_cols = denom_grad_all[:, row_start : row_start + block_rows].astype(jnp.float32)

        def visit_back(
            column_block,
            carried,
            phi_rows=phi_rows,
            row_start=row_start,
            numer_rows=numer_rows,
            denom_cols=denom_cols,
        ):
            dquery_acc, dkey_all, dvalue_all, drpe_all = carried
            col_start = column_block * block_rows
            phi_cols = lax.dynamic_slice_in_dim(feat_key, col_start, block_rows, 2)
            value_cols = lax.dynamic_slice_in_dim(values_rows, col_start, block_rows, 0)
            window_start = window_begin(row_start, col_start, block_rows, rows_total)
            coefficient = block_coeff(rpe_exp, window_start, block_rows)
            scores = jnp.einsum(
                "hmi,hmj->hij", phi_rows, phi_cols, preferred_element_type=jnp.float32
            )
            weights = (coefficient * scores).astype(jnp.bfloat16)
            grad_weights = (
                jnp.einsum(
                    "ihe,jhe->hij", numer_rows, value_cols, preferred_element_type=jnp.float32
                )
                + denom_cols[:, :, None]
            )
            dvalue_block = jnp.einsum(
                "hij,ihe->jhe", weights, numer_rows, preferred_element_type=jnp.float32
            )
            dvalue_all = lax.dynamic_update_slice_in_dim(
                dvalue_all,
                lax.dynamic_slice_in_dim(dvalue_all, col_start, block_rows, 0) + dvalue_block,
                col_start,
                0,
            )
            grad_scores = (grad_weights * coefficient).astype(jnp.bfloat16)
            diagonal = diagonal_sums(grad_weights * scores * coefficient, block_rows)
            drpe_all = lax.dynamic_update_slice_in_dim(
                drpe_all,
                lax.dynamic_slice_in_dim(drpe_all, window_start, 2 * block_rows - 1, 1) + diagonal,
                window_start,
                1,
            )
            dquery_acc = dquery_acc + jnp.einsum(
                "hij,hmj->hmi", grad_scores, phi_cols, preferred_element_type=jnp.float32
            )
            dkey_block = jnp.einsum(
                "hij,hmi->hmj", grad_scores, phi_rows, preferred_element_type=jnp.float32
            )
            dkey_all = lax.dynamic_update_slice_in_dim(
                dkey_all,
                lax.dynamic_slice_in_dim(dkey_all, col_start, block_rows, 2) + dkey_block,
                col_start,
                2,
            )
            return (dquery_acc, dkey_all, dvalue_all, drpe_all)

        start_state = (
            jnp.zeros((local_heads, local_feats, block_rows), jnp.float32),
            dphi_key,
            dvalues,
            grad_rpe,
        )
        dquery_block, dphi_key, dvalues, grad_rpe = lax.fori_loop(
            first_block, first_block + block_count, visit_back, start_state
        )
        dquery_parts.append(dquery_block)
    dphi_query = jnp.concatenate(dquery_parts, axis=2)
    grad_query = feature_back(dphi_query, logits_query, unit_query, inverse_query, omega)
    grad_key = feature_back(dphi_key, logits_key, unit_key, inverse_key, omega)
    grad_qkv_all = jnp.stack((grad_query, grad_key, dvalues), axis=1).reshape(
        rows_total, 3 * head_cols
    )
    grad_qkv_own = lax.psum_scatter(
        grad_qkv_all.astype(jnp.bfloat16), "feat", scatter_dimension=0, tiled=True
    )
    grad_bias_qkv = jnp.sum(grad_qkv_own.astype(jnp.float32), axis=0).reshape(bias_qkv.shape)
    grad_qkv_weight = jnp.einsum(
        "rd,rc->dc", tokens, grad_qkv_own, preferred_element_type=jnp.float32
    ).reshape(qkv_full.shape)
    input_terms = jnp.einsum(
        "rc,dc->rd",
        grad_qkv_own,
        qkv_full.reshape(model_width, 3 * head_cols),
        preferred_element_type=jnp.float32,
    )
    grad_tokens = resid_one + lax.psum(input_terms.astype(jnp.bfloat16), "heads").astype(
        jnp.float32
    )
    grad_gains = jnp.stack((grad_gain_one, grad_gain_two), axis=0)
    grad_shifts = jnp.stack((grad_bias_out, grad_shift_one, grad_bias_down, grad_shift_two), axis=0)
    (
        sent_qkv,
        sent_out,
        sent_up,
        sent_down,
        sent_gains,
        sent_shifts,
        sent_bias_qkv,
        sent_bias_up,
        sent_rpe,
    ) = (
        lax.psum_scatter(
            grad_qkv_weight.astype(jnp.bfloat16), ("dp", "feat"), scatter_dimension=0, tiled=True
        ).astype(jnp.float32),
        lax.psum_scatter(
            grad_out.astype(jnp.bfloat16), ("dp", "feat"), scatter_dimension=1, tiled=True
        ).astype(jnp.float32),
        lax.psum_scatter(
            grad_up.astype(jnp.bfloat16), ("dp", "feat"), scatter_dimension=0, tiled=True
        ).astype(jnp.float32),
        lax.psum_scatter(
            grad_down.astype(jnp.bfloat16), ("dp", "feat"), scatter_dimension=1, tiled=True
        ).astype(jnp.float32),
        lax.psum_scatter(
            grad_gains.astype(jnp.bfloat16), ("dp", "feat"), scatter_dimension=1, tiled=True
        ).astype(jnp.float32),
        lax.psum_scatter(
            grad_shifts.astype(jnp.bfloat16), ("dp", "feat"), scatter_dimension=1, tiled=True
        ).astype(jnp.float32),
        lax.psum_scatter(
            grad_bias_qkv.astype(jnp.bfloat16), ("dp", "feat"), scatter_dimension=2, tiled=True
        ).astype(jnp.float32),
        lax.psum_scatter(
            grad_bias_up.astype(jnp.bfloat16), ("dp", "feat"), scatter_dimension=1, tiled=True
        ).astype(jnp.float32),
        lax.psum_scatter(
            grad_rpe.astype(jnp.bfloat16), ("dp", "feat"), scatter_dimension=1, tiled=True
        ).astype(jnp.float32),
    )
    return (
        mixed,
        grad_tokens,
        sent_qkv,
        sent_bias_qkv,
        sent_out,
        sent_gains,
        sent_shifts,
        sent_up,
        sent_bias_up,
        sent_down,
        sent_rpe,
    )


MESH = pl.DeviceIdType.MESH
PLANES = 4
SENDS, RECEIVES = 86, 215
F32 = jnp.float32
BF16 = jnp.bfloat16
SCALE = HEAD ** (-0.25)
NT = (((1,), (1,)), ((), ()))
TN = (((0,), (0,)), ((), ()))
NN = (((1,), (0,)), ((), ()))


def dot(left, right, dims=NN):
    return lax.dot_general(left, right, dims, preferred_element_type=F32)


def split_dot(left, right, dims=NN):
    high = left.astype(BF16)
    rest = (left - high.astype(F32)).astype(BF16)
    return dot(high, right, dims) + dot(rest, right, dims)


def iota(shape, axis):
    return lax.broadcasted_iota(jnp.int32, shape, axis)


class Sems:
    def __init__(self):
        self.used = 0

    def take(self, count=1):
        first = self.used
        self.used += count
        return first


def layer_kernel(
    tok, wq_h, qb_h, wo_h, gain_h, bias_h, wu_h, ub_h, wd_h, rpe_h, om_h, bk_h, cot,
    mixed_h, gtok_h, gq_h, gqb_h, go_h, ggain_h, gbias_h, gu_h, gub_h, gd_h, grpe_h,
    qb_v, gain_v, bias_v, ub_v, rpe_v, om_v, bk_v, small_s, om_s,
    mixed_o, gtok_o, gq_o, gqb_o, go_o, ggain_o, gbias_o, gu_o, gub_o, gd_o, grpe_o,
    wq, wo, wu, wd, small, om2, xg, cotb,
    qkv, phi, ex, unit, inv, r0, pp, num, den, quo, att, attf,
    pb, rb_f, rb_d, rb_i, fb, hid, dgel, efb, dub, dzb, acc,
    fst, n1, i1, dr, dat_s, dat, out_s, anti, ones64, rows_v,
    dn, dd, ds_, gg, dph, dvv, dqkv, xt, ppt,
    g_k, g_v, g_o, g_u, g_d, r_k, r_v, r_o, r_u, r_d, rz_k, rz_v, rz_o, rz_u, rz_d, cb_k, cb_v, cb_o, cb_u, cb_d,
    fs, xs_k, xs_v, xs_o, xs_u, xs_d, xr_k, xr_v, xr_o, xr_u, xr_d,
    sd, sd_r, st_a, st_b, work_a, work_b, recv_a, recv_b, swap, mix_s, gt_r,
    ss, rs, ls,
):
    dp, y, c = lax.axis_index("dp"), lax.axis_index("heads"), lax.axis_index("feat")
    z, x = dp // 2, dp % 2
    shard = 2 * dp + c

    def dev(zz, xx, yy, cc):
        return {"dp": zz * 2 + xx, "heads": yy, "feat": cc}

    sib, xn, yn, dg = dev(z, x, y, 1 - c), dev(z, 1 - x, y, c), dev(z, x, 1 - y, c), dev(z, 1 - x, 1 - y, c)
    xs_dev, ds_dev = dev(z, 1 - x, y, 1 - c), dev(z, 1 - x, 1 - y, 1 - c)

    barrier = pltpu.get_barrier_semaphore()
    for other in (sib, xn, yn, dg, xs_dev, ds_dev, dev(z, x, 1 - y, 1 - c)):
        pl.semaphore_signal(barrier, inc=1, device_id=other, device_id_type=MESH)
    for zz in range(PLANES):
        @pl.when(z != zz)
        def _(zz=zz):
            pl.semaphore_signal(barrier, inc=1, device_id=dev(zz, x, y, c), device_id_type=MESH)

    s_sems, r_sems, locals_ = Sems(), Sems(), Sems()
    pending = []

    def bring(src, dst, cond=None):
        copy = pltpu.make_async_copy(src, dst, ls.at[locals_.take()])
        if cond is None:
            copy.start()
            return copy.wait
        pl.when(cond)(copy.start)
        return lambda: pl.when(cond)(copy.wait)

    home = c == x
    away = c != x
    own_block = 2 * x + y

    def half_cols(half, width):
        return pl.ds(pl.multiple_of(half * width, width), width)

    def rows_of(index, count):
        return pl.ds(pl.multiple_of(index * count, count), count)

    in_o = bring(wo_h.at[:, half_cols(x, 256)], wo.at[own_block, 2 * z + x, c])
    in_q = bring(wq_h.at[:, :, half_cols(x, 256)], wq.at[:, 2 * z + x, c])
    in_small = [
        bring(src, dst)
        for src, dst in (
            (gain_h, gain_v), (bias_h, bias_v), (rpe_h, rpe_v), (qb_h, qb_v), (ub_h, ub_v), (om_h, om_v), (bk_h, bk_v),
        )
    ]
    in_tok = bring(tok, xg.at[rows_of(c, 256)], home)
    in_u = bring(wu_h.at[:, half_cols(x, 1024)], wu.at[2 * z + x, c])
    in_d = bring(wd_h.at[:, half_cols(x, 1024)], wd.at[2 * z + x, c])
    in_cot = bring(cot.at[rows_of(y, 128)], cotb, home)

    plane = (dg, xn, yn)
    plane_block = (2 * (1 - x) + 1 - y, 2 * (1 - x) + y, 2 * x + 1 - y)

    def rc(src, dst, s, r, device):
        return pltpu.make_async_remote_copy(
            src_ref=src, dst_ref=dst, send_sem=ss.at[s], recv_sem=rs.at[r], device_id=device, device_id_type=MESH
        )

    def send(src, dst, s, r, device, cond=None):
        def go():
            rc(src, dst, s, r, device).start()

        def done():
            rc(src, dst, s, r, device).wait_send()

        if cond is None:
            go()
            pending.append(done)
        else:
            pl.when(cond)(go)
            pending.append(lambda: pl.when(cond)(done))

    def got(dst, r):
        rc(dst, dst, r, r, sib).wait_recv()

    def take(count=1):
        return s_sems.take(count), r_sems.take(count)

    def give(src, dst, pair, device, cond=None, s=0, r=0):
        send(src, dst, pair[0] + s, pair[1] + r, device, cond)

    def valid(dz):
        return jnp.logical_and(z + dz >= 0, z + dz < PLANES)

    def by_plane(table):
        found = []
        for k in range(PLANES):
            block = jnp.int32(table[0][k])
            for zz in range(1, PLANES):
                block = jnp.where(z == zz, table[zz][k], block)
            found.append(block)
        return found

    arrive = by_plane(((0, 1, 2, 3), (1, 2, 3, 0), (2, 1, 0, 3), (3, 2, 1, 0)))
    leave = by_plane(((3, 2, 1, 0), (0, 3, 2, 1), (3, 0, 1, 2), (0, 1, 2, 3)))

    def at_step(blocks, k):
        block = blocks[0]
        for i in range(1, PLANES):
            block = jnp.where(k == i, blocks[i], block)
        return block

    def cols256(n):
        return pl.ds(pl.multiple_of(n * 256, 256), 256)

    pl.semaphore_wait(barrier, 10)

    inner, outer = (z == 1) | (z == 2), (z == 0) | (z == 3)

    class Item:
        def __init__(self, ref, kind):
            self.ref, self.kind = ref, kind
            self.z_out, self.c_out = s_sems.take(), s_sems.take()
            self.zs, self.sb = r_sems.take(PLANES), r_sems.take(PLANES)

        def block(self, zz, cc):
            if self.kind == "both":
                return self.ref.at[pl.ds(2 * zz, 2), cc]
            at = 2 * zz + (x if self.kind == "own" else 1 - x)
            return self.ref.at[:, at, cc] if len(self.ref.shape) == 5 else self.ref.at[at, cc]

        def some(self, count):
            if self.kind == "both":
                return self.ref.at[pl.ds(0, count)]
            return self.ref.at[:, pl.ds(0, count), 0] if len(self.ref.shape) == 5 else self.ref.at[pl.ds(0, count), 0]

        def onward(self, n, step):
            here = self.block(n, c)
            rc(here, here, self.z_out, self.zs + n, dev(z + step, x, y, c)).start()

        def start(self):
            pl.when(z == 0)(lambda: self.onward(z, 2))
            pl.when(z == 3)(lambda: self.onward(z, -2))
            pl.when(z > 0)(lambda: self.onward(z, -1))
            pl.when(z < PLANES - 1)(lambda: self.onward(z, 1))
            mine = self.block(z, c)
            rc(mine, mine, self.c_out, self.sb + z, sib).start()

        def pump_step(self, n):
            here = self.block(n, c)

            @pl.when(n != z)
            def _():
                got(here, self.zs + n)
                pl.when(jnp.logical_and(z == 1, n > z))(lambda: self.onward(n, -1))
                pl.when(jnp.logical_and(z == 2, n < z))(lambda: self.onward(n, 1))
                rc(here, here, self.c_out, self.sb + n, sib).start()

        def pump_done(self):
            def sent(sem, count):
                rc(self.some(count), self.some(count), sem, 0, sib).wait_send()

            pending.append(lambda: sent(self.c_out, 4))
            pending.append(lambda: pl.when(outer)(lambda: sent(self.z_out, 2)))
            pending.append(lambda: pl.when(inner)(lambda: sent(self.z_out, 4)))

        def pump(self, where):
            @pl.when(where)
            def _():
                for k in range(1, PLANES):
                    self.pump_step(arrive[k])

            if where is outer:
                self.pump_done()

        def need_step(self, n):
            got(self.block(n, 1 - c), self.sb + n)

        def need(self):
            for zz in range(PLANES):
                self.need_step(zz)

    half_of = {}

    def place(ref, xx):
        return ref.at[:, 2 * z + xx, c] if len(ref.shape) == 5 else ref.at[2 * z + xx, c]

    def give_half(name, src, ref):
        i = take()
        half_of[name] = (ref, i[1])
        give(src, place(ref, x), i, xn)

    def have_half(name):
        ref, i = half_of[name]
        got(place(ref, 1 - x), i)

    wo_own = wo.at[own_block]
    i_oh = take()
    give(wo_h.at[:, half_cols(1 - x, 256)], wo.at[2 * (1 - x) + y, 2 * z + x, c], i_oh, xn)
    give_half("q", wq_h.at[:, :, half_cols(1 - x, 256)], wq)
    i_tok, i_tx, i_ty = take(), take(2), take(2)
    give(tok, xg.at[rows_of(c, 256)], i_tok, sib, away)
    give(tok.at[rows_of(y, 128)], xg.at[rows_of(2 * c + y, 128)], i_tx, dev(z, 1 - x, y, x), None, 0, c)
    it_oa, it_ob = Item(wo_own, "own"), Item(wo_own, "other")
    it_qa, it_s, it_qb = Item(wq, "own"), Item(small, "both"), Item(wq, "other")
    it_ua, it_ub, it_da, it_db = Item(wu, "own"), Item(wu, "other"), Item(wd, "own"), Item(wd, "other")
    in_o()
    it_oa.start()
    in_q()
    it_qa.start()

    for done in in_small:
        done()

    def pick(shape, hit):
        return jnp.where(hit(iota(shape, 0), iota(shape, 1)), 1.0, 0.0)

    vec_sel = pick((64, 128), lambda k, l: l == c * 64 + k).astype(BF16)
    rpe_sel = pick((64, 128), lambda k, l: l == (1 - c) * 64 + 63 - k).astype(BF16)
    bias_sel = [pick((4, 128), lambda k, l, par=par: l == par * 64 + 4 * shard + k).astype(BF16) for par in range(2)]
    rpe_rows = dot(rpe_v[...], rpe_sel)
    level = jnp.full((1, 128), bk_v[0].astype(F32))
    top = jnp.concatenate(
        [dot(gain_v[...], vec_sel), dot(bias_v[...], vec_sel), level, jnp.zeros((1, 128), F32)], axis=0
    )

    def spread(values):
        rows = values.shape[1]
        even = (iota((rows, 1), 0) % 2) == 0
        wide = jnp.where(even, dot(values, bias_sel[0], TN), dot(values, bias_sel[1], TN))
        return dot(pick((rows // 2, rows), lambda k, l: l // 2 == k).astype(BF16), wide.astype(BF16))

    up_rows = spread(ub_v[...])
    qkv_rows = [spread(qb_v[p]) for p in range(3)]
    for half in range(2):
        mine = [rows[2 * half : 2 * half + 2] for rows in qkv_rows] + [jnp.zeros((2, 128), F32)]
        position = jnp.concatenate([rpe_rows[4 * half : 4 * half + 4], jnp.zeros((4, 128), F32)], axis=0)
        small_s[half] = jnp.concatenate(
            [top, position] + mine + [up_rows[8 * half : 8 * half + 8]], axis=0
        ).astype(BF16)
    small[2 * z + x, c] = small_s[x]
    give_half("s", small_s.at[1 - x], small)
    for h in range(4):
        sel = pick((32, 256), lambda k, l: l == h * 64 + c * 32 + k).astype(BF16)
        om_s[h * 64 : (h + 1) * 64] = dot(om_v[4 * x + h], sel, TN).astype(BF16)
    i_om = take()
    give(om_s, om2, i_om, sib)
    give_half("u", wu_h.at[:, half_cols(1 - x, 1024)], wu)

    same = (iota((256, 256), 0) // HEAD) == (iota((256, 256), 1) // HEAD)
    ones64[...] = jnp.where(same, 1.0, 0.0).astype(BF16)
    anti[...] = jnp.where(iota((128, 128), 0) + iota((128, 128), 1) == 127, 1.0, 0.0).astype(BF16)

    it_oa.pump(inner)
    got(wo.at[own_block, 2 * z + 1 - x, c], i_oh[1])
    it_ob.start()
    have_half("q")
    it_qb.start()
    it_qa.pump(inner)
    it_ob.pump(inner)
    it_qb.pump(inner)

    @pl.when(away)
    def _():
        for f in range(2):
            got(xg.at[rows_of(2 * f + y, 128)], i_tx[1] + f)

    for f in range(2):
        part = xg.at[rows_of(2 * f + y, 128)]
        give(part, part, i_ty, yn, away, f, f)
    it_oa.pump(outer)
    it_ob.pump(outer)
    i_oq, i_os = take(3), take(3)
    quarter = wo.at[own_block, :, c]
    give(quarter, quarter, i_oq, yn, None, 2, 2)
    give(quarter, quarter, i_oq, xn, None, 1, 1)
    give_half("d", wd_h.at[:, half_cols(1 - x, 1024)], wd)
    have_half("s")
    it_s.start()
    in_u()
    it_ua.start()
    it_s.pump(inner)
    it_qa.pump(outer)
    have_half("u")
    it_ub.start()
    in_d()
    it_da.start()
    it_qb.pump(outer)

    def other_quarter(slot):
        part = wo.at[plane_block[slot], :, c]
        got(part, i_oq[1] + slot)
        give(part, part, i_os, sib, None, slot, slot)
        return part

    it_s.pump(outer)

    it_s.need()
    for t in range(8):
        tile = small[t, 0].astype(F32) + small[t, 1].astype(F32)
        rows_v[0:8, t * 128 : (t + 1) * 128] = tile[0:8]
        rows_v[8:16, (7 - t) * 128 : (8 - t) * 128] = tile[8:16]
        total = tile[16:32] if t == 0 else total + tile[16:32]
    for r in range(6):
        rows_v[16:17, r * 128 : (r + 1) * 128] = total[r : r + 1]
    for r in range(8):
        rows_v[17:18, r * 128 : (r + 1) * 128] = total[8 + r : 9 + r]
    level = small[2 * z + c, 0][6:7].astype(F32)
    wide1 = jnp.where(level > 0.5, 1.0, 0.0)
    wide2 = jnp.where(level > 1.5, 1.0, 0.0)
    one_row = jnp.ones((1, 128), F32)

    def mask_row(bi):
        parts = [one_row if bj == bi else (wide1 if bj // 2 == bi // 2 else wide2) for bj in range(4)]
        return jnp.concatenate(parts, axis=1)

    masks = [mask_row(bi) for bi in range(4)]

    def coeff_body(h, carry):
        row = jnp.exp(rows_v[pl.ds(8 + h, 1), :])
        r0[h] = pltpu.roll(jnp.broadcast_to(row, (128, 1024)), 1, 1, stride=1, stride_axis=0)
        return carry

    lax.fori_loop(0, 4, coeff_body, 0)
    num[...] = jnp.zeros_like(num)
    den[...] = jnp.zeros_like(den)

    in_tok()
    pl.when(home)(lambda: got(xg.at[rows_of(1 - c, 256)], i_tok[1]))

    @pl.when(away)
    def _():
        for f in range(2):
            got(xg.at[rows_of(2 * f + 1 - y, 128)], i_ty[1] + f)

    other_quarter(2)
    part = other_quarter(1)
    give(part, part, i_oq, yn, None, 0, 0)
    it_ua.pump(inner)
    it_qa.need()
    it_qb.need()

    def qkv_body(p, carry):
        qkv[p] = (dot(xg[...], wq[p].reshape(1024, 256)) + rows_v[16:17, cols256(p)]).astype(BF16)
        return carry

    lax.fori_loop(0, 3, qkv_body, 0)
    got(om2, i_om[1])
    om2[...] = om2[...] + om_s[...]

    def feature_body(t, carry):
        wide = qkv[t].astype(F32)
        sums = split_dot(wide * wide, ones64[...])
        inverse = lax.rsqrt(sums * (1.0 / HEAD) + UNIT_EPS)
        units = wide * inverse
        logits = SCALE * split_dot(units, om2[...]) - 0.5 * SCALE * SCALE * (sums * inverse * inverse)
        value = jnp.exp(logits) * M ** (-0.5)
        ex[t] = value
        unit[t] = units
        inv[t] = inverse
        phi[t] = value.astype(BF16)
        return carry

    lax.fori_loop(0, 2, feature_body, 0)
    lane_head = iota((1, 128), 1) // HEAD

    def head_cols(h):
        return pl.ds(pl.multiple_of((h // 2) * 128, 128), 128), (lane_head == h % 2)

    def head_body(h, carry):
        cols, mine = head_cols(h)
        keep = jnp.where(mine, 1.0, 0.0).astype(BF16)
        scores = dot(phi[0, :, cols] * keep, phi[1, :, cols], NT)
        for b in range(4):
            coefficient = r0[h, :, 512 - 128 * b : 1024 - 128 * b] * masks[b]
            pp[h, b * 128 : (b + 1) * 128] = (scores[b * 128 : (b + 1) * 128] * coefficient).astype(BF16)
        right = jnp.concatenate([qkv[2, :, cols] * keep, jnp.broadcast_to(keep, (512, 128))], axis=1)
        both = dot(pp[h], right)
        num[:, cols] += both[:, :128]
        den[:, cols] += both[:, 128:]
        return carry

    i_at = [take(3), take(3)]

    def tile_of(ref, block, t):
        return ref.at[block, :, t * 128 : (t + 1) * 128]

    for t in range(2):
        lax.fori_loop(2 * t, 2 * t + 2, head_body, 0)
        cols = slice(t * 128, (t + 1) * 128)
        quo[:, cols] = num[:, cols] / den[:, cols]
        att[:, :, cols] = quo[:, cols].astype(BF16).reshape(4, 128, 128)
        for slot in range(3):
            give(tile_of(att, plane_block[slot], t), tile_of(attf, own_block, t), i_at[t], plane[slot], None, slot, slot)
    have_half("d")
    it_db.start()
    i_cot = take()
    give(cot.at[rows_of(y, 128)], cotb, i_cot, xs_dev, away)
    it_ub.pump(inner)
    other_quarter(0)
    it_oa.need()
    it_ob.need()

    def out_part(rows, block):
        return dot(rows, wo[block].reshape(1024, 256), NT)

    mixed_z = out_part(att[own_block], own_block)
    for slot in (2, 1, 0):
        got(wo.at[plane_block[slot], :, 1 - c], i_os[1] + slot)
        for t in range(2):
            got(tile_of(attf, plane_block[slot], t), i_at[t][1] + slot)
        mixed_z = mixed_z + out_part(attf[plane_block[slot]], plane_block[slot])

    def norm(values):
        centred = values - jnp.mean(values, axis=-1, keepdims=True)
        inverse = lax.rsqrt(jnp.mean(centred * centred, axis=-1, keepdims=True) + EPSILON)
        return centred * inverse, inverse

    residual = mixed_z + xg[rows_of(own_block, 128)].astype(F32) + rows_v[2:3, :]
    normed, inverse = norm(residual)
    first = normed * rows_v[0:1, :] + rows_v[3:4, :]
    fb[own_block] = first.astype(BF16)

    class Scatter:
        def __init__(self, ref):
            self.ref, self.out, self.base = ref, s_sems.take(), r_sems.take(4)

        def part(self, n, value):
            cols = cols256(n)
            pb[:, :, cols] = value.astype(BF16).reshape(4, 128, 256)
            for slot in range(3):
                rc(
                    pb.at[plane_block[slot], :, cols], self.ref.at[slot, :, cols], self.out, self.base + n, plane[slot]
                ).start()

        def column(self, n):
            cols = slice(n * 256, (n + 1) * 256)
            got(self.ref.at[:, :, cols], self.base + n)
            value = pb[own_block, :, cols].astype(F32)
            for slot in range(3):
                value = value + self.ref[slot, :, cols].astype(F32)
            return value

        def total(self):
            return jnp.concatenate([self.column(n) for n in range(4)], axis=1)

        def sent(self):
            rc(self.ref, self.ref, self.out, 0, sib).wait_send()

    class RelayScatter:
        def __init__(self, ref):
            self.ref, self.out = ref, s_sems.take()
            self.near, self.far, self.last = r_sems.take(4), r_sems.take(4), r_sems.take(4)

        def part(self, n, value):
            cols = cols256(n)
            pb[:, :, cols] = value.astype(BF16).reshape(4, 128, 256)
            even = n % 2 == 0
            beside = dev(z, jnp.where(even, 1 - x, x), jnp.where(even, y, 1 - y), c)
            block = jnp.where(even, plane_block[1], plane_block[2])
            rc(pb.at[plane_block[0], :, cols], self.ref.at[1, :, cols], self.out, self.far + n, beside).start()
            rc(pb.at[block, :, cols], self.ref.at[0, :, cols], self.out, self.near + n, beside).start()

        def pass_on(self, n):
            cols, slot = slice(n * 256, (n + 1) * 256), 2 - n % 2
            part = self.ref.at[1, :, cols]
            got(part, self.far + n)
            part[...] = (part[...].astype(F32) + pb[plane_block[slot], :, cols].astype(F32)).astype(BF16)
            rc(part, self.ref.at[2, :, cols], self.out, self.last + n, plane[slot]).start()

        def total(self):
            pieces = []
            for n in range(4):
                cols = slice(n * 256, (n + 1) * 256)
                got(self.ref.at[0, :, cols], self.near + n)
                got(self.ref.at[2, :, cols], self.last + n)
                value = pb[own_block, :, cols].astype(F32) + self.ref[0, :, cols].astype(F32)
                pieces.append(value + self.ref[2, :, cols].astype(F32))
            return jnp.concatenate(pieces, axis=1)

        def sent(self):
            rc(self.ref, self.ref, self.out, 0, sib).wait_send()

    class Gather:
        def __init__(self, ref, order):
            self.ref, self.out, self.base, self.order = ref, s_sems.take(), r_sems.take(5), order
            pending.append(lambda: rc(ref.at[pl.ds(0, 3)], ref.at[pl.ds(0, 3)], self.out, 0, sib).wait_send())

        def start(self):
            for half in range(2):
                for slot in range(3):
                    mine = self.ref.at[own_block, :, self.half_cols(half)]
                    rc(mine, mine, self.out, self.base + 3 + half, plane[slot]).start()
            for k in range(1, 4):
                for slot in range(3):
                    mine = self.ref.at[own_block, :, cols256(self.order[k])]
                    rc(mine, mine, self.out, self.base + k - 1, plane[slot]).start()

        def half_cols(self, half):
            return pl.ds(pl.multiple_of(self.order[0] * 256 + half * 128, 128), 128)

        def need_half(self, half):
            got(self.ref.at[pl.ds(0, 3), :, self.half_cols(half)], self.base + 3 + half)

        def need(self, k):
            got(self.ref.at[pl.ds(0, 3), :, cols256(at_step(self.order, k))], self.base + k - 1)

    class RelayGather:
        def __init__(self, ref, order):
            self.ref, self.out, self.base, self.order = ref, s_sems.take(), r_sems.take(12), order
            pending.append(lambda: rc(ref.at[pl.ds(0, 3)], ref.at[pl.ds(0, 3)], self.out, 0, sib).wait_send())

        def piece(self, slot, n):
            return self.ref.at[plane_block[slot], :, cols256(n)]

        def start(self):
            for n in self.order:
                mine = self.ref.at[own_block, :, cols256(n)]
                for slot in (1, 2):
                    rc(mine, mine, self.out, self.base + slot * 4 + n, plane[slot]).start()

        def pass_on(self, k):
            n, slot = self.order[k], 1 + k % 2
            part = self.piece(slot, n)
            got(part, self.base + slot * 4 + n)
            rc(part, part, self.out, self.base + n, plane[3 - slot]).start()

        def need(self, k):
            n, slot = self.order[k], 2 - k % 2
            got(self.piece(slot, n), self.base + slot * 4 + n)
            got(self.piece(0, n), self.base + n)

    g_first = RelayGather(fb, range(4))
    g_first.start()
    it_da.pump(inner)
    g_first.pass_on(0)
    it_db.pump(inner)
    for k in range(1, 4):
        g_first.pass_on(k)
    it_ua.pump(outer)
    it_ub.pump(outer)
    fst[...] = first
    n1[...] = normed
    i1[...] = jnp.broadcast_to(inverse, (128, 128))

    def d_cols(ref, m):
        return ref[:, :, cols256(m)].reshape(512, 256)

    acc[...] = jnp.zeros_like(acc)
    it_ua.need()
    it_ub.need()

    for k in range(4):
        g_first.need(k)
        left = d_cols(fb, k)
        if k == 2:
            it_da.pump(outer)

        def hidden_part(j, carry, k=k, left=left):
            cols = cols256(j)
            acc[:, cols] += dot(left, wu[2 * k : 2 * k + 2, :, :, cols].reshape(256, 256))
            return carry

        lax.fori_loop(0, 4, hidden_part, 0)

    def hidden_body(n, carry):
        cols = cols256(n)
        pre = acc[:, cols] + rows_v[17:18, cols]
        cdf = 0.5 * (1.0 + lax.erf(pre * 0.7071067811865476))
        hid[:, cols] = (pre * cdf).astype(BF16)
        dgel[:, cols] = cdf + pre * (0.3989422804014327 * jnp.exp(-0.5 * pre * pre))
        return carry

    lax.fori_loop(0, 4, hidden_body, 0)
    sc_f = Scatter(rb_f)

    def down_part(k, carry):
        n = at_step(arrive, k)
        pl.when(outer)(lambda: it_db.pump_step(n))
        it_da.need_step(n)
        it_db.need_step(n)
        sc_f.part(n, dot(hid[...], wd[pl.ds(2 * n, 2)].reshape(256, 1024), NT))
        return carry

    lax.fori_loop(0, 4, down_part, 0)
    it_db.pump_done()
    pl.when(away)(lambda: got(cotb, i_cot[1]))
    in_cot()
    upstream = cotb[...].astype(F32)

    def down(values):
        return jnp.sum(values, axis=0, keepdims=True)

    sd[5:6, :] = down(upstream)
    acc[...] = jnp.zeros_like(acc)
    second = fst[...] + sc_f.total() + rows_v[4:5, :]
    normed2, inverse2 = norm(second)

    def norm_back(upstream, normed, inverse, gain):
        scaled = upstream * gain
        mean = jnp.mean(scaled, axis=-1, keepdims=True)
        slope = jnp.mean(scaled * normed, axis=-1, keepdims=True)
        return inverse * (scaled - mean - normed * slope)

    err = norm_back(upstream, normed2, inverse2, rows_v[1:2, :])
    efb[own_block] = err.astype(BF16)
    g_ef = Gather(efb, leave)
    g_ef.start()
    mix_s[...] = (normed2 * rows_v[1:2, :] + rows_v[5:6, :]).astype(BF16)
    dr[...] = err
    sd[1:2, :] = down(upstream * normed2)
    sd[4:5, :] = down(err.astype(BF16).astype(F32))
    sc_f.sent()

    class Owner:
        def __init__(self, dst, pieces):
            self.dst, self.width = dst, 1024 // pieces
            self.ids = [take(2) for _ in range(pieces)]

        def part(self, half, n):
            return self.dst.at[rows_of(half, 128), n * self.width : (n + 1) * self.width]

        def start(self, src, n):
            cols = slice(n * self.width, (n + 1) * self.width)

            @pl.when(home)
            def _():
                self.dst[rows_of(y, 128), cols] = src[:, cols]

            give(src.at[:, cols], self.part(y, n), self.ids[n], yn, home, 1, 1)
            give(src.at[:, cols], self.part(y, n), self.ids[n], xs_dev, away, 0, 0)

        def pass_on(self, n):
            part = self.part(y, n)
            pl.when(away)(lambda: got(part, self.ids[n][1]))
            give(part, part, self.ids[n], yn, away, 1, 1)

        def need(self, n):
            got(self.part(1 - y, n), self.ids[n][1] + 1)

    own_mix = Owner(mixed_o, 1)
    own_mix.start(mix_s, 0)

    class Grad:
        def __init__(self, g, r, rz, cb, xs, xr, first):
            self.first = first
            self.g, self.r, self.rz, self.cb, self.xs, self.xr = g, r, rz, cb, xs, xr
            self.d, self.z, self.k, self.x = r_sems.take(4), r_sems.take(2), r_sems.take(2), take()
            self.mine = z // 2
            self.d_out, self.z_out = s_sems.take(), s_sems.take()
            self.width = r.shape[-1]

        def give(self, m):
            rc(self.g.at[m, :, 1 - c], self.r.at[m], self.d_out, self.d + m, sib).start()

        def pair_step(self, m):
            got(self.r.at[m], self.d + m)
            self.r[m] = (self.g[m, :, c].astype(F32) + self.r[m].astype(F32)).astype(BF16)
            far = jnp.abs(m - z)
            part = self.r.at[m]
            beside = dev(jnp.where(z == 0, 1, jnp.where(z == 1, 0, jnp.where(z == 2, 3, 2))), x, y, c)

            @pl.when(jnp.logical_or(outer if self.first else False, m == jnp.where(z == 1, 0, 3)) & (far == 1))
            def _():
                rc(part, self.rz.at[self.mine], self.z_out, self.z + self.mine, beside).start()

            for slot in range(2):
                @pl.when(outer & (far == 3 - slot))
                def _(slot=slot):
                    rc(part, self.cb.at[slot], self.z_out, self.k + slot, beside).start()

        def pair_half(self, m, half, i):
            part = self.r.at[m, half]
            got(part, i)
            part[...] = (self.g[m, half, c].astype(F32) + part[...].astype(F32)).astype(BF16)
            beside = dev(jnp.where(z == 0, 1, jnp.where(z == 1, 0, jnp.where(z == 2, 3, 2))), x, y, c)

            @pl.when(outer)
            def _():
                rc(part, self.cb.at[0, half], self.z_out, self.k, beside).start()

            @pl.when(inner)
            def _():
                rc(part, self.rz.at[self.mine, half], self.z_out, self.z + self.mine, beside).start()

        def near(self):
            for at, m in ((0, 1), (3, 2)):
                @pl.when(z == at)
                def _(at=at, m=m):
                    rc(self.r.at[m], self.rz.at[at // 2], self.z_out, self.z + at // 2, dev(m, x, y, c)).start()

        def relay(self, *slots):
            for at, blocks in ((1, (3, 2)), (2, (0, 1))):
                @pl.when(z == at)
                def _(at=at, blocks=blocks):
                    for slot in slots:
                        m = blocks[slot]
                        got(self.cb.at[slot], self.k + slot)
                        self.r[m] = (self.r[m].astype(F32) + self.cb[slot].astype(F32)).astype(BF16)
                        rc(self.r.at[m], self.rz.at[at // 2], self.z_out, self.z + at // 2, dev(m, x, y, c)).start()

        def run(self, make):
            def body(k, carry):
                m = at_step(leave, k)
                make(m)
                self.give(m)
                pl.when(k > 0)(lambda: self.pair_step(at_step(leave, k - 1)))
                return carry

            lax.fori_loop(0, PLANES, body, 0)
            self.pair_step(leave[3])

        def finish(self):
            total = fs.at[:, :, 0 : self.width]
            total[...] = self.r[z].astype(F32)
            for dz in (1, -1, 2, -2):
                @pl.when(valid(dz) if abs(dz) == 1 else z == (0 if dz > 0 else 3))
                def _(dz=dz):
                    slot = (z + dz) // 2
                    got(self.rz.at[slot], self.z + slot)
                    total[...] += self.rz[slot].astype(F32)
            self.xs[...] = fs[1 - x, :, 0 : self.width].astype(BF16)
            give(self.xs, self.xr, self.x, xn)

        def sent(self):
            rc(self.r, self.r, self.d_out, 0, sib).wait_send()
            part = self.r.at[pl.ds(0, 3)]
            rc(part, part, self.z_out, 0, sib).wait_send()

        def columns(self, out, half, value, at=0):
            if len(out.shape) == 3:
                for p in range(self.width // 256):
                    out[at + p, :, half_cols(half, 256)] = value[:, p * 256 : (p + 1) * 256]
            else:
                out[:, half_cols(half, self.width)] = value

        def write_own(self, out, at=0):
            self.columns(out, x, fs[x, :, 0 : self.width], at)

        def write_other(self, out, at=0):
            got(self.xr, self.x[1])
            self.columns(out, 1 - x, self.xr[...].astype(F32), at)

    gr_d = Grad(g_d, r_d, rz_d, cb_d, xs_d, xr_d, True)
    gr_u = Grad(g_u, r_u, rz_u, cb_u, xs_u, xr_u, True)
    gr_o = Grad(g_o, r_o, rz_o, cb_o, xs_o, xr_o, False)
    gr_v = Grad(g_v, r_v, rz_v, cb_v, xs_v, xr_v, False)
    gr_k = Grad(g_k, r_k, rz_k, cb_k, xs_k, xr_k, False)

    def act_part(m):
        left = d_cols(efb, m)
        for j in range(4):
            cols = slice(j * 256, (j + 1) * 256)
            acc[:, cols] += dot(left, wd[pl.ds(2 * m, 2), :, :, cols].reshape(256, 256))

    i_half = r_sems.take(2)
    for half in range(2):
        g_ef.need_half(half)
        left = efb[:, :, g_ef.half_cols(half)].reshape(512, 128)
        g_d[leave[0], half] = dot(left, hid[...], TN).astype(BF16).reshape(2, 64, 1024)
        rc(g_d.at[leave[0], half, 1 - c], r_d.at[leave[0], half], gr_d.d_out, i_half + half, sib).start()
    for half in range(2):
        gr_d.pair_half(leave[0], half, i_half + half)
        if half == 0:
            act_part(leave[0])

    def down_grads(k, carry):
        m = at_step(leave, k)
        g_ef.need(k)
        g_d[m] = dot(d_cols(efb, m), hid[...], TN).astype(BF16).reshape(2, 2, 64, 1024)
        gr_d.give(m)
        act_part(m)
        gr_d.pair_step(m)
        return carry

    lax.fori_loop(1, PLANES, down_grads, 0)
    def du_body(n, carry):
        cols = cols256(n)
        du = (acc[:, cols] * dgel[:, cols]).astype(BF16)
        dub[:, cols] = du
        for zz in range(PLANES):
            st_b[zz, pl.ds(8 + n, 1), :] = down(du.astype(F32))
        return carry

    lax.fori_loop(0, 4, du_body, 0)
    sc_d = RelayScatter(rb_d)

    def back_part(n, carry):
        sc_d.part(n, dot(dub[...], wu[pl.ds(2 * n, 2)].reshape(256, 1024), NT))
        return carry

    lax.fori_loop(0, 4, back_part, 0)
    own_mix.pass_on(0)
    for m in range(4):
        xt[m * 256 : (m + 1) * 256] = xg[:, m * 256 : (m + 1) * 256].T

    def transpose_body(h, carry):
        ppt[h] = pp[h].T
        return carry
    gr_d.relay(0)
    sc_d.pass_on(0)
    sc_d.pass_on(1)

    def make_up(m):
        g_u[m] = dot(d_cols(fb, m), dub[...], TN).astype(BF16).reshape(2, 2, 64, 1024)

    gr_u.run(make_up)
    sc_d.pass_on(2)
    sc_d.pass_on(3)
    lax.fori_loop(0, 4, transpose_body, 0)
    gr_d.relay(1)
    dfirst = dr[...] + sc_d.total()
    back = norm_back(dfirst, n1[...], i1[:, 0:1], rows_v[0:1, :])
    dz = back.astype(BF16)
    dzb[own_block] = dz

    i_da = take(3)

    def attention_grad(block):
        dat_s[block] = dot(dz, wo[block].reshape(1024, 256)).astype(BF16)

    for slot in range(3):
        attention_grad(plane_block[slot])
        give(dat_s.at[plane_block[slot]], dat.at[own_block], i_da, plane[slot], None, slot, slot)
    attention_grad(own_block)
    dat[own_block] = dat_s[own_block]
    g_dz = RelayGather(dzb, leave)
    g_dz.start()
    sd[0:1, :] = down(dfirst * n1[...])
    sd[3:4, :] = down(dfirst)
    sd[2:3, :] = down(dz.astype(F32))
    sd[6:8, :] = jnp.zeros((2, 1024), F32)
    class Total:
        def __init__(self, ref, work, recv):
            self.ref, self.work, self.recv = ref, work, recv
            self.c, self.z = take(), take(PLANES)

        def pair(self):
            give(self.ref, self.work, self.c, sib)

        def over_planes(self):
            got(self.work, self.c[1])
            self.work[...] = self.ref[...] + self.work[...]
            for zz in range(PLANES):
                give(self.work.at[zz], self.recv.at[z], self.z, dev(zz, x, y, c), z != zz, zz, z)

        def finish(self):
            for zz in range(PLANES):
                @pl.when(z != zz)
                def _(zz=zz):
                    got(self.recv.at[zz], self.z[1] + zz)

                @pl.when(z == zz)
                def _(zz=zz):
                    self.recv[zz] = self.work[zz]
            return self.recv[0] + self.recv[1] + self.recv[2] + self.recv[3]

    early, late = Total(st_a, work_a, recv_a), Total(st_b, work_b, recv_b)
    i_swap = take()
    i_sd = take(3)
    for k, device in enumerate(plane):
        give(sd, sd_r.at[k], i_sd, device, None, k, k)
    dr[...] = back
    sc_d.sent()
    dph[...] = jnp.zeros_like(dph)
    dvv[...] = jnp.zeros_like(dvv)
    gr_u.relay(0)
    for slot in range(3):
        got(dat.at[plane_block[slot]], i_da[1] + slot)

    dattn = dat[...].reshape(512, 256).astype(F32)
    recip = 1.0 / den[...]
    dn[...] = (dattn * recip).astype(BF16)
    dsum = split_dot(dattn * quo[...], ones64[...])
    dd[...] = ((-dsum * recip).astype(BF16).astype(F32) * (1.0 / HEAD)).astype(BF16)

    def value_back(h, carry):
        cols, mine = head_cols(h)
        keep = jnp.where(mine, 1.0, 0.0).astype(BF16)
        dvv[:, cols] += dot(ppt[h], dn[:, cols] * keep)
        return carry

    lax.fori_loop(0, 4, value_back, 0)
    dqkv[2] = dvv[...].astype(BF16)

    def x_rows(m):
        return xt[rows_of(m, 256)]

    def make_v(m):
        g_v[m] = dot(x_rows(m), dqkv[2]).astype(BF16).reshape(2, 2, 64, 256)

    def head_back(h, carry):
        cols, mine = head_cols(h)
        keep = jnp.where(mine, 1.0, 0.0).astype(BF16)
        left = jnp.concatenate([dn[:, cols] * keep, dd[:, cols] * keep], axis=1)
        right = jnp.concatenate([qkv[2, :, cols], jnp.ones((512, 128), BF16)], axis=1)
        grad_p = dot(left, right, NT)
        for b in range(4):
            rows = slice(b * 128, (b + 1) * 128)
            coefficient = r0[h, :, 512 - 128 * b : 1024 - 128 * b] * masks[b]
            part = grad_p[rows]
            ds_[rows] = (part * coefficient).astype(BF16)
            gg[h, rows] = (part * pp[h, rows].astype(F32)).astype(BF16)
        dph[0, :, cols] += dot(ds_[...], phi[1, :, cols] * keep)
        dph[1, :, cols] += dot(ds_[...], phi[0, :, cols] * keep, TN)
        return carry

    lax.fori_loop(0, 4, head_back, 0)
    gr_u.relay(1)
    g_dz.pass_on(0)
    g_dz.pass_on(1)
    gr_v.run(make_v)
    g_dz.pass_on(2)
    g_dz.pass_on(3)

    def feature_back_body(t, carry):
        dlog = (dph[t] * ex[t]).astype(BF16)
        units = unit[t]
        dunit = SCALE * dot(dlog, om2[...], NT) - SCALE * SCALE * dot(dlog, ones64[...]) * units
        mean = split_dot(dunit * units, ones64[...]) * (1.0 / HEAD)
        dqkv[t] = (inv[t] * (dunit - units * mean)).astype(BF16)
        return carry

    lax.fori_loop(0, 2, feature_back_body, 0)
    class Return:
        def __init__(self, ref):
            self.ref, self.out, self.base, self.last = ref, s_sems.take(), r_sems.take(4), take(4)
            pending.append(lambda: pl.when(home)(lambda: rc(ref.at[0:3], ref.at[0:3], self.out, 0, sib).wait_send()))
            pending.append(lambda: pl.when(away)(lambda: rc(ref, ref, self.out, 0, sib).wait_send()))

        def part(self, n, value):
            cols = cols256(n)
            for b in range(4):
                rows = value[b * 128 : (b + 1) * 128]
                pb[b, :, cols] = jnp.where(own_block == b, rows + dr[:, cols], rows).astype(BF16)
                here = home & (c == b // 2) & (y == b % 2)

                @pl.when(here)
                def _(b=b):
                    self.ref[own_block, :, cols] = pb[b, :, cols]

                @pl.when(jnp.logical_not(here))
                def _(b=b):
                    there = self.ref.at[own_block, :, cols]
                    rc(pb.at[b, :, cols], there, self.out, self.base + n, dev(z, c, b % 2, b // 2)).start()

        def column(self, n):
            cols = slice(n * 256, (n + 1) * 256)
            pl.when(home)(lambda: got(self.ref.at[0:3, :, cols], self.base + n))
            pl.when(away)(lambda: got(self.ref.at[0:4, :, cols], self.base + n))
            value = self.ref[0, :, cols].astype(F32)
            for slot in range(1, 4):
                value = value + self.ref[slot, :, cols].astype(F32)
            mine = gt_r.at[rows_of(y, 128), cols]
            mine[...] = value.astype(BF16)
            give(mine, mine, self.last, yn, None, n, n)
            gtok_o[rows_of(y, 128), cols] = value

        def need(self, n):
            cols = slice(n * 256, (n + 1) * 256)
            rows = rows_of(1 - y, 128)
            got(gt_r.at[rows, cols], self.last[1] + n)
            gtok_o[rows, cols] = gt_r[rows, cols].astype(F32)

    sc_i = Return(rb_i)

    def input_part(n, carry):
        value = jnp.zeros((512, 256), F32)
        for p in range(3):
            value = value + dot(dqkv[p], wq[p, pl.ds(2 * n, 2)].reshape(256, 256), NT)
        sc_i.part(n, value)
        return carry

    lax.fori_loop(0, 4, input_part, 0)

    def make_k(m):
        for p in range(2):
            g_k[m, :, :, :, p * 256 : (p + 1) * 256] = (
                dot(x_rows(m), dqkv[p]).astype(BF16).reshape(2, 2, 64, 256)
            )

    gr_k.run(make_k)

    def make_out(m):
        g_o[m] = dot(d_cols(dzb, m), att[...].reshape(512, 256), TN).astype(BF16).reshape(2, 2, 64, 256)

    for k in range(4):
        g_dz.need(k)
    gr_o.run(make_out)
    gr_v.near()
    gr_k.near()
    gr_v.relay(0, 1)
    for k in range(3):
        got(sd_r.at[k], i_sd[1] + k)
    sums = sd[...] + sd_r[0] + sd_r[1] + sd_r[2]
    for zz in range(PLANES):
        st_a[zz] = sums[:, zz * 256 : (zz + 1) * 256]
    early.pair()
    gr_d.finish()
    gr_d.write_own(gd_o)

    def diagonal_body(h, carry):
        sums = jnp.zeros((1, 1024), F32)
        for b in range(4):
            flipped = dot(anti[...], gg[h, (3 - b) * 128 : (4 - b) * 128])
            wide = jnp.concatenate([flipped, jnp.zeros((128, 128), F32)], axis=1)
            line = down(pltpu.roll(wide, 0, 1, stride=1, stride_axis=0))
            pieces = [line]
            if b > 0:
                pieces = [jnp.zeros((1, 128 * b), F32)] + pieces
            if b < 3:
                pieces = pieces + [jnp.zeros((1, 384 - 128 * b), F32)]
            sums = sums + jnp.concatenate(pieces, axis=1)
        for zz in range(PLANES):
            st_b[zz, pl.ds(h, 1), :] = sums[:, (3 - zz) * 256 : (4 - zz) * 256]
        return carry

    lax.fori_loop(0, 4, diagonal_body, 0)
    for p in range(3):
        line = down(dqkv[p].astype(F32))
        for zz in range(PLANES):
            st_b[zz, 12 + p : 13 + p, :] = line
    for zz in range(PLANES):
        st_b[zz, 4:8, :] = jnp.zeros((4, 256), F32)
        st_b[zz, 15:16, :] = jnp.zeros((1, 256), F32)
    late.pair()
    gr_k.relay(0)
    early.over_planes()
    late.over_planes()
    gr_o.near()
    gr_k.relay(1)
    outs = []
    own_mix.need(0)
    outs.append(bring(mixed_o, mixed_h))
    gr_o.relay(0, 1)
    gr_u.finish()
    gr_u.write_own(gu_o)
    sc_i.column(0)
    sc_i.column(1)
    sc_i.column(2)
    sc_i.column(3)
    gr_d.write_other(gd_o)
    outs.append(bring(gd_o, gd_h))
    gr_v.finish()
    gr_v.write_own(gq_o, 2)
    gr_u.write_other(gu_o)
    outs.append(bring(gu_o, gu_h))

    def exact(left, right):
        return lax.dot_general(left, right, NN, precision=lax.Precision.HIGHEST, preferred_element_type=F32)

    sd_r[0, :, 0:256] = early.finish()
    mine = sd_r[0, :, pl.ds(pl.multiple_of(x * 128, 128), 128)]
    own = exact(mine, pick((128, 64), lambda k, l: k == c * 64 + l))
    ggain_o[...] = own[0:2]
    gbias_o[...] = own[2:6]
    outs.append(bring(ggain_o, ggain_h))
    outs.append(bring(gbias_o, gbias_h))
    swap[0] = late.finish()
    give(swap.at[0], swap.at[1], i_swap, xn)
    gr_k.finish()
    gr_k.write_own(gq_o)
    gr_o.finish()
    gr_o.write_own(go_o)
    for n in range(4):
        sc_i.need(n)
    outs.append(bring(gtok_o, gtok_h))
    got(swap.at[1], i_swap[1])
    tile = pl.ds(pl.multiple_of((1 - x) * 128, 128), 128)
    ours, theirs = swap[0, 0:4, tile], swap[1, 0:4, tile]
    lines = jnp.concatenate([jnp.where(x == 0, ours, theirs), jnp.where(x == 0, theirs, ours)], axis=0)
    grpe_o[...] = exact(lines, pick((128, 64), lambda k, l: k == (1 - c) * 64 + 63 - l))
    outs.append(bring(grpe_o, grpe_h))
    ours, theirs = swap[0, 8:16], swap[1, 8:16]
    rest = [jnp.where(x == half, ours, theirs) for half in range(2)]
    lines = [rest[half][4 + p : 5 + p, t * 128 : (t + 1) * 128] for p in range(3) for half in range(2) for t in range(2)]
    lines += [
        rest[half][t // 2 : t // 2 + 1, (t % 2) * 128 : (t % 2 + 1) * 128] for half in range(2) for t in range(8)
    ]
    lines = jnp.concatenate(lines + [jnp.zeros((4, 128), F32)], axis=0)
    found = jnp.zeros((4, 56), F32)
    for par in range(2):
        hit = pick((4, 128), lambda k, l: l == par * 64 + 4 * shard + k)
        values = lax.dot_general(hit, lines, NT, precision=lax.Precision.HIGHEST, preferred_element_type=F32)
        found = found + exact(values, pick((32, 56), lambda k, l: (l // 2 == k) & (l % 2 == par)))
    for p in range(3):
        gqb_o[p] = found[:, 8 * p : 8 * p + 8]
    gub_o[...] = found[:, 24:56]
    outs.append(bring(gqb_o, gqb_h))
    outs.append(bring(gub_o, gub_h))
    gr_v.write_other(gq_o, 2)
    gr_k.write_other(gq_o)
    outs.append(bring(gq_o, gq_h))
    gr_o.write_other(go_o)
    outs.append(bring(go_o, go_h))
    for gr in (gr_d, gr_u, gr_o, gr_v, gr_k):
        gr.sent()
    assert (s_sems.used, r_sems.used, locals_.used) == (SENDS, RECEIVES, 24), (s_sems.used, r_sems.used, locals_.used)
    for done in pending + outs:
        done()


def copy_kernel(*refs):
    count = len(refs) // 3
    sem = refs[-1]
    ins = [pltpu.make_async_copy(refs[i], refs[2 * count + i], sem.at[0, i]) for i in range(count)]
    outs = [pltpu.make_async_copy(refs[2 * count + i], refs[count + i], sem.at[1, i]) for i in range(count)]
    for copy in ins:
        copy.start()
    for one, two in zip(ins, outs):
        one.wait()
        two.start()
    for copy in outs:
        copy.wait()


def fast_local(
    tokens, qkv_weight, qkv_bias, out_weight, norm_gains, row_biases, up_weight, up_bias, down_weight, rpe_bias, omega,
    bucket, cotangent,
):
    def vm(shape, dtype=BF16):
        return pltpu.VMEM(shape, dtype)

    widths = (512, 256, 256, 1024, 1024)
    scratch = [vm((3, 4, 8)), vm((2, 64)), vm((4, 64)), vm((4, 32)), vm((8, 64)), vm((8, 32, 64))]
    scratch += [pltpu.SMEM((1,), jnp.int32), vm((2, 32, 128)), vm((256, 256))]
    results = (
        ((256, 1024), BF16), ((256, 1024), F32), ((3, 64, 512), F32), ((3, 4, 8), F32), ((64, 512), F32), ((2, 64), F32),
        ((4, 64), F32), ((64, 2048), F32), ((4, 32), F32), ((64, 2048), F32), ((8, 64), F32),
    )
    scratch += [vm(*result) for result in results]
    scratch += [vm((3, 8, 2, 64, 256)), vm((4, 8, 2, 64, 256)), vm((8, 2, 64, 1024)), vm((8, 2, 64, 1024))]
    scratch += [vm((8, 2, 32, 128)), vm((256, 256)), vm((512, 1024)), vm((128, 1024))]
    scratch += [vm((3, 512, 256)), vm((2, 512, 256))] + [vm((2, 512, 256), F32)] * 3
    scratch += [vm((4, 128, 1024), F32), vm((4, 512, 512))] + [vm((512, 256), F32)] * 3 + [vm((4, 128, 256))] * 2
    scratch += [vm((4, 128, 1024))] + [vm((3, 128, 1024))] * 2 + [vm((4, 128, 1024))]
    scratch += [vm((4, 128, 1024)), vm((512, 1024)), vm((512, 1024), F32)]
    scratch += [vm((4, 128, 1024)), vm((512, 1024)), vm((4, 128, 1024)), vm((512, 1024), F32)]
    scratch += [vm((128, 1024), F32)] * 2 + [vm((128, 128), F32), vm((128, 1024), F32)]
    scratch += [vm((4, 128, 256))] * 2 + [vm((16, 128)), vm((128, 128)), vm((256, 256)), vm((24, 1024), F32)]
    scratch += [vm((512, 256))] * 2 + [vm((512, 512)), vm((4, 512, 512)), vm((2, 512, 256), F32), vm((512, 256), F32)]
    scratch += [vm((3, 512, 256)), vm((1024, 512)), vm((4, 512, 512))]
    scratch += [vm((4, 2, 2, 64, n)) for n in widths]
    scratch += [vm((4, 2, 64, n)) for n in widths] + [vm((2, 2, 64, n)) for n in widths] * 2
    scratch += [vm((2, 64, 1024), F32)] + [vm((64, n)) for n in widths] * 2
    scratch += [vm((8, 1024), F32), vm((3, 8, 1024), F32)] + [vm((4, 8, 256), F32), vm((4, 16, 256), F32)] * 3
    scratch += [vm((2, 16, 256), F32)]
    scratch += [vm((128, 1024)), vm((256, 1024))]
    scratch += [pltpu.SemaphoreType.DMA((SENDS,)), pltpu.SemaphoreType.DMA((RECEIVES,)), pltpu.SemaphoreType.DMA((24,))]

    shapes = tuple(jax.ShapeDtypeStruct(*result) for result in results)
    anywhere = pl.BlockSpec(memory_space=pl.ANY)
    made = pl.pallas_call(
        layer_kernel,
        out_shape=shapes,
        in_specs=[anywhere] * 13,
        out_specs=(anywhere,) * len(shapes),
        scratch_shapes=scratch,
        compiler_params=pltpu.CompilerParams(
            collective_id=0, has_side_effects=True, vmem_limit_bytes=63 * 2**20
        ),
        name="layer",
    )(
        tokens, qkv_weight.transpose(1, 0, 2), qkv_bias.transpose(0, 2, 1), out_weight.T, norm_gains, row_biases, up_weight,
        up_bias.T, down_weight.T, rpe_bias, omega.transpose(0, 2, 1), bucket, cotangent,
    )
    mixed, gtok, gq, gqb, go, ggain, gbias, gu, gub, gd, grpe = pl.pallas_call(
        copy_kernel,
        out_shape=shapes,
        in_specs=[anywhere] * len(shapes),
        out_specs=(anywhere,) * len(shapes),
        scratch_shapes=[vm(*result) for result in results] + [pltpu.SemaphoreType.DMA((2, len(shapes)))],
        compiler_params=pltpu.CompilerParams(vmem_limit_bytes=63 * 2**20),
        name="results",
    )(*made)
    return (
        mixed, gtok, gq.transpose(1, 0, 2), gqb.transpose(0, 2, 1), go.T, ggain, gbias, gu, gub.T, gd.T, grpe,
    )


def solution(mesh):
    sizes = (mesh.shape["dp"], mesh.shape["heads"], mesh.shape["feat"])
    return jax.shard_map(
        fast_local if sizes == (2 * PLANES, 2, 2) else local,
        mesh=mesh,
        in_specs=(
            P(("dp", "feat"), None),
            P(("dp", "feat"), None, "heads"),
            P(None, "heads", ("dp", "feat")),
            P("heads", ("dp", "feat")),
            P(None, ("dp", "feat")),
            P(None, ("dp", "feat")),
            P(("dp", "feat"), "heads"),
            P("heads", ("dp", "feat")),
            P("heads", ("dp", "feat")),
            P("heads", ("dp", "feat")),
            P("heads", None, "feat"),
            P("dp"),
            P(("dp", "feat"), None),
        ),
        out_specs=(
            P(("dp", "feat"), None),
            P(("dp", "feat"), None),
            P(("dp", "feat"), None, "heads"),
            P(None, "heads", ("dp", "feat")),
            P("heads", ("dp", "feat")),
            P(None, ("dp", "feat")),
            P(None, ("dp", "feat")),
            P(("dp", "feat"), "heads"),
            P("heads", ("dp", "feat")),
            P("heads", ("dp", "feat")),
            P("heads", ("dp", "feat")),
        ),
        check_vma=False,
    )
```

```python
import functools

import jax
import jax.numpy as jnp
from jax import lax
from jax.experimental import pallas as pl
from jax.experimental.pallas import tpu as pltpu
from jax.sharding import PartitionSpec as P

HEAD = 64
M = 64


EPSILON = 1e-12
UNIT_EPS = 1e-06


def toeplitz_block(window, extent):
    leading = window.shape[0]
    tiled_rows = jnp.broadcast_to(window[:, None, :], (leading, extent, 2 * extent - 1)).reshape(
        leading, -1
    )
    padded = jnp.pad(tiled_rows, ((0, 0), (0, extent)))
    sheared = padded.reshape(leading, extent, 2 * extent)[:, :, :extent]
    return sheared[:, :, ::-1]


def diagonal_sums(values_grid, extent):
    leading = values_grid.shape[0]
    flipped = values_grid[:, :, ::-1]
    padded = jnp.pad(flipped, ((0, 0), (0, 0), (0, extent))).reshape(leading, -1)
    sheared = padded[:, : extent * (2 * extent - 1)].reshape(leading, extent, 2 * extent - 1)
    return jnp.sum(sheared, axis=1)


def norm_forward(values, gain, shift):
    centred = values - jnp.mean(values, axis=-1, keepdims=True)
    inverse = lax.rsqrt(jnp.mean(centred * centred, axis=-1, keepdims=True) + EPSILON)
    normed = centred * inverse
    return (normed * gain + shift, normed, inverse)


def norm_backward(upstream, normed, inverse, gain):
    scaled_grad = upstream * gain
    return inverse * (
        scaled_grad
        - jnp.mean(scaled_grad, axis=-1, keepdims=True)
        - normed * jnp.mean(scaled_grad * normed, axis=-1, keepdims=True)
    )


def feature_logits(entries, omega_local):
    factor = HEAD ** (-0.25)
    wide = entries.astype(jnp.float32)
    inverse = lax.rsqrt(jnp.mean(wide * wide, axis=-1, keepdims=True) + UNIT_EPS)
    unit = wide * inverse
    projected = jnp.einsum(
        "rhe,hem->hmr",
        unit,
        omega_local.astype(jnp.float32),
        precision=lax.Precision.HIGHEST,
        preferred_element_type=jnp.float32,
    )
    squares = jnp.sum(unit * unit, axis=-1)
    return (factor * projected - 0.5 * factor * factor * squares.T[:, None, :], unit, inverse)


def feature_back(grad_phi, logits, unit, inverse, omega_local):
    factor = HEAD ** (-0.25)
    grad_logits = (grad_phi * (jnp.exp(logits) * M ** (-0.5))).astype(jnp.bfloat16)
    projected = jnp.einsum(
        "hmr,hem->rhe", grad_logits, omega_local, preferred_element_type=jnp.float32
    )
    totals = jnp.sum(grad_logits.astype(jnp.float32), axis=1)
    grad_unit = factor * projected - factor * factor * totals.T[:, :, None] * unit
    return inverse * (grad_unit - unit * jnp.mean(grad_unit * unit, axis=-1, keepdims=True))


def window_begin(row_start, col_start, extent, rows_total):
    return row_start - col_start + rows_total - extent + 1


def block_coeff(rpe_exp, window_start, extent):
    window = lax.dynamic_slice_in_dim(rpe_exp, window_start, 2 * extent - 1, 1)
    return toeplitz_block(window, extent)


def local(
    tokens,
    qkv_weight,
    qkv_bias,
    out_weight,
    norm_gains,
    row_biases,
    up_weight,
    up_bias,
    down_weight,
    rpe_bias,
    omega,
    bucket,
    cotangent,
):
    qkv_full, out_full, up_full, down_full, gains_all, biases_all, bias_qkv, bias_up, rpe_all = (
        lax.all_gather(qkv_weight, ("dp", "feat"), axis=0, tiled=True),
        lax.all_gather(out_weight, ("dp", "feat"), axis=1, tiled=True),
        lax.all_gather(up_weight, ("dp", "feat"), axis=0, tiled=True),
        lax.all_gather(down_weight, ("dp", "feat"), axis=1, tiled=True),
        lax.all_gather(norm_gains, ("dp", "feat"), axis=1, tiled=True),
        lax.all_gather(row_biases, ("dp", "feat"), axis=1, tiled=True),
        lax.all_gather(qkv_bias, ("dp", "feat"), axis=2, tiled=True),
        lax.all_gather(up_bias, ("dp", "feat"), axis=1, tiled=True),
        lax.all_gather(rpe_bias, ("dp", "feat"), axis=1, tiled=True),
    )
    model_width = qkv_full.shape[0]
    head_cols = qkv_full.shape[2]
    local_heads = omega.shape[0]
    local_feats = omega.shape[2]
    rows_own = tokens.shape[0]
    rows_total = rows_own * lax.axis_size("feat")
    block_rows = min(512, rows_total // 4)
    blocks = rows_total // block_rows
    seq_length = rows_total // 4 * jnp.where(bucket[0] == 0, 1, jnp.where(bucket[0] == 1, 2, 4))
    block_count = seq_length // block_rows
    gain_rows = gains_all.astype(jnp.float32)
    bias_rows = biases_all.astype(jnp.float32)
    rpe_exp = jnp.exp(rpe_all.astype(jnp.float32))
    projected = jnp.dot(
        tokens, qkv_full.reshape(model_width, 3 * head_cols), preferred_element_type=jnp.float32
    )
    projected = projected + bias_qkv.reshape(-1).astype(jnp.float32)
    qkv_own = projected.astype(jnp.bfloat16)
    qkv_all = lax.all_gather(qkv_own, "feat", axis=0, tiled=True).reshape(
        rows_total, 3, local_heads, HEAD
    )
    queries = qkv_all[:, 0]
    keys_rows = qkv_all[:, 1]
    values_rows = qkv_all[:, 2]
    logits_query, unit_query, inverse_query = feature_logits(queries, omega)
    logits_key, unit_key, inverse_key = feature_logits(keys_rows, omega)
    feat_query = (jnp.exp(logits_query) * M ** (-0.5)).astype(jnp.bfloat16)
    feat_key = (jnp.exp(logits_key) * M ** (-0.5)).astype(jnp.bfloat16)
    numer_parts = []
    denom_parts = []
    for row_block in range(blocks):
        row_start = row_block * block_rows
        first_block = row_start // seq_length * block_count
        phi_rows = feat_query[:, :, row_start : row_start + block_rows]

        def visit(column_block, carried, phi_rows=phi_rows, row_start=row_start):
            numer_acc, denom_acc = carried
            col_start = column_block * block_rows
            phi_cols = lax.dynamic_slice_in_dim(feat_key, col_start, block_rows, 2)
            value_cols = lax.dynamic_slice_in_dim(values_rows, col_start, block_rows, 0)
            coefficient = block_coeff(
                rpe_exp, window_begin(row_start, col_start, block_rows, rows_total), block_rows
            )
            scores = jnp.einsum(
                "hmi,hmj->hij", phi_rows, phi_cols, preferred_element_type=jnp.float32
            )
            weights = (coefficient * scores).astype(jnp.bfloat16)
            numer_acc = numer_acc + jnp.einsum(
                "hij,jhe->ihe", weights, value_cols, preferred_element_type=jnp.float32
            )
            denom_acc = denom_acc + jnp.sum(weights.astype(jnp.float32), axis=-1)
            return (numer_acc, denom_acc)

        start_pair = (
            jnp.zeros((block_rows, local_heads, HEAD), jnp.float32),
            jnp.zeros((local_heads, block_rows), jnp.float32),
        )
        numer_block, denom_block = lax.fori_loop(
            first_block, first_block + block_count, visit, start_pair
        )
        numer_parts.append(numer_block)
        denom_parts.append(denom_block)
    numer_all = jnp.concatenate(numer_parts, axis=0).reshape(rows_total, head_cols)
    denom_all = jnp.concatenate(denom_parts, axis=1)
    numer_own, denom_own = (
        lax.psum_scatter(
            numer_all.astype(jnp.bfloat16), "feat", scatter_dimension=0, tiled=True
        ).astype(jnp.float32),
        lax.psum_scatter(
            denom_all.astype(jnp.bfloat16), "feat", scatter_dimension=1, tiled=True
        ).astype(jnp.float32),
    )
    denom_rows = denom_own.T
    quotient = numer_own.reshape(rows_own, local_heads, HEAD) / denom_rows[:, :, None]
    attn_low = quotient.reshape(rows_own, head_cols).astype(jnp.bfloat16)
    z_part = jnp.dot(attn_low, out_full, preferred_element_type=jnp.float32)
    mixed_z = lax.psum(z_part.astype(jnp.bfloat16), "heads").astype(jnp.float32) + bias_rows[0]
    first_out, normed_one, inverse_one = norm_forward(
        tokens.astype(jnp.float32) + mixed_z, gain_rows[0], bias_rows[1]
    )
    first_low = first_out.astype(jnp.bfloat16)
    pre_act = jnp.dot(first_low, up_full, preferred_element_type=jnp.float32) + bias_up.reshape(
        -1
    ).astype(jnp.float32)
    act_value, act_pull = jax.vjp(lambda inner: jax.nn.gelu(inner, approximate=False), pre_act)
    act_low = act_value.astype(jnp.bfloat16)
    ffn_part = jnp.dot(act_low, down_full, preferred_element_type=jnp.float32)
    ffn_out = lax.psum(ffn_part.astype(jnp.bfloat16), "heads").astype(jnp.float32) + bias_rows[2]
    final_rows, normed_two, inverse_two = norm_forward(
        first_out + ffn_out, gain_rows[1], bias_rows[3]
    )
    mixed = final_rows.astype(jnp.bfloat16)
    qkv_full, out_full, up_full, down_full, gains_all, rpe_all = (
        lax.all_gather(qkv_weight, ("dp", "feat"), axis=0, tiled=True),
        lax.all_gather(out_weight, ("dp", "feat"), axis=1, tiled=True),
        lax.all_gather(up_weight, ("dp", "feat"), axis=0, tiled=True),
        lax.all_gather(down_weight, ("dp", "feat"), axis=1, tiled=True),
        lax.all_gather(norm_gains, ("dp", "feat"), axis=1, tiled=True),
        lax.all_gather(rpe_bias, ("dp", "feat"), axis=1, tiled=True),
    )
    gain_rows = gains_all.astype(jnp.float32)
    rpe_exp = jnp.exp(rpe_all.astype(jnp.float32))
    upstream = cotangent.astype(jnp.float32)
    grad_gain_two = jnp.sum(upstream * normed_two, axis=0)
    grad_shift_two = jnp.sum(upstream, axis=0)
    resid_two = norm_backward(upstream, normed_two, inverse_two, gain_rows[1])
    resid_low = resid_two.astype(jnp.bfloat16)
    grad_bias_down = jnp.sum(resid_low.astype(jnp.float32), axis=0)
    grad_down = jnp.einsum("rf,rd->fd", act_low, resid_low, preferred_element_type=jnp.float32)
    grad_act = jnp.einsum("rd,fd->rf", resid_low, down_full, preferred_element_type=jnp.float32)
    grad_pre = act_pull(grad_act)[0].astype(jnp.bfloat16)
    grad_up = jnp.einsum("rd,rf->df", first_low, grad_pre, preferred_element_type=jnp.float32)
    grad_bias_up = jnp.sum(grad_pre.astype(jnp.float32), axis=0).reshape(bias_up.shape)
    first_back = lax.psum(
        jnp.einsum("rf,df->rd", grad_pre, up_full, preferred_element_type=jnp.float32).astype(
            jnp.bfloat16
        ),
        "heads",
    ).astype(jnp.float32)
    grad_first = resid_two + first_back
    grad_gain_one = jnp.sum(grad_first * normed_one, axis=0)
    grad_shift_one = jnp.sum(grad_first, axis=0)
    resid_one = norm_backward(grad_first, normed_one, inverse_one, gain_rows[0])
    resid_one_low = resid_one.astype(jnp.bfloat16)
    grad_bias_out = jnp.sum(resid_one_low.astype(jnp.float32), axis=0)
    grad_out = jnp.einsum("rc,rd->cd", attn_low, resid_one_low, preferred_element_type=jnp.float32)
    grad_attn = jnp.einsum(
        "rd,cd->rc", resid_one_low, out_full, preferred_element_type=jnp.float32
    ).reshape(rows_own, local_heads, HEAD)
    grad_numer = (grad_attn / denom_rows[:, :, None]).astype(jnp.bfloat16)
    grad_denom = (-jnp.sum(grad_attn * quotient, axis=-1) / denom_rows).astype(jnp.bfloat16)
    numer_grad_all, denom_grad_all = (
        lax.all_gather(grad_numer.reshape(rows_own, head_cols), "feat", axis=0, tiled=True),
        lax.all_gather(grad_denom.T, "feat", axis=1, tiled=True),
    )
    numer_grad_all = numer_grad_all.reshape(rows_total, local_heads, HEAD)
    dphi_key = jnp.zeros((local_heads, local_feats, rows_total), jnp.float32)
    dvalues = jnp.zeros((rows_total, local_heads, HEAD), jnp.float32)
    grad_rpe = jnp.zeros(rpe_exp.shape, jnp.float32)
    dquery_parts = []
    for row_block in range(blocks):
        row_start = row_block * block_rows
        first_block = row_start // seq_length * block_count
        phi_rows = feat_query[:, :, row_start : row_start + block_rows]
        numer_rows = numer_grad_all[row_start : row_start + block_rows]
        denom_cols = denom_grad_all[:, row_start : row_start + block_rows].astype(jnp.float32)

        def visit_back(
            column_block,
            carried,
            phi_rows=phi_rows,
            row_start=row_start,
            numer_rows=numer_rows,
            denom_cols=denom_cols,
        ):
            dquery_acc, dkey_all, dvalue_all, drpe_all = carried
            col_start = column_block * block_rows
            phi_cols = lax.dynamic_slice_in_dim(feat_key, col_start, block_rows, 2)
            value_cols = lax.dynamic_slice_in_dim(values_rows, col_start, block_rows, 0)
            window_start = window_begin(row_start, col_start, block_rows, rows_total)
            coefficient = block_coeff(rpe_exp, window_start, block_rows)
            scores = jnp.einsum(
                "hmi,hmj->hij", phi_rows, phi_cols, preferred_element_type=jnp.float32
            )
            weights = (coefficient * scores).astype(jnp.bfloat16)
            grad_weights = (
                jnp.einsum(
                    "ihe,jhe->hij", numer_rows, value_cols, preferred_element_type=jnp.float32
                )
                + denom_cols[:, :, None]
            )
            dvalue_block = jnp.einsum(
                "hij,ihe->jhe", weights, numer_rows, preferred_element_type=jnp.float32
            )
            dvalue_all = lax.dynamic_update_slice_in_dim(
                dvalue_all,
                lax.dynamic_slice_in_dim(dvalue_all, col_start, block_rows, 0) + dvalue_block,
                col_start,
                0,
            )
            grad_scores = (grad_weights * coefficient).astype(jnp.bfloat16)
            diagonal = diagonal_sums(grad_weights * scores * coefficient, block_rows)
            drpe_all = lax.dynamic_update_slice_in_dim(
                drpe_all,
                lax.dynamic_slice_in_dim(drpe_all, window_start, 2 * block_rows - 1, 1) + diagonal,
                window_start,
                1,
            )
            dquery_acc = dquery_acc + jnp.einsum(
                "hij,hmj->hmi", grad_scores, phi_cols, preferred_element_type=jnp.float32
            )
            dkey_block = jnp.einsum(
                "hij,hmi->hmj", grad_scores, phi_rows, preferred_element_type=jnp.float32
            )
            dkey_all = lax.dynamic_update_slice_in_dim(
                dkey_all,
                lax.dynamic_slice_in_dim(dkey_all, col_start, block_rows, 2) + dkey_block,
                col_start,
                2,
            )
            return (dquery_acc, dkey_all, dvalue_all, drpe_all)

        start_state = (
            jnp.zeros((local_heads, local_feats, block_rows), jnp.float32),
            dphi_key,
            dvalues,
            grad_rpe,
        )
        dquery_block, dphi_key, dvalues, grad_rpe = lax.fori_loop(
            first_block, first_block + block_count, visit_back, start_state
        )
        dquery_parts.append(dquery_block)
    dphi_query = jnp.concatenate(dquery_parts, axis=2)
    grad_query = feature_back(dphi_query, logits_query, unit_query, inverse_query, omega)
    grad_key = feature_back(dphi_key, logits_key, unit_key, inverse_key, omega)
    grad_qkv_all = jnp.stack((grad_query, grad_key, dvalues), axis=1).reshape(
        rows_total, 3 * head_cols
    )
    grad_qkv_own = lax.psum_scatter(
        grad_qkv_all.astype(jnp.bfloat16), "feat", scatter_dimension=0, tiled=True
    )
    grad_bias_qkv = jnp.sum(grad_qkv_own.astype(jnp.float32), axis=0).reshape(bias_qkv.shape)
    grad_qkv_weight = jnp.einsum(
        "rd,rc->dc", tokens, grad_qkv_own, preferred_element_type=jnp.float32
    ).reshape(qkv_full.shape)
    input_terms = jnp.einsum(
        "rc,dc->rd",
        grad_qkv_own,
        qkv_full.reshape(model_width, 3 * head_cols),
        preferred_element_type=jnp.float32,
    )
    grad_tokens = resid_one + lax.psum(input_terms.astype(jnp.bfloat16), "heads").astype(
        jnp.float32
    )
    grad_gains = jnp.stack((grad_gain_one, grad_gain_two), axis=0)
    grad_shifts = jnp.stack((grad_bias_out, grad_shift_one, grad_bias_down, grad_shift_two), axis=0)
    (
        sent_qkv,
        sent_out,
        sent_up,
        sent_down,
        sent_gains,
        sent_shifts,
        sent_bias_qkv,
        sent_bias_up,
        sent_rpe,
    ) = (
        lax.psum_scatter(
            grad_qkv_weight.astype(jnp.bfloat16), ("dp", "feat"), scatter_dimension=0, tiled=True
        ).astype(jnp.float32),
        lax.psum_scatter(
            grad_out.astype(jnp.bfloat16), ("dp", "feat"), scatter_dimension=1, tiled=True
        ).astype(jnp.float32),
        lax.psum_scatter(
            grad_up.astype(jnp.bfloat16), ("dp", "feat"), scatter_dimension=0, tiled=True
        ).astype(jnp.float32),
        lax.psum_scatter(
            grad_down.astype(jnp.bfloat16), ("dp", "feat"), scatter_dimension=1, tiled=True
        ).astype(jnp.float32),
        lax.psum_scatter(
            grad_gains.astype(jnp.bfloat16), ("dp", "feat"), scatter_dimension=1, tiled=True
        ).astype(jnp.float32),
        lax.psum_scatter(
            grad_shifts.astype(jnp.bfloat16), ("dp", "feat"), scatter_dimension=1, tiled=True
        ).astype(jnp.float32),
        lax.psum_scatter(
            grad_bias_qkv.astype(jnp.bfloat16), ("dp", "feat"), scatter_dimension=2, tiled=True
        ).astype(jnp.float32),
        lax.psum_scatter(
            grad_bias_up.astype(jnp.bfloat16), ("dp", "feat"), scatter_dimension=1, tiled=True
        ).astype(jnp.float32),
        lax.psum_scatter(
            grad_rpe.astype(jnp.bfloat16), ("dp", "feat"), scatter_dimension=1, tiled=True
        ).astype(jnp.float32),
    )
    return (
        mixed,
        grad_tokens,
        sent_qkv,
        sent_bias_qkv,
        sent_out,
        sent_gains,
        sent_shifts,
        sent_up,
        sent_bias_up,
        sent_down,
        sent_rpe,
    )


MESH = pl.DeviceIdType.MESH
PLANES = 4
SENDS, RECEIVES = 86, 202
F32 = jnp.float32
BF16 = jnp.bfloat16
SCALE = HEAD ** (-0.25)
NT = (((1,), (1,)), ((), ()))
TN = (((0,), (0,)), ((), ()))
NN = (((1,), (0,)), ((), ()))


def dot(left, right, dims=NN):
    return lax.dot_general(left, right, dims, preferred_element_type=F32)


def split_dot(left, right, dims=NN):
    high = left.astype(BF16)
    rest = (left - high.astype(F32)).astype(BF16)
    return dot(high, right, dims) + dot(rest, right, dims)


def iota(shape, axis):
    return lax.broadcasted_iota(jnp.int32, shape, axis)


class Sems:
    def __init__(self):
        self.used = 0

    def take(self, count=1):
        first = self.used
        self.used += count
        return first


def layer_kernel(
    tok, wq_h, qb_h, wo_h, gain_h, bias_h, wu_h, ub_h, wd_h, rpe_h, om_h, bk_h, cot,
    mixed_h, gtok_h, gq_h, gqb_h, go_h, ggain_h, gbias_h, gu_h, gub_h, gd_h, grpe_h,
    qb_v, gain_v, bias_v, ub_v, rpe_v, om_v, bk_v, small_s, om_s,
    mixed_o, gq_o, gqb_o, go_o, ggain_o, gbias_o, gu_o, gub_o, gd_o, grpe_o,
    wq, wo, wu, wd, small, om2, xg, cotb,
    qkv, phi, ex, unit, inv, r0, pp, num, den, quo, att, attf,
    pb, rb_f, rb_d, rb_i, fb, hid, dgel, efb, dub, dzb, acc,
    fst, n1, i1, dr, summed, dat_s, dat, anti, ones64, rows_v,
    dn, dd, ds_, gg, dph, dvv, dqkv, xt, ppt,
    g_k, g_v, g_o, g_u, g_d, r_k, r_v, r_o, r_u, r_d, rz_k, rz_v, rz_o, rz_u, rz_d, cb_k, cb_v, cb_o, cb_u, cb_d,
    fs, xs_k, xs_v, xs_o, xs_u, xs_d, xr_k, xr_v, xr_o, xr_u, xr_d,
    sd, sd_r, st_a, st_b, work_a, work_b, recv_a, recv_b, swap, mix_s, gt_r,
    ss, rs, ls,
):
    dp, y, c = lax.axis_index("dp"), lax.axis_index("heads"), lax.axis_index("feat")
    z, x = dp // 2, dp % 2
    shard = 2 * dp + c

    def dev(zz, xx, yy, cc):
        return {"dp": zz * 2 + xx, "heads": yy, "feat": cc}

    sib, xn, yn, dg = dev(z, x, y, 1 - c), dev(z, 1 - x, y, c), dev(z, x, 1 - y, c), dev(z, 1 - x, 1 - y, c)
    xs_dev, ds_dev = dev(z, 1 - x, y, 1 - c), dev(z, 1 - x, 1 - y, 1 - c)

    barrier = pltpu.get_barrier_semaphore()
    for other in (sib, xn, yn, dg, xs_dev, ds_dev, dev(z, x, 1 - y, 1 - c)):
        pl.semaphore_signal(barrier, inc=1, device_id=other, device_id_type=MESH)
    for zz in range(PLANES):
        @pl.when(z != zz)
        def _(zz=zz):
            pl.semaphore_signal(barrier, inc=1, device_id=dev(zz, x, y, c), device_id_type=MESH)

    s_sems, r_sems, locals_ = Sems(), Sems(), Sems()
    pending = []

    def bring(src, dst, cond=None):
        copy = pltpu.make_async_copy(src, dst, ls.at[locals_.take()])
        if cond is None:
            copy.start()
            return copy.wait
        pl.when(cond)(copy.start)
        return lambda: pl.when(cond)(copy.wait)

    home = c == x
    away = c != x
    own_block = 2 * x + y

    def half_cols(half, width):
        return pl.ds(pl.multiple_of(half * width, width), width)

    def rows_of(index, count):
        return pl.ds(pl.multiple_of(index * count, count), count)

    in_o = bring(wo_h.at[:, half_cols(x, 256)], wo.at[own_block, 2 * z + x, c])
    in_q = bring(wq_h.at[:, :, half_cols(x, 256)], wq.at[:, 2 * z + x, c])
    in_small = [
        bring(src, dst)
        for src, dst in (
            (gain_h, gain_v), (bias_h, bias_v), (rpe_h, rpe_v), (qb_h, qb_v), (ub_h, ub_v), (om_h, om_v), (bk_h, bk_v),
        )
    ]
    in_tok = bring(tok, xg.at[rows_of(c, 256)], home)
    in_u = bring(wu_h.at[:, half_cols(x, 1024)], wu.at[2 * z + x, c])
    in_d = bring(wd_h.at[:, half_cols(x, 1024)], wd.at[2 * z + x, c])
    in_cot = bring(cot.at[rows_of(y, 128)], cotb, home)

    plane = (dg, xn, yn)
    plane_block = (2 * (1 - x) + 1 - y, 2 * (1 - x) + y, 2 * x + 1 - y)

    def rc(src, dst, s, r, device):
        return pltpu.make_async_remote_copy(
            src_ref=src, dst_ref=dst, send_sem=ss.at[s], recv_sem=rs.at[r], device_id=device, device_id_type=MESH
        )

    def send(src, dst, s, r, device, cond=None):
        def go():
            rc(src, dst, s, r, device).start()

        def done():
            rc(src, dst, s, r, device).wait_send()

        if cond is None:
            go()
            pending.append(done)
        else:
            pl.when(cond)(go)
            pending.append(lambda: pl.when(cond)(done))

    def got(dst, r):
        rc(dst, dst, r, r, sib).wait_recv()

    def take(count=1):
        return s_sems.take(count), r_sems.take(count)

    def give(src, dst, pair, device, cond=None, s=0, r=0):
        send(src, dst, pair[0] + s, pair[1] + r, device, cond)

    def valid(dz):
        return jnp.logical_and(z + dz >= 0, z + dz < PLANES)

    def by_plane(table):
        found = []
        for k in range(PLANES):
            block = jnp.int32(table[0][k])
            for zz in range(1, PLANES):
                block = jnp.where(z == zz, table[zz][k], block)
            found.append(block)
        return found

    arrive = by_plane(((0, 1, 2, 3), (1, 2, 3, 0), (2, 1, 0, 3), (3, 2, 1, 0)))
    leave = by_plane(((3, 2, 1, 0), (0, 3, 2, 1), (3, 0, 1, 2), (0, 1, 2, 3)))

    def at_step(blocks, k):
        block = blocks[0]
        for i in range(1, PLANES):
            block = jnp.where(k == i, blocks[i], block)
        return block

    def cols256(n):
        return pl.ds(pl.multiple_of(n * 256, 256), 256)

    pl.semaphore_wait(barrier, 10)

    inner, outer = (z == 1) | (z == 2), (z == 0) | (z == 3)

    class Item:
        def __init__(self, ref, kind, whole=True):
            self.ref, self.kind, self.whole = ref, kind, whole
            self.z_out, self.c_out = s_sems.take(), s_sems.take()
            self.zs, self.sb = r_sems.take(PLANES), r_sems.take(1 if whole else PLANES)

        def block(self, zz, cc):
            if self.kind == "both":
                return self.ref.at[pl.ds(2 * zz, 2), cc]
            at = 2 * zz + (x if self.kind == "own" else 1 - x)
            return self.ref.at[:, at, cc] if len(self.ref.shape) == 5 else self.ref.at[at, cc]

        def some(self, count):
            if self.kind == "both":
                return self.ref.at[pl.ds(0, count)]
            return self.ref.at[:, pl.ds(0, count), 0] if len(self.ref.shape) == 5 else self.ref.at[pl.ds(0, count), 0]

        def onward(self, n, step):
            here = self.block(n, c)
            rc(here, here, self.z_out, self.zs + n, dev(z + step, x, y, c)).start()

        def start(self):
            pl.when(z == 0)(lambda: self.onward(z, 2))
            pl.when(z == 3)(lambda: self.onward(z, -2))
            pl.when(z > 0)(lambda: self.onward(z, -1))
            pl.when(z < PLANES - 1)(lambda: self.onward(z, 1))
            mine = self.block(z, c)
            rc(mine, mine, self.c_out, self.sb if self.whole else self.sb + z, sib).start()

        def pump_step(self, n):
            here = self.block(n, c)

            @pl.when(n != z)
            def _():
                got(here, self.zs + n)
                pl.when(jnp.logical_and(z == 1, n > z))(lambda: self.onward(n, -1))
                pl.when(jnp.logical_and(z == 2, n < z))(lambda: self.onward(n, 1))
                rc(here, here, self.c_out, self.sb if self.whole else self.sb + n, sib).start()

        def pump_done(self):
            def sent(sem, count):
                rc(self.some(count), self.some(count), sem, 0, sib).wait_send()

            pending.append(lambda: sent(self.c_out, 4))
            pending.append(lambda: pl.when(outer)(lambda: sent(self.z_out, 2)))
            pending.append(lambda: pl.when(inner)(lambda: sent(self.z_out, 4)))

        def pump(self, where):
            @pl.when(where)
            def _():
                for k in range(1, PLANES):
                    self.pump_step(arrive[k])

            if where is outer:
                self.pump_done()

        def need_step(self, n):
            got(self.block(n, 1 - c), self.sb + n)

        def need(self):
            got(self.some(PLANES), self.sb)

    half_of = {}

    def place(ref, xx):
        return ref.at[:, 2 * z + xx, c] if len(ref.shape) == 5 else ref.at[2 * z + xx, c]

    def give_half(name, src, ref):
        i = take()
        half_of[name] = (ref, i[1])
        give(src, place(ref, x), i, xn)

    def have_half(name):
        ref, i = half_of[name]
        got(place(ref, 1 - x), i)

    wo_own = wo.at[own_block]
    i_oh = take()
    give(wo_h.at[:, half_cols(1 - x, 256)], wo.at[2 * (1 - x) + y, 2 * z + x, c], i_oh, xn)
    give_half("q", wq_h.at[:, :, half_cols(1 - x, 256)], wq)
    i_tok, i_tx, i_ty = take(), take(2), take(2)
    give(tok, xg.at[rows_of(c, 256)], i_tok, sib, away)
    give(tok.at[rows_of(y, 128)], xg.at[rows_of(2 * c + y, 128)], i_tx, dev(z, 1 - x, y, x), None, 0, c)
    it_oa, it_ob = Item(wo_own, "own"), Item(wo_own, "other")
    it_qa, it_s, it_qb = Item(wq, "own"), Item(small, "both"), Item(wq, "other")
    it_ua, it_ub, it_da, it_db = Item(wu, "own"), Item(wu, "other"), Item(wd, "own", False), Item(wd, "other", False)
    in_o()
    it_oa.start()
    in_q()
    it_qa.start()

    for done in in_small:
        done()

    def pick(shape, hit):
        return jnp.where(hit(iota(shape, 0), iota(shape, 1)), 1.0, 0.0)

    vec_sel = pick((64, 128), lambda k, l: l == c * 64 + k).astype(BF16)
    rpe_sel = pick((64, 128), lambda k, l: l == (1 - c) * 64 + 63 - k).astype(BF16)
    bias_sel = [pick((4, 128), lambda k, l, par=par: l == par * 64 + 4 * shard + k).astype(BF16) for par in range(2)]
    rpe_rows = dot(rpe_v[...], rpe_sel)
    level = jnp.full((1, 128), bk_v[0].astype(F32))
    top = jnp.concatenate(
        [dot(gain_v[...], vec_sel), dot(bias_v[...], vec_sel), level, jnp.zeros((1, 128), F32)], axis=0
    )

    def spread(values):
        rows = values.shape[1]
        even = (iota((rows, 1), 0) % 2) == 0
        wide = jnp.where(even, dot(values, bias_sel[0], TN), dot(values, bias_sel[1], TN))
        return dot(pick((rows // 2, rows), lambda k, l: l // 2 == k).astype(BF16), wide.astype(BF16))

    up_rows = spread(ub_v[...])
    qkv_rows = [spread(qb_v[p]) for p in range(3)]
    for half in range(2):
        mine = [rows[2 * half : 2 * half + 2] for rows in qkv_rows] + [jnp.zeros((2, 128), F32)]
        position = jnp.concatenate([rpe_rows[4 * half : 4 * half + 4], jnp.zeros((4, 128), F32)], axis=0)
        small_s[half] = jnp.concatenate(
            [top, position] + mine + [up_rows[8 * half : 8 * half + 8]], axis=0
        ).astype(BF16)
    small[2 * z + x, c] = small_s[x]
    give_half("s", small_s.at[1 - x], small)
    for h in range(4):
        sel = pick((32, 256), lambda k, l: l == h * 64 + c * 32 + k).astype(BF16)
        om_s[h * 64 : (h + 1) * 64] = dot(om_v[4 * x + h], sel, TN).astype(BF16)
    i_om = take()
    give(om_s, om2, i_om, sib)
    give_half("u", wu_h.at[:, half_cols(1 - x, 1024)], wu)

    same = (iota((256, 256), 0) // HEAD) == (iota((256, 256), 1) // HEAD)
    ones64[...] = jnp.where(same, 1.0, 0.0).astype(BF16)
    anti[...] = jnp.where(iota((128, 128), 0) + iota((128, 128), 1) == 127, 1.0, 0.0).astype(BF16)

    it_oa.pump(inner)
    got(wo.at[own_block, 2 * z + 1 - x, c], i_oh[1])
    it_ob.start()
    have_half("q")
    it_qb.start()
    it_qa.pump(inner)
    it_ob.pump(inner)
    it_qb.pump(inner)

    @pl.when(away)
    def _():
        for f in range(2):
            got(xg.at[rows_of(2 * f + y, 128)], i_tx[1] + f)

    for f in range(2):
        part = xg.at[rows_of(2 * f + y, 128)]
        give(part, part, i_ty, yn, away, f, f)
    it_oa.pump(outer)
    it_ob.pump(outer)
    i_oq, i_os = take(3), take(3)
    quarter = wo.at[own_block, :, c]
    give(quarter, quarter, i_oq, yn, None, 2, 2)
    give(quarter, quarter, i_oq, xn, None, 1, 1)
    give_half("d", wd_h.at[:, half_cols(1 - x, 1024)], wd)
    have_half("s")
    it_s.start()
    in_u()
    it_ua.start()
    it_s.pump(inner)
    it_qa.pump(outer)
    have_half("u")
    it_ub.start()
    in_d()
    it_da.start()
    it_qb.pump(outer)

    def other_quarter(slot):
        part = wo.at[plane_block[slot], :, c]
        got(part, i_oq[1] + slot)
        give(part, part, i_os, sib, None, slot, slot)
        return part

    it_s.pump(outer)

    it_s.need()
    for t in range(8):
        tile = small[t, 0].astype(F32) + small[t, 1].astype(F32)
        rows_v[0:8, t * 128 : (t + 1) * 128] = tile[0:8]
        rows_v[8:16, (7 - t) * 128 : (8 - t) * 128] = tile[8:16]
        total = tile[16:32] if t == 0 else total + tile[16:32]
    for r in range(6):
        rows_v[16:17, r * 128 : (r + 1) * 128] = total[r : r + 1]
    for r in range(8):
        rows_v[17:18, r * 128 : (r + 1) * 128] = total[8 + r : 9 + r]
    level = small[2 * z + c, 0][6:7].astype(F32)
    wide1 = jnp.where(level > 0.5, 1.0, 0.0)
    wide2 = jnp.where(level > 1.5, 1.0, 0.0)
    one_row = jnp.ones((1, 128), F32)

    def mask_row(bi):
        parts = [one_row if bj == bi else (wide1 if bj // 2 == bi // 2 else wide2) for bj in range(4)]
        return jnp.concatenate(parts, axis=1)

    masks = [mask_row(bi) for bi in range(4)]

    def coeff_body(h, carry):
        row = jnp.exp(rows_v[pl.ds(8 + h, 1), :])
        r0[h] = pltpu.roll(jnp.broadcast_to(row, (128, 1024)), 1, 1, stride=1, stride_axis=0)
        return carry

    lax.fori_loop(0, 4, coeff_body, 0)
    num[...] = jnp.zeros_like(num)
    den[...] = jnp.zeros_like(den)

    in_tok()
    pl.when(home)(lambda: got(xg.at[rows_of(1 - c, 256)], i_tok[1]))

    @pl.when(away)
    def _():
        for f in range(2):
            got(xg.at[rows_of(2 * f + 1 - y, 128)], i_ty[1] + f)

    other_quarter(2)
    part = other_quarter(1)
    give(part, part, i_oq, yn, None, 0, 0)
    it_ua.pump(inner)
    it_qa.need()
    it_qb.need()

    def qkv_body(p, carry):
        qkv[p] = (dot(xg[...], wq[p].reshape(1024, 256)) + rows_v[16:17, cols256(p)]).astype(BF16)
        return carry

    lax.fori_loop(0, 3, qkv_body, 0)
    got(om2, i_om[1])
    om2[...] = om2[...] + om_s[...]

    def feature_body(t, carry):
        wide = qkv[t].astype(F32)
        sums = split_dot(wide * wide, ones64[...])
        inverse = lax.rsqrt(sums * (1.0 / HEAD) + UNIT_EPS)
        units = wide * inverse
        logits = SCALE * split_dot(units, om2[...]) - 0.5 * SCALE * SCALE * (sums * inverse * inverse)
        value = jnp.exp(logits) * M ** (-0.5)
        ex[t] = value
        unit[t] = units
        inv[t] = inverse
        phi[t] = value.astype(BF16)
        return carry

    lax.fori_loop(0, 2, feature_body, 0)
    lane_head = iota((1, 128), 1) // HEAD

    def head_cols(h):
        return pl.ds(pl.multiple_of((h // 2) * 128, 128), 128), (lane_head == h % 2)

    def head_body(h, carry):
        cols, mine = head_cols(h)
        keep = jnp.where(mine, 1.0, 0.0).astype(BF16)
        scores = dot(phi[0, :, cols] * keep, phi[1, :, cols], NT)
        for b in range(4):
            coefficient = r0[h, :, 512 - 128 * b : 1024 - 128 * b] * masks[b]
            pp[h, b * 128 : (b + 1) * 128] = (scores[b * 128 : (b + 1) * 128] * coefficient).astype(BF16)
        right = jnp.concatenate([qkv[2, :, cols] * keep, jnp.broadcast_to(keep, (512, 128))], axis=1)
        both = dot(pp[h], right)
        num[:, cols] += both[:, :128]
        den[:, cols] += both[:, 128:]
        return carry

    i_at = [take(3), take(3)]

    def tile_of(ref, block, t):
        return ref.at[block, :, t * 128 : (t + 1) * 128]

    for t in range(2):
        lax.fori_loop(2 * t, 2 * t + 2, head_body, 0)
        cols = slice(t * 128, (t + 1) * 128)
        quo[:, cols] = num[:, cols] / den[:, cols]
        att[:, :, cols] = quo[:, cols].astype(BF16).reshape(4, 128, 128)
        for slot in range(3):
            give(tile_of(att, plane_block[slot], t), tile_of(attf, own_block, t), i_at[t], plane[slot], None, slot, slot)
    have_half("d")
    it_db.start()
    i_cot = take()
    give(cot.at[rows_of(y, 128)], cotb, i_cot, xs_dev, away)
    it_ub.pump(inner)
    other_quarter(0)
    it_oa.need()
    it_ob.need()

    def out_part(rows, block):
        return dot(rows, wo[block].reshape(1024, 256), NT)

    mixed_z = out_part(att[own_block], own_block)
    for slot in (2, 1, 0):
        got(wo.at[plane_block[slot], :, 1 - c], i_os[1] + slot)
        for t in range(2):
            got(tile_of(attf, plane_block[slot], t), i_at[t][1] + slot)
        mixed_z = mixed_z + out_part(attf[plane_block[slot]], plane_block[slot])

    def norm(values):
        centred = values - jnp.mean(values, axis=-1, keepdims=True)
        inverse = lax.rsqrt(jnp.mean(centred * centred, axis=-1, keepdims=True) + EPSILON)
        return centred * inverse, inverse

    residual = mixed_z + xg[rows_of(own_block, 128)].astype(F32) + rows_v[2:3, :]
    normed, inverse = norm(residual)
    first = normed * rows_v[0:1, :] + rows_v[3:4, :]
    fb[own_block] = first.astype(BF16)

    class RelayScatter:
        def __init__(self, ref, order, last_direct=False):
            self.ref, self.out, self.order, self.relayed = ref, s_sems.take(), order, 3 if last_direct else 4
            self.near, self.far, self.last = r_sems.take(4), r_sems.take(4), r_sems.take(4)

        def cols(self, k):
            return cols256(self.order[k])

        def part(self, k, value):
            cols = cols256(at_step(self.order, k))
            pb[:, :, cols] = value.astype(BF16).reshape(4, 128, 256)

            def out(block, slot, sem, device):
                rc(pb.at[block, :, cols], self.ref.at[slot, :, cols], self.out, sem + k, device).start()

            @pl.when(k < self.relayed)
            def _():
                even = k % 2 == 0
                beside = dev(z, jnp.where(even, 1 - x, x), jnp.where(even, y, 1 - y), c)
                out(plane_block[0], 1, self.far, beside)
                out(jnp.where(even, plane_block[1], plane_block[2]), 0, self.near, beside)

            @pl.when(k >= self.relayed)
            def _():
                out(plane_block[0], 1, self.far, dg)
                out(plane_block[1], 0, self.near, xn)
                out(plane_block[2], 2, self.last, yn)

        def pass_on(self, k):
            cols, slot = self.cols(k), 2 - k % 2
            part = self.ref.at[1, :, cols]
            got(part, self.far + k)
            part[...] = (part[...].astype(F32) + pb[plane_block[slot], :, cols].astype(F32)).astype(BF16)
            rc(part, self.ref.at[2, :, cols], self.out, self.last + k, plane[slot]).start()

        def total(self):
            for k in range(4):
                cols = self.cols(k)
                got(self.ref.at[0, :, cols], self.near + k)
                if k >= self.relayed:
                    got(self.ref.at[1, :, cols], self.far + k)
                got(self.ref.at[2, :, cols], self.last + k)
                value = pb[own_block, :, cols].astype(F32) + self.ref[0, :, cols].astype(F32)
                value = value + self.ref[2, :, cols].astype(F32)
                summed[:, cols] = value + self.ref[1, :, cols].astype(F32) if k >= self.relayed else value
            return summed[...]

        def sent(self):
            rc(self.ref, self.ref, self.out, 0, sib).wait_send()

    class Gather:
        def __init__(self, ref, order):
            self.ref, self.out, self.base, self.order = ref, s_sems.take(), r_sems.take(5), order
            pending.append(lambda: rc(ref.at[pl.ds(0, 3)], ref.at[pl.ds(0, 3)], self.out, 0, sib).wait_send())

        def start(self):
            for half in range(2):
                for slot in range(3):
                    mine = self.ref.at[own_block, :, self.half_cols(half)]
                    rc(mine, mine, self.out, self.base + 3 + half, plane[slot]).start()
            for k in range(1, 4):
                for slot in range(3):
                    mine = self.ref.at[own_block, :, cols256(self.order[k])]
                    rc(mine, mine, self.out, self.base + k - 1, plane[slot]).start()

        def half_cols(self, half):
            return pl.ds(pl.multiple_of(self.order[0] * 256 + half * 128, 128), 128)

        def need_half(self, half):
            got(self.ref.at[pl.ds(0, 3), :, self.half_cols(half)], self.base + 3 + half)

        def need(self, k):
            got(self.ref.at[pl.ds(0, 3), :, cols256(at_step(self.order, k))], self.base + k - 1)

    class RelayGather:
        def __init__(self, ref, order):
            self.ref, self.out, self.base, self.order = ref, s_sems.take(), r_sems.take(12), order
            pending.append(lambda: rc(ref.at[pl.ds(0, 3)], ref.at[pl.ds(0, 3)], self.out, 0, sib).wait_send())

        def piece(self, slot, n):
            return self.ref.at[plane_block[slot], :, cols256(n)]

        def start(self):
            for n in self.order:
                mine = self.ref.at[own_block, :, cols256(n)]
                for slot in (1, 2):
                    rc(mine, mine, self.out, self.base + slot * 4 + n, plane[slot]).start()

        def pass_on(self, k):
            n, slot = self.order[k], 1 + k % 2
            part = self.piece(slot, n)
            got(part, self.base + slot * 4 + n)
            rc(part, part, self.out, self.base + n, plane[3 - slot]).start()

        def need(self, k):
            n, slot = self.order[k], 2 - k % 2
            got(self.piece(slot, n), self.base + slot * 4 + n)
            got(self.piece(0, n), self.base + n)

    g_first = RelayGather(fb, range(4))
    g_first.start()
    it_da.pump(inner)
    g_first.pass_on(0)
    it_db.pump(inner)
    for k in range(1, 4):
        g_first.pass_on(k)
    it_ua.pump(outer)
    it_ub.pump(outer)
    fst[...] = first
    n1[...] = normed
    i1[...] = jnp.broadcast_to(inverse, (128, 128))

    def d_cols(ref, m):
        return ref[:, :, cols256(m)].reshape(512, 256)

    acc[...] = jnp.zeros_like(acc)
    it_ua.need()
    it_ub.need()

    for k in range(4):
        g_first.need(k)
        left = d_cols(fb, k)
        if k == 2:
            it_da.pump(outer)

        def hidden_part(j, carry, k=k, left=left):
            cols = cols256(j)
            acc[:, cols] += dot(left, wu[2 * k : 2 * k + 2, :, :, cols].reshape(256, 256))
            return carry

        lax.fori_loop(0, 4, hidden_part, 0)

    def hidden_body(n, carry):
        cols = cols256(n)
        pre = acc[:, cols] + rows_v[17:18, cols]
        cdf = 0.5 * (1.0 + lax.erf(pre * 0.7071067811865476))
        hid[:, cols] = (pre * cdf).astype(BF16)
        dgel[:, cols] = cdf + pre * (0.3989422804014327 * jnp.exp(-0.5 * pre * pre))
        return carry

    lax.fori_loop(0, 4, hidden_body, 0)
    sc_f = RelayScatter(rb_f, arrive, True)

    def down_part(k, carry):
        n = at_step(arrive, k)
        pl.when(outer)(lambda: it_db.pump_step(n))
        it_da.need_step(n)
        it_db.need_step(n)
        sc_f.part(k, dot(hid[...], wd[pl.ds(2 * n, 2)].reshape(256, 1024), NT))
        return carry

    lax.fori_loop(0, 4, down_part, 0)
    it_db.pump_done()
    for k in range(3):
        sc_f.pass_on(k)
    pl.when(away)(lambda: got(cotb, i_cot[1]))
    in_cot()
    upstream = cotb[...].astype(F32)

    def down(values):
        return jnp.sum(values, axis=0, keepdims=True)

    sd[5:6, :] = down(upstream)
    acc[...] = jnp.zeros_like(acc)
    second = fst[...] + sc_f.total() + rows_v[4:5, :]
    normed2, inverse2 = norm(second)

    def norm_back(upstream, normed, inverse, gain):
        scaled = upstream * gain
        mean = jnp.mean(scaled, axis=-1, keepdims=True)
        slope = jnp.mean(scaled * normed, axis=-1, keepdims=True)
        return inverse * (scaled - mean - normed * slope)

    err = norm_back(upstream, normed2, inverse2, rows_v[1:2, :])
    efb[own_block] = err.astype(BF16)
    g_ef = Gather(efb, leave)
    g_ef.start()
    mix_s[...] = (normed2 * rows_v[1:2, :] + rows_v[5:6, :]).astype(BF16)
    dr[...] = err
    sd[1:2, :] = down(upstream * normed2)
    sd[4:5, :] = down(err.astype(BF16).astype(F32))
    sc_f.sent()

    class Owner:
        def __init__(self, dst, pieces):
            self.dst, self.width = dst, 1024 // pieces
            self.ids = [take(2) for _ in range(pieces)]

        def part(self, half, n):
            return self.dst.at[rows_of(half, 128), n * self.width : (n + 1) * self.width]

        def start(self, src, n):
            cols = slice(n * self.width, (n + 1) * self.width)

            @pl.when(home)
            def _():
                self.dst[rows_of(y, 128), cols] = src[:, cols]

            give(src.at[:, cols], self.part(y, n), self.ids[n], yn, home, 1, 1)
            give(src.at[:, cols], self.part(y, n), self.ids[n], xs_dev, away, 0, 0)

        def pass_on(self, n):
            part = self.part(y, n)
            pl.when(away)(lambda: got(part, self.ids[n][1]))
            give(part, part, self.ids[n], yn, away, 1, 1)

        def need(self, n):
            got(self.part(1 - y, n), self.ids[n][1] + 1)

    own_mix = Owner(mixed_o, 1)
    own_mix.start(mix_s, 0)

    class Grad:
        def __init__(self, g, r, rz, cb, xs, xr, first):
            self.first = first
            self.g, self.r, self.rz, self.cb, self.xs, self.xr = g, r, rz, cb, xs, xr
            self.d, self.z, self.k, self.x = r_sems.take(4), r_sems.take(2), r_sems.take(2), take()
            self.mine = z // 2
            self.d_out, self.z_out = s_sems.take(), s_sems.take()
            self.width = r.shape[-1]

        def give(self, m):
            rc(self.g.at[m, :, 1 - c], self.r.at[m], self.d_out, self.d + m, sib).start()

        def pair_step(self, m):
            got(self.r.at[m], self.d + m)
            self.r[m] = (self.g[m, :, c].astype(F32) + self.r[m].astype(F32)).astype(BF16)
            far = jnp.abs(m - z)
            part = self.r.at[m]
            beside = dev(jnp.where(z == 0, 1, jnp.where(z == 1, 0, jnp.where(z == 2, 3, 2))), x, y, c)

            @pl.when(jnp.logical_or(outer if self.first else False, m == jnp.where(z == 1, 0, 3)) & (far == 1))
            def _():
                rc(part, self.rz.at[self.mine], self.z_out, self.z + self.mine, beside).start()

            for slot in range(2):
                @pl.when(outer & (far == 3 - slot))
                def _(slot=slot):
                    rc(part, self.cb.at[slot], self.z_out, self.k + slot, beside).start()

        def pair_half(self, m, half, i):
            part = self.r.at[m, half]
            got(part, i)
            part[...] = (self.g[m, half, c].astype(F32) + part[...].astype(F32)).astype(BF16)
            beside = dev(jnp.where(z == 0, 1, jnp.where(z == 1, 0, jnp.where(z == 2, 3, 2))), x, y, c)

            @pl.when(outer)
            def _():
                rc(part, self.cb.at[0, half], self.z_out, self.k, beside).start()

            @pl.when(inner)
            def _():
                rc(part, self.rz.at[self.mine, half], self.z_out, self.z + self.mine, beside).start()

        def near(self):
            for at, m in ((0, 1), (3, 2)):
                @pl.when(z == at)
                def _(at=at, m=m):
                    rc(self.r.at[m], self.rz.at[at // 2], self.z_out, self.z + at // 2, dev(m, x, y, c)).start()

        def relay(self, *slots):
            for at, blocks in ((1, (3, 2)), (2, (0, 1))):
                @pl.when(z == at)
                def _(at=at, blocks=blocks):
                    for slot in slots:
                        m = blocks[slot]
                        got(self.cb.at[slot], self.k + slot)
                        self.r[m] = (self.r[m].astype(F32) + self.cb[slot].astype(F32)).astype(BF16)
                        rc(self.r.at[m], self.rz.at[at // 2], self.z_out, self.z + at // 2, dev(m, x, y, c)).start()

        def run(self, make):
            def body(k, carry):
                m = at_step(leave, k)
                make(m)
                self.give(m)
                pl.when(k > 0)(lambda: self.pair_step(at_step(leave, k - 1)))
                return carry

            lax.fori_loop(0, PLANES, body, 0)
            self.pair_step(leave[3])

        def finish(self):
            total = fs.at[:, :, 0 : self.width]
            total[...] = self.r[z].astype(F32)
            for dz in (1, -1, 2, -2):
                @pl.when(valid(dz) if abs(dz) == 1 else z == (0 if dz > 0 else 3))
                def _(dz=dz):
                    slot = (z + dz) // 2
                    got(self.rz.at[slot], self.z + slot)
                    total[...] += self.rz[slot].astype(F32)
            self.xs[...] = fs[1 - x, :, 0 : self.width].astype(BF16)
            give(self.xs, self.xr, self.x, xn)

        def sent(self):
            rc(self.r, self.r, self.d_out, 0, sib).wait_send()
            part = self.r.at[pl.ds(0, 3)]
            rc(part, part, self.z_out, 0, sib).wait_send()

        def columns(self, out, half, value, at=0):
            if len(out.shape) == 3:
                for p in range(self.width // 256):
                    out[at + p, :, half_cols(half, 256)] = value[:, p * 256 : (p + 1) * 256].astype(BF16)
            else:
                out[:, half_cols(half, self.width)] = value.astype(BF16)

        def write_own(self, out, at=0):
            self.columns(out, x, fs[x, :, 0 : self.width], at)

        def write_other(self, out, at=0):
            got(self.xr, self.x[1])
            self.columns(out, 1 - x, self.xr[...], at)

    gr_d = Grad(g_d, r_d, rz_d, cb_d, xs_d, xr_d, True)
    gr_u = Grad(g_u, r_u, rz_u, cb_u, xs_u, xr_u, True)
    gr_o = Grad(g_o, r_o, rz_o, cb_o, xs_o, xr_o, False)
    gr_v = Grad(g_v, r_v, rz_v, cb_v, xs_v, xr_v, False)
    gr_k = Grad(g_k, r_k, rz_k, cb_k, xs_k, xr_k, False)

    def act_part(m):
        left = d_cols(efb, m)
        for j in range(4):
            cols = slice(j * 256, (j + 1) * 256)
            acc[:, cols] += dot(left, wd[pl.ds(2 * m, 2), :, :, cols].reshape(256, 256))

    i_half = r_sems.take(2)
    for half in range(2):
        g_ef.need_half(half)
        left = efb[:, :, g_ef.half_cols(half)].reshape(512, 128)
        g_d[leave[0], half] = dot(left, hid[...], TN).astype(BF16).reshape(2, 64, 1024)
        rc(g_d.at[leave[0], half, 1 - c], r_d.at[leave[0], half], gr_d.d_out, i_half + half, sib).start()
    for half in range(2):
        gr_d.pair_half(leave[0], half, i_half + half)
        if half == 0:
            act_part(leave[0])

    def down_grads(k, carry):
        m = at_step(leave, k)
        g_ef.need(k)
        g_d[m] = dot(d_cols(efb, m), hid[...], TN).astype(BF16).reshape(2, 2, 64, 1024)
        gr_d.give(m)
        act_part(m)
        gr_d.pair_step(m)
        return carry

    lax.fori_loop(1, PLANES, down_grads, 0)
    def du_body(n, carry):
        cols = cols256(n)
        du = (acc[:, cols] * dgel[:, cols]).astype(BF16)
        dub[:, cols] = du
        for zz in range(PLANES):
            st_b[zz, pl.ds(8 + n, 1), :] = down(du.astype(F32))
        return carry

    lax.fori_loop(0, 4, du_body, 0)
    sc_d = RelayScatter(rb_d, [jnp.int32(k) for k in range(4)])

    def back_part(n, carry):
        sc_d.part(n, dot(dub[...], wu[pl.ds(2 * n, 2)].reshape(256, 1024), NT))
        return carry

    lax.fori_loop(0, 4, back_part, 0)
    own_mix.pass_on(0)
    for m in range(4):
        xt[m * 256 : (m + 1) * 256] = xg[:, m * 256 : (m + 1) * 256].T

    def transpose_body(h, carry):
        ppt[h] = pp[h].T
        return carry
    gr_d.relay(0)
    sc_d.pass_on(0)
    sc_d.pass_on(1)

    def make_up(m):
        g_u[m] = dot(d_cols(fb, m), dub[...], TN).astype(BF16).reshape(2, 2, 64, 1024)

    gr_u.run(make_up)
    sc_d.pass_on(2)
    sc_d.pass_on(3)
    lax.fori_loop(0, 4, transpose_body, 0)
    gr_d.relay(1)
    dfirst = dr[...] + sc_d.total()
    back = norm_back(dfirst, n1[...], i1[:, 0:1], rows_v[0:1, :])
    dz = back.astype(BF16)
    dzb[own_block] = dz

    i_da = take(3)

    def attention_grad(block):
        dat_s[block] = dot(dz, wo[block].reshape(1024, 256)).astype(BF16)

    for slot in range(3):
        attention_grad(plane_block[slot])
        give(dat_s.at[plane_block[slot]], dat.at[own_block], i_da, plane[slot], None, slot, slot)
    attention_grad(own_block)
    dat[own_block] = dat_s[own_block]
    g_dz = RelayGather(dzb, leave)
    g_dz.start()
    sd[0:1, :] = down(dfirst * n1[...])
    sd[3:4, :] = down(dfirst)
    sd[2:3, :] = down(dz.astype(F32))
    sd[6:8, :] = jnp.zeros((2, 1024), F32)
    class Total:
        def __init__(self, ref, work, recv):
            self.ref, self.work, self.recv = ref, work, recv
            self.c, self.z = take(), take(PLANES)

        def pair(self):
            give(self.ref, self.work, self.c, sib)

        def over_planes(self):
            got(self.work, self.c[1])
            self.work[...] = self.ref[...] + self.work[...]
            for zz in range(PLANES):
                give(self.work.at[zz], self.recv.at[z], self.z, dev(zz, x, y, c), z != zz, zz, z)

        def finish(self):
            for zz in range(PLANES):
                @pl.when(z != zz)
                def _(zz=zz):
                    got(self.recv.at[zz], self.z[1] + zz)

                @pl.when(z == zz)
                def _(zz=zz):
                    self.recv[zz] = self.work[zz]
            return self.recv[0] + self.recv[1] + self.recv[2] + self.recv[3]

    early, late = Total(st_a, work_a, recv_a), Total(st_b, work_b, recv_b)
    i_swap = take()
    i_sd = take(3)
    for k, device in enumerate(plane):
        give(sd, sd_r.at[k], i_sd, device, None, k, k)
    dr[...] = back
    sc_d.sent()
    dph[...] = jnp.zeros_like(dph)
    dvv[...] = jnp.zeros_like(dvv)
    gr_u.relay(0)
    for slot in range(3):
        got(dat.at[plane_block[slot]], i_da[1] + slot)

    dattn = dat[...].reshape(512, 256).astype(F32)
    recip = 1.0 / den[...]
    dn[...] = (dattn * recip).astype(BF16)
    dsum = split_dot(dattn * quo[...], ones64[...])
    dd[...] = ((-dsum * recip).astype(BF16).astype(F32) * (1.0 / HEAD)).astype(BF16)

    def value_back(h, carry):
        cols, mine = head_cols(h)
        keep = jnp.where(mine, 1.0, 0.0).astype(BF16)
        dvv[:, cols] += dot(ppt[h], dn[:, cols] * keep)
        return carry

    lax.fori_loop(0, 4, value_back, 0)
    dqkv[2] = dvv[...].astype(BF16)

    def x_rows(m):
        return xt[rows_of(m, 256)]

    def make_v(m):
        g_v[m] = dot(x_rows(m), dqkv[2]).astype(BF16).reshape(2, 2, 64, 256)

    def head_back(h, carry):
        cols, mine = head_cols(h)
        keep = jnp.where(mine, 1.0, 0.0).astype(BF16)
        left = jnp.concatenate([dn[:, cols] * keep, dd[:, cols] * keep], axis=1)
        right = jnp.concatenate([qkv[2, :, cols], jnp.ones((512, 128), BF16)], axis=1)
        grad_p = dot(left, right, NT)
        for b in range(4):
            rows = slice(b * 128, (b + 1) * 128)
            coefficient = r0[h, :, 512 - 128 * b : 1024 - 128 * b] * masks[b]
            part = grad_p[rows]
            ds_[rows] = (part * coefficient).astype(BF16)
            gg[h, rows] = (part * pp[h, rows].astype(F32)).astype(BF16)
        dph[0, :, cols] += dot(ds_[...], phi[1, :, cols] * keep)
        dph[1, :, cols] += dot(ds_[...], phi[0, :, cols] * keep, TN)
        return carry

    lax.fori_loop(0, 4, head_back, 0)
    gr_u.relay(1)
    g_dz.pass_on(0)
    g_dz.pass_on(1)
    gr_v.run(make_v)
    g_dz.pass_on(2)
    g_dz.pass_on(3)

    def feature_back_body(t, carry):
        dlog = (dph[t] * ex[t]).astype(BF16)
        units = unit[t]
        dunit = SCALE * dot(dlog, om2[...], NT) - SCALE * SCALE * dot(dlog, ones64[...]) * units
        mean = split_dot(dunit * units, ones64[...]) * (1.0 / HEAD)
        dqkv[t] = (inv[t] * (dunit - units * mean)).astype(BF16)
        return carry

    lax.fori_loop(0, 2, feature_back_body, 0)
    class Return:
        def __init__(self, ref):
            self.ref, self.out, self.base, self.last = ref, s_sems.take(), r_sems.take(4), take(4)
            pending.append(lambda: pl.when(home)(lambda: rc(ref.at[0:3], ref.at[0:3], self.out, 0, sib).wait_send()))
            pending.append(lambda: pl.when(away)(lambda: rc(ref, ref, self.out, 0, sib).wait_send()))

        def part(self, n, value):
            cols = cols256(n)
            for b in range(4):
                rows = value[b * 128 : (b + 1) * 128]
                pb[b, :, cols] = jnp.where(own_block == b, rows + dr[:, cols], rows).astype(BF16)
                here = home & (c == b // 2) & (y == b % 2)

                @pl.when(here)
                def _(b=b):
                    self.ref[own_block, :, cols] = pb[b, :, cols]

                @pl.when(jnp.logical_not(here))
                def _(b=b):
                    there = self.ref.at[own_block, :, cols]
                    rc(pb.at[b, :, cols], there, self.out, self.base + n, dev(z, c, b % 2, b // 2)).start()

        def column(self, n):
            cols = slice(n * 256, (n + 1) * 256)
            pl.when(home)(lambda: got(self.ref.at[0:3, :, cols], self.base + n))
            pl.when(away)(lambda: got(self.ref.at[0:4, :, cols], self.base + n))
            value = self.ref[0, :, cols].astype(F32)
            for slot in range(1, 4):
                value = value + self.ref[slot, :, cols].astype(F32)
            mine = gt_r.at[rows_of(y, 128), cols]
            mine[...] = value.astype(BF16)
            give(mine, mine, self.last, yn, None, n, n)

        def need(self, n):
            cols = slice(n * 256, (n + 1) * 256)
            rows = rows_of(1 - y, 128)
            got(gt_r.at[rows, cols], self.last[1] + n)

    sc_i = Return(rb_i)

    def input_part(n, carry):
        value = jnp.zeros((512, 256), F32)
        for p in range(3):
            value = value + dot(dqkv[p], wq[p, pl.ds(2 * n, 2)].reshape(256, 256), NT)
        sc_i.part(n, value)
        return carry

    lax.fori_loop(0, 4, input_part, 0)

    def make_k(m):
        for p in range(2):
            g_k[m, :, :, :, p * 256 : (p + 1) * 256] = (
                dot(x_rows(m), dqkv[p]).astype(BF16).reshape(2, 2, 64, 256)
            )

    gr_k.run(make_k)

    def make_out(m):
        g_o[m] = dot(d_cols(dzb, m), att[...].reshape(512, 256), TN).astype(BF16).reshape(2, 2, 64, 256)

    for k in range(4):
        g_dz.need(k)
    gr_o.run(make_out)
    gr_v.near()
    gr_k.near()
    gr_v.relay(0, 1)
    for k in range(3):
        got(sd_r.at[k], i_sd[1] + k)
    sums = sd[...] + sd_r[0] + sd_r[1] + sd_r[2]
    for zz in range(PLANES):
        st_a[zz] = sums[:, zz * 256 : (zz + 1) * 256]
    early.pair()
    gr_d.finish()
    gr_d.write_own(gd_o)

    def diagonal_body(h, carry):
        sums = jnp.zeros((1, 1024), F32)
        for b in range(4):
            flipped = dot(anti[...], gg[h, (3 - b) * 128 : (4 - b) * 128])
            wide = jnp.concatenate([flipped, jnp.zeros((128, 128), F32)], axis=1)
            line = down(pltpu.roll(wide, 0, 1, stride=1, stride_axis=0))
            pieces = [line]
            if b > 0:
                pieces = [jnp.zeros((1, 128 * b), F32)] + pieces
            if b < 3:
                pieces = pieces + [jnp.zeros((1, 384 - 128 * b), F32)]
            sums = sums + jnp.concatenate(pieces, axis=1)
        for zz in range(PLANES):
            st_b[zz, pl.ds(h, 1), :] = sums[:, (3 - zz) * 256 : (4 - zz) * 256]
        return carry

    lax.fori_loop(0, 4, diagonal_body, 0)
    for p in range(3):
        line = down(dqkv[p].astype(F32))
        for zz in range(PLANES):
            st_b[zz, 12 + p : 13 + p, :] = line
    for zz in range(PLANES):
        st_b[zz, 4:8, :] = jnp.zeros((4, 256), F32)
        st_b[zz, 15:16, :] = jnp.zeros((1, 256), F32)
    late.pair()
    gr_k.relay(0)
    early.over_planes()
    late.over_planes()
    gr_o.near()
    gr_k.relay(1)
    outs = []
    own_mix.need(0)
    outs.append(bring(mixed_o, mixed_h))
    gr_o.relay(0, 1)
    gr_u.finish()
    gr_u.write_own(gu_o)
    sc_i.column(0)
    sc_i.column(1)
    sc_i.column(2)
    sc_i.column(3)
    gr_d.write_other(gd_o)
    outs.append(bring(gd_o, gd_h))
    gr_v.finish()
    gr_v.write_own(gq_o, 2)
    gr_u.write_other(gu_o)
    outs.append(bring(gu_o, gu_h))

    def exact(left, right):
        return lax.dot_general(left, right, NN, precision=lax.Precision.HIGHEST, preferred_element_type=F32)

    sd_r[0, :, 0:256] = early.finish()
    mine = sd_r[0, :, pl.ds(pl.multiple_of(x * 128, 128), 128)]
    own = exact(mine, pick((128, 64), lambda k, l: k == c * 64 + l))
    ggain_o[...] = own[0:2]
    gbias_o[...] = own[2:6]
    outs.append(bring(ggain_o, ggain_h))
    outs.append(bring(gbias_o, gbias_h))
    swap[0] = late.finish()
    give(swap.at[0], swap.at[1], i_swap, xn)
    gr_k.finish()
    gr_k.write_own(gq_o)
    gr_o.finish()
    gr_o.write_own(go_o)
    for n in range(4):
        sc_i.need(n)
    outs.append(bring(gt_r, gtok_h))
    got(swap.at[1], i_swap[1])
    tile = pl.ds(pl.multiple_of((1 - x) * 128, 128), 128)
    ours, theirs = swap[0, 0:4, tile], swap[1, 0:4, tile]
    lines = jnp.concatenate([jnp.where(x == 0, ours, theirs), jnp.where(x == 0, theirs, ours)], axis=0)
    grpe_o[...] = exact(lines, pick((128, 64), lambda k, l: k == (1 - c) * 64 + 63 - l))
    outs.append(bring(grpe_o, grpe_h))
    ours, theirs = swap[0, 8:16], swap[1, 8:16]
    rest = [jnp.where(x == half, ours, theirs) for half in range(2)]
    lines = [rest[half][4 + p : 5 + p, t * 128 : (t + 1) * 128] for p in range(3) for half in range(2) for t in range(2)]
    lines += [
        rest[half][t // 2 : t // 2 + 1, (t % 2) * 128 : (t % 2 + 1) * 128] for half in range(2) for t in range(8)
    ]
    lines = jnp.concatenate(lines + [jnp.zeros((4, 128), F32)], axis=0)
    found = jnp.zeros((4, 56), F32)
    for par in range(2):
        hit = pick((4, 128), lambda k, l: l == par * 64 + 4 * shard + k)
        values = lax.dot_general(hit, lines, NT, precision=lax.Precision.HIGHEST, preferred_element_type=F32)
        found = found + exact(values, pick((32, 56), lambda k, l: (l // 2 == k) & (l % 2 == par)))
    for p in range(3):
        gqb_o[p] = found[:, 8 * p : 8 * p + 8]
    gub_o[...] = found[:, 24:56]
    outs.append(bring(gqb_o, gqb_h))
    outs.append(bring(gub_o, gub_h))
    gr_v.write_other(gq_o, 2)
    gr_k.write_other(gq_o)
    outs.append(bring(gq_o, gq_h))
    gr_o.write_other(go_o)
    outs.append(bring(go_o, go_h))
    for gr in (gr_d, gr_u, gr_o, gr_v, gr_k):
        gr.sent()
    assert (s_sems.used, r_sems.used, locals_.used) == (SENDS, RECEIVES, 24), (s_sems.used, r_sems.used, locals_.used)
    for done in pending + outs:
        done()


def copy_kernel(*refs):
    count = (len(refs) - 1) // 4
    sem = refs[-1]
    given, held, wide, kept = (refs[k * count : (k + 1) * count] for k in (0, 2, 3, 1))
    ins = [pltpu.make_async_copy(given[i], held[i], sem.at[0, i]) for i in range(count)]
    for copy in ins:
        copy.start()
    outs = []
    for i in range(count):
        ins[i].wait()
        if held[i].dtype == kept[i].dtype:
            outs.append(pltpu.make_async_copy(held[i], kept[i], sem.at[1, i]))
        else:
            wide[i][...] = held[i][...].astype(kept[i].dtype)
            outs.append(pltpu.make_async_copy(wide[i], kept[i], sem.at[1, i]))
        outs[-1].start()
    for copy in outs:
        copy.wait()


def fast_local(
    tokens, qkv_weight, qkv_bias, out_weight, norm_gains, row_biases, up_weight, up_bias, down_weight, rpe_bias, omega,
    bucket, cotangent,
):
    def vm(shape, dtype=BF16):
        return pltpu.VMEM(shape, dtype)

    widths = (512, 256, 256, 1024, 1024)
    scratch = [vm((3, 4, 8)), vm((2, 64)), vm((4, 64)), vm((4, 32)), vm((8, 64)), vm((8, 32, 64))]
    scratch += [pltpu.SMEM((1,), jnp.int32), vm((2, 32, 128)), vm((256, 256))]
    results = (
        ((256, 1024), BF16), ((256, 1024), F32), ((3, 64, 512), F32), ((3, 4, 8), F32), ((64, 512), F32), ((2, 64), F32),
        ((4, 64), F32), ((64, 2048), F32), ((4, 32), F32), ((64, 2048), F32), ((8, 64), F32),
    )
    large = ((256, 1024), (3, 64, 512), (64, 512), (64, 2048))
    sent = tuple((shape, BF16 if shape in large else dtype) for shape, dtype in results)
    scratch += [vm(*result) for i, result in enumerate(sent) if i != 1]
    scratch += [vm((3, 8, 2, 64, 256)), vm((4, 8, 2, 64, 256)), vm((8, 2, 64, 1024)), vm((8, 2, 64, 1024))]
    scratch += [vm((8, 2, 32, 128)), vm((256, 256)), vm((512, 1024)), vm((128, 1024))]
    scratch += [vm((3, 512, 256)), vm((2, 512, 256))] + [vm((2, 512, 256), F32)] * 3
    scratch += [vm((4, 128, 1024), F32), vm((4, 512, 512))] + [vm((512, 256), F32)] * 3 + [vm((4, 128, 256))] * 2
    scratch += [vm((4, 128, 1024))] + [vm((3, 128, 1024))] * 2 + [vm((4, 128, 1024))]
    scratch += [vm((4, 128, 1024)), vm((512, 1024)), vm((512, 1024), F32)]
    scratch += [vm((4, 128, 1024)), vm((512, 1024)), vm((4, 128, 1024)), vm((512, 1024), F32)]
    scratch += [vm((128, 1024), F32)] * 2 + [vm((128, 128), F32)] + [vm((128, 1024), F32)] * 2
    scratch += [vm((4, 128, 256))] * 2 + [vm((128, 128)), vm((256, 256)), vm((24, 1024), F32)]
    scratch += [vm((512, 256))] * 2 + [vm((512, 512)), vm((4, 512, 512)), vm((2, 512, 256), F32), vm((512, 256), F32)]
    scratch += [vm((3, 512, 256)), vm((1024, 512)), vm((4, 512, 512))]
    scratch += [vm((4, 2, 2, 64, n)) for n in widths]
    scratch += [vm((4, 2, 64, n)) for n in widths] + [vm((2, 2, 64, n)) for n in widths] * 2
    scratch += [vm((2, 64, 1024), F32)] + [vm((64, n)) for n in widths] * 2
    scratch += [vm((8, 1024), F32), vm((3, 8, 1024), F32)] + [vm((4, 8, 256), F32), vm((4, 16, 256), F32)] * 3
    scratch += [vm((2, 16, 256), F32)]
    scratch += [vm((128, 1024)), vm((256, 1024))]
    scratch += [pltpu.SemaphoreType.DMA((SENDS,)), pltpu.SemaphoreType.DMA((RECEIVES,)), pltpu.SemaphoreType.DMA((24,))]

    shapes = tuple(jax.ShapeDtypeStruct(*result) for result in results)
    narrow = tuple(jax.ShapeDtypeStruct(*result) for result in sent)
    anywhere = pl.BlockSpec(memory_space=pl.ANY)
    made = pl.pallas_call(
        layer_kernel,
        out_shape=narrow,
        in_specs=[anywhere] * 13,
        out_specs=(anywhere,) * len(shapes),
        scratch_shapes=scratch,
        compiler_params=pltpu.CompilerParams(
            collective_id=0, has_side_effects=True, vmem_limit_bytes=63 * 2**20
        ),
        name="layer",
    )(
        tokens, qkv_weight.transpose(1, 0, 2), qkv_bias.transpose(0, 2, 1), out_weight.T, norm_gains, row_biases, up_weight,
        up_bias.T, down_weight.T, rpe_bias, omega.transpose(0, 2, 1), bucket, cotangent,
    )
    mixed, gtok, gq, gqb, go, ggain, gbias, gu, gub, gd, grpe = pl.pallas_call(
        copy_kernel,
        out_shape=shapes,
        in_specs=[anywhere] * len(shapes),
        out_specs=(anywhere,) * len(shapes),
        scratch_shapes=[vm(*result) for result in sent + results] + [pltpu.SemaphoreType.DMA((2, len(shapes)))],
        compiler_params=pltpu.CompilerParams(vmem_limit_bytes=63 * 2**20),
        name="results",
    )(*made)
    return (
        mixed, gtok, gq.transpose(1, 0, 2), gqb.transpose(0, 2, 1), go.T, ggain, gbias, gu, gub.T, gd.T, grpe,
    )


def solution(mesh):
    sizes = (mesh.shape["dp"], mesh.shape["heads"], mesh.shape["feat"])
    return jax.shard_map(
        fast_local if sizes == (2 * PLANES, 2, 2) else local,
        mesh=mesh,
        in_specs=(
            P(("dp", "feat"), None),
            P(("dp", "feat"), None, "heads"),
            P(None, "heads", ("dp", "feat")),
            P("heads", ("dp", "feat")),
            P(None, ("dp", "feat")),
            P(None, ("dp", "feat")),
            P(("dp", "feat"), "heads"),
            P("heads", ("dp", "feat")),
            P("heads", ("dp", "feat")),
            P("heads", ("dp", "feat")),
            P("heads", None, "feat"),
            P("dp"),
            P(("dp", "feat"), None),
        ),
        out_specs=(
            P(("dp", "feat"), None),
            P(("dp", "feat"), None),
            P(("dp", "feat"), None, "heads"),
            P(None, "heads", ("dp", "feat")),
            P("heads", ("dp", "feat")),
            P(None, ("dp", "feat")),
            P(None, ("dp", "feat")),
            P(("dp", "feat"), "heads"),
            P("heads", ("dp", "feat")),
            P("heads", ("dp", "feat")),
            P("heads", ("dp", "feat")),
        ),
        check_vma=False,
    )
```

```python
import functools

import jax
import jax.numpy as jnp
from jax import lax
from jax.experimental import pallas as pl
from jax.experimental.pallas import tpu as pltpu
from jax.sharding import PartitionSpec as P

HEAD = 64
M = 64


EPSILON = 1e-12
UNIT_EPS = 1e-06


def toeplitz_block(window, extent):
    leading = window.shape[0]
    tiled_rows = jnp.broadcast_to(window[:, None, :], (leading, extent, 2 * extent - 1)).reshape(
        leading, -1
    )
    padded = jnp.pad(tiled_rows, ((0, 0), (0, extent)))
    sheared = padded.reshape(leading, extent, 2 * extent)[:, :, :extent]
    return sheared[:, :, ::-1]


def diagonal_sums(values_grid, extent):
    leading = values_grid.shape[0]
    flipped = values_grid[:, :, ::-1]
    padded = jnp.pad(flipped, ((0, 0), (0, 0), (0, extent))).reshape(leading, -1)
    sheared = padded[:, : extent * (2 * extent - 1)].reshape(leading, extent, 2 * extent - 1)
    return jnp.sum(sheared, axis=1)


def norm_forward(values, gain, shift):
    centred = values - jnp.mean(values, axis=-1, keepdims=True)
    inverse = lax.rsqrt(jnp.mean(centred * centred, axis=-1, keepdims=True) + EPSILON)
    normed = centred * inverse
    return (normed * gain + shift, normed, inverse)


def norm_backward(upstream, normed, inverse, gain):
    scaled_grad = upstream * gain
    return inverse * (
        scaled_grad
        - jnp.mean(scaled_grad, axis=-1, keepdims=True)
        - normed * jnp.mean(scaled_grad * normed, axis=-1, keepdims=True)
    )


def feature_logits(entries, omega_local):
    factor = HEAD ** (-0.25)
    wide = entries.astype(jnp.float32)
    inverse = lax.rsqrt(jnp.mean(wide * wide, axis=-1, keepdims=True) + UNIT_EPS)
    unit = wide * inverse
    projected = jnp.einsum(
        "rhe,hem->hmr",
        unit,
        omega_local.astype(jnp.float32),
        precision=lax.Precision.HIGHEST,
        preferred_element_type=jnp.float32,
    )
    squares = jnp.sum(unit * unit, axis=-1)
    return (factor * projected - 0.5 * factor * factor * squares.T[:, None, :], unit, inverse)


def feature_back(grad_phi, logits, unit, inverse, omega_local):
    factor = HEAD ** (-0.25)
    grad_logits = (grad_phi * (jnp.exp(logits) * M ** (-0.5))).astype(jnp.bfloat16)
    projected = jnp.einsum(
        "hmr,hem->rhe", grad_logits, omega_local, preferred_element_type=jnp.float32
    )
    totals = jnp.sum(grad_logits.astype(jnp.float32), axis=1)
    grad_unit = factor * projected - factor * factor * totals.T[:, :, None] * unit
    return inverse * (grad_unit - unit * jnp.mean(grad_unit * unit, axis=-1, keepdims=True))


def window_begin(row_start, col_start, extent, rows_total):
    return row_start - col_start + rows_total - extent + 1


def block_coeff(rpe_exp, window_start, extent):
    window = lax.dynamic_slice_in_dim(rpe_exp, window_start, 2 * extent - 1, 1)
    return toeplitz_block(window, extent)


def local(
    tokens,
    qkv_weight,
    qkv_bias,
    out_weight,
    norm_gains,
    row_biases,
    up_weight,
    up_bias,
    down_weight,
    rpe_bias,
    omega,
    bucket,
    cotangent,
):
    qkv_full, out_full, up_full, down_full, gains_all, biases_all, bias_qkv, bias_up, rpe_all = (
        lax.all_gather(qkv_weight, ("dp", "feat"), axis=0, tiled=True),
        lax.all_gather(out_weight, ("dp", "feat"), axis=1, tiled=True),
        lax.all_gather(up_weight, ("dp", "feat"), axis=0, tiled=True),
        lax.all_gather(down_weight, ("dp", "feat"), axis=1, tiled=True),
        lax.all_gather(norm_gains, ("dp", "feat"), axis=1, tiled=True),
        lax.all_gather(row_biases, ("dp", "feat"), axis=1, tiled=True),
        lax.all_gather(qkv_bias, ("dp", "feat"), axis=2, tiled=True),
        lax.all_gather(up_bias, ("dp", "feat"), axis=1, tiled=True),
        lax.all_gather(rpe_bias, ("dp", "feat"), axis=1, tiled=True),
    )
    model_width = qkv_full.shape[0]
    head_cols = qkv_full.shape[2]
    local_heads = omega.shape[0]
    local_feats = omega.shape[2]
    rows_own = tokens.shape[0]
    rows_total = rows_own * lax.axis_size("feat")
    block_rows = min(512, rows_total // 4)
    blocks = rows_total // block_rows
    seq_length = rows_total // 4 * jnp.where(bucket[0] == 0, 1, jnp.where(bucket[0] == 1, 2, 4))
    block_count = seq_length // block_rows
    gain_rows = gains_all.astype(jnp.float32)
    bias_rows = biases_all.astype(jnp.float32)
    rpe_exp = jnp.exp(rpe_all.astype(jnp.float32))
    projected = jnp.dot(
        tokens, qkv_full.reshape(model_width, 3 * head_cols), preferred_element_type=jnp.float32
    )
    projected = projected + bias_qkv.reshape(-1).astype(jnp.float32)
    qkv_own = projected.astype(jnp.bfloat16)
    qkv_all = lax.all_gather(qkv_own, "feat", axis=0, tiled=True).reshape(
        rows_total, 3, local_heads, HEAD
    )
    queries = qkv_all[:, 0]
    keys_rows = qkv_all[:, 1]
    values_rows = qkv_all[:, 2]
    logits_query, unit_query, inverse_query = feature_logits(queries, omega)
    logits_key, unit_key, inverse_key = feature_logits(keys_rows, omega)
    feat_query = (jnp.exp(logits_query) * M ** (-0.5)).astype(jnp.bfloat16)
    feat_key = (jnp.exp(logits_key) * M ** (-0.5)).astype(jnp.bfloat16)
    numer_parts = []
    denom_parts = []
    for row_block in range(blocks):
        row_start = row_block * block_rows
        first_block = row_start // seq_length * block_count
        phi_rows = feat_query[:, :, row_start : row_start + block_rows]

        def visit(column_block, carried, phi_rows=phi_rows, row_start=row_start):
            numer_acc, denom_acc = carried
            col_start = column_block * block_rows
            phi_cols = lax.dynamic_slice_in_dim(feat_key, col_start, block_rows, 2)
            value_cols = lax.dynamic_slice_in_dim(values_rows, col_start, block_rows, 0)
            coefficient = block_coeff(
                rpe_exp, window_begin(row_start, col_start, block_rows, rows_total), block_rows
            )
            scores = jnp.einsum(
                "hmi,hmj->hij", phi_rows, phi_cols, preferred_element_type=jnp.float32
            )
            weights = (coefficient * scores).astype(jnp.bfloat16)
            numer_acc = numer_acc + jnp.einsum(
                "hij,jhe->ihe", weights, value_cols, preferred_element_type=jnp.float32
            )
            denom_acc = denom_acc + jnp.sum(weights.astype(jnp.float32), axis=-1)
            return (numer_acc, denom_acc)

        start_pair = (
            jnp.zeros((block_rows, local_heads, HEAD), jnp.float32),
            jnp.zeros((local_heads, block_rows), jnp.float32),
        )
        numer_block, denom_block = lax.fori_loop(
            first_block, first_block + block_count, visit, start_pair
        )
        numer_parts.append(numer_block)
        denom_parts.append(denom_block)
    numer_all = jnp.concatenate(numer_parts, axis=0).reshape(rows_total, head_cols)
    denom_all = jnp.concatenate(denom_parts, axis=1)
    numer_own, denom_own = (
        lax.psum_scatter(
            numer_all.astype(jnp.bfloat16), "feat", scatter_dimension=0, tiled=True
        ).astype(jnp.float32),
        lax.psum_scatter(
            denom_all.astype(jnp.bfloat16), "feat", scatter_dimension=1, tiled=True
        ).astype(jnp.float32),
    )
    denom_rows = denom_own.T
    quotient = numer_own.reshape(rows_own, local_heads, HEAD) / denom_rows[:, :, None]
    attn_low = quotient.reshape(rows_own, head_cols).astype(jnp.bfloat16)
    z_part = jnp.dot(attn_low, out_full, preferred_element_type=jnp.float32)
    mixed_z = lax.psum(z_part.astype(jnp.bfloat16), "heads").astype(jnp.float32) + bias_rows[0]
    first_out, normed_one, inverse_one = norm_forward(
        tokens.astype(jnp.float32) + mixed_z, gain_rows[0], bias_rows[1]
    )
    first_low = first_out.astype(jnp.bfloat16)
    pre_act = jnp.dot(first_low, up_full, preferred_element_type=jnp.float32) + bias_up.reshape(
        -1
    ).astype(jnp.float32)
    act_value, act_pull = jax.vjp(lambda inner: jax.nn.gelu(inner, approximate=False), pre_act)
    act_low = act_value.astype(jnp.bfloat16)
    ffn_part = jnp.dot(act_low, down_full, preferred_element_type=jnp.float32)
    ffn_out = lax.psum(ffn_part.astype(jnp.bfloat16), "heads").astype(jnp.float32) + bias_rows[2]
    final_rows, normed_two, inverse_two = norm_forward(
        first_out + ffn_out, gain_rows[1], bias_rows[3]
    )
    mixed = final_rows.astype(jnp.bfloat16)
    qkv_full, out_full, up_full, down_full, gains_all, rpe_all = (
        lax.all_gather(qkv_weight, ("dp", "feat"), axis=0, tiled=True),
        lax.all_gather(out_weight, ("dp", "feat"), axis=1, tiled=True),
        lax.all_gather(up_weight, ("dp", "feat"), axis=0, tiled=True),
        lax.all_gather(down_weight, ("dp", "feat"), axis=1, tiled=True),
        lax.all_gather(norm_gains, ("dp", "feat"), axis=1, tiled=True),
        lax.all_gather(rpe_bias, ("dp", "feat"), axis=1, tiled=True),
    )
    gain_rows = gains_all.astype(jnp.float32)
    rpe_exp = jnp.exp(rpe_all.astype(jnp.float32))
    upstream = cotangent.astype(jnp.float32)
    grad_gain_two = jnp.sum(upstream * normed_two, axis=0)
    grad_shift_two = jnp.sum(upstream, axis=0)
    resid_two = norm_backward(upstream, normed_two, inverse_two, gain_rows[1])
    resid_low = resid_two.astype(jnp.bfloat16)
    grad_bias_down = jnp.sum(resid_low.astype(jnp.float32), axis=0)
    grad_down = jnp.einsum("rf,rd->fd", act_low, resid_low, preferred_element_type=jnp.float32)
    grad_act = jnp.einsum("rd,fd->rf", resid_low, down_full, preferred_element_type=jnp.float32)
    grad_pre = act_pull(grad_act)[0].astype(jnp.bfloat16)
    grad_up = jnp.einsum("rd,rf->df", first_low, grad_pre, preferred_element_type=jnp.float32)
    grad_bias_up = jnp.sum(grad_pre.astype(jnp.float32), axis=0).reshape(bias_up.shape)
    first_back = lax.psum(
        jnp.einsum("rf,df->rd", grad_pre, up_full, preferred_element_type=jnp.float32).astype(
            jnp.bfloat16
        ),
        "heads",
    ).astype(jnp.float32)
    grad_first = resid_two + first_back
    grad_gain_one = jnp.sum(grad_first * normed_one, axis=0)
    grad_shift_one = jnp.sum(grad_first, axis=0)
    resid_one = norm_backward(grad_first, normed_one, inverse_one, gain_rows[0])
    resid_one_low = resid_one.astype(jnp.bfloat16)
    grad_bias_out = jnp.sum(resid_one_low.astype(jnp.float32), axis=0)
    grad_out = jnp.einsum("rc,rd->cd", attn_low, resid_one_low, preferred_element_type=jnp.float32)
    grad_attn = jnp.einsum(
        "rd,cd->rc", resid_one_low, out_full, preferred_element_type=jnp.float32
    ).reshape(rows_own, local_heads, HEAD)
    grad_numer = (grad_attn / denom_rows[:, :, None]).astype(jnp.bfloat16)
    grad_denom = (-jnp.sum(grad_attn * quotient, axis=-1) / denom_rows).astype(jnp.bfloat16)
    numer_grad_all, denom_grad_all = (
        lax.all_gather(grad_numer.reshape(rows_own, head_cols), "feat", axis=0, tiled=True),
        lax.all_gather(grad_denom.T, "feat", axis=1, tiled=True),
    )
    numer_grad_all = numer_grad_all.reshape(rows_total, local_heads, HEAD)
    dphi_key = jnp.zeros((local_heads, local_feats, rows_total), jnp.float32)
    dvalues = jnp.zeros((rows_total, local_heads, HEAD), jnp.float32)
    grad_rpe = jnp.zeros(rpe_exp.shape, jnp.float32)
    dquery_parts = []
    for row_block in range(blocks):
        row_start = row_block * block_rows
        first_block = row_start // seq_length * block_count
        phi_rows = feat_query[:, :, row_start : row_start + block_rows]
        numer_rows = numer_grad_all[row_start : row_start + block_rows]
        denom_cols = denom_grad_all[:, row_start : row_start + block_rows].astype(jnp.float32)

        def visit_back(
            column_block,
            carried,
            phi_rows=phi_rows,
            row_start=row_start,
            numer_rows=numer_rows,
            denom_cols=denom_cols,
        ):
            dquery_acc, dkey_all, dvalue_all, drpe_all = carried
            col_start = column_block * block_rows
            phi_cols = lax.dynamic_slice_in_dim(feat_key, col_start, block_rows, 2)
            value_cols = lax.dynamic_slice_in_dim(values_rows, col_start, block_rows, 0)
            window_start = window_begin(row_start, col_start, block_rows, rows_total)
            coefficient = block_coeff(rpe_exp, window_start, block_rows)
            scores = jnp.einsum(
                "hmi,hmj->hij", phi_rows, phi_cols, preferred_element_type=jnp.float32
            )
            weights = (coefficient * scores).astype(jnp.bfloat16)
            grad_weights = (
                jnp.einsum(
                    "ihe,jhe->hij", numer_rows, value_cols, preferred_element_type=jnp.float32
                )
                + denom_cols[:, :, None]
            )
            dvalue_block = jnp.einsum(
                "hij,ihe->jhe", weights, numer_rows, preferred_element_type=jnp.float32
            )
            dvalue_all = lax.dynamic_update_slice_in_dim(
                dvalue_all,
                lax.dynamic_slice_in_dim(dvalue_all, col_start, block_rows, 0) + dvalue_block,
                col_start,
                0,
            )
            grad_scores = (grad_weights * coefficient).astype(jnp.bfloat16)
            diagonal = diagonal_sums(grad_weights * scores * coefficient, block_rows)
            drpe_all = lax.dynamic_update_slice_in_dim(
                drpe_all,
                lax.dynamic_slice_in_dim(drpe_all, window_start, 2 * block_rows - 1, 1) + diagonal,
                window_start,
                1,
            )
            dquery_acc = dquery_acc + jnp.einsum(
                "hij,hmj->hmi", grad_scores, phi_cols, preferred_element_type=jnp.float32
            )
            dkey_block = jnp.einsum(
                "hij,hmi->hmj", grad_scores, phi_rows, preferred_element_type=jnp.float32
            )
            dkey_all = lax.dynamic_update_slice_in_dim(
                dkey_all,
                lax.dynamic_slice_in_dim(dkey_all, col_start, block_rows, 2) + dkey_block,
                col_start,
                2,
            )
            return (dquery_acc, dkey_all, dvalue_all, drpe_all)

        start_state = (
            jnp.zeros((local_heads, local_feats, block_rows), jnp.float32),
            dphi_key,
            dvalues,
            grad_rpe,
        )
        dquery_block, dphi_key, dvalues, grad_rpe = lax.fori_loop(
            first_block, first_block + block_count, visit_back, start_state
        )
        dquery_parts.append(dquery_block)
    dphi_query = jnp.concatenate(dquery_parts, axis=2)
    grad_query = feature_back(dphi_query, logits_query, unit_query, inverse_query, omega)
    grad_key = feature_back(dphi_key, logits_key, unit_key, inverse_key, omega)
    grad_qkv_all = jnp.stack((grad_query, grad_key, dvalues), axis=1).reshape(
        rows_total, 3 * head_cols
    )
    grad_qkv_own = lax.psum_scatter(
        grad_qkv_all.astype(jnp.bfloat16), "feat", scatter_dimension=0, tiled=True
    )
    grad_bias_qkv = jnp.sum(grad_qkv_own.astype(jnp.float32), axis=0).reshape(bias_qkv.shape)
    grad_qkv_weight = jnp.einsum(
        "rd,rc->dc", tokens, grad_qkv_own, preferred_element_type=jnp.float32
    ).reshape(qkv_full.shape)
    input_terms = jnp.einsum(
        "rc,dc->rd",
        grad_qkv_own,
        qkv_full.reshape(model_width, 3 * head_cols),
        preferred_element_type=jnp.float32,
    )
    grad_tokens = resid_one + lax.psum(input_terms.astype(jnp.bfloat16), "heads").astype(
        jnp.float32
    )
    grad_gains = jnp.stack((grad_gain_one, grad_gain_two), axis=0)
    grad_shifts = jnp.stack((grad_bias_out, grad_shift_one, grad_bias_down, grad_shift_two), axis=0)
    (
        sent_qkv,
        sent_out,
        sent_up,
        sent_down,
        sent_gains,
        sent_shifts,
        sent_bias_qkv,
        sent_bias_up,
        sent_rpe,
    ) = (
        lax.psum_scatter(
            grad_qkv_weight.astype(jnp.bfloat16), ("dp", "feat"), scatter_dimension=0, tiled=True
        ).astype(jnp.float32),
        lax.psum_scatter(
            grad_out.astype(jnp.bfloat16), ("dp", "feat"), scatter_dimension=1, tiled=True
        ).astype(jnp.float32),
        lax.psum_scatter(
            grad_up.astype(jnp.bfloat16), ("dp", "feat"), scatter_dimension=0, tiled=True
        ).astype(jnp.float32),
        lax.psum_scatter(
            grad_down.astype(jnp.bfloat16), ("dp", "feat"), scatter_dimension=1, tiled=True
        ).astype(jnp.float32),
        lax.psum_scatter(
            grad_gains.astype(jnp.bfloat16), ("dp", "feat"), scatter_dimension=1, tiled=True
        ).astype(jnp.float32),
        lax.psum_scatter(
            grad_shifts.astype(jnp.bfloat16), ("dp", "feat"), scatter_dimension=1, tiled=True
        ).astype(jnp.float32),
        lax.psum_scatter(
            grad_bias_qkv.astype(jnp.bfloat16), ("dp", "feat"), scatter_dimension=2, tiled=True
        ).astype(jnp.float32),
        lax.psum_scatter(
            grad_bias_up.astype(jnp.bfloat16), ("dp", "feat"), scatter_dimension=1, tiled=True
        ).astype(jnp.float32),
        lax.psum_scatter(
            grad_rpe.astype(jnp.bfloat16), ("dp", "feat"), scatter_dimension=1, tiled=True
        ).astype(jnp.float32),
    )
    return (
        mixed,
        grad_tokens,
        sent_qkv,
        sent_bias_qkv,
        sent_out,
        sent_gains,
        sent_shifts,
        sent_up,
        sent_bias_up,
        sent_down,
        sent_rpe,
    )


MESH = pl.DeviceIdType.MESH
PLANES = 4
SENDS, RECEIVES = 86, 202
F32 = jnp.float32
BF16 = jnp.bfloat16
SCALE = HEAD ** (-0.25)
NT = (((1,), (1,)), ((), ()))
TN = (((0,), (0,)), ((), ()))
NN = (((1,), (0,)), ((), ()))


def dot(left, right, dims=NN):
    return lax.dot_general(left, right, dims, preferred_element_type=F32)


def split_dot(left, right, dims=NN):
    high = left.astype(BF16)
    rest = (left - high.astype(F32)).astype(BF16)
    return dot(high, right, dims) + dot(rest, right, dims)


def iota(shape, axis):
    return lax.broadcasted_iota(jnp.int32, shape, axis)


class Sems:
    def __init__(self):
        self.used = 0

    def take(self, count=1):
        first = self.used
        self.used += count
        return first


def layer_kernel(
    tok, wq_h, qb_h, wo_h, gain_h, bias_h, wu_h, ub_h, wd_h, rpe_h, om_h, bk_h, cot,
    mixed_h, gtok_h, gq_h, gqb_h, go_h, ggain_h, gbias_h, gu_h, gub_h, gd_h, grpe_h,
    qb_v, gain_v, bias_v, ub_v, rpe_v, om_v, bk_v, small_s, om_s,
    mixed_o, gq_o, gqb_o, go_o, ggain_o, gbias_o, gu_o, gub_o, gd_o, grpe_o,
    wq, wo, wu, wd, small, om2, xg, cotb,
    qkv, phi, ex, unit, inv, r0, pp, num, den, quo, att, attf,
    pb, rb_f, rb_d, rb_i, fb, hid, dgel, efb, dub, dzb, acc,
    fst, n1, i1, dr, summed, dat_s, dat, anti, ones64, rows_v,
    dn, dd, ds_, gg, dph, dvv, dqkv, xt, ppt,
    g_k, g_v, g_o, g_u, g_d, r_k, r_v, r_o, r_u, r_d, rz_k, rz_v, rz_o, rz_u, rz_d, cb_k, cb_v, cb_o, cb_u, cb_d,
    fs, xs_k, xs_v, xs_o, xs_u, xs_d, xr_k, xr_v, xr_o, xr_u, xr_d,
    sd, sd_r, st_a, st_b, work_a, work_b, recv_a, recv_b, swap, mix_s, gt_r,
    ss, rs, ls,
):
    dp, y, c = lax.axis_index("dp"), lax.axis_index("heads"), lax.axis_index("feat")
    z, x = dp // 2, dp % 2
    shard = 2 * dp + c

    def dev(zz, xx, yy, cc):
        return {"dp": zz * 2 + xx, "heads": yy, "feat": cc}

    sib, xn, yn, dg = dev(z, x, y, 1 - c), dev(z, 1 - x, y, c), dev(z, x, 1 - y, c), dev(z, 1 - x, 1 - y, c)
    xs_dev, ds_dev = dev(z, 1 - x, y, 1 - c), dev(z, 1 - x, 1 - y, 1 - c)

    barrier = pltpu.get_barrier_semaphore()
    for other in (sib, xn, yn, dg, xs_dev, ds_dev, dev(z, x, 1 - y, 1 - c)):
        pl.semaphore_signal(barrier, inc=1, device_id=other, device_id_type=MESH)
    for zz in range(PLANES):
        @pl.when(z != zz)
        def _(zz=zz):
            pl.semaphore_signal(barrier, inc=1, device_id=dev(zz, x, y, c), device_id_type=MESH)

    s_sems, r_sems, locals_ = Sems(), Sems(), Sems()
    pending = []

    def bring(src, dst, cond=None):
        copy = pltpu.make_async_copy(src, dst, ls.at[locals_.take()])
        if cond is None:
            copy.start()
            return copy.wait
        pl.when(cond)(copy.start)
        return lambda: pl.when(cond)(copy.wait)

    home = c == x
    away = c != x
    own_block = 2 * x + y

    def half_cols(half, width):
        return pl.ds(pl.multiple_of(half * width, width), width)

    def rows_of(index, count):
        return pl.ds(pl.multiple_of(index * count, count), count)

    in_o = bring(wo_h.at[:, half_cols(x, 256)], wo.at[own_block, 2 * z + x, c])
    in_q = bring(wq_h.at[:, :, half_cols(x, 256)], wq.at[:, 2 * z + x, c])
    in_small = [
        bring(src, dst)
        for src, dst in (
            (gain_h, gain_v), (bias_h, bias_v), (rpe_h, rpe_v), (qb_h, qb_v), (ub_h, ub_v), (om_h, om_v), (bk_h, bk_v),
        )
    ]
    in_tok = bring(tok, xg.at[rows_of(c, 256)], home)
    in_u = bring(wu_h.at[:, half_cols(x, 1024)], wu.at[2 * z + x, c])
    in_d = bring(wd_h.at[:, half_cols(x, 1024)], wd.at[2 * z + x, c])
    in_cot = bring(cot.at[rows_of(y, 128)], cotb, home)

    plane = (dg, xn, yn)
    plane_block = (2 * (1 - x) + 1 - y, 2 * (1 - x) + y, 2 * x + 1 - y)

    def rc(src, dst, s, r, device):
        return pltpu.make_async_remote_copy(
            src_ref=src, dst_ref=dst, send_sem=ss.at[s], recv_sem=rs.at[r], device_id=device, device_id_type=MESH
        )

    def send(src, dst, s, r, device, cond=None):
        def go():
            rc(src, dst, s, r, device).start()

        def done():
            rc(src, dst, s, r, device).wait_send()

        if cond is None:
            go()
            pending.append(done)
        else:
            pl.when(cond)(go)
            pending.append(lambda: pl.when(cond)(done))

    def got(dst, r):
        rc(dst, dst, r, r, sib).wait_recv()

    def take(count=1):
        return s_sems.take(count), r_sems.take(count)

    def give(src, dst, pair, device, cond=None, s=0, r=0):
        send(src, dst, pair[0] + s, pair[1] + r, device, cond)

    def valid(dz):
        return jnp.logical_and(z + dz >= 0, z + dz < PLANES)

    def by_plane(table):
        found = []
        for k in range(PLANES):
            block = jnp.int32(table[0][k])
            for zz in range(1, PLANES):
                block = jnp.where(z == zz, table[zz][k], block)
            found.append(block)
        return found

    arrive = by_plane(((0, 1, 2, 3), (1, 2, 3, 0), (2, 1, 0, 3), (3, 2, 1, 0)))
    leave = by_plane(((3, 2, 1, 0), (0, 3, 2, 1), (3, 0, 1, 2), (0, 1, 2, 3)))

    def at_step(blocks, k):
        block = blocks[0]
        for i in range(1, PLANES):
            block = jnp.where(k == i, blocks[i], block)
        return block

    def cols256(n):
        return pl.ds(pl.multiple_of(n * 256, 256), 256)

    pl.semaphore_wait(barrier, 10)

    inner, outer = (z == 1) | (z == 2), (z == 0) | (z == 3)

    class Item:
        def __init__(self, ref, kind, whole=True):
            self.ref, self.kind, self.whole = ref, kind, whole
            self.z_out, self.c_out = s_sems.take(), s_sems.take()
            self.zs, self.sb = r_sems.take(PLANES), r_sems.take(1 if whole else PLANES)

        def block(self, zz, cc):
            if self.kind == "both":
                return self.ref.at[pl.ds(2 * zz, 2), cc]
            at = 2 * zz + (x if self.kind == "own" else 1 - x)
            return self.ref.at[:, at, cc] if len(self.ref.shape) == 5 else self.ref.at[at, cc]

        def some(self, count):
            if self.kind == "both":
                return self.ref.at[pl.ds(0, count)]
            return self.ref.at[:, pl.ds(0, count), 0] if len(self.ref.shape) == 5 else self.ref.at[pl.ds(0, count), 0]

        def onward(self, n, step):
            here = self.block(n, c)
            rc(here, here, self.z_out, self.zs + n, dev(z + step, x, y, c)).start()

        def start(self):
            pl.when(z == 0)(lambda: self.onward(z, 2))
            pl.when(z == 3)(lambda: self.onward(z, -2))
            pl.when(z > 0)(lambda: self.onward(z, -1))
            pl.when(z < PLANES - 1)(lambda: self.onward(z, 1))
            mine = self.block(z, c)
            rc(mine, mine, self.c_out, self.sb if self.whole else self.sb + z, sib).start()

        def pump_step(self, n):
            here = self.block(n, c)

            @pl.when(n != z)
            def _():
                got(here, self.zs + n)
                pl.when(jnp.logical_and(z == 1, n > z))(lambda: self.onward(n, -1))
                pl.when(jnp.logical_and(z == 2, n < z))(lambda: self.onward(n, 1))
                rc(here, here, self.c_out, self.sb if self.whole else self.sb + n, sib).start()

        def pump_done(self):
            def sent(sem, count):
                rc(self.some(count), self.some(count), sem, 0, sib).wait_send()

            pending.append(lambda: sent(self.c_out, 4))
            pending.append(lambda: pl.when(outer)(lambda: sent(self.z_out, 2)))
            pending.append(lambda: pl.when(inner)(lambda: sent(self.z_out, 4)))

        def pump(self, where):
            @pl.when(where)
            def _():
                for k in range(1, PLANES):
                    self.pump_step(arrive[k])

            if where is outer:
                self.pump_done()

        def need_step(self, n):
            got(self.block(n, 1 - c), self.sb + n)

        def need(self):
            got(self.some(PLANES), self.sb)

    half_of = {}

    def place(ref, xx):
        return ref.at[:, 2 * z + xx, c] if len(ref.shape) == 5 else ref.at[2 * z + xx, c]

    def give_half(name, src, ref):
        i = take()
        half_of[name] = (ref, i[1])
        give(src, place(ref, x), i, xn)

    def have_half(name):
        ref, i = half_of[name]
        got(place(ref, 1 - x), i)

    wo_own = wo.at[own_block]
    i_oh = take()
    give(wo_h.at[:, half_cols(1 - x, 256)], wo.at[2 * (1 - x) + y, 2 * z + x, c], i_oh, xn)
    give_half("q", wq_h.at[:, :, half_cols(1 - x, 256)], wq)
    i_tok, i_tx, i_ty = take(), take(2), take(2)
    give(tok, xg.at[rows_of(c, 256)], i_tok, sib, away)
    give(tok.at[rows_of(y, 128)], xg.at[rows_of(2 * c + y, 128)], i_tx, dev(z, 1 - x, y, x), None, 0, c)
    it_oa, it_ob = Item(wo_own, "own"), Item(wo_own, "other")
    it_qa, it_s, it_qb = Item(wq, "own"), Item(small, "both"), Item(wq, "other")
    it_ua, it_ub, it_da, it_db = Item(wu, "own"), Item(wu, "other"), Item(wd, "own", False), Item(wd, "other", False)
    in_o()
    it_oa.start()
    in_q()
    it_qa.start()

    for done in in_small:
        done()

    def pick(shape, hit):
        return jnp.where(hit(iota(shape, 0), iota(shape, 1)), 1.0, 0.0)

    vec_sel = pick((64, 128), lambda k, l: l == c * 64 + k).astype(BF16)
    rpe_sel = pick((64, 128), lambda k, l: l == (1 - c) * 64 + 63 - k).astype(BF16)
    bias_sel = [pick((4, 128), lambda k, l, par=par: l == par * 64 + 4 * shard + k).astype(BF16) for par in range(2)]
    rpe_rows = dot(rpe_v[...], rpe_sel)
    level = jnp.full((1, 128), bk_v[0].astype(F32))
    top = jnp.concatenate(
        [dot(gain_v[...], vec_sel), dot(bias_v[...], vec_sel), level, jnp.zeros((1, 128), F32)], axis=0
    )

    def spread(values):
        rows = values.shape[1]
        even = (iota((rows, 1), 0) % 2) == 0
        wide = jnp.where(even, dot(values, bias_sel[0], TN), dot(values, bias_sel[1], TN))
        return dot(pick((rows // 2, rows), lambda k, l: l // 2 == k).astype(BF16), wide.astype(BF16))

    up_rows = spread(ub_v[...])
    qkv_rows = [spread(qb_v[p]) for p in range(3)]
    for half in range(2):
        mine = [rows[2 * half : 2 * half + 2] for rows in qkv_rows] + [jnp.zeros((2, 128), F32)]
        position = jnp.concatenate([rpe_rows[4 * half : 4 * half + 4], jnp.zeros((4, 128), F32)], axis=0)
        small_s[half] = jnp.concatenate(
            [top, position] + mine + [up_rows[8 * half : 8 * half + 8]], axis=0
        ).astype(BF16)
    small[2 * z + x, c] = small_s[x]
    give_half("s", small_s.at[1 - x], small)
    for h in range(4):
        sel = pick((32, 256), lambda k, l: l == h * 64 + c * 32 + k).astype(BF16)
        om_s[h * 64 : (h + 1) * 64] = dot(om_v[4 * x + h], sel, TN).astype(BF16)
    i_om = take()
    give(om_s, om2, i_om, sib)
    give_half("u", wu_h.at[:, half_cols(1 - x, 1024)], wu)

    same = (iota((256, 256), 0) // HEAD) == (iota((256, 256), 1) // HEAD)
    ones64[...] = jnp.where(same, 1.0, 0.0).astype(BF16)
    anti[...] = jnp.where(iota((128, 128), 0) + iota((128, 128), 1) == 127, 1.0, 0.0).astype(BF16)

    it_oa.pump(inner)
    got(wo.at[own_block, 2 * z + 1 - x, c], i_oh[1])
    it_ob.start()
    have_half("q")
    it_qb.start()
    it_qa.pump(inner)
    it_ob.pump(inner)
    it_qb.pump(inner)

    @pl.when(away)
    def _():
        for f in range(2):
            got(xg.at[rows_of(2 * f + y, 128)], i_tx[1] + f)

    for f in range(2):
        part = xg.at[rows_of(2 * f + y, 128)]
        give(part, part, i_ty, yn, away, f, f)
    it_oa.pump(outer)
    it_ob.pump(outer)
    i_oq, i_os = take(3), take(3)
    quarter = wo.at[own_block, :, c]
    give(quarter, quarter, i_oq, yn, None, 2, 2)
    give(quarter, quarter, i_oq, xn, None, 1, 1)
    give_half("d", wd_h.at[:, half_cols(1 - x, 1024)], wd)
    have_half("s")
    it_s.start()
    in_u()
    it_ua.start()
    it_s.pump(inner)
    it_qa.pump(outer)
    have_half("u")
    it_ub.start()
    in_d()
    it_da.start()
    it_qb.pump(outer)

    def other_quarter(slot):
        part = wo.at[plane_block[slot], :, c]
        got(part, i_oq[1] + slot)
        give(part, part, i_os, sib, None, slot, slot)
        return part

    it_s.pump(outer)

    it_s.need()
    for t in range(8):
        tile = small[t, 0].astype(F32) + small[t, 1].astype(F32)
        rows_v[0:8, t * 128 : (t + 1) * 128] = tile[0:8]
        rows_v[8:16, (7 - t) * 128 : (8 - t) * 128] = tile[8:16]
        total = tile[16:32] if t == 0 else total + tile[16:32]
    for r in range(6):
        rows_v[16:17, r * 128 : (r + 1) * 128] = total[r : r + 1]
    for r in range(8):
        rows_v[17:18, r * 128 : (r + 1) * 128] = total[8 + r : 9 + r]
    level = small[2 * z + c, 0][6:7].astype(F32)
    wide1 = jnp.where(level > 0.5, 1.0, 0.0)
    wide2 = jnp.where(level > 1.5, 1.0, 0.0)
    one_row = jnp.ones((1, 128), F32)

    def mask_row(bi):
        parts = [one_row if bj == bi else (wide1 if bj // 2 == bi // 2 else wide2) for bj in range(4)]
        return jnp.concatenate(parts, axis=1)

    masks = [mask_row(bi) for bi in range(4)]

    def coeff_body(h, carry):
        row = jnp.exp(rows_v[pl.ds(8 + h, 1), :])
        r0[h] = pltpu.roll(jnp.broadcast_to(row, (128, 1024)), 1, 1, stride=1, stride_axis=0)
        return carry

    lax.fori_loop(0, 4, coeff_body, 0)
    num[...] = jnp.zeros_like(num)
    den[...] = jnp.zeros_like(den)

    in_tok()
    pl.when(home)(lambda: got(xg.at[rows_of(1 - c, 256)], i_tok[1]))

    @pl.when(away)
    def _():
        for f in range(2):
            got(xg.at[rows_of(2 * f + 1 - y, 128)], i_ty[1] + f)

    other_quarter(2)
    part = other_quarter(1)
    give(part, part, i_oq, yn, None, 0, 0)
    it_ua.pump(inner)
    it_qa.need()
    it_qb.need()

    def qkv_body(p, carry):
        qkv[p] = (dot(xg[...], wq[p].reshape(1024, 256)) + rows_v[16:17, cols256(p)]).astype(BF16)
        return carry

    lax.fori_loop(0, 3, qkv_body, 0, unroll=True)
    got(om2, i_om[1])
    om2[...] = om2[...] + om_s[...]

    def feature_body(t, carry):
        wide = qkv[t].astype(F32)
        sums = split_dot(wide * wide, ones64[...])
        inverse = lax.rsqrt(sums * (1.0 / HEAD) + UNIT_EPS)
        units = wide * inverse
        logits = SCALE * split_dot(units, om2[...]) - 0.5 * SCALE * SCALE * (sums * inverse * inverse)
        value = jnp.exp(logits) * M ** (-0.5)
        ex[t] = value
        unit[t] = units
        inv[t] = inverse
        phi[t] = value.astype(BF16)
        return carry

    lax.fori_loop(0, 2, feature_body, 0, unroll=True)
    lane_head = iota((1, 128), 1) // HEAD

    def head_cols(h):
        return pl.ds(pl.multiple_of((h // 2) * 128, 128), 128), (lane_head == h % 2)

    def head_body(h, carry):
        cols, mine = head_cols(h)
        keep = jnp.where(mine, 1.0, 0.0).astype(BF16)
        scores = dot(phi[0, :, cols] * keep, phi[1, :, cols], NT)
        for b in range(4):
            coefficient = r0[h, :, 512 - 128 * b : 1024 - 128 * b] * masks[b]
            pp[h, b * 128 : (b + 1) * 128] = (scores[b * 128 : (b + 1) * 128] * coefficient).astype(BF16)
        right = jnp.concatenate([qkv[2, :, cols] * keep, jnp.broadcast_to(keep, (512, 128))], axis=1)
        both = dot(pp[h], right)
        num[:, cols] += both[:, :128]
        den[:, cols] += both[:, 128:]
        return carry

    i_at = [take(3), take(3)]

    def tile_of(ref, block, t):
        return ref.at[block, :, t * 128 : (t + 1) * 128]

    for t in range(2):
        lax.fori_loop(2 * t, 2 * t + 2, head_body, 0, unroll=True)
        cols = slice(t * 128, (t + 1) * 128)
        quo[:, cols] = num[:, cols] / den[:, cols]
        att[:, :, cols] = quo[:, cols].astype(BF16).reshape(4, 128, 128)
        for slot in range(3):
            give(tile_of(att, plane_block[slot], t), tile_of(attf, own_block, t), i_at[t], plane[slot], None, slot, slot)
    have_half("d")
    it_db.start()
    i_cot = take()
    give(cot.at[rows_of(y, 128)], cotb, i_cot, xs_dev, away)
    it_ub.pump(inner)
    other_quarter(0)
    it_oa.need()
    it_ob.need()

    def out_part(rows, block):
        return dot(rows, wo[block].reshape(1024, 256), NT)

    mixed_z = out_part(att[own_block], own_block)
    for slot in (2, 1, 0):
        got(wo.at[plane_block[slot], :, 1 - c], i_os[1] + slot)
        for t in range(2):
            got(tile_of(attf, plane_block[slot], t), i_at[t][1] + slot)
        mixed_z = mixed_z + out_part(attf[plane_block[slot]], plane_block[slot])

    def norm(values):
        centred = values - jnp.mean(values, axis=-1, keepdims=True)
        inverse = lax.rsqrt(jnp.mean(centred * centred, axis=-1, keepdims=True) + EPSILON)
        return centred * inverse, inverse

    residual = mixed_z + xg[rows_of(own_block, 128)].astype(F32) + rows_v[2:3, :]
    normed, inverse = norm(residual)
    first = normed * rows_v[0:1, :] + rows_v[3:4, :]
    fb[own_block] = first.astype(BF16)

    class RelayScatter:
        def __init__(self, ref, order, last_direct=False):
            self.ref, self.out, self.order, self.relayed = ref, s_sems.take(), order, 3 if last_direct else 4
            self.near, self.far, self.last = r_sems.take(4), r_sems.take(4), r_sems.take(4)

        def cols(self, k):
            return cols256(self.order[k])

        def part(self, k, value):
            cols = cols256(at_step(self.order, k))
            pb[:, :, cols] = value.astype(BF16).reshape(4, 128, 256)

            def out(block, slot, sem, device):
                rc(pb.at[block, :, cols], self.ref.at[slot, :, cols], self.out, sem + k, device).start()

            @pl.when(k < self.relayed)
            def _():
                even = k % 2 == 0
                beside = dev(z, jnp.where(even, 1 - x, x), jnp.where(even, y, 1 - y), c)
                out(plane_block[0], 1, self.far, beside)
                out(jnp.where(even, plane_block[1], plane_block[2]), 0, self.near, beside)

            @pl.when(k >= self.relayed)
            def _():
                out(plane_block[0], 1, self.far, dg)
                out(plane_block[1], 0, self.near, xn)
                out(plane_block[2], 2, self.last, yn)

        def pass_on(self, k):
            cols, slot = self.cols(k), 2 - k % 2
            part = self.ref.at[1, :, cols]
            got(part, self.far + k)
            part[...] = (part[...].astype(F32) + pb[plane_block[slot], :, cols].astype(F32)).astype(BF16)
            rc(part, self.ref.at[2, :, cols], self.out, self.last + k, plane[slot]).start()

        def total(self):
            for k in range(4):
                cols = self.cols(k)
                got(self.ref.at[0, :, cols], self.near + k)
                if k >= self.relayed:
                    got(self.ref.at[1, :, cols], self.far + k)
                got(self.ref.at[2, :, cols], self.last + k)
                value = pb[own_block, :, cols].astype(F32) + self.ref[0, :, cols].astype(F32)
                value = value + self.ref[2, :, cols].astype(F32)
                summed[:, cols] = value + self.ref[1, :, cols].astype(F32) if k >= self.relayed else value
            return summed[...]

        def sent(self):
            rc(self.ref, self.ref, self.out, 0, sib).wait_send()

    class Gather:
        def __init__(self, ref, order):
            self.ref, self.out, self.base, self.order = ref, s_sems.take(), r_sems.take(5), order
            pending.append(lambda: rc(ref.at[pl.ds(0, 3)], ref.at[pl.ds(0, 3)], self.out, 0, sib).wait_send())

        def start(self):
            for half in range(2):
                for slot in range(3):
                    mine = self.ref.at[own_block, :, self.half_cols(half)]
                    rc(mine, mine, self.out, self.base + 3 + half, plane[slot]).start()
            for k in range(1, 4):
                for slot in range(3):
                    mine = self.ref.at[own_block, :, cols256(self.order[k])]
                    rc(mine, mine, self.out, self.base + k - 1, plane[slot]).start()

        def half_cols(self, half):
            return pl.ds(pl.multiple_of(self.order[0] * 256 + half * 128, 128), 128)

        def need_half(self, half):
            got(self.ref.at[pl.ds(0, 3), :, self.half_cols(half)], self.base + 3 + half)

        def need(self, k):
            got(self.ref.at[pl.ds(0, 3), :, cols256(at_step(self.order, k))], self.base + k - 1)

    class RelayGather:
        def __init__(self, ref, order):
            self.ref, self.out, self.base, self.order = ref, s_sems.take(), r_sems.take(12), order
            pending.append(lambda: rc(ref.at[pl.ds(0, 3)], ref.at[pl.ds(0, 3)], self.out, 0, sib).wait_send())

        def piece(self, slot, n):
            return self.ref.at[plane_block[slot], :, cols256(n)]

        def start(self):
            for n in self.order:
                mine = self.ref.at[own_block, :, cols256(n)]
                for slot in (1, 2):
                    rc(mine, mine, self.out, self.base + slot * 4 + n, plane[slot]).start()

        def pass_on(self, k):
            n, slot = self.order[k], 1 + k % 2
            part = self.piece(slot, n)
            got(part, self.base + slot * 4 + n)
            rc(part, part, self.out, self.base + n, plane[3 - slot]).start()

        def need(self, k):
            n, slot = self.order[k], 2 - k % 2
            got(self.piece(slot, n), self.base + slot * 4 + n)
            got(self.piece(0, n), self.base + n)

    g_first = RelayGather(fb, range(4))
    g_first.start()
    it_da.pump(inner)
    g_first.pass_on(0)
    it_db.pump(inner)
    for k in range(1, 4):
        g_first.pass_on(k)
    it_ua.pump(outer)
    it_ub.pump(outer)
    fst[...] = first
    n1[...] = normed
    i1[...] = jnp.broadcast_to(inverse, (128, 128))

    def d_cols(ref, m):
        return ref[:, :, cols256(m)].reshape(512, 256)

    acc[...] = jnp.zeros_like(acc)
    it_ua.need()
    it_ub.need()

    for k in range(4):
        g_first.need(k)
        left = d_cols(fb, k)
        if k == 2:
            it_da.pump(outer)

        def hidden_part(j, carry, k=k, left=left):
            cols = cols256(j)
            acc[:, cols] += dot(left, wu[2 * k : 2 * k + 2, :, :, cols].reshape(256, 256))
            return carry

        lax.fori_loop(0, 4, hidden_part, 0)

    def hidden_body(n, carry):
        cols = cols256(n)
        pre = acc[:, cols] + rows_v[17:18, cols]
        cdf = 0.5 * (1.0 + lax.erf(pre * 0.7071067811865476))
        hid[:, cols] = (pre * cdf).astype(BF16)
        dgel[:, cols] = cdf + pre * (0.3989422804014327 * jnp.exp(-0.5 * pre * pre))
        return carry

    lax.fori_loop(0, 4, hidden_body, 0, unroll=2)
    sc_f = RelayScatter(rb_f, arrive, True)

    def down_part(k, carry):
        n = at_step(arrive, k)
        pl.when(outer)(lambda: it_db.pump_step(n))
        it_da.need_step(n)
        it_db.need_step(n)
        sc_f.part(k, dot(hid[...], wd[pl.ds(2 * n, 2)].reshape(256, 1024), NT))
        return carry

    lax.fori_loop(0, 4, down_part, 0)
    it_db.pump_done()
    for k in range(3):
        sc_f.pass_on(k)
    pl.when(away)(lambda: got(cotb, i_cot[1]))
    in_cot()
    upstream = cotb[...].astype(F32)

    def down(values):
        return jnp.sum(values, axis=0, keepdims=True)

    sd[5:6, :] = down(upstream)
    acc[...] = jnp.zeros_like(acc)
    second = fst[...] + sc_f.total() + rows_v[4:5, :]
    normed2, inverse2 = norm(second)

    def norm_back(upstream, normed, inverse, gain):
        scaled = upstream * gain
        mean = jnp.mean(scaled, axis=-1, keepdims=True)
        slope = jnp.mean(scaled * normed, axis=-1, keepdims=True)
        return inverse * (scaled - mean - normed * slope)

    err = norm_back(upstream, normed2, inverse2, rows_v[1:2, :])
    efb[own_block] = err.astype(BF16)
    g_ef = Gather(efb, leave)
    g_ef.start()
    mix_s[...] = (normed2 * rows_v[1:2, :] + rows_v[5:6, :]).astype(BF16)
    dr[...] = err
    sd[1:2, :] = down(upstream * normed2)
    sd[4:5, :] = down(err.astype(BF16).astype(F32))
    sc_f.sent()

    class Owner:
        def __init__(self, dst, pieces):
            self.dst, self.width = dst, 1024 // pieces
            self.ids = [take(2) for _ in range(pieces)]

        def part(self, half, n):
            return self.dst.at[rows_of(half, 128), n * self.width : (n + 1) * self.width]

        def start(self, src, n):
            cols = slice(n * self.width, (n + 1) * self.width)

            @pl.when(home)
            def _():
                self.dst[rows_of(y, 128), cols] = src[:, cols]

            give(src.at[:, cols], self.part(y, n), self.ids[n], yn, home, 1, 1)
            give(src.at[:, cols], self.part(y, n), self.ids[n], xs_dev, away, 0, 0)

        def pass_on(self, n):
            part = self.part(y, n)
            pl.when(away)(lambda: got(part, self.ids[n][1]))
            give(part, part, self.ids[n], yn, away, 1, 1)

        def need(self, n):
            got(self.part(1 - y, n), self.ids[n][1] + 1)

    own_mix = Owner(mixed_o, 1)
    own_mix.start(mix_s, 0)

    class Grad:
        def __init__(self, g, r, rz, cb, xs, xr, first):
            self.first = first
            self.g, self.r, self.rz, self.cb, self.xs, self.xr = g, r, rz, cb, xs, xr
            self.d, self.z, self.k, self.x = r_sems.take(4), r_sems.take(2), r_sems.take(2), take()
            self.mine = z // 2
            self.d_out, self.z_out = s_sems.take(), s_sems.take()
            self.width = r.shape[-1]

        def give(self, m):
            rc(self.g.at[m, :, 1 - c], self.r.at[m], self.d_out, self.d + m, sib).start()

        def pair_step(self, m):
            got(self.r.at[m], self.d + m)
            self.r[m] = (self.g[m, :, c].astype(F32) + self.r[m].astype(F32)).astype(BF16)
            far = jnp.abs(m - z)
            part = self.r.at[m]
            beside = dev(jnp.where(z == 0, 1, jnp.where(z == 1, 0, jnp.where(z == 2, 3, 2))), x, y, c)

            @pl.when(jnp.logical_or(outer if self.first else False, m == jnp.where(z == 1, 0, 3)) & (far == 1))
            def _():
                rc(part, self.rz.at[self.mine], self.z_out, self.z + self.mine, beside).start()

            for slot in range(2):
                @pl.when(outer & (far == 3 - slot))
                def _(slot=slot):
                    rc(part, self.cb.at[slot], self.z_out, self.k + slot, beside).start()

        def pair_half(self, m, half, i):
            part = self.r.at[m, half]
            got(part, i)
            part[...] = (self.g[m, half, c].astype(F32) + part[...].astype(F32)).astype(BF16)
            beside = dev(jnp.where(z == 0, 1, jnp.where(z == 1, 0, jnp.where(z == 2, 3, 2))), x, y, c)

            @pl.when(outer)
            def _():
                rc(part, self.cb.at[0, half], self.z_out, self.k, beside).start()

            @pl.when(inner)
            def _():
                rc(part, self.rz.at[self.mine, half], self.z_out, self.z + self.mine, beside).start()

        def near(self):
            for at, m in ((0, 1), (3, 2)):
                @pl.when(z == at)
                def _(at=at, m=m):
                    rc(self.r.at[m], self.rz.at[at // 2], self.z_out, self.z + at // 2, dev(m, x, y, c)).start()

        def relay(self, *slots):
            for at, blocks in ((1, (3, 2)), (2, (0, 1))):
                @pl.when(z == at)
                def _(at=at, blocks=blocks):
                    for slot in slots:
                        m = blocks[slot]
                        got(self.cb.at[slot], self.k + slot)
                        self.r[m] = (self.r[m].astype(F32) + self.cb[slot].astype(F32)).astype(BF16)
                        rc(self.r.at[m], self.rz.at[at // 2], self.z_out, self.z + at // 2, dev(m, x, y, c)).start()

        def run(self, make):
            def body(k, carry):
                m = at_step(leave, k)
                make(m)
                self.give(m)
                pl.when(k > 0)(lambda: self.pair_step(at_step(leave, k - 1)))
                return carry

            lax.fori_loop(0, PLANES, body, 0)
            self.pair_step(leave[3])

        def finish(self):
            total = fs.at[:, :, 0 : self.width]
            total[...] = self.r[z].astype(F32)
            for dz in (1, -1, 2, -2):
                @pl.when(valid(dz) if abs(dz) == 1 else z == (0 if dz > 0 else 3))
                def _(dz=dz):
                    slot = (z + dz) // 2
                    got(self.rz.at[slot], self.z + slot)
                    total[...] += self.rz[slot].astype(F32)
            self.xs[...] = fs[1 - x, :, 0 : self.width].astype(BF16)
            give(self.xs, self.xr, self.x, xn)

        def sent(self):
            rc(self.r, self.r, self.d_out, 0, sib).wait_send()
            part = self.r.at[pl.ds(0, 3)]
            rc(part, part, self.z_out, 0, sib).wait_send()

        def columns(self, out, half, value, at=0):
            if len(out.shape) == 3:
                for p in range(self.width // 256):
                    out[at + p, :, half_cols(half, 256)] = value[:, p * 256 : (p + 1) * 256].astype(BF16)
            else:
                out[:, half_cols(half, self.width)] = value.astype(BF16)

        def write_own(self, out, at=0):
            self.columns(out, x, fs[x, :, 0 : self.width], at)

        def write_other(self, out, at=0):
            got(self.xr, self.x[1])
            self.columns(out, 1 - x, self.xr[...], at)

    gr_d = Grad(g_d, r_d, rz_d, cb_d, xs_d, xr_d, True)
    gr_u = Grad(g_u, r_u, rz_u, cb_u, xs_u, xr_u, True)
    gr_o = Grad(g_o, r_o, rz_o, cb_o, xs_o, xr_o, False)
    gr_v = Grad(g_v, r_v, rz_v, cb_v, xs_v, xr_v, False)
    gr_k = Grad(g_k, r_k, rz_k, cb_k, xs_k, xr_k, False)

    def act_part(m):
        left = d_cols(efb, m)
        for j in range(4):
            cols = slice(j * 256, (j + 1) * 256)
            acc[:, cols] += dot(left, wd[pl.ds(2 * m, 2), :, :, cols].reshape(256, 256))

    i_half = r_sems.take(2)
    for half in range(2):
        g_ef.need_half(half)
        left = efb[:, :, g_ef.half_cols(half)].reshape(512, 128)
        g_d[leave[0], half] = dot(left, hid[...], TN).astype(BF16).reshape(2, 64, 1024)
        rc(g_d.at[leave[0], half, 1 - c], r_d.at[leave[0], half], gr_d.d_out, i_half + half, sib).start()
    for half in range(2):
        gr_d.pair_half(leave[0], half, i_half + half)
        if half == 0:
            act_part(leave[0])

    def down_grads(k, carry):
        m = at_step(leave, k)
        g_ef.need(k)
        g_d[m] = dot(d_cols(efb, m), hid[...], TN).astype(BF16).reshape(2, 2, 64, 1024)
        gr_d.give(m)
        act_part(m)
        gr_d.pair_step(m)
        return carry

    lax.fori_loop(1, PLANES, down_grads, 0)
    def du_body(n, carry):
        cols = cols256(n)
        du = (acc[:, cols] * dgel[:, cols]).astype(BF16)
        dub[:, cols] = du
        for zz in range(PLANES):
            st_b[zz, pl.ds(8 + n, 1), :] = down(du.astype(F32))
        return carry

    lax.fori_loop(0, 4, du_body, 0, unroll=2)
    sc_d = RelayScatter(rb_d, [jnp.int32(k) for k in range(4)])

    def back_part(n, carry):
        sc_d.part(n, dot(dub[...], wu[pl.ds(2 * n, 2)].reshape(256, 1024), NT))
        return carry

    lax.fori_loop(0, 4, back_part, 0)
    own_mix.pass_on(0)
    for m in range(4):
        xt[m * 256 : (m + 1) * 256] = xg[:, m * 256 : (m + 1) * 256].T

    def transpose_body(h, carry):
        ppt[h] = pp[h].T
        return carry
    gr_d.relay(0)
    sc_d.pass_on(0)
    sc_d.pass_on(1)

    def make_up(m):
        g_u[m] = dot(d_cols(fb, m), dub[...], TN).astype(BF16).reshape(2, 2, 64, 1024)

    gr_u.run(make_up)
    sc_d.pass_on(2)
    sc_d.pass_on(3)
    lax.fori_loop(0, 4, transpose_body, 0)
    gr_d.relay(1)
    dfirst = dr[...] + sc_d.total()
    back = norm_back(dfirst, n1[...], i1[:, 0:1], rows_v[0:1, :])
    dz = back.astype(BF16)
    dzb[own_block] = dz

    i_da = take(3)

    def attention_grad(block):
        dat_s[block] = dot(dz, wo[block].reshape(1024, 256)).astype(BF16)

    for slot in range(3):
        attention_grad(plane_block[slot])
        give(dat_s.at[plane_block[slot]], dat.at[own_block], i_da, plane[slot], None, slot, slot)
    attention_grad(own_block)
    dat[own_block] = dat_s[own_block]
    g_dz = RelayGather(dzb, leave)
    g_dz.start()
    sd[0:1, :] = down(dfirst * n1[...])
    sd[3:4, :] = down(dfirst)
    sd[2:3, :] = down(dz.astype(F32))
    sd[6:8, :] = jnp.zeros((2, 1024), F32)
    class Total:
        def __init__(self, ref, work, recv):
            self.ref, self.work, self.recv = ref, work, recv
            self.c, self.z = take(), take(PLANES)

        def pair(self):
            give(self.ref, self.work, self.c, sib)

        def over_planes(self):
            got(self.work, self.c[1])
            self.work[...] = self.ref[...] + self.work[...]
            for zz in range(PLANES):
                give(self.work.at[zz], self.recv.at[z], self.z, dev(zz, x, y, c), z != zz, zz, z)

        def finish(self):
            for zz in range(PLANES):
                @pl.when(z != zz)
                def _(zz=zz):
                    got(self.recv.at[zz], self.z[1] + zz)

                @pl.when(z == zz)
                def _(zz=zz):
                    self.recv[zz] = self.work[zz]
            return self.recv[0] + self.recv[1] + self.recv[2] + self.recv[3]

    early, late = Total(st_a, work_a, recv_a), Total(st_b, work_b, recv_b)
    i_swap = take()
    i_sd = take(3)
    for k, device in enumerate(plane):
        give(sd, sd_r.at[k], i_sd, device, None, k, k)
    dr[...] = back
    sc_d.sent()
    dph[...] = jnp.zeros_like(dph)
    dvv[...] = jnp.zeros_like(dvv)
    gr_u.relay(0)
    for slot in range(3):
        got(dat.at[plane_block[slot]], i_da[1] + slot)

    dattn = dat[...].reshape(512, 256).astype(F32)
    recip = 1.0 / den[...]
    dn[...] = (dattn * recip).astype(BF16)
    dsum = split_dot(dattn * quo[...], ones64[...])
    dd[...] = ((-dsum * recip).astype(BF16).astype(F32) * (1.0 / HEAD)).astype(BF16)

    def value_back(h, carry):
        cols, mine = head_cols(h)
        keep = jnp.where(mine, 1.0, 0.0).astype(BF16)
        dvv[:, cols] += dot(ppt[h], dn[:, cols] * keep)
        return carry

    lax.fori_loop(0, 4, value_back, 0, unroll=True)
    dqkv[2] = dvv[...].astype(BF16)

    def x_rows(m):
        return xt[rows_of(m, 256)]

    def make_v(m):
        g_v[m] = dot(x_rows(m), dqkv[2]).astype(BF16).reshape(2, 2, 64, 256)

    def head_back(h, carry):
        cols, mine = head_cols(h)
        keep = jnp.where(mine, 1.0, 0.0).astype(BF16)
        left = jnp.concatenate([dn[:, cols] * keep, dd[:, cols] * keep], axis=1)
        right = jnp.concatenate([qkv[2, :, cols], jnp.ones((512, 128), BF16)], axis=1)
        grad_p = dot(left, right, NT)
        for b in range(4):
            rows = slice(b * 128, (b + 1) * 128)
            coefficient = r0[h, :, 512 - 128 * b : 1024 - 128 * b] * masks[b]
            part = grad_p[rows]
            ds_[rows] = (part * coefficient).astype(BF16)
            gg[h, rows] = (part * pp[h, rows].astype(F32)).astype(BF16)
        dph[0, :, cols] += dot(ds_[...], phi[1, :, cols] * keep)
        dph[1, :, cols] += dot(ds_[...], phi[0, :, cols] * keep, TN)
        return carry

    lax.fori_loop(0, 4, head_back, 0, unroll=True)
    gr_u.relay(1)
    g_dz.pass_on(0)
    g_dz.pass_on(1)
    gr_v.run(make_v)
    g_dz.pass_on(2)
    g_dz.pass_on(3)

    def feature_back_body(t, carry):
        dlog = (dph[t] * ex[t]).astype(BF16)
        units = unit[t]
        dunit = SCALE * dot(dlog, om2[...], NT) - SCALE * SCALE * dot(dlog, ones64[...]) * units
        mean = split_dot(dunit * units, ones64[...]) * (1.0 / HEAD)
        dqkv[t] = (inv[t] * (dunit - units * mean)).astype(BF16)
        return carry

    lax.fori_loop(0, 2, feature_back_body, 0, unroll=True)
    class Return:
        def __init__(self, ref):
            self.ref, self.out, self.base, self.last = ref, s_sems.take(), r_sems.take(4), take(4)
            pending.append(lambda: pl.when(home)(lambda: rc(ref.at[0:3], ref.at[0:3], self.out, 0, sib).wait_send()))
            pending.append(lambda: pl.when(away)(lambda: rc(ref, ref, self.out, 0, sib).wait_send()))

        def part(self, n, value):
            cols = cols256(n)
            for b in range(4):
                rows = value[b * 128 : (b + 1) * 128]
                pb[b, :, cols] = jnp.where(own_block == b, rows + dr[:, cols], rows).astype(BF16)
                here = home & (c == b // 2) & (y == b % 2)

                @pl.when(here)
                def _(b=b):
                    self.ref[own_block, :, cols] = pb[b, :, cols]

                @pl.when(jnp.logical_not(here))
                def _(b=b):
                    there = self.ref.at[own_block, :, cols]
                    rc(pb.at[b, :, cols], there, self.out, self.base + n, dev(z, c, b % 2, b // 2)).start()

        def column(self, n):
            cols = slice(n * 256, (n + 1) * 256)
            pl.when(home)(lambda: got(self.ref.at[0:3, :, cols], self.base + n))
            pl.when(away)(lambda: got(self.ref.at[0:4, :, cols], self.base + n))
            value = self.ref[0, :, cols].astype(F32)
            for slot in range(1, 4):
                value = value + self.ref[slot, :, cols].astype(F32)
            mine = gt_r.at[rows_of(y, 128), cols]
            mine[...] = value.astype(BF16)
            give(mine, mine, self.last, yn, None, n, n)

        def need(self, n):
            cols = slice(n * 256, (n + 1) * 256)
            rows = rows_of(1 - y, 128)
            got(gt_r.at[rows, cols], self.last[1] + n)

    sc_i = Return(rb_i)

    def input_part(n, carry):
        value = jnp.zeros((512, 256), F32)
        for p in range(3):
            value = value + dot(dqkv[p], wq[p, pl.ds(2 * n, 2)].reshape(256, 256), NT)
        sc_i.part(n, value)
        return carry

    lax.fori_loop(0, 4, input_part, 0, unroll=2)

    def make_k(m):
        for p in range(2):
            g_k[m, :, :, :, p * 256 : (p + 1) * 256] = (
                dot(x_rows(m), dqkv[p]).astype(BF16).reshape(2, 2, 64, 256)
            )

    gr_k.run(make_k)

    def make_out(m):
        g_o[m] = dot(d_cols(dzb, m), att[...].reshape(512, 256), TN).astype(BF16).reshape(2, 2, 64, 256)

    for k in range(4):
        g_dz.need(k)
    gr_o.run(make_out)
    gr_v.near()
    gr_k.near()
    gr_v.relay(0, 1)
    for k in range(3):
        got(sd_r.at[k], i_sd[1] + k)
    sums = sd[...] + sd_r[0] + sd_r[1] + sd_r[2]
    for zz in range(PLANES):
        st_a[zz] = sums[:, zz * 256 : (zz + 1) * 256]
    early.pair()
    gr_d.finish()
    gr_d.write_own(gd_o)

    def diagonal_body(h, carry):
        sums = jnp.zeros((1, 1024), F32)
        for b in range(4):
            flipped = dot(anti[...], gg[h, (3 - b) * 128 : (4 - b) * 128])
            wide = jnp.concatenate([flipped, jnp.zeros((128, 128), F32)], axis=1)
            line = down(pltpu.roll(wide, 0, 1, stride=1, stride_axis=0))
            pieces = [line]
            if b > 0:
                pieces = [jnp.zeros((1, 128 * b), F32)] + pieces
            if b < 3:
                pieces = pieces + [jnp.zeros((1, 384 - 128 * b), F32)]
            sums = sums + jnp.concatenate(pieces, axis=1)
        for zz in range(PLANES):
            st_b[zz, pl.ds(h, 1), :] = sums[:, (3 - zz) * 256 : (4 - zz) * 256]
        return carry

    lax.fori_loop(0, 4, diagonal_body, 0)
    for p in range(3):
        line = down(dqkv[p].astype(F32))
        for zz in range(PLANES):
            st_b[zz, 12 + p : 13 + p, :] = line
    for zz in range(PLANES):
        st_b[zz, 4:8, :] = jnp.zeros((4, 256), F32)
        st_b[zz, 15:16, :] = jnp.zeros((1, 256), F32)
    late.pair()
    gr_k.relay(0)
    early.over_planes()
    late.over_planes()
    gr_o.near()
    gr_k.relay(1)
    outs = []
    own_mix.need(0)
    outs.append(bring(mixed_o, mixed_h))
    gr_o.relay(0, 1)
    gr_u.finish()
    gr_u.write_own(gu_o)
    sc_i.column(0)
    sc_i.column(1)
    sc_i.column(2)
    sc_i.column(3)
    gr_d.write_other(gd_o)
    outs.append(bring(gd_o, gd_h))
    gr_v.finish()
    gr_v.write_own(gq_o, 2)
    gr_u.write_other(gu_o)
    outs.append(bring(gu_o, gu_h))

    def exact(left, right):
        return lax.dot_general(left, right, NN, precision=lax.Precision.HIGHEST, preferred_element_type=F32)

    sd_r[0, :, 0:256] = early.finish()
    mine = sd_r[0, :, pl.ds(pl.multiple_of(x * 128, 128), 128)]
    own = exact(mine, pick((128, 64), lambda k, l: k == c * 64 + l))
    ggain_o[...] = own[0:2]
    gbias_o[...] = own[2:6]
    outs.append(bring(ggain_o, ggain_h))
    outs.append(bring(gbias_o, gbias_h))
    swap[0] = late.finish()
    give(swap.at[0], swap.at[1], i_swap, xn)
    gr_k.finish()
    gr_k.write_own(gq_o)
    gr_o.finish()
    gr_o.write_own(go_o)
    for n in range(4):
        sc_i.need(n)
    outs.append(bring(gt_r, gtok_h))
    got(swap.at[1], i_swap[1])
    tile = pl.ds(pl.multiple_of((1 - x) * 128, 128), 128)
    ours, theirs = swap[0, 0:4, tile], swap[1, 0:4, tile]
    lines = jnp.concatenate([jnp.where(x == 0, ours, theirs), jnp.where(x == 0, theirs, ours)], axis=0)
    grpe_o[...] = exact(lines, pick((128, 64), lambda k, l: k == (1 - c) * 64 + 63 - l))
    outs.append(bring(grpe_o, grpe_h))
    ours, theirs = swap[0, 8:16], swap[1, 8:16]
    rest = [jnp.where(x == half, ours, theirs) for half in range(2)]
    lines = [rest[half][4 + p : 5 + p, t * 128 : (t + 1) * 128] for p in range(3) for half in range(2) for t in range(2)]
    lines += [
        rest[half][t // 2 : t // 2 + 1, (t % 2) * 128 : (t % 2 + 1) * 128] for half in range(2) for t in range(8)
    ]
    lines = jnp.concatenate(lines + [jnp.zeros((4, 128), F32)], axis=0)
    found = jnp.zeros((4, 56), F32)
    for par in range(2):
        hit = pick((4, 128), lambda k, l: l == par * 64 + 4 * shard + k)
        values = lax.dot_general(hit, lines, NT, precision=lax.Precision.HIGHEST, preferred_element_type=F32)
        found = found + exact(values, pick((32, 56), lambda k, l: (l // 2 == k) & (l % 2 == par)))
    for p in range(3):
        gqb_o[p] = found[:, 8 * p : 8 * p + 8]
    gub_o[...] = found[:, 24:56]
    outs.append(bring(gqb_o, gqb_h))
    outs.append(bring(gub_o, gub_h))
    gr_v.write_other(gq_o, 2)
    gr_k.write_other(gq_o)
    outs.append(bring(gq_o, gq_h))
    gr_o.write_other(go_o)
    outs.append(bring(go_o, go_h))
    for gr in (gr_d, gr_u, gr_o, gr_v, gr_k):
        gr.sent()
    assert (s_sems.used, r_sems.used, locals_.used) == (SENDS, RECEIVES, 24), (s_sems.used, r_sems.used, locals_.used)
    for done in pending + outs:
        done()


def copy_kernel(*refs):
    count = (len(refs) - 1) // 4
    sem = refs[-1]
    given, held, wide, kept = (refs[k * count : (k + 1) * count] for k in (0, 2, 3, 1))
    ins = [pltpu.make_async_copy(given[i], held[i], sem.at[0, i]) for i in range(count)]
    for copy in ins:
        copy.start()
    outs = []
    for i in range(count):
        ins[i].wait()
        if held[i].dtype == kept[i].dtype:
            outs.append(pltpu.make_async_copy(held[i], kept[i], sem.at[1, i]))
        else:
            wide[i][...] = held[i][...].astype(kept[i].dtype)
            outs.append(pltpu.make_async_copy(wide[i], kept[i], sem.at[1, i]))
        outs[-1].start()
    for copy in outs:
        copy.wait()


def fast_local(
    tokens, qkv_weight, qkv_bias, out_weight, norm_gains, row_biases, up_weight, up_bias, down_weight, rpe_bias, omega,
    bucket, cotangent,
):
    def vm(shape, dtype=BF16):
        return pltpu.VMEM(shape, dtype)

    widths = (512, 256, 256, 1024, 1024)
    scratch = [vm((3, 4, 8)), vm((2, 64)), vm((4, 64)), vm((4, 32)), vm((8, 64)), vm((8, 32, 64))]
    scratch += [pltpu.SMEM((1,), jnp.int32), vm((2, 32, 128)), vm((256, 256))]
    results = (
        ((256, 1024), BF16), ((256, 1024), F32), ((3, 64, 512), F32), ((3, 4, 8), F32), ((64, 512), F32), ((2, 64), F32),
        ((4, 64), F32), ((64, 2048), F32), ((4, 32), F32), ((64, 2048), F32), ((8, 64), F32),
    )
    large = ((256, 1024), (3, 64, 512), (64, 512), (64, 2048))
    sent = tuple((shape, BF16 if shape in large else dtype) for shape, dtype in results)
    scratch += [vm(*result) for i, result in enumerate(sent) if i != 1]
    scratch += [vm((3, 8, 2, 64, 256)), vm((4, 8, 2, 64, 256)), vm((8, 2, 64, 1024)), vm((8, 2, 64, 1024))]
    scratch += [vm((8, 2, 32, 128)), vm((256, 256)), vm((512, 1024)), vm((128, 1024))]
    scratch += [vm((3, 512, 256)), vm((2, 512, 256))] + [vm((2, 512, 256), F32)] * 3
    scratch += [vm((4, 128, 1024), F32), vm((4, 512, 512))] + [vm((512, 256), F32)] * 3 + [vm((4, 128, 256))] * 2
    scratch += [vm((4, 128, 1024))] + [vm((3, 128, 1024))] * 2 + [vm((4, 128, 1024))]
    scratch += [vm((4, 128, 1024)), vm((512, 1024)), vm((512, 1024), F32)]
    scratch += [vm((4, 128, 1024)), vm((512, 1024)), vm((4, 128, 1024)), vm((512, 1024), F32)]
    scratch += [vm((128, 1024), F32)] * 2 + [vm((128, 128), F32)] + [vm((128, 1024), F32)] * 2
    scratch += [vm((4, 128, 256))] * 2 + [vm((128, 128)), vm((256, 256)), vm((24, 1024), F32)]
    scratch += [vm((512, 256))] * 2 + [vm((512, 512)), vm((4, 512, 512)), vm((2, 512, 256), F32), vm((512, 256), F32)]
    scratch += [vm((3, 512, 256)), vm((1024, 512)), vm((4, 512, 512))]
    scratch += [vm((4, 2, 2, 64, n)) for n in widths]
    scratch += [vm((4, 2, 64, n)) for n in widths] + [vm((2, 2, 64, n)) for n in widths] * 2
    scratch += [vm((2, 64, 1024), F32)] + [vm((64, n)) for n in widths] * 2
    scratch += [vm((8, 1024), F32), vm((3, 8, 1024), F32)] + [vm((4, 8, 256), F32), vm((4, 16, 256), F32)] * 3
    scratch += [vm((2, 16, 256), F32)]
    scratch += [vm((128, 1024)), vm((256, 1024))]
    scratch += [pltpu.SemaphoreType.DMA((SENDS,)), pltpu.SemaphoreType.DMA((RECEIVES,)), pltpu.SemaphoreType.DMA((24,))]

    shapes = tuple(jax.ShapeDtypeStruct(*result) for result in results)
    narrow = tuple(jax.ShapeDtypeStruct(*result) for result in sent)
    anywhere = pl.BlockSpec(memory_space=pl.ANY)
    made = pl.pallas_call(
        layer_kernel,
        out_shape=narrow,
        in_specs=[anywhere] * 13,
        out_specs=(anywhere,) * len(shapes),
        scratch_shapes=scratch,
        compiler_params=pltpu.CompilerParams(
            collective_id=0, has_side_effects=True, vmem_limit_bytes=63 * 2**20
        ),
        name="layer",
    )(
        tokens, qkv_weight.transpose(1, 0, 2), qkv_bias.transpose(0, 2, 1), out_weight.T, norm_gains, row_biases, up_weight,
        up_bias.T, down_weight.T, rpe_bias, omega.transpose(0, 2, 1), bucket, cotangent,
    )
    mixed, gtok, gq, gqb, go, ggain, gbias, gu, gub, gd, grpe = pl.pallas_call(
        copy_kernel,
        out_shape=shapes,
        in_specs=[anywhere] * len(shapes),
        out_specs=(anywhere,) * len(shapes),
        scratch_shapes=[vm(*result) for result in sent + results] + [pltpu.SemaphoreType.DMA((2, len(shapes)))],
        compiler_params=pltpu.CompilerParams(vmem_limit_bytes=63 * 2**20),
        name="results",
    )(*made)
    return (
        mixed, gtok, gq.transpose(1, 0, 2), gqb.transpose(0, 2, 1), go.T, ggain, gbias, gu, gub.T, gd.T, grpe,
    )


def solution(mesh):
    sizes = (mesh.shape["dp"], mesh.shape["heads"], mesh.shape["feat"])
    return jax.shard_map(
        fast_local if sizes == (2 * PLANES, 2, 2) else local,
        mesh=mesh,
        in_specs=(
            P(("dp", "feat"), None),
            P(("dp", "feat"), None, "heads"),
            P(None, "heads", ("dp", "feat")),
            P("heads", ("dp", "feat")),
            P(None, ("dp", "feat")),
            P(None, ("dp", "feat")),
            P(("dp", "feat"), "heads"),
            P("heads", ("dp", "feat")),
            P("heads", ("dp", "feat")),
            P("heads", ("dp", "feat")),
            P("heads", None, "feat"),
            P("dp"),
            P(("dp", "feat"), None),
        ),
        out_specs=(
            P(("dp", "feat"), None),
            P(("dp", "feat"), None),
            P(("dp", "feat"), None, "heads"),
            P(None, "heads", ("dp", "feat")),
            P("heads", ("dp", "feat")),
            P(None, ("dp", "feat")),
            P(None, ("dp", "feat")),
            P(("dp", "feat"), "heads"),
            P("heads", ("dp", "feat")),
            P("heads", ("dp", "feat")),
            P("heads", ("dp", "feat")),
        ),
        check_vma=False,
    )
```
